32 devices in a mesh: groups: 2 (over x), dp: 16 (over z, y, core).
Axes of the slice: x: 2, y: 2, z: 4, core: 2. Of those that a mesh axis runs over, the one named last changes fastest.
Arguments:
- hidden: bfloat16 [16384, 5120], P(('groups', 'dp')), parts along dimension 0, may hold values from -6 to 6
- queries: bfloat16 [16384, 2560], P(('groups', 'dp')), parts along dimension 0, may hold values from -84 to 84
- route: int32 [16384], P(('groups', 'dp')), parts along dimension 0, may hold values from 0 to 16383, as said below
- positions: int32 [32768], P(('groups', 'dp')), parts along dimension 0, may hold values from 0 to 383, as said below
- key_matrix: bfloat16 [5120, 512], P('dp'), may hold values from -0.078125 to 0.078125
- value_matrix: bfloat16 [5120, 512], P('dp'), may hold values from -0.078125 to 0.078125
- key_projection_bias: bfloat16 [512], replicated, may hold values from -3 to 3
- value_projection_bias: bfloat16 [512], replicated, may hold values from -3 to 3
Outputs:
- attended: bfloat16 [16384, 2560], P(('groups', 'dp')), parts along dimension 0
The draws below stay inside these ranges and needn't reach their ends.
There are 2 independent parts, one for each index of `groups`. The reference program is written for one: setup_inputs(seed, part) draws one part's arguments, and reference() takes and returns one part's arrays. A program takes and returns all parts, laid end to end along the dimension named above; an argument that names none is the same for every part. Nothing has to cross between parts.
Inputs may be any that keep to these rules, and one draw needn't show every extreme that they name: `route`: all values differ. Device r of dp owns slots r * 1024 to (r + 1) * 1024 - 1, in blocks of 512, and receives exactly 512 tokens. The tokens of one device go to one device at most 34 at a time, and this is reached. A rollout fills consecutive slots of one block with positions 0, 1, 2 and so on; the slots that route names are the live ones; a block's unnamed slots come before its rollouts and hold 0. Some block holds a rollout of exactly 384 tokens.
All inputs are finite; a program needn't handle non-finite values.
Results may differ from the reference program's by a relative error of at most 0.012.
Values may be sent and summed in bfloat16 or wider, within the bound.
No kernel may reach another device: no remote copies, remote signals or barrier semaphores. Data moves between devices by JAX's collectives and lax.ppermute only.
A program may use at most 128 MiB of HBM per device.

```python
import math
import jax
import jax.numpy as jnp
from jax import lax

MODEL_WIDTH = 5120
QUERY_HEADS = 20
KEY_VALUE_HEADS = 4
HEAD_SIZE = 128
BLOCK_SLOTS = 512
TOK_DEV = 512
TOKENS = 8192
SLOTS = 1024


def plan_layout(key):
    ranks = TOKENS // TOK_DEV
    share = TOK_DEV // ranks
    block_list = SLOTS // BLOCK_SLOTS
    streams = jax.random.split(key, 5)
    coins = jax.random.randint(streams[0], (ranks, ranks), 0, 2)
    coins = coins.at[0, ranks - 1].set(0).at[ranks - 1, 0].set(0).at[0, 0].set(1).at[ranks - 1, ranks - 1].set(1)
    before = jnp.roll(coins, 1, axis=0)
    counts = share + coins - jnp.roll(coins, 1, axis=1) - before + jnp.roll(before, 1, axis=1)
    lifts = jax.random.randint(streams[1], (ranks, block_list), 0, BLOCK_SLOTS // 4 + 1)
    lifts = lifts.at[0, 0].set(BLOCK_SLOTS // 4).at[0, 1].set(0)
    fills = BLOCK_SLOTS // 2 + lifts - jnp.roll(lifts, -1, axis=1)
    inner = jnp.arange(BLOCK_SLOTS, dtype=jnp.int32)[None, None, :]
    first = BLOCK_SLOTS - fills[:, :, None]
    live = inner >= first
    cuts = jax.random.randint(streams[2], (ranks, block_list, BLOCK_SLOTS), 0, BLOCK_SLOTS // 4) == 0
    cuts = cuts.at[0, 0, :].set(False)
    fresh = (inner == first) | cuts & live | jnp.logical_not(live)
    begins = lax.cummax(jnp.where(fresh, inner, 0), axis=2)
    positions = (inner - begins).reshape(ranks * SLOTS).astype(jnp.int32)
    bounds = jnp.cumsum(counts, axis=0)
    slot_index = jnp.arange(TOK_DEV, dtype=jnp.int32)
    owners = jnp.sum((bounds.T[:, None, :] <= slot_index[None, :, None]).astype(jnp.int32), axis=2)
    owners = jax.random.permutation(streams[3], owners, axis=1, independent=True)
    live_flat = live.reshape(ranks, SLOTS).astype(jnp.int32)
    live_slots = jnp.argsort(1 - live_flat, axis=1, stable=True)[:, :TOK_DEV].astype(jnp.int32)
    global_slots = (jnp.arange(ranks, dtype=jnp.int32)[:, None] * SLOTS + live_slots).reshape(-1)
    whole = ranks * TOK_DEV
    shuffle = jax.random.permutation(streams[4], whole).astype(jnp.int32)
    order = jnp.argsort(owners.reshape(-1) * whole + shuffle)
    route = global_slots[order].astype(jnp.int32)
    return (route, positions)


def draw_route(key, part):
    return plan_layout(key)[0]


def draw_positions(key, part):
    return plan_layout(key)[1]


def draw_queries(key, part):
    key = jax.random.fold_in(key, 7)
    first = jax.random.fold_in(key, 0)
    shape = (TOKENS, QUERY_HEADS * HEAD_SIZE)
    base = jnp.clip(jax.random.normal(first, shape, jnp.float32), -4.0, 4.0)
    return base.astype(jnp.bfloat16)


def shard_levels(key, shape, cuts, smallest, high):
    def one(axis_at, shards_of):
        steps = jax.random.uniform(jax.random.fold_in(jax.random.fold_in(key, 6), axis_at), (shards_of,), jnp.float32, smallest / len(cuts), high / len(cuts))
        return jnp.repeat(jnp.exp(steps), shape[axis_at] // shards_of).reshape((-1,) + (1,) * (len(shape) - axis_at - 1))

    factor_of = one(*cuts[0])
    for cut in cuts[1:]:
        factor_of = factor_of * one(*cut)
    return factor_of


def gaussian(rng, shape, spread, most, shards=(), kind=jnp.bfloat16):
    result = spread * jax.random.normal(rng, shape, jnp.float32)
    if shards:
        result = result * shard_levels(rng, shape, shards, -0.22, 0.18)
    return jnp.clip(result, -most, most).astype(kind)


def setup_inputs(seed: int = 0, part: int = 0) -> dict:
    splits = jax.random.split(jax.random.key(seed), 9)
    part_keys = jax.random.split(jax.random.fold_in(splits[8], part), 9)
    return {
        "hidden": gaussian(part_keys[0], (TOKENS, MODEL_WIDTH), 1.0, 6.0, ((0, 16),)),
        "queries": draw_queries(jax.random.fold_in(jax.random.fold_in(splits[8], part), 71), part),
        "route": draw_route(jax.random.fold_in(jax.random.fold_in(splits[8], part), 71), part),
        "positions": draw_positions(jax.random.fold_in(jax.random.fold_in(splits[8], part), 71), part),
        "key_matrix": gaussian(splits[4], (MODEL_WIDTH, KEY_VALUE_HEADS * HEAD_SIZE), MODEL_WIDTH ** -0.5, 0.078125, ((0, 16),)),
        "value_matrix": gaussian(splits[5], (MODEL_WIDTH, KEY_VALUE_HEADS * HEAD_SIZE), MODEL_WIDTH ** -0.5, 0.078125, ((0, 16),)),
        "key_projection_bias": gaussian(splits[6], (KEY_VALUE_HEADS * HEAD_SIZE,), 0.5, 3.0),
        "value_projection_bias": gaussian(splits[7], (KEY_VALUE_HEADS * HEAD_SIZE,), 0.5, 3.0),
    }


def apply_rotary(rows, slot_offset, heads):
    block_count = rows.shape[0]
    half = HEAD_SIZE // 2
    frequency = 1000000.0 ** (-(jnp.arange(half, dtype=jnp.float32) * 2.0 / HEAD_SIZE))
    angle = slot_offset.astype(jnp.float32)[:, None] * frequency[None, :]
    cosine = jnp.cos(angle)[:, None, :]
    sine = jnp.sin(angle)[:, None, :]
    grid = rows.astype(jnp.float32).reshape(block_count, heads, HEAD_SIZE)
    first = grid[:, :, :half]
    second = grid[:, :, half:]
    turned = jnp.concatenate([first * cosine - second * sine, second * cosine + first * sine], axis=2)
    return turned.reshape(block_count, heads * HEAD_SIZE).astype(jnp.bfloat16)

def causal_block_attention(pieces):
    query_tile_rows, key_tile_rows, value_tile_rows, spot_block = pieces
    block_count = query_tile_rows.shape[0]
    head_groups = QUERY_HEADS // KEY_VALUE_HEADS
    query_block_grid = query_tile_rows.astype(jnp.float32).reshape(block_count, KEY_VALUE_HEADS, head_groups, HEAD_SIZE)
    key_block_grid = key_tile_rows.astype(jnp.float32).reshape(block_count, KEY_VALUE_HEADS, HEAD_SIZE)
    value_block_grid = value_tile_rows.astype(jnp.float32).reshape(block_count, KEY_VALUE_HEADS, HEAD_SIZE)
    scores = jnp.einsum('qhgd,khd->hgqk', query_block_grid, key_block_grid) / math.sqrt(HEAD_SIZE)
    inner = jnp.arange(block_count, dtype=jnp.int32)
    visible = (inner[None, :] <= inner[:, None]) & (inner[None, :] >= inner[:, None] - spot_block[:, None])
    scores = jnp.where(visible, scores, -jnp.inf)
    top = lax.optimization_barrier(jnp.max(scores, axis=3, keepdims=True))
    weights = jnp.exp(scores - top)
    totals = lax.optimization_barrier(jnp.sum(weights, axis=3))
    probs = weights.astype(jnp.bfloat16)
    mixed = jnp.einsum('hgqk,khd->qhgd', probs.astype(jnp.float32), value_block_grid)
    mixed = mixed / jnp.transpose(totals, (2, 0, 1))[:, :, :, None]
    return mixed.reshape(block_count, QUERY_HEADS * HEAD_SIZE).astype(jnp.bfloat16)

def reference(hidden, queries, route, positions, key_matrix, value_matrix, key_projection_bias, value_projection_bias):
    key_rows = (jnp.dot(hidden, key_matrix, preferred_element_type=jnp.float32) + key_projection_bias.astype(jnp.float32)).astype(jnp.bfloat16)
    value_rows = (jnp.dot(hidden, value_matrix, preferred_element_type=jnp.float32) + value_projection_bias.astype(jnp.float32)).astype(jnp.bfloat16)
    slot_offset = positions[route]
    turned_queries = apply_rotary(queries, slot_offset, QUERY_HEADS)
    rotated_key_rows = apply_rotary(key_rows, slot_offset, KEY_VALUE_HEADS)
    overall_slot_count = positions.shape[0]
    query_slot_rows = jnp.zeros((overall_slot_count, QUERY_HEADS * HEAD_SIZE), jnp.bfloat16).at[route].set(turned_queries)
    key_slot_rows = jnp.zeros((overall_slot_count, KEY_VALUE_HEADS * HEAD_SIZE), jnp.bfloat16).at[route].set(rotated_key_rows)
    value_slot_rows = jnp.zeros((overall_slot_count, KEY_VALUE_HEADS * HEAD_SIZE), jnp.bfloat16).at[route].set(value_rows)
    block_list = overall_slot_count // BLOCK_SLOTS
    attended = lax.map(causal_block_attention, (query_slot_rows.reshape(block_list, BLOCK_SLOTS, QUERY_HEADS * HEAD_SIZE), key_slot_rows.reshape(block_list, BLOCK_SLOTS, KEY_VALUE_HEADS * HEAD_SIZE), value_slot_rows.reshape(block_list, BLOCK_SLOTS, KEY_VALUE_HEADS * HEAD_SIZE), positions.reshape(block_list, BLOCK_SLOTS)))
    return attended.reshape(overall_slot_count, QUERY_HEADS * HEAD_SIZE)[route]
```

```python
import functools
import math

import jax
import jax.numpy as jnp
from jax import lax
from jax.experimental import pallas as pl
from jax.experimental.pallas import tpu as pltpu
from jax.sharding import PartitionSpec as P

QUERY_HEADS = 20
KEY_VALUE_HEADS = 4
HEAD_SIZE = 128
BLOCK_SLOTS = 512
HEAD_GROUPS = QUERY_HEADS // KEY_VALUE_HEADS
CHUNKS = 2
CHUNK_HEADS = KEY_VALUE_HEADS // CHUNKS
PLANE = 4
GATHER_LIMIT = 40 * 2**20
MASKED = -1e30
VMEM = pl.BlockSpec(memory_space=pltpu.VMEM)
SMEM = pl.BlockSpec(memory_space=pltpu.SMEM)
ANY = pl.BlockSpec(memory_space=pl.ANY)


def grant(mebibytes):
    return pltpu.CompilerParams(vmem_limit_bytes=mebibytes * 2**20)


def one_hot_rows(count, index_row):
    rows = lax.broadcasted_iota(jnp.int32, (count, index_row.shape[1]), 0)
    return (rows == index_row).astype(jnp.float32).astype(jnp.bfloat16)


def contract(left, right, left_dim, right_dim):
    return lax.dot_general(
        left, right, (((left_dim,), (right_dim,)), ((), ())), preferred_element_type=jnp.float32
    )


def turn(rows, cosine, sine):
    return (rows * cosine + pltpu.roll(rows, HEAD_SIZE // 2, 1) * sine).astype(jnp.bfloat16)


def order_kernel(ranks, slots, spare, stride, route_ref, bucket_ref, seat_ref, sorted_ref):
    route = route_ref[...]
    count = route.shape[1]
    target = lax.div(route, slots)
    member = (lax.broadcasted_iota(jnp.int32, (ranks, count), 0) == target).astype(jnp.float32)
    before = lax.broadcasted_iota(jnp.int32, (count, count), 0) < lax.broadcasted_iota(
        jnp.int32, (count, count), 1
    )
    ahead = contract(
        member.astype(jnp.bfloat16), before.astype(jnp.float32).astype(jnp.bfloat16), 1, 0
    )
    order = jnp.sum(member * ahead, axis=0, keepdims=True).astype(jnp.int32)
    bucket = target * spare + order
    bucket_ref[...] = bucket
    seat_ref[...] = target * stride + order
    high = lax.div(route, HEAD_SIZE)
    low = route - high * HEAD_SIZE
    line = lax.broadcasted_iota(jnp.int32, (8, count), 0)
    digits = jnp.where(line == 0, high, jnp.where(line == 1, low, jnp.where(line == 2, 1, 0)))
    placed = contract(
        digits.astype(jnp.float32).astype(jnp.bfloat16), one_hot_rows(ranks * spare, bucket), 1, 1
    )
    found = placed[0:1] * HEAD_SIZE + placed[1:2] + placed[2:3] - 1.0
    sorted_ref[...] = found.astype(jnp.int32)


def query_kernel(
    route_ref, seat_ref, positions_ref, frequency_ref, queries_ref,
    turned_ref, bounds_ref, cosine_ref, sine_ref,
):
    route = route_ref[...]
    count = route.shape[0]
    lines = positions_ref.shape[0]
    line = lax.div(route, HEAD_SIZE)
    lane = route - line * HEAD_SIZE
    pick = (lax.broadcasted_iota(jnp.int32, (count, lines), 1) == line).astype(jnp.float32)
    pick = pick.astype(jnp.bfloat16)
    positions = positions_ref[...]
    half = lax.div(positions, 2)
    rest = positions - half * 2
    rows = 2.0 * contract(pick, half.astype(jnp.float32).astype(jnp.bfloat16), 1, 0) + contract(
        pick, rest.astype(jnp.float32).astype(jnp.bfloat16), 1, 0
    )
    lanes = lax.broadcasted_iota(jnp.int32, (count, HEAD_SIZE), 1)
    spot = jnp.sum(jnp.where(lanes == lane, rows, 0.0), axis=1, keepdims=True)
    angle = spot * frequency_ref[...]
    cosine = jnp.cos(angle)
    sine = jnp.sin(angle)
    sine = jnp.where(lanes < HEAD_SIZE // 2, -sine, sine)
    cosine_ref[...] = cosine
    sine_ref[...] = sine
    seats = one_hot_rows(turned_ref.shape[0], seat_ref[...])
    first = route - spot.astype(jnp.int32)
    first_line = lax.div(first, HEAD_SIZE)
    first_lane = first - first_line * HEAD_SIZE
    digits = jnp.where(lanes == 0, line, 0)
    digits = jnp.where(lanes == 1, lane, digits)
    digits = jnp.where(lanes == 2, first_line, digits)
    digits = jnp.where(lanes == 3, first_lane, digits)
    digits = jnp.where(lanes == 4, 1, digits)
    placed = contract(seats, digits.astype(jnp.float32).astype(jnp.bfloat16), 1, 0)
    live = placed[:, 4:5] - 1.0
    last = placed[:, 0:1] * HEAD_SIZE + placed[:, 1:2] + live
    start = placed[:, 2:3] * HEAD_SIZE + placed[:, 3:4] + live
    seat_lanes = lax.broadcasted_iota(jnp.int32, placed.shape, 1)
    bounds_ref[...] = jnp.where(seat_lanes == 0, last, start).astype(jnp.int32)
    for head in range(queries_ref.shape[1] // HEAD_SIZE):
        span = slice(head * HEAD_SIZE, (head + 1) * HEAD_SIZE)
        turned = turn(queries_ref[:, span].astype(jnp.float32), cosine, sine)
        turned_ref[:, span] = contract(seats, turned, 1, 0).astype(jnp.bfloat16)


def project_kernel(
    owners_ref, hidden_ref, bias_ref, cosine_ref, sine_ref, bucket_ref, *refs
):
    ranks = owners_ref.shape[0]
    blocks, outs = refs[:ranks], refs[ranks : ranks + CHUNKS]
    matrix, done = refs[ranks + CHUNKS :]
    depth = blocks[0].shape[0]
    copies = [
        pltpu.make_async_copy(
            blocks[j],
            matrix.at[pl.ds(pl.multiple_of(owners_ref[j] * depth, 16), depth)],
            done.at[j],
        )
        for j in range(ranks)
    ]
    for copy in copies:
        copy.start()
    places = one_hot_rows(outs[0].shape[0], bucket_ref[...])
    for copy in copies:
        copy.wait()
    wide = CHUNK_HEADS * HEAD_SIZE
    for chunk in range(CHUNKS):
        for part in range(2):
            first = part * KEY_VALUE_HEADS * HEAD_SIZE + chunk * wide
            span = slice(first, first + wide)
            rows = contract(hidden_ref[...], matrix[:, span], 1, 0) + bias_ref[:, span]
            rows = rows.astype(jnp.bfloat16)
            for head in range(CHUNK_HEADS):
                one = rows[:, head * HEAD_SIZE : (head + 1) * HEAD_SIZE]
                if part == 0:
                    one = turn(one.astype(jnp.float32), cosine_ref[...], sine_ref[...])
                at = part * wide + head * HEAD_SIZE
                outs[chunk][:, at : at + HEAD_SIZE] = contract(places, one, 1, 0).astype(
                    jnp.bfloat16
                )


def attend_kernel(
    chunk, spare, window, stride, queries_ref, bounds_ref, routes_ref, seat_ref, *refs
):
    ranks = routes_ref.shape[0]
    blocks, out_ref, mixed_ref = refs[:ranks], refs[ranks], refs[ranks + 1]
    wide = CHUNK_HEADS * HEAD_SIZE
    scale = math.log2(math.e) / math.sqrt(HEAD_SIZE)

    def one_group(group, carry):
        seats = pl.ds(pl.multiple_of(group * stride, 16), stride)
        start = pl.multiple_of(lax.div(group * spare, 16) * 16, 16)
        keys_at = pl.ds(start, window)
        routes = routes_ref[group]
        visible = (routes <= bounds_ref[seats, 0:1]) & (routes >= bounds_ref[seats, 1:2])
        veil = jnp.where(visible, 0.0, MASKED)
        veil = jnp.concatenate([veil] * HEAD_GROUPS, axis=0)
        for head in range(CHUNK_HEADS):
            span = slice(head * HEAD_SIZE, (head + 1) * HEAD_SIZE)
            value_span = slice(wide + head * HEAD_SIZE, wide + (head + 1) * HEAD_SIZE)
            heads = [
                slice(at * HEAD_SIZE, (at + 1) * HEAD_SIZE)
                for at in range(head * HEAD_GROUPS, (head + 1) * HEAD_GROUPS)
            ]
            query = jnp.concatenate([queries_ref[seats, one] for one in heads], axis=0)
            keys = jnp.concatenate([block[keys_at, span] for block in blocks], axis=0)
            values = jnp.concatenate([block[keys_at, value_span] for block in blocks], axis=0)
            scores = contract(query, keys, 1, 1) * scale + veil
            weights = jnp.exp2(scores - jnp.max(scores, axis=1, keepdims=True))
            totals = jnp.sum(weights, axis=1, keepdims=True)
            mixed = contract(weights.astype(jnp.bfloat16), values, 1, 0) / totals
            mixed = mixed.astype(jnp.bfloat16)
            for place, one in enumerate(heads):
                mixed_ref[seats, one] = mixed[place * stride : (place + 1) * stride]
        return carry

    lax.fori_loop(0, ranks, one_group, 0)
    seats = one_hot_rows(mixed_ref.shape[0], seat_ref[...])
    for head in range(out_ref.shape[1] // HEAD_SIZE):
        span = slice(head * HEAD_SIZE, (head + 1) * HEAD_SIZE)
        out_ref[:, span] = contract(seats, mixed_ref[:, span], 0, 0).astype(jnp.bfloat16)


def spread(block, ranks):
    ring = [(rank, (rank + PLANE) % ranks) for rank in range(ranks)]
    across = [(rank, rank ^ 2) for rank in range(ranks)]
    beside = [(rank, rank ^ 1) for rank in range(ranks)]
    lanes = [block]
    for _ in range(ranks // PLANE - 1):
        lanes.append(lax.ppermute(lanes[-1], "dp", ring))
    others = [lax.ppermute(lane, "dp", across) for lane in lanes]
    held = lanes + others
    return held + [lax.ppermute(one, "dp", beside) for one in held]


def source_order(ranks):
    me = lax.axis_index("dp")
    lane, plane = me % PLANE, me // PLANE
    steps = ranks // PLANE
    planes = (plane - jnp.arange(steps, dtype=jnp.int32)) % steps
    return jnp.concatenate([planes * PLANE + (lane ^ flip) for flip in (0, 2, 1, 3)])


def gather_plan(
    hidden,
    queries,
    route,
    positions,
    key_matrix,
    value_matrix,
    key_projection_bias,
    value_projection_bias,
):
    ranks = lax.axis_size("dp")
    rows = hidden.shape[0]
    slots = positions.shape[0]
    spare = rows // ranks + 2
    width = ranks * spare
    stride = -(-spare // 16) * 16
    starts = [group * spare // 16 * 16 for group in range(ranks)]
    window = max(
        -(-(group + 1) * spare // 16) * 16 - starts[group] for group in range(ranks)
    )
    pair_width = 2 * key_matrix.shape[1]
    chunk_width = pair_width // CHUNKS
    query_width = queries.shape[1]
    shape = jax.ShapeDtypeStruct

    matrices = spread(jnp.concatenate([key_matrix, value_matrix], axis=1), ranks)

    bucket, seat, sorted_route = pl.pallas_call(
        functools.partial(order_kernel, ranks, slots, spare, stride),
        out_shape=(
            shape((1, rows), jnp.int32),
            shape((1, rows), jnp.int32),
            shape((1, width), jnp.int32),
        ),
        in_specs=[VMEM],
        out_specs=(VMEM, VMEM, VMEM),
        compiler_params=grant(16),
        name="order",
    )(route.reshape(1, rows))
    plan = lax.all_gather(
        jnp.concatenate([sorted_route.reshape(width), positions]), "dp", axis=0, tiled=False
    )
    all_positions = plan[:, width:].reshape(-1, HEAD_SIZE)
    owners = source_order(ranks)
    key_routes = plan[:, :width][owners]
    key_routes = jnp.stack(
        [key_routes[:, at : at + window].reshape(1, ranks * window) for at in starts]
    )

    half = HEAD_SIZE // 2
    frequency = 1000000.0 ** (-(jnp.arange(half, dtype=jnp.float32) * 2.0 / HEAD_SIZE))
    turned, bounds, cosine, sine = pl.pallas_call(
        query_kernel,
        out_shape=(
            shape((ranks * stride, query_width), jnp.bfloat16),
            shape((ranks * stride, HEAD_SIZE), jnp.int32),
            shape((rows, HEAD_SIZE), jnp.float32),
            shape((rows, HEAD_SIZE), jnp.float32),
        ),
        in_specs=[VMEM] * 5,
        out_specs=(VMEM,) * 4,
        compiler_params=grant(32),
        name="turn_queries",
    )(
        route.reshape(rows, 1),
        seat,
        all_positions,
        jnp.concatenate([frequency, frequency]).reshape(1, HEAD_SIZE),
        queries,
    )

    bias = jnp.concatenate([key_projection_bias, value_projection_bias])
    pairs = pl.pallas_call(
        project_kernel,
        out_shape=(shape((width, chunk_width), jnp.bfloat16),) * CHUNKS,
        in_specs=[SMEM] + [VMEM] * 5 + [ANY] * ranks,
        out_specs=(VMEM,) * CHUNKS,
        scratch_shapes=[
            pltpu.VMEM((hidden.shape[1], pair_width), jnp.bfloat16),
            pltpu.SemaphoreType.DMA((ranks,)),
        ],
        compiler_params=grant(44),
        name="project",
    )(
        owners,
        hidden,
        bias.astype(jnp.float32).reshape(1, pair_width),
        cosine,
        sine,
        bucket,
        *matrices,
    )

    outs = []
    for chunk in range(CHUNKS):
        columns = query_width // CHUNKS
        blocks = spread(pairs[chunk], ranks)
        outs.append(
            pl.pallas_call(
                functools.partial(attend_kernel, chunk, spare, window, stride),
                grid=(1,),
                out_shape=shape((rows, columns), jnp.bfloat16),
                in_specs=[pl.BlockSpec((ranks * stride, columns), lambda i, c=chunk: (0, c))]
                + [VMEM] * (3 + ranks),
                out_specs=VMEM,
                scratch_shapes=[pltpu.VMEM((ranks * stride, columns), jnp.bfloat16)],
                compiler_params=grant(40),
                name="attend",
            )(turned, bounds, key_routes, seat, *blocks)
        )
    return jnp.concatenate(outs, axis=1)


def apply_rotary(rows, slot_offset, heads):
    block_count = rows.shape[0]
    half = HEAD_SIZE // 2
    frequency = 1000000.0 ** (-(jnp.arange(half, dtype=jnp.float32) * 2.0 / HEAD_SIZE))
    angle = slot_offset.astype(jnp.float32)[:, None] * frequency[None, :]
    cosine = jnp.cos(angle)[:, None, :]
    sine = jnp.sin(angle)[:, None, :]
    grid = rows.astype(jnp.float32).reshape(block_count, heads, HEAD_SIZE)
    first = grid[:, :, :half]
    second = grid[:, :, half:]
    turned = jnp.concatenate(
        [first * cosine - second * sine, second * cosine + first * sine], axis=2
    )
    return turned.reshape(block_count, heads * HEAD_SIZE).astype(jnp.bfloat16)


def causal_block_attention(pieces):
    query_tile_rows, key_tile_rows, value_tile_rows, spot_block = pieces
    block_count = query_tile_rows.shape[0]
    head_groups = QUERY_HEADS // KEY_VALUE_HEADS
    query_block_grid = query_tile_rows.reshape(block_count, KEY_VALUE_HEADS, head_groups, HEAD_SIZE)
    key_block_grid = key_tile_rows.reshape(block_count, KEY_VALUE_HEADS, HEAD_SIZE)
    value_block_grid = value_tile_rows.reshape(block_count, KEY_VALUE_HEADS, HEAD_SIZE)
    scores = jnp.einsum(
        "qhgd,khd->hgqk", query_block_grid, key_block_grid, preferred_element_type=jnp.float32
    ) / math.sqrt(HEAD_SIZE)
    inner = jnp.arange(block_count, dtype=jnp.int32)
    visible = (inner[None, :] <= inner[:, None]) & (
        inner[None, :] >= inner[:, None] - spot_block[:, None]
    )
    scores = jnp.where(visible, scores, -jnp.inf)
    top = jnp.max(scores, axis=3, keepdims=True)
    weights = jnp.exp(scores - top)
    totals = jnp.sum(weights, axis=3)
    probs = weights.astype(jnp.bfloat16)
    mixed = jnp.einsum(
        "hgqk,khd->qhgd", probs, value_block_grid, preferred_element_type=jnp.float32
    )
    mixed = mixed / jnp.transpose(totals, (2, 0, 1))[:, :, :, None]
    return mixed.reshape(block_count, QUERY_HEADS * HEAD_SIZE).astype(jnp.bfloat16)


def add_projection(left, pieces):
    return (
        jnp.dot(left, pieces[0], preferred_element_type=jnp.float32),
        jnp.dot(left, pieces[1], preferred_element_type=jnp.float32),
    )


def project_own(hidden, key_matrix, value_matrix, key_projection_bias, value_projection_bias):
    totals = add_projection(
        hidden,
        (
            lax.all_gather(key_matrix, "dp", axis=0, tiled=True),
            lax.all_gather(value_matrix, "dp", axis=0, tiled=True),
        ),
    )
    key_rows = (totals[0] + key_projection_bias.astype(jnp.float32)).astype(jnp.bfloat16)
    value_rows = (totals[1] + value_projection_bias.astype(jnp.float32)).astype(jnp.bfloat16)
    return jnp.concatenate([key_rows, value_rows], axis=1)


def send_plan(
    hidden,
    queries,
    route,
    positions,
    key_matrix,
    value_matrix,
    key_projection_bias,
    value_projection_bias,
):
    ranks = lax.axis_size("dp")
    rows = hidden.shape[0]
    slots = positions.shape[0]
    spare = rows // ranks + 2
    width = ranks * spare
    paired_width = key_matrix.shape[1]
    target = route // slots
    place = route - target * slots
    member = (target[:, None] == jnp.arange(ranks, dtype=jnp.int32)[None, :]).astype(jnp.int32)
    order = jnp.sum(jnp.cumsum(member, axis=0) * member, axis=1) - 1
    bucket = target * spare + order
    outgoing = jnp.full((width,), slots, jnp.int32).at[bucket].set(place)
    arrived = lax.all_to_all(
        outgoing.reshape(ranks, spare), "dp", split_axis=0, concat_axis=0, tiled=True
    ).reshape(width)
    query_buf = jnp.zeros((width, queries.shape[1]), jnp.bfloat16).at[bucket].set(queries)
    own_pairs = project_own(
        hidden, key_matrix, value_matrix, key_projection_bias, value_projection_bias
    )
    pair_buf = jnp.zeros((width, 2 * paired_width), jnp.bfloat16).at[bucket].set(own_pairs)
    got_query, got_pairs = (
        lax.all_to_all(
            query_buf.reshape(ranks, spare, -1), "dp", split_axis=0, concat_axis=0, tiled=True
        ),
        lax.all_to_all(
            pair_buf.reshape(ranks, spare, -1), "dp", split_axis=0, concat_axis=0, tiled=True
        ),
    )
    got_query = got_query.reshape(width, -1)
    got_pairs = got_pairs.reshape(width, -1)
    query_slot_rows = (
        jnp.zeros((slots, got_query.shape[1]), jnp.bfloat16).at[arrived].set(got_query, mode="drop")
    )
    paired_slot_rows = (
        jnp.zeros((slots, 2 * paired_width), jnp.bfloat16).at[arrived].set(got_pairs, mode="drop")
    )
    query_turned = apply_rotary(query_slot_rows, positions, QUERY_HEADS)
    key_rotated = apply_rotary(paired_slot_rows[:, :paired_width], positions, KEY_VALUE_HEADS)
    block_list = slots // BLOCK_SLOTS
    attended = lax.map(
        causal_block_attention,
        (
            query_turned.reshape(block_list, BLOCK_SLOTS, -1),
            key_rotated.reshape(block_list, BLOCK_SLOTS, -1),
            paired_slot_rows[:, paired_width:].reshape(block_list, BLOCK_SLOTS, -1),
            positions.reshape(block_list, BLOCK_SLOTS),
        ),
    )
    attended = attended.reshape(slots, -1)
    leaving = attended[jnp.minimum(arrived, slots - 1)]
    returned = lax.all_to_all(
        leaving.reshape(ranks, spare, -1), "dp", split_axis=0, concat_axis=0, tiled=True
    ).reshape(width, -1)
    return returned[bucket]


def local(*args):
    hidden, queries, _, positions, key_matrix = args[:5]
    ranks = lax.axis_size("dp")
    rows = hidden.shape[0]
    gathered = ranks * ranks * (rows // ranks + 2) * 4 * key_matrix.shape[1]
    if ranks % PLANE == 0 and rows % ranks == 0 and gathered <= GATHER_LIMIT:
        return gather_plan(*args)
    return send_plan(*args)


def solution(mesh):
    placed = (
        P(("groups", "dp"), None),
        P(("groups", "dp"), None),
        P(("groups", "dp")),
        P(("groups", "dp")),
        P("dp", None),
        P("dp", None),
        P(),
        P(),
    )
    return jax.shard_map(
        local, mesh=mesh, in_specs=placed, out_specs=P(("groups", "dp"), None), check_vma=False
    )
```

```python
import functools
import math

import jax
import jax.numpy as jnp
from jax import lax
from jax.experimental import pallas as pl
from jax.experimental.pallas import tpu as pltpu
from jax.sharding import PartitionSpec as P

QUERY_HEADS = 20
KEY_VALUE_HEADS = 4
HEAD_SIZE = 128
BLOCK_SLOTS = 512
HEAD_GROUPS = QUERY_HEADS // KEY_VALUE_HEADS
CHUNKS = ((0, 3), (3, 1))
PLANE = 4
GATHER_LIMIT = 40 * 2**20
MASKED = -1e30
VMEM = pl.BlockSpec(memory_space=pltpu.VMEM)
SMEM = pl.BlockSpec(memory_space=pltpu.SMEM)
HBM = pl.BlockSpec(memory_space=pltpu.HBM)


def grant(mebibytes):
    return pltpu.CompilerParams(vmem_limit_bytes=mebibytes * 2**20)


def cost(flops, moved):
    return pl.CostEstimate(flops=flops, bytes_accessed=moved, transcendentals=0)


def one_hot_rows(count, index_row):
    rows = lax.broadcasted_iota(jnp.int32, (count, index_row.shape[1]), 0)
    return (rows == index_row).astype(jnp.float32).astype(jnp.bfloat16)


def contract(left, right, left_dim, right_dim):
    return lax.dot_general(
        left, right, (((left_dim,), (right_dim,)), ((), ())), preferred_element_type=jnp.float32
    )


def turn(rows, cosine, sine):
    return (rows * cosine + pltpu.roll(rows, HEAD_SIZE // 2, 1) * sine).astype(jnp.bfloat16)


def order_kernel(ranks, slots, spare, stride, route_ref, bucket_ref, seat_ref, sorted_ref):
    route = route_ref[...]
    count = route.shape[1]
    target = lax.div(route, slots)
    member = (lax.broadcasted_iota(jnp.int32, (ranks, count), 0) == target).astype(jnp.float32)
    before = lax.broadcasted_iota(jnp.int32, (count, count), 0) < lax.broadcasted_iota(
        jnp.int32, (count, count), 1
    )
    ahead = contract(
        member.astype(jnp.bfloat16), before.astype(jnp.float32).astype(jnp.bfloat16), 1, 0
    )
    order = jnp.sum(member * ahead, axis=0, keepdims=True).astype(jnp.int32)
    bucket = target * spare + order
    bucket_ref[...] = bucket
    seat_ref[...] = target * stride + order
    high = lax.div(route, HEAD_SIZE)
    low = route - high * HEAD_SIZE
    line = lax.broadcasted_iota(jnp.int32, (8, count), 0)
    digits = jnp.where(line == 0, high, jnp.where(line == 1, low, jnp.where(line == 2, 1, 0)))
    placed = contract(
        digits.astype(jnp.float32).astype(jnp.bfloat16), one_hot_rows(ranks * spare, bucket), 1, 1
    )
    found = placed[0:1] * HEAD_SIZE + placed[1:2] + placed[2:3] - 1.0
    sorted_ref[...] = found.astype(jnp.int32)


def query_kernel(
    route_ref, seat_ref, positions_ref, frequency_ref, queries_ref, *refs
):
    turned_refs, (bounds_ref, cosine_ref, sine_ref) = refs[: len(CHUNKS)], refs[len(CHUNKS) :]
    route = route_ref[...]
    count = route.shape[0]
    lines = positions_ref.shape[0]
    line = lax.div(route, HEAD_SIZE)
    lane = route - line * HEAD_SIZE
    pick = (lax.broadcasted_iota(jnp.int32, (count, lines), 1) == line).astype(jnp.float32)
    pick = pick.astype(jnp.bfloat16)
    positions = positions_ref[...]
    half = lax.div(positions, 2)
    rest = positions - half * 2
    rows = 2.0 * contract(pick, half.astype(jnp.float32).astype(jnp.bfloat16), 1, 0) + contract(
        pick, rest.astype(jnp.float32).astype(jnp.bfloat16), 1, 0
    )
    lanes = lax.broadcasted_iota(jnp.int32, (count, HEAD_SIZE), 1)
    spot = jnp.sum(jnp.where(lanes == lane, rows, 0.0), axis=1, keepdims=True)
    angle = spot * frequency_ref[...]
    cosine = jnp.cos(angle)
    sine = jnp.sin(angle)
    sine = jnp.where(lanes < HEAD_SIZE // 2, -sine, sine)
    cosine_ref[...] = cosine
    sine_ref[...] = sine
    seats = one_hot_rows(bounds_ref.shape[0], seat_ref[...])
    first = route - spot.astype(jnp.int32)
    first_line = lax.div(first, HEAD_SIZE)
    first_lane = first - first_line * HEAD_SIZE
    digits = jnp.where(lanes == 0, line, 0)
    digits = jnp.where(lanes == 1, lane, digits)
    digits = jnp.where(lanes == 2, first_line, digits)
    digits = jnp.where(lanes == 3, first_lane, digits)
    digits = jnp.where(lanes == 4, 1, digits)
    placed = contract(seats, digits.astype(jnp.float32).astype(jnp.bfloat16), 1, 0)
    live = placed[:, 4:5] - 1.0
    last = placed[:, 0:1] * HEAD_SIZE + placed[:, 1:2] + live
    start = placed[:, 2:3] * HEAD_SIZE + placed[:, 3:4] + live
    seat_lanes = lax.broadcasted_iota(jnp.int32, placed.shape, 1)
    bounds_ref[...] = jnp.where(seat_lanes == 0, last, start).astype(jnp.int32)
    for (first_head, heads), turned_ref in zip(CHUNKS, turned_refs):
        for head in range(heads * HEAD_GROUPS):
            at = (first_head * HEAD_GROUPS + head) * HEAD_SIZE
            one = queries_ref[:, at : at + HEAD_SIZE].astype(jnp.float32)
            turned_ref[:, head * HEAD_SIZE : (head + 1) * HEAD_SIZE] = contract(
                seats, turn(one, cosine, sine), 1, 0
            ).astype(jnp.bfloat16)


def fetch(pieces, refs, place, done):
    copies = []
    for at, ((source, first), ref) in enumerate(zip(pieces, refs)):
        copies.append(
            pltpu.make_async_copy(ref, place(source, first, ref.shape[0]), done.at[at])
        )
        copies[-1].start()
    return copies


def project_kernel(
    heads, pieces, owners_ref, hidden_ref, bias_ref, cosine_ref, sine_ref, bucket_ref, *refs
):
    parts, out_ref, matrix, done = refs[: len(pieces)], *refs[len(pieces) :]
    depth = matrix.shape[0] // owners_ref.shape[0]
    copies = fetch(
        pieces,
        parts,
        lambda source, first, rows: matrix.at[
            pl.ds(pl.multiple_of(owners_ref[source] * depth + first, 16), rows)
        ],
        done,
    )
    places = one_hot_rows(out_ref.shape[0], bucket_ref[...])
    for copy in copies:
        copy.wait()
    wide = heads * HEAD_SIZE
    for part in range(2):
        span = slice(part * wide, (part + 1) * wide)
        rows = contract(hidden_ref[...], matrix[:, span], 1, 0) + bias_ref[:, span]
        rows = rows.astype(jnp.bfloat16)
        for head in range(heads):
            one = rows[:, head * HEAD_SIZE : (head + 1) * HEAD_SIZE]
            if part == 0:
                one = turn(one.astype(jnp.float32), cosine_ref[...], sine_ref[...])
            at = part * wide + head * HEAD_SIZE
            out_ref[:, at : at + HEAD_SIZE] = contract(places, one, 1, 0).astype(jnp.bfloat16)


def attend_kernel(
    chunk, pieces, spare, window, stride, queries_ref, bounds_ref, routes_ref, seat_ref, *refs
):
    first_head, heads = chunk
    ranks = routes_ref.shape[0]
    parts, out_ref, blocks, mixed_ref, result_ref, done = refs[: len(pieces)], *refs[-5:]
    copies = fetch(
        pieces, parts, lambda source, first, rows: blocks.at[source, pl.ds(first, rows)], done
    )
    for copy in copies:
        copy.wait()
    wide = heads * HEAD_SIZE
    scale = math.log2(math.e) / math.sqrt(HEAD_SIZE)

    def one_group(group, carry):
        seats = pl.ds(pl.multiple_of(group * stride, 16), stride)
        keys_at = pl.ds(pl.multiple_of(lax.div(group * spare, 16) * 16, 16), window)
        routes = routes_ref[group]
        visible = (routes <= bounds_ref[seats, 0:1]) & (routes >= bounds_ref[seats, 1:2])
        veil = jnp.where(visible, 0.0, MASKED)
        veil = jnp.concatenate([veil] * HEAD_GROUPS, axis=0)
        for head in range(heads):
            span = slice(head * HEAD_SIZE, (head + 1) * HEAD_SIZE)
            value_span = slice(wide + head * HEAD_SIZE, wide + (head + 1) * HEAD_SIZE)
            turns = [
                slice(at * HEAD_SIZE, (at + 1) * HEAD_SIZE)
                for at in range(head * HEAD_GROUPS, (head + 1) * HEAD_GROUPS)
            ]
            query = jnp.concatenate([queries_ref[seats, one] for one in turns], axis=0)
            keys = jnp.concatenate([blocks[j, keys_at, span] for j in range(ranks)], axis=0)
            values = jnp.concatenate(
                [blocks[j, keys_at, value_span] for j in range(ranks)], axis=0
            )
            scores = contract(query, keys, 1, 1) * scale + veil
            weights = jnp.exp2(scores - jnp.max(scores, axis=1, keepdims=True))
            totals = jnp.sum(weights, axis=1, keepdims=True)
            mixed = contract(weights.astype(jnp.bfloat16), values, 1, 0) / totals
            mixed = mixed.astype(jnp.bfloat16)
            for place, one in enumerate(turns):
                mixed_ref[seats, one] = mixed[place * stride : (place + 1) * stride]
        return carry

    lax.fori_loop(0, ranks, one_group, 0)
    seats = one_hot_rows(mixed_ref.shape[0], seat_ref[...])
    for head in range(result_ref.shape[1] // HEAD_SIZE):
        span = slice(head * HEAD_SIZE, (head + 1) * HEAD_SIZE)
        result_ref[:, span] = contract(seats, mixed_ref[:, span], 0, 0).astype(jnp.bfloat16)
    columns = pl.ds(first_head * HEAD_GROUPS * HEAD_SIZE, result_ref.shape[1])
    leave = pltpu.make_async_copy(result_ref, out_ref.at[:, columns], done.at[len(pieces)])
    leave.start()
    leave.wait()


def spread(block, ranks, after=None):
    ring = [(rank, (rank + PLANE) % ranks) for rank in range(ranks)]
    across = [(rank, rank ^ 2) for rank in range(ranks)]
    beside = [(rank, rank ^ 1) for rank in range(ranks)]
    steps = ranks // PLANE
    half = block.shape[0] // 32 * 16
    if after is not None:
        block, after = lax.optimization_barrier((block, after))
    pieces, arrays = [], []

    def keep(source, first, array):
        pieces.extend([(source, first), (source + 2 * steps, first)])
        arrays.extend([array, lax.ppermute(array, "dp", beside)])

    lane, other = block, None
    for step in range(steps - 1):
        lane_next = lax.ppermute(lane, "dp", ring)
        other_next = lax.ppermute(lane, "dp", across)
        keep(step, 0, lane)
        if step:
            keep(steps + step - 1, 0, other)
        lane, other = lax.optimization_barrier((lane_next, other_next))
    mark = other
    over = lax.ppermute(lane[:half], "dp", across)
    round_ = lax.ppermute(other[half:], "dp", ring)
    keep(steps - 1, 0, lane)
    keep(2 * steps - 2, 0, other)
    keep(2 * steps - 1, 0, over)
    keep(2 * steps - 1, half, round_)
    return pieces, arrays, mark


def source_order(ranks):
    me = lax.axis_index("dp")
    lane, plane = me % PLANE, me // PLANE
    steps = ranks // PLANE
    planes = (plane - jnp.arange(steps, dtype=jnp.int32)) % steps
    return jnp.concatenate([planes * PLANE + (lane ^ flip) for flip in (0, 2, 1, 3)])


def gather_plan(
    hidden,
    queries,
    route,
    positions,
    key_matrix,
    value_matrix,
    key_projection_bias,
    value_projection_bias,
):
    ranks = lax.axis_size("dp")
    rows = hidden.shape[0]
    slots = positions.shape[0]
    spare = rows // ranks + 2
    width = ranks * spare
    stride = -(-spare // 16) * 16
    starts = [group * spare // 16 * 16 for group in range(ranks)]
    window = max(
        -(-(group + 1) * spare // 16) * 16 - starts[group] for group in range(ranks)
    )
    depth, query_width = hidden.shape[1], queries.shape[1]
    shape = jax.ShapeDtypeStruct

    def columns(array, chunk):
        first, heads = chunk
        return array[..., first * HEAD_SIZE : (first + heads) * HEAD_SIZE]

    matrices, mark = [], None
    for chunk in CHUNKS:
        block = jnp.concatenate([columns(key_matrix, chunk), columns(value_matrix, chunk)], axis=1)
        *matrix, mark = spread(block, ranks, mark)
        matrices.append(matrix)

    bucket, seat, sorted_route = pl.pallas_call(
        functools.partial(order_kernel, ranks, slots, spare, stride),
        out_shape=(
            shape((1, rows), jnp.int32),
            shape((1, rows), jnp.int32),
            shape((1, width), jnp.int32),
        ),
        in_specs=[VMEM],
        out_specs=(VMEM, VMEM, VMEM),
        compiler_params=grant(16),
        name="order",
    )(route.reshape(1, rows))
    plan = jnp.concatenate([sorted_route.reshape(width), positions])
    plan = lax.all_to_all(
        jnp.broadcast_to(plan, (ranks, width + slots)), "dp", split_axis=0, concat_axis=0, tiled=True
    )
    all_positions = plan[:, width:].reshape(-1, HEAD_SIZE)
    owners = source_order(ranks)
    key_routes = plan[:, :width][owners]
    key_routes = jnp.stack(
        [key_routes[:, at : at + window].reshape(1, ranks * window) for at in starts]
    )

    half = HEAD_SIZE // 2
    frequency = 1000000.0 ** (-(jnp.arange(half, dtype=jnp.float32) * 2.0 / HEAD_SIZE))
    *turned, bounds, cosine, sine = pl.pallas_call(
        query_kernel,
        out_shape=tuple(
            shape((ranks * stride, heads * HEAD_GROUPS * HEAD_SIZE), jnp.bfloat16)
            for _, heads in CHUNKS
        )
        + (
            shape((ranks * stride, HEAD_SIZE), jnp.int32),
            shape((rows, HEAD_SIZE), jnp.float32),
            shape((rows, HEAD_SIZE), jnp.float32),
        ),
        in_specs=[VMEM] * 5,
        out_specs=(VMEM,) * (len(CHUNKS) + 3),
        compiler_params=grant(32),
        cost_estimate=cost(4 * stride * ranks * rows * query_width, 4 * rows * query_width),
        name="turn_queries",
    )(
        route.reshape(rows, 1),
        seat,
        all_positions,
        jnp.concatenate([frequency, frequency]).reshape(1, HEAD_SIZE),
        queries,
    )

    pairs = []
    for chunk, (pieces, arrays) in zip(CHUNKS, matrices):
        bias = jnp.concatenate(
            [columns(key_projection_bias, chunk), columns(value_projection_bias, chunk)]
        )
        wide = bias.shape[0]
        pairs.append(
            pl.pallas_call(
                functools.partial(project_kernel, chunk[1], pieces),
                out_shape=shape((width, wide), jnp.bfloat16),
                in_specs=[SMEM] + [VMEM] * 5 + [HBM] * len(pieces),
                out_specs=VMEM,
                scratch_shapes=[
                    pltpu.VMEM((depth, wide), jnp.bfloat16),
                    pltpu.SemaphoreType.DMA((len(pieces),)),
                ],
                compiler_params=grant(36),
                cost_estimate=cost(2 * rows * depth * wide, 2 * depth * (rows + wide)),
                name="project",
            )(
                owners,
                hidden,
                bias.astype(jnp.float32).reshape(1, wide),
                cosine,
                sine,
                bucket,
                *arrays,
            )
        )

    out, mark = None, None
    for index, chunk in enumerate(CHUNKS):
        query_heads = chunk[1] * HEAD_GROUPS
        pieces, arrays, mark = spread(pairs[index], ranks, mark)
        wide = pairs[index].shape[1]
        taken = [] if out is None else [out]
        fixed = [turned[index], bounds, key_routes, seat]
        out = pl.pallas_call(
            functools.partial(attend_kernel, chunk, pieces, spare, window, stride),
            out_shape=shape((rows, query_width), jnp.bfloat16),
            in_specs=[VMEM] * len(fixed) + [HBM] * (len(pieces) + len(taken)),
            out_specs=HBM,
            scratch_shapes=[
                pltpu.VMEM((ranks, width, wide), jnp.bfloat16),
                pltpu.VMEM((ranks * stride, query_heads * HEAD_SIZE), jnp.bfloat16),
                pltpu.VMEM((rows, query_heads * HEAD_SIZE), jnp.bfloat16),
                pltpu.SemaphoreType.DMA((len(pieces) + 1,)),
            ],
            input_output_aliases={len(fixed) + len(pieces): 0} if taken else {},
            compiler_params=grant(32),
            cost_estimate=cost(
                16 * rows * stride * ranks * query_heads * HEAD_SIZE, 2 * ranks * width * wide
            ),
            name="attend",
        )(*fixed, *arrays, *taken)
    return out


def apply_rotary(rows, slot_offset, heads):
    block_count = rows.shape[0]
    half = HEAD_SIZE // 2
    frequency = 1000000.0 ** (-(jnp.arange(half, dtype=jnp.float32) * 2.0 / HEAD_SIZE))
    angle = slot_offset.astype(jnp.float32)[:, None] * frequency[None, :]
    cosine = jnp.cos(angle)[:, None, :]
    sine = jnp.sin(angle)[:, None, :]
    grid = rows.astype(jnp.float32).reshape(block_count, heads, HEAD_SIZE)
    first = grid[:, :, :half]
    second = grid[:, :, half:]
    turned = jnp.concatenate(
        [first * cosine - second * sine, second * cosine + first * sine], axis=2
    )
    return turned.reshape(block_count, heads * HEAD_SIZE).astype(jnp.bfloat16)


def causal_block_attention(pieces):
    query_tile_rows, key_tile_rows, value_tile_rows, spot_block = pieces
    block_count = query_tile_rows.shape[0]
    head_groups = QUERY_HEADS // KEY_VALUE_HEADS
    query_block_grid = query_tile_rows.reshape(block_count, KEY_VALUE_HEADS, head_groups, HEAD_SIZE)
    key_block_grid = key_tile_rows.reshape(block_count, KEY_VALUE_HEADS, HEAD_SIZE)
    value_block_grid = value_tile_rows.reshape(block_count, KEY_VALUE_HEADS, HEAD_SIZE)
    scores = jnp.einsum(
        "qhgd,khd->hgqk", query_block_grid, key_block_grid, preferred_element_type=jnp.float32
    ) / math.sqrt(HEAD_SIZE)
    inner = jnp.arange(block_count, dtype=jnp.int32)
    visible = (inner[None, :] <= inner[:, None]) & (
        inner[None, :] >= inner[:, None] - spot_block[:, None]
    )
    scores = jnp.where(visible, scores, -jnp.inf)
    top = jnp.max(scores, axis=3, keepdims=True)
    weights = jnp.exp(scores - top)
    totals = jnp.sum(weights, axis=3)
    probs = weights.astype(jnp.bfloat16)
    mixed = jnp.einsum(
        "hgqk,khd->qhgd", probs, value_block_grid, preferred_element_type=jnp.float32
    )
    mixed = mixed / jnp.transpose(totals, (2, 0, 1))[:, :, :, None]
    return mixed.reshape(block_count, QUERY_HEADS * HEAD_SIZE).astype(jnp.bfloat16)


def add_projection(left, pieces):
    return (
        jnp.dot(left, pieces[0], preferred_element_type=jnp.float32),
        jnp.dot(left, pieces[1], preferred_element_type=jnp.float32),
    )


def project_own(hidden, key_matrix, value_matrix, key_projection_bias, value_projection_bias):
    totals = add_projection(
        hidden,
        (
            lax.all_gather(key_matrix, "dp", axis=0, tiled=True),
            lax.all_gather(value_matrix, "dp", axis=0, tiled=True),
        ),
    )
    key_rows = (totals[0] + key_projection_bias.astype(jnp.float32)).astype(jnp.bfloat16)
    value_rows = (totals[1] + value_projection_bias.astype(jnp.float32)).astype(jnp.bfloat16)
    return jnp.concatenate([key_rows, value_rows], axis=1)


def send_plan(
    hidden,
    queries,
    route,
    positions,
    key_matrix,
    value_matrix,
    key_projection_bias,
    value_projection_bias,
):
    ranks = lax.axis_size("dp")
    rows = hidden.shape[0]
    slots = positions.shape[0]
    spare = rows // ranks + 2
    width = ranks * spare
    paired_width = key_matrix.shape[1]
    target = route // slots
    place = route - target * slots
    member = (target[:, None] == jnp.arange(ranks, dtype=jnp.int32)[None, :]).astype(jnp.int32)
    order = jnp.sum(jnp.cumsum(member, axis=0) * member, axis=1) - 1
    bucket = target * spare + order
    outgoing = jnp.full((width,), slots, jnp.int32).at[bucket].set(place)
    arrived = lax.all_to_all(
        outgoing.reshape(ranks, spare), "dp", split_axis=0, concat_axis=0, tiled=True
    ).reshape(width)
    query_buf = jnp.zeros((width, queries.shape[1]), jnp.bfloat16).at[bucket].set(queries)
    own_pairs = project_own(
        hidden, key_matrix, value_matrix, key_projection_bias, value_projection_bias
    )
    pair_buf = jnp.zeros((width, 2 * paired_width), jnp.bfloat16).at[bucket].set(own_pairs)
    got_query, got_pairs = (
        lax.all_to_all(
            query_buf.reshape(ranks, spare, -1), "dp", split_axis=0, concat_axis=0, tiled=True
        ),
        lax.all_to_all(
            pair_buf.reshape(ranks, spare, -1), "dp", split_axis=0, concat_axis=0, tiled=True
        ),
    )
    got_query = got_query.reshape(width, -1)
    got_pairs = got_pairs.reshape(width, -1)
    query_slot_rows = (
        jnp.zeros((slots, got_query.shape[1]), jnp.bfloat16).at[arrived].set(got_query, mode="drop")
    )
    paired_slot_rows = (
        jnp.zeros((slots, 2 * paired_width), jnp.bfloat16).at[arrived].set(got_pairs, mode="drop")
    )
    query_turned = apply_rotary(query_slot_rows, positions, QUERY_HEADS)
    key_rotated = apply_rotary(paired_slot_rows[:, :paired_width], positions, KEY_VALUE_HEADS)
    block_list = slots // BLOCK_SLOTS
    attended = lax.map(
        causal_block_attention,
        (
            query_turned.reshape(block_list, BLOCK_SLOTS, -1),
            key_rotated.reshape(block_list, BLOCK_SLOTS, -1),
            paired_slot_rows[:, paired_width:].reshape(block_list, BLOCK_SLOTS, -1),
            positions.reshape(block_list, BLOCK_SLOTS),
        ),
    )
    attended = attended.reshape(slots, -1)
    leaving = attended[jnp.minimum(arrived, slots - 1)]
    returned = lax.all_to_all(
        leaving.reshape(ranks, spare, -1), "dp", split_axis=0, concat_axis=0, tiled=True
    ).reshape(width, -1)
    return returned[bucket]


def local(*args):
    hidden, queries, _, positions, key_matrix = args[:5]
    ranks = lax.axis_size("dp")
    rows = hidden.shape[0]
    gathered = ranks * ranks * (rows // ranks + 2) * 4 * key_matrix.shape[1]
    if ranks % PLANE == 0 and rows % ranks == 0 and gathered <= GATHER_LIMIT:
        return gather_plan(*args)
    return send_plan(*args)


def solution(mesh):
    placed = (
        P(("groups", "dp"), None),
        P(("groups", "dp"), None),
        P(("groups", "dp")),
        P(("groups", "dp")),
        P("dp", None),
        P("dp", None),
        P(),
        P(),
    )
    return jax.shard_map(
        local, mesh=mesh, in_specs=placed, out_specs=P(("groups", "dp"), None), check_vma=False
    )
```

```python
import functools
import math

import jax
import jax.numpy as jnp
from jax import lax
from jax.experimental import pallas as pl
from jax.experimental.pallas import tpu as pltpu
from jax.sharding import PartitionSpec as P

QUERY_HEADS = 20
KEY_VALUE_HEADS = 4
HEAD_SIZE = 128
BLOCK_SLOTS = 512
HEAD_GROUPS = QUERY_HEADS // KEY_VALUE_HEADS
CHUNKS = ((0, 3), (3, 1))
PLANE = 4
PLANES = 4
GATHER_LIMIT = 40 * 2**20
MASKED = -1e30
VMEM = pl.BlockSpec(memory_space=pltpu.VMEM)
SMEM = pl.BlockSpec(memory_space=pltpu.SMEM)
HBM = pl.BlockSpec(memory_space=pltpu.HBM)


def grant(mebibytes):
    return pltpu.CompilerParams(vmem_limit_bytes=mebibytes * 2**20)


def cost(flops, moved):
    return pl.CostEstimate(flops=flops, bytes_accessed=moved, transcendentals=0)


def one_hot_rows(count, index_row):
    rows = lax.broadcasted_iota(jnp.int32, (count, index_row.shape[1]), 0)
    return (rows == index_row).astype(jnp.float32).astype(jnp.bfloat16)


def contract(left, right, left_dim, right_dim):
    return lax.dot_general(
        left, right, (((left_dim,), (right_dim,)), ((), ())), preferred_element_type=jnp.float32
    )


def turn(rows, cosine, sine):
    return (rows * cosine + pltpu.roll(rows, HEAD_SIZE // 2, 1) * sine).astype(jnp.bfloat16)


def order_kernel(ranks, slots, spare, stride, route_ref, bucket_ref, seat_ref, sorted_ref):
    route = route_ref[...]
    count = route.shape[1]
    target = lax.div(route, slots)
    member = (lax.broadcasted_iota(jnp.int32, (ranks, count), 0) == target).astype(jnp.float32)
    before = lax.broadcasted_iota(jnp.int32, (count, count), 0) < lax.broadcasted_iota(
        jnp.int32, (count, count), 1
    )
    ahead = contract(
        member.astype(jnp.bfloat16), before.astype(jnp.float32).astype(jnp.bfloat16), 1, 0
    )
    order = jnp.sum(member * ahead, axis=0, keepdims=True).astype(jnp.int32)
    bucket = target * spare + order
    bucket_ref[...] = bucket
    seat_ref[...] = target * stride + order
    high = lax.div(route, HEAD_SIZE)
    low = route - high * HEAD_SIZE
    line = lax.broadcasted_iota(jnp.int32, (8, count), 0)
    digits = jnp.where(line == 0, high, jnp.where(line == 1, low, jnp.where(line == 2, 1, 0)))
    placed = contract(
        digits.astype(jnp.float32).astype(jnp.bfloat16), one_hot_rows(ranks * spare, bucket), 1, 1
    )
    found = placed[0:1] * HEAD_SIZE + placed[1:2] + placed[2:3] - 1.0
    sorted_ref[...] = found.astype(jnp.int32)


def query_kernel(
    route_ref, seat_ref, positions_ref, frequency_ref, queries_ref, *refs
):
    turned_refs, (bounds_ref, cosine_ref, sine_ref) = refs[: len(CHUNKS)], refs[len(CHUNKS) :]
    route = route_ref[...]
    count = route.shape[0]
    lines = positions_ref.shape[0]
    line = lax.div(route, HEAD_SIZE)
    lane = route - line * HEAD_SIZE
    pick = (lax.broadcasted_iota(jnp.int32, (count, lines), 1) == line).astype(jnp.float32)
    pick = pick.astype(jnp.bfloat16)
    positions = positions_ref[...]
    half = lax.div(positions, 2)
    rest = positions - half * 2
    rows = 2.0 * contract(pick, half.astype(jnp.float32).astype(jnp.bfloat16), 1, 0) + contract(
        pick, rest.astype(jnp.float32).astype(jnp.bfloat16), 1, 0
    )
    lanes = lax.broadcasted_iota(jnp.int32, (count, HEAD_SIZE), 1)
    spot = jnp.sum(jnp.where(lanes == lane, rows, 0.0), axis=1, keepdims=True)
    angle = spot * frequency_ref[...]
    cosine = jnp.cos(angle)
    sine = jnp.sin(angle)
    sine = jnp.where(lanes < HEAD_SIZE // 2, -sine, sine)
    cosine_ref[...] = cosine
    sine_ref[...] = sine
    seats = one_hot_rows(bounds_ref.shape[0], seat_ref[...])
    first = route - spot.astype(jnp.int32)
    first_line = lax.div(first, HEAD_SIZE)
    first_lane = first - first_line * HEAD_SIZE
    digits = jnp.where(lanes == 0, line, 0)
    digits = jnp.where(lanes == 1, lane, digits)
    digits = jnp.where(lanes == 2, first_line, digits)
    digits = jnp.where(lanes == 3, first_lane, digits)
    digits = jnp.where(lanes == 4, 1, digits)
    placed = contract(seats, digits.astype(jnp.float32).astype(jnp.bfloat16), 1, 0)
    live = placed[:, 4:5] - 1.0
    last = placed[:, 0:1] * HEAD_SIZE + placed[:, 1:2] + live
    start = placed[:, 2:3] * HEAD_SIZE + placed[:, 3:4] + live
    seat_lanes = lax.broadcasted_iota(jnp.int32, placed.shape, 1)
    bounds_ref[...] = jnp.where(seat_lanes == 0, last, start).astype(jnp.int32)
    for (first_head, heads), turned_ref in zip(CHUNKS, turned_refs):
        for head in range(heads * HEAD_GROUPS):
            at = (first_head * HEAD_GROUPS + head) * HEAD_SIZE
            one = queries_ref[:, at : at + HEAD_SIZE].astype(jnp.float32)
            turned_ref[:, head * HEAD_SIZE : (head + 1) * HEAD_SIZE] = contract(
                seats, turn(one, cosine, sine), 1, 0
            ).astype(jnp.bfloat16)


def add_products(chips, owners_ref, hidden_ref, refs, columns, matrix, done):
    shard = matrix.shape[1] // 2
    copies, at, taken = [], 0, 0
    for place, chip in enumerate(chips):
        first = pl.multiple_of(lax.div(owners_ref[chip[0][0]], 2) * (2 * shard), HEAD_SIZE)
        copies.append(
            (hidden_ref.at[:, pl.ds(first, 2 * shard)], columns.at[place])
        )
        for source, row in chip:
            core = lax.rem(owners_ref[source], 2)
            rows = pl.ds(pl.multiple_of(core * shard + row, 16), refs[taken].shape[0])
            copies.append((refs[taken], matrix.at[place, rows]))
            taken += 1
    copies = [pltpu.make_async_copy(*pair, done.at[at]) for at, pair in enumerate(copies)]
    for copy in copies:
        copy.start()

    def product(span):
        total = contract(columns[0], matrix[0, :, span], 1, 0)
        for place in range(1, len(chips)):
            total = total + contract(columns[place], matrix[place, :, span], 1, 0)
        return total

    return copies, product


def part_kernel(chips, more, owners_ref, hidden_ref, *refs):
    count = sum(len(chip) for chip in chips)
    parts, refs = refs[:count], refs[count:]
    if more:
        total_ref, refs = refs[0], refs[1:]
    out_ref, columns, matrix, done = refs
    copies, product = add_products(chips, owners_ref, hidden_ref, parts, columns, matrix, done)
    for copy in copies:
        copy.wait()
    for first in range(0, out_ref.shape[1], 2 * HEAD_SIZE):
        span = slice(first, first + 2 * HEAD_SIZE)
        if more:
            out_ref[:, span] = total_ref[:, span] + product(span)
        else:
            out_ref[:, span] = product(span)


def finish_kernel(
    chips, owners_ref, hidden_ref, bias_ref, cosine_ref, sine_ref, bucket_ref, *refs
):
    count = sum(len(chip) for chip in chips)
    parts, total_ref = refs[:count], refs[count]
    outs, (columns, matrix, done) = refs[count + 1 : -3], refs[-3:]
    copies, product = add_products(chips, owners_ref, hidden_ref, parts, columns, matrix, done)
    places = one_hot_rows(outs[0].shape[0], bucket_ref[...])
    for copy in copies:
        copy.wait()
    wide = KEY_VALUE_HEADS * HEAD_SIZE
    for first in range(0, 2 * wide, 2 * HEAD_SIZE):
        span = slice(first, first + 2 * HEAD_SIZE)
        rows = (total_ref[:, span] + product(span) + bias_ref[:, span]).astype(jnp.bfloat16)
        if first < wide:
            cosine, sine = cosine_ref[...], sine_ref[...]
            halves = [
                turn(rows[:, at : at + HEAD_SIZE].astype(jnp.float32), cosine, sine)
                for at in (0, HEAD_SIZE)
            ]
            rows = jnp.concatenate(halves, axis=1)
        rows = contract(places, rows, 1, 0).astype(jnp.bfloat16)
        for half in range(2):
            head = first % wide // HEAD_SIZE + half
            for (first_head, heads), out_ref in zip(CHUNKS, outs):
                if first_head <= head < first_head + heads:
                    at = (head - first_head + first // wide * heads) * HEAD_SIZE
                    out_ref[:, at : at + HEAD_SIZE] = rows[
                        :, half * HEAD_SIZE : (half + 1) * HEAD_SIZE
                    ]


def attend_kernel(
    head, heads, pieces, spare, window, stride, queries_ref, bounds_ref, routes_ref, seat_ref, *refs
):
    first_head, place = head
    ranks = routes_ref.shape[0]
    parts, out_ref, blocks, mixed_ref, result_ref, done = refs[: len(pieces)], *refs[-5:]
    copies = []
    for at, ((source, first), ref) in enumerate(zip(pieces, parts)):
        for part in range(2):
            lanes = pl.ds((part * heads + place) * HEAD_SIZE, HEAD_SIZE)
            copies.append(
                pltpu.make_async_copy(
                    ref.at[:, lanes],
                    blocks.at[part, source, pl.ds(first, ref.shape[0])],
                    done.at[2 * at + part],
                )
            )
            copies[-1].start()
    for copy in copies:
        copy.wait()
    scale = math.log2(math.e) / math.sqrt(HEAD_SIZE)
    turns = [slice(at * HEAD_SIZE, (at + 1) * HEAD_SIZE) for at in range(HEAD_GROUPS)]

    def one_group(group, carry):
        seats = pl.ds(pl.multiple_of(group * stride, 16), stride)
        keys_at = pl.ds(pl.multiple_of(lax.div(group * spare, 16) * 16, 16), window)
        routes = routes_ref[group]
        visible = (routes <= bounds_ref[seats, 0:1]) & (routes >= bounds_ref[seats, 1:2])
        veil = jnp.where(visible, 0.0, MASKED)
        veil = jnp.concatenate([veil] * HEAD_GROUPS, axis=0)
        query = jnp.concatenate([queries_ref[seats, one] for one in turns], axis=0)
        keys = jnp.concatenate([blocks[0, j, keys_at] for j in range(ranks)], axis=0)
        values = jnp.concatenate([blocks[1, j, keys_at] for j in range(ranks)], axis=0)
        scores = contract(query, keys, 1, 1) * scale + veil
        weights = jnp.exp2(scores - jnp.max(scores, axis=1, keepdims=True))
        totals = jnp.sum(weights, axis=1, keepdims=True)
        mixed = contract(weights.astype(jnp.bfloat16), values, 1, 0) / totals
        mixed = mixed.astype(jnp.bfloat16)
        for at, one in enumerate(turns):
            mixed_ref[seats, one] = mixed[at * stride : (at + 1) * stride]
        return carry

    lax.fori_loop(0, ranks, one_group, 0)
    seats = one_hot_rows(mixed_ref.shape[0], seat_ref[...])
    result_ref[...] = contract(seats, mixed_ref[...], 0, 0).astype(jnp.bfloat16)
    lanes = pl.ds((first_head + place) * HEAD_GROUPS * HEAD_SIZE, HEAD_GROUPS * HEAD_SIZE)
    leave = pltpu.make_async_copy(result_ref, out_ref.at[:, lanes], done.at[2 * len(pieces)])
    leave.start()
    leave.wait()


def spread(block, ranks, held):
    ring = [(rank, (rank + PLANE) % ranks) for rank in range(ranks)]
    across = [(rank, rank ^ 2) for rank in range(ranks)]
    beside = [(rank, rank ^ 1) for rank in range(ranks)]
    steps = ranks // PLANE
    half = block.shape[0] // 32 * 16

    def keep(source, first, array):
        held.setdefault(source, []).append((first, array))
        held.setdefault(source + 2 * steps, []).append((first, lax.ppermute(array, "dp", beside)))

    lane, other = block, None
    for step in range(steps - 1):
        following = lax.ppermute(lane, "dp", ring), lax.ppermute(lane, "dp", across)
        keep(step, 0, lane)
        if step:
            keep(steps + step - 1, 0, other)
        extra = yield
        lane, other, extra = lax.optimization_barrier((*following, extra))
        yield extra
    over = lax.ppermute(lane[:half], "dp", across)
    around = lax.ppermute(other[half:], "dp", ring)
    keep(steps - 1, 0, lane)
    keep(2 * steps - 2, 0, other)
    keep(2 * steps - 1, 0, over)
    keep(2 * steps - 1, half, around)
    yield other


def source_order(ranks):
    me = lax.axis_index("dp")
    lane, plane = me % PLANE, me // PLANE
    steps = ranks // PLANE
    planes = (plane - jnp.arange(steps, dtype=jnp.int32)) % steps
    return jnp.concatenate([planes * PLANE + (lane ^ flip) for flip in (0, 2, 1, 3)])


def gather_plan(
    hidden,
    queries,
    route,
    positions,
    key_matrix,
    value_matrix,
    key_projection_bias,
    value_projection_bias,
):
    ranks = lax.axis_size("dp")
    rows = hidden.shape[0]
    slots = positions.shape[0]
    spare = rows // ranks + 2
    width = ranks * spare
    stride = -(-spare // 16) * 16
    starts = [group * spare // 16 * 16 for group in range(ranks)]
    window = max(
        -(-(group + 1) * spare // 16) * 16 - starts[group] for group in range(ranks)
    )
    depth, query_width = hidden.shape[1], queries.shape[1]
    shape = jax.ShapeDtypeStruct

    def columns(array, chunk):
        first, heads = chunk
        return array[..., first * HEAD_SIZE : (first + heads) * HEAD_SIZE]

    matrices = {}
    sending = spread(jnp.concatenate([key_matrix, value_matrix], axis=1), ranks, matrices)
    next(sending)
    bucket, seat, sorted_route = pl.pallas_call(
        functools.partial(order_kernel, ranks, slots, spare, stride),
        out_shape=(
            shape((1, rows), jnp.int32),
            shape((1, rows), jnp.int32),
            shape((1, width), jnp.int32),
        ),
        in_specs=[VMEM],
        out_specs=(VMEM, VMEM, VMEM),
        compiler_params=grant(16),
        name="order",
    )(route.reshape(1, rows))
    plan = jnp.concatenate([sorted_route.reshape(width), positions])
    plan = lax.all_to_all(
        jnp.broadcast_to(plan, (ranks, width + slots)), "dp", split_axis=0, concat_axis=0, tiled=True
    )
    plan, bucket, seat = sending.send((plan, bucket, seat))
    next(sending)
    all_positions = plan[:, width:].reshape(-1, HEAD_SIZE)
    owners = source_order(ranks)
    key_routes = plan[:, :width][owners]
    key_routes = jnp.stack(
        [key_routes[:, at : at + window].reshape(1, ranks * window) for at in starts]
    )

    half = HEAD_SIZE // 2
    frequency = 1000000.0 ** (-(jnp.arange(half, dtype=jnp.float32) * 2.0 / HEAD_SIZE))
    *turned, bounds, cosine, sine = pl.pallas_call(
        query_kernel,
        out_shape=tuple(
            shape((ranks * stride, heads * HEAD_GROUPS * HEAD_SIZE), jnp.bfloat16)
            for _, heads in CHUNKS
        )
        + (
            shape((ranks * stride, HEAD_SIZE), jnp.int32),
            shape((rows, HEAD_SIZE), jnp.float32),
            shape((rows, HEAD_SIZE), jnp.float32),
        ),
        in_specs=[VMEM] * 5,
        out_specs=(VMEM,) * (len(CHUNKS) + 3),
        compiler_params=grant(32),
        cost_estimate=cost(4 * stride * ranks * rows * query_width, 4 * rows * query_width),
        name="turn_queries",
    )(
        route.reshape(rows, 1),
        seat,
        all_positions,
        jnp.concatenate([frequency, frequency]).reshape(1, HEAD_SIZE),
        queries,
    )

    turned, bounds, cosine, sine, key_routes = sending.send(
        (turned, bounds, cosine, sine, key_routes)
    )
    next(sending)

    shard, wide = key_matrix.shape[0], 2 * key_matrix.shape[1]
    planes = ranks // PLANE

    def chip_parts(sources):
        chips, arrays = [], []
        for source in sources:
            chip = []
            for one in (source, source + 2 * planes):
                for first, array in matrices[one]:
                    chip.append((one, first))
                    arrays.append(array)
            chips.append(tuple(chip))
        return chips, arrays

    def scratch(chips, arrays):
        return [
            pltpu.VMEM((len(chips), rows, 2 * shard), jnp.bfloat16),
            pltpu.VMEM((len(chips), 2 * shard, wide), jnp.bfloat16),
            pltpu.SemaphoreType.DMA((len(chips) + len(arrays),)),
        ]

    def product_cost(chips):
        depth = 2 * shard * len(chips)
        return cost(2 * rows * depth * wide, 2 * depth * (rows + wide) + 8 * rows * wide)

    def add_part(total, sources):
        chips, arrays = chip_parts(sources)
        more = [] if total is None else [total]
        return pl.pallas_call(
            functools.partial(part_kernel, chips, bool(more)),
            out_shape=shape((rows, wide), jnp.float32),
            in_specs=[SMEM] + [HBM] * (1 + len(arrays)) + [VMEM] * len(more),
            out_specs=VMEM,
            scratch_shapes=scratch(chips, arrays),
            compiler_params=grant(28),
            cost_estimate=product_cost(chips),
            name="add_part",
        )(owners, hidden, *arrays, *more)

    total = add_part(None, (0, 1, planes))
    (total,) = sending.send((total,))
    next(sending)
    total = add_part(total, (2, planes + 1))
    total = add_part(total, (3, planes + 2))
    chips, arrays = chip_parts((planes + 3,))
    bias = jnp.concatenate([key_projection_bias, value_projection_bias])
    pairs = pl.pallas_call(
        functools.partial(finish_kernel, chips),
        out_shape=tuple(
            shape((width, 2 * heads * HEAD_SIZE), jnp.bfloat16) for _, heads in CHUNKS
        ),
        in_specs=[SMEM, HBM] + [VMEM] * 4 + [HBM] * len(arrays) + [VMEM],
        out_specs=(VMEM,) * len(CHUNKS),
        scratch_shapes=scratch(chips, arrays),
        compiler_params=grant(28),
        cost_estimate=product_cost(chips),
        name="finish",
    )(
        owners,
        hidden,
        bias.astype(jnp.float32).reshape(1, wide),
        cosine,
        sine,
        bucket,
        *arrays,
        total,
    )

    def attend(out, chunk, held, place):
        first_head, heads = CHUNKS[chunk]
        pieces = [(source, first) for source in held for first, _ in held[source]]
        arrays = [array for source in held for _, array in held[source]]
        taken = [] if out is None else [out]
        fixed = [turned[chunk], bounds, key_routes, seat]
        span = HEAD_GROUPS * HEAD_SIZE
        return pl.pallas_call(
            functools.partial(
                attend_kernel, (first_head, place), heads, pieces, spare, window, stride
            ),
            grid=(1,),
            out_shape=shape((rows, query_width), jnp.bfloat16),
            in_specs=[pl.BlockSpec((ranks * stride, span), lambda i, p=place: (0, p))]
            + [VMEM] * 3
            + [HBM] * (len(pieces) + len(taken)),
            out_specs=HBM,
            scratch_shapes=[
                pltpu.VMEM((2, ranks, width, HEAD_SIZE), jnp.bfloat16),
                pltpu.VMEM((ranks * stride, span), jnp.bfloat16),
                pltpu.VMEM((rows, span), jnp.bfloat16),
                pltpu.SemaphoreType.DMA((2 * len(pieces) + 1,)),
            ],
            input_output_aliases={len(fixed) + len(pieces): 0} if taken else {},
            compiler_params=grant(28),
            cost_estimate=cost(
                16 * rows * stride * ranks * span, 4 * ranks * width * HEAD_SIZE
            ),
            name="attend",
        )(*fixed, *arrays, *taken)

    early, late = {}, {}
    sending = spread(pairs[0], ranks, early)
    for _ in range(planes - 1):
        next(sending)
        sending.send(())
    mark = next(sending)
    last, _ = lax.optimization_barrier((pairs[1], mark))
    sending = spread(last, ranks, late)
    out = None
    next(sending)
    sending.send(())
    for place in range(2):
        next(sending)
        out = attend(out, 0, early, place)
        (out,) = sending.send((out,))
    next(sending)
    out = attend(out, 0, early, 2)
    return attend(out, 1, late, 0)


def apply_rotary(rows, slot_offset, heads):
    block_count = rows.shape[0]
    half = HEAD_SIZE // 2
    frequency = 1000000.0 ** (-(jnp.arange(half, dtype=jnp.float32) * 2.0 / HEAD_SIZE))
    angle = slot_offset.astype(jnp.float32)[:, None] * frequency[None, :]
    cosine = jnp.cos(angle)[:, None, :]
    sine = jnp.sin(angle)[:, None, :]
    grid = rows.astype(jnp.float32).reshape(block_count, heads, HEAD_SIZE)
    first = grid[:, :, :half]
    second = grid[:, :, half:]
    turned = jnp.concatenate(
        [first * cosine - second * sine, second * cosine + first * sine], axis=2
    )
    return turned.reshape(block_count, heads * HEAD_SIZE).astype(jnp.bfloat16)


def causal_block_attention(pieces):
    query_tile_rows, key_tile_rows, value_tile_rows, spot_block = pieces
    block_count = query_tile_rows.shape[0]
    head_groups = QUERY_HEADS // KEY_VALUE_HEADS
    query_block_grid = query_tile_rows.reshape(block_count, KEY_VALUE_HEADS, head_groups, HEAD_SIZE)
    key_block_grid = key_tile_rows.reshape(block_count, KEY_VALUE_HEADS, HEAD_SIZE)
    value_block_grid = value_tile_rows.reshape(block_count, KEY_VALUE_HEADS, HEAD_SIZE)
    scores = jnp.einsum(
        "qhgd,khd->hgqk", query_block_grid, key_block_grid, preferred_element_type=jnp.float32
    ) / math.sqrt(HEAD_SIZE)
    inner = jnp.arange(block_count, dtype=jnp.int32)
    visible = (inner[None, :] <= inner[:, None]) & (
        inner[None, :] >= inner[:, None] - spot_block[:, None]
    )
    scores = jnp.where(visible, scores, -jnp.inf)
    top = jnp.max(scores, axis=3, keepdims=True)
    weights = jnp.exp(scores - top)
    totals = jnp.sum(weights, axis=3)
    probs = weights.astype(jnp.bfloat16)
    mixed = jnp.einsum(
        "hgqk,khd->qhgd", probs, value_block_grid, preferred_element_type=jnp.float32
    )
    mixed = mixed / jnp.transpose(totals, (2, 0, 1))[:, :, :, None]
    return mixed.reshape(block_count, QUERY_HEADS * HEAD_SIZE).astype(jnp.bfloat16)


def add_projection(left, pieces):
    return (
        jnp.dot(left, pieces[0], preferred_element_type=jnp.float32),
        jnp.dot(left, pieces[1], preferred_element_type=jnp.float32),
    )


def project_own(hidden, key_matrix, value_matrix, key_projection_bias, value_projection_bias):
    totals = add_projection(
        hidden,
        (
            lax.all_gather(key_matrix, "dp", axis=0, tiled=True),
            lax.all_gather(value_matrix, "dp", axis=0, tiled=True),
        ),
    )
    key_rows = (totals[0] + key_projection_bias.astype(jnp.float32)).astype(jnp.bfloat16)
    value_rows = (totals[1] + value_projection_bias.astype(jnp.float32)).astype(jnp.bfloat16)
    return jnp.concatenate([key_rows, value_rows], axis=1)


def send_plan(
    hidden,
    queries,
    route,
    positions,
    key_matrix,
    value_matrix,
    key_projection_bias,
    value_projection_bias,
):
    ranks = lax.axis_size("dp")
    rows = hidden.shape[0]
    slots = positions.shape[0]
    spare = rows // ranks + 2
    width = ranks * spare
    paired_width = key_matrix.shape[1]
    target = route // slots
    place = route - target * slots
    member = (target[:, None] == jnp.arange(ranks, dtype=jnp.int32)[None, :]).astype(jnp.int32)
    order = jnp.sum(jnp.cumsum(member, axis=0) * member, axis=1) - 1
    bucket = target * spare + order
    outgoing = jnp.full((width,), slots, jnp.int32).at[bucket].set(place)
    arrived = lax.all_to_all(
        outgoing.reshape(ranks, spare), "dp", split_axis=0, concat_axis=0, tiled=True
    ).reshape(width)
    query_buf = jnp.zeros((width, queries.shape[1]), jnp.bfloat16).at[bucket].set(queries)
    own_pairs = project_own(
        hidden, key_matrix, value_matrix, key_projection_bias, value_projection_bias
    )
    pair_buf = jnp.zeros((width, 2 * paired_width), jnp.bfloat16).at[bucket].set(own_pairs)
    got_query, got_pairs = (
        lax.all_to_all(
            query_buf.reshape(ranks, spare, -1), "dp", split_axis=0, concat_axis=0, tiled=True
        ),
        lax.all_to_all(
            pair_buf.reshape(ranks, spare, -1), "dp", split_axis=0, concat_axis=0, tiled=True
        ),
    )
    got_query = got_query.reshape(width, -1)
    got_pairs = got_pairs.reshape(width, -1)
    query_slot_rows = (
        jnp.zeros((slots, got_query.shape[1]), jnp.bfloat16).at[arrived].set(got_query, mode="drop")
    )
    paired_slot_rows = (
        jnp.zeros((slots, 2 * paired_width), jnp.bfloat16).at[arrived].set(got_pairs, mode="drop")
    )
    query_turned = apply_rotary(query_slot_rows, positions, QUERY_HEADS)
    key_rotated = apply_rotary(paired_slot_rows[:, :paired_width], positions, KEY_VALUE_HEADS)
    block_list = slots // BLOCK_SLOTS
    attended = lax.map(
        causal_block_attention,
        (
            query_turned.reshape(block_list, BLOCK_SLOTS, -1),
            key_rotated.reshape(block_list, BLOCK_SLOTS, -1),
            paired_slot_rows[:, paired_width:].reshape(block_list, BLOCK_SLOTS, -1),
            positions.reshape(block_list, BLOCK_SLOTS),
        ),
    )
    attended = attended.reshape(slots, -1)
    leaving = attended[jnp.minimum(arrived, slots - 1)]
    returned = lax.all_to_all(
        leaving.reshape(ranks, spare, -1), "dp", split_axis=0, concat_axis=0, tiled=True
    ).reshape(width, -1)
    return returned[bucket]


def local(*args):
    hidden, queries, _, positions, key_matrix = args[:5]
    ranks = lax.axis_size("dp")
    rows = hidden.shape[0]
    gathered = ranks * ranks * (rows // ranks + 2) * 4 * key_matrix.shape[1]
    chip_rows = 2 * key_matrix.shape[0]
    fits = rows % ranks == 0 and chip_rows % HEAD_SIZE == 0 and gathered <= GATHER_LIMIT
    if ranks == PLANES * PLANE and fits:
        return gather_plan(*args)
    return send_plan(*args)


def solution(mesh):
    placed = (
        P(("groups", "dp"), None),
        P(("groups", "dp"), None),
        P(("groups", "dp")),
        P(("groups", "dp")),
        P("dp", None),
        P("dp", None),
        P(),
        P(),
    )
    return jax.shard_map(
        local, mesh=mesh, in_specs=placed, out_specs=P(("groups", "dp"), None), check_vma=False
    )
```

```python
import functools
import math

import jax
import jax.numpy as jnp
from jax import lax
from jax.experimental import pallas as pl
from jax.experimental.pallas import tpu as pltpu
from jax.sharding import PartitionSpec as P

QUERY_HEADS = 20
KEY_VALUE_HEADS = 4
HEAD_SIZE = 128
BLOCK_SLOTS = 512
HEAD_GROUPS = QUERY_HEADS // KEY_VALUE_HEADS
CHUNKS = ((0, 3), (3, 1))
PLANE = 4
PLANES = 4
UNROLL = 4
GATHER_LIMIT = 40 * 2**20
MASKED = -1e30
VMEM = pl.BlockSpec(memory_space=pltpu.VMEM)
SMEM = pl.BlockSpec(memory_space=pltpu.SMEM)
HBM = pl.BlockSpec(memory_space=pltpu.HBM)


def grant(mebibytes):
    return pltpu.CompilerParams(vmem_limit_bytes=mebibytes * 2**20)


def cost(flops, moved):
    return pl.CostEstimate(flops=flops, bytes_accessed=moved, transcendentals=0)


def one_hot_rows(count, index_row):
    rows = lax.broadcasted_iota(jnp.int32, (count, index_row.shape[1]), 0)
    return (rows == index_row).astype(jnp.float32).astype(jnp.bfloat16)


def contract(left, right, left_dim, right_dim):
    return lax.dot_general(
        left, right, (((left_dim,), (right_dim,)), ((), ())), preferred_element_type=jnp.float32
    )


def turn(rows, cosine, sine):
    return (rows * cosine + pltpu.roll(rows, HEAD_SIZE // 2, 1) * sine).astype(jnp.bfloat16)


def order_kernel(
    ranks, slots, extra, stride, route_ref, bucket_ref, seat_ref, sorted_ref, more_ref
):
    route = route_ref[...]
    count = route.shape[1]
    share = count // ranks
    target = lax.div(route, slots)
    member = (lax.broadcasted_iota(jnp.int32, (ranks, count), 0) == target).astype(jnp.float32)
    before = lax.broadcasted_iota(jnp.int32, (count, count), 0) < lax.broadcasted_iota(
        jnp.int32, (count, count), 1
    )
    before = before.astype(jnp.float32).astype(jnp.bfloat16)
    ahead = contract(member.astype(jnp.bfloat16), before, 1, 0)
    order = jnp.sum(member * ahead, axis=0, keepdims=True).astype(jnp.int32)
    beyond = order >= share
    beyond_rows = jnp.broadcast_to(beyond.astype(jnp.float32), (8, count)).astype(jnp.bfloat16)
    number = contract(beyond_rows, before, 1, 0)[0:1]
    counts = jnp.sum(member, axis=1, keepdims=True)
    free = jnp.maximum(share - counts, 0.0)
    group = lax.broadcasted_iota(jnp.int32, (ranks, ranks), 0)
    lower = (group > lax.broadcasted_iota(jnp.int32, (ranks, ranks), 1)).astype(jnp.float32)
    free_rows = jnp.broadcast_to(free, (ranks, HEAD_SIZE)).astype(jnp.bfloat16)
    free_before = contract(lower.astype(jnp.bfloat16), free_rows, 1, 0)[:, 0:1]
    inside = (number >= free_before) & (number < free_before + free)
    base = lax.broadcasted_iota(jnp.int32, (ranks, 1), 0).astype(jnp.float32) * share + counts
    hole = jnp.sum(jnp.where(inside, base + number - free_before, 0.0), axis=0, keepdims=True)
    bucket = jnp.where(beyond, hole.astype(jnp.int32), target * share + order)
    bucket_ref[...] = bucket
    seat_ref[...] = target * stride + order
    high = lax.div(route, HEAD_SIZE)
    place_high = lax.div(bucket, HEAD_SIZE)
    line = lax.broadcasted_iota(jnp.int32, (8, count), 0)
    digits = jnp.where(line == 0, high, 0)
    digits = jnp.where(line == 1, route - high * HEAD_SIZE, digits)
    digits = jnp.where(line == 2, place_high, digits)
    digits = jnp.where(line == 3, bucket - place_high * HEAD_SIZE, digits)
    digits = jnp.where(line == 4, 1, digits).astype(jnp.float32).astype(jnp.bfloat16)
    placed = contract(digits, one_hot_rows(count, bucket), 1, 1)
    sorted_ref[...] = (placed[0:1] * HEAD_SIZE + placed[1:2]).astype(jnp.int32)
    listed = jnp.where(beyond, target * extra + order - share, -1)
    found = contract(digits, one_hot_rows(ranks * extra, listed), 1, 1)
    none = found[4:5] - 1.0
    more_ref[0:1] = (found[0:1] * HEAD_SIZE + found[1:2] + none).astype(jnp.int32)
    more_ref[1:2] = (found[2:3] * HEAD_SIZE + found[3:4] + none).astype(jnp.int32)


def query_kernel(
    ranks, spare, stride, packed, route_ref, seat_ref, positions_ref, frequency_ref, queries_ref, *refs
):
    turned_ref, bounds_ref, cosine_ref, sine_ref, rows_ref = refs
    route = route_ref[...]
    count = route.shape[0]
    lines = positions_ref.shape[0]
    line = lax.div(route, HEAD_SIZE)
    lane = route - line * HEAD_SIZE
    pick = (lax.broadcasted_iota(jnp.int32, (count, lines), 1) == line).astype(jnp.float32)
    pick = pick.astype(jnp.bfloat16)
    positions = positions_ref[...]
    half = lax.div(positions, 2)
    rest = positions - half * 2
    rows = 2.0 * contract(pick, half.astype(jnp.float32).astype(jnp.bfloat16), 1, 0) + contract(
        pick, rest.astype(jnp.float32).astype(jnp.bfloat16), 1, 0
    )
    lanes = lax.broadcasted_iota(jnp.int32, (count, HEAD_SIZE), 1)
    spot = jnp.sum(jnp.where(lanes == lane, rows, 0.0), axis=1, keepdims=True)
    angle = spot * frequency_ref[...]
    cosine = jnp.cos(angle)
    sine = jnp.sin(angle)
    sine = jnp.where(lanes < HEAD_SIZE // 2, -sine, sine)
    cosine_ref[...] = cosine
    sine_ref[...] = sine
    seats = one_hot_rows(ranks * stride, seat_ref[...])
    first = route - spot.astype(jnp.int32)
    first_line = lax.div(first, HEAD_SIZE)
    first_lane = first - first_line * HEAD_SIZE
    digits = jnp.where(lanes == 0, line, 0)
    digits = jnp.where(lanes == 1, lane, digits)
    digits = jnp.where(lanes == 2, first_line, digits)
    digits = jnp.where(lanes == 3, first_lane, digits)
    digits = jnp.where(lanes == 4, 1, digits)
    placed = contract(seats, digits.astype(jnp.float32).astype(jnp.bfloat16), 1, 0)
    live = placed[:, 4:5] - 1.0
    last = placed[:, 0:1] * HEAD_SIZE + placed[:, 1:2] + live
    start = placed[:, 2:3] * HEAD_SIZE + placed[:, 3:4] + live
    seat_lanes = lax.broadcasted_iota(jnp.int32, placed.shape, 1)
    bounds = jnp.where(seat_lanes == 0, last, start).astype(jnp.int32)
    bounds_ref[...] = jnp.full(bounds_ref.shape, -1, jnp.int32)
    rows_ref[...] = jnp.zeros(rows_ref.shape, jnp.float32)
    for group in range(ranks):
        for place in range(HEAD_GROUPS):
            at = group * packed + place * spare
            bounds_ref[at : at + spare] = bounds[group * stride : group * stride + spare]
    for head in range(KEY_VALUE_HEADS):
        for place in range(HEAD_GROUPS):
            at = (head * HEAD_GROUPS + place) * HEAD_SIZE
            one = queries_ref[:, at : at + HEAD_SIZE].astype(jnp.float32)
            rows = contract(seats, turn(one, cosine, sine), 1, 0)
            for group in range(ranks):
                at = group * packed + place * spare
                rows_ref[at : at + spare] = rows[group * stride : group * stride + spare]
        turned_ref[head] = rows_ref[...].astype(jnp.bfloat16)


def add_products(chips, owners_ref, hidden_ref, refs, columns, matrix, done):
    shard = matrix.shape[1] // 2
    copies, at, taken = [], 0, 0
    for place, chip in enumerate(chips):
        first = pl.multiple_of(lax.div(owners_ref[chip[0][0]], 2) * (2 * shard), HEAD_SIZE)
        copies.append(
            (hidden_ref.at[:, pl.ds(first, 2 * shard)], columns.at[place])
        )
        for source, row in chip:
            core = lax.rem(owners_ref[source], 2)
            rows = pl.ds(pl.multiple_of(core * shard + row, 16), refs[taken].shape[0])
            copies.append((refs[taken], matrix.at[place, rows]))
            taken += 1
    copies = [pltpu.make_async_copy(*pair, done.at[at]) for at, pair in enumerate(copies)]
    for copy in copies:
        copy.start()

    def product(span):
        total = contract(columns[0], matrix[0, :, span], 1, 0)
        for place in range(1, len(chips)):
            total = total + contract(columns[place], matrix[place, :, span], 1, 0)
        return total

    return copies, product


def part_kernel(chips, more, owners_ref, hidden_ref, *refs):
    count = sum(len(chip) for chip in chips)
    parts, refs = refs[:count], refs[count:]
    if more:
        total_ref, refs = refs[0], refs[1:]
    out_ref, columns, matrix, done = refs
    copies, product = add_products(chips, owners_ref, hidden_ref, parts, columns, matrix, done)
    for copy in copies:
        copy.wait()
    for first in range(0, out_ref.shape[1], 2 * HEAD_SIZE):
        span = slice(first, first + 2 * HEAD_SIZE)
        if more:
            out_ref[:, span] = total_ref[:, span] + product(span)
        else:
            out_ref[:, span] = product(span)


def finish_kernel(
    chips, owners_ref, hidden_ref, bias_ref, cosine_ref, sine_ref, bucket_ref, *refs
):
    count = sum(len(chip) for chip in chips)
    parts, total_ref = refs[:count], refs[count]
    outs, (columns, matrix, done) = refs[count + 1 : -3], refs[-3:]
    copies, product = add_products(chips, owners_ref, hidden_ref, parts, columns, matrix, done)
    places = one_hot_rows(outs[0].shape[0], bucket_ref[...])
    for copy in copies:
        copy.wait()
    wide = KEY_VALUE_HEADS * HEAD_SIZE
    for first in range(0, 2 * wide, 2 * HEAD_SIZE):
        span = slice(first, first + 2 * HEAD_SIZE)
        rows = (total_ref[:, span] + product(span) + bias_ref[:, span]).astype(jnp.bfloat16)
        if first < wide:
            cosine, sine = cosine_ref[...], sine_ref[...]
            halves = [
                turn(rows[:, at : at + HEAD_SIZE].astype(jnp.float32), cosine, sine)
                for at in (0, HEAD_SIZE)
            ]
            rows = jnp.concatenate(halves, axis=1)
        rows = contract(places, rows, 1, 0).astype(jnp.bfloat16)
        for half in range(2):
            head = first % wide // HEAD_SIZE + half
            for (first_head, heads), out_ref in zip(CHUNKS, outs):
                if first_head <= head < first_head + heads:
                    at = (head - first_head + first // wide * heads) * HEAD_SIZE
                    out_ref[:, at : at + HEAD_SIZE] = rows[
                        :, half * HEAD_SIZE : (half + 1) * HEAD_SIZE
                    ]


def attend_kernel(
    head, heads, pieces, extra, stride, packed,
    queries_ref, bounds_ref, routes_ref, seat_ref, more_ref, *refs
):
    first_head, place = head
    ranks = routes_ref.shape[0]
    parts, refs = refs[: len(pieces)], refs[-(6 + 3 * UNROLL) :]
    out_ref, blocks, more, mixed_ref, result_ref, done = refs[:6]
    score_refs, weight_refs, total_refs = (
        refs[6 + at * UNROLL : 6 + (at + 1) * UNROLL] for at in range(3)
    )
    count = blocks.shape[2]
    share = count // ranks
    spare = share + extra
    copies = []
    for at, ((source, first), ref) in enumerate(zip(pieces, parts)):
        for part in range(2):
            lanes = pl.ds((part * heads + place) * HEAD_SIZE, HEAD_SIZE)
            copies.append(
                pltpu.make_async_copy(
                    ref.at[:, lanes],
                    blocks.at[part, source, pl.ds(first, ref.shape[0])],
                    done.at[2 * at + part],
                )
            )
            copies[-1].start()
    mixed_ref[...] = jnp.zeros(mixed_ref.shape, jnp.bfloat16)
    listed = ranks * extra
    lines = lax.broadcasted_iota(jnp.int32, (listed, count), 1)
    picks = [
        (lines == more_ref[j * listed : (j + 1) * listed]).astype(jnp.float32).astype(jnp.bfloat16)
        for j in range(ranks)
    ]
    row = lax.broadcasted_iota(jnp.int32, (ranks * listed, ranks * listed), 0)
    column = lax.broadcasted_iota(jnp.int32, (ranks * listed, ranks * listed), 1)
    group, rest = lax.div(row, listed), lax.rem(row, listed)
    source, index = lax.div(rest, extra), lax.rem(rest, extra)
    regroup = (column == source * listed + group * extra + index).astype(jnp.float32)
    regroup = regroup.astype(jnp.bfloat16)
    for copy in copies:
        copy.wait()
    for part in range(2):
        found = [
            contract(picks[j], blocks[part, j], 1, 0).astype(jnp.bfloat16) for j in range(ranks)
        ]
        more[part] = contract(regroup, jnp.concatenate(found, axis=0), 1, 0).astype(jnp.bfloat16)
    scale = math.log2(math.e) / math.sqrt(HEAD_SIZE)

    def rows_of(part, group):
        window = pl.ds(pl.multiple_of(group * share, 16), share)
        rows = [blocks[part, j, window] for j in range(ranks)]
        rows.append(more[part, pl.ds(pl.multiple_of(group * listed, 16), listed)])
        return jnp.concatenate(rows, axis=0)

    def score(group, score_ref):
        query = queries_ref[0, pl.ds(pl.multiple_of(group * packed, 16), packed)]
        score_ref[...] = contract(query, rows_of(0, group), 1, 1)

    def weigh(group, score_ref, weight_ref, total_ref):
        routes = routes_ref[group]
        for first in range(0, packed, 16):
            at = pl.ds(pl.multiple_of(group * packed + first, 16), 16)
            visible = (routes <= bounds_ref[at, 0:1]) & (routes >= bounds_ref[at, 1:2])
            scores = jnp.where(visible, score_ref[first : first + 16], MASKED)
            top = jnp.max(scores, axis=1, keepdims=True)
            weights = jnp.exp2((scores - top) * scale)
            total = jnp.sum(weights, axis=1, keepdims=True)
            weight_ref[first : first + 16] = weights.astype(jnp.bfloat16)
            total_ref[first : first + 16] = jnp.broadcast_to(1.0 / total, (16, HEAD_SIZE))

    def mix(group, weight_ref, total_ref):
        mixed = contract(weight_ref[...], rows_of(1, group), 1, 0) * total_ref[...]
        seats = pl.ds(pl.multiple_of(group * stride, 16), spare)
        for at in range(HEAD_GROUPS):
            lanes = slice(at * HEAD_SIZE, (at + 1) * HEAD_SIZE)
            mixed_ref[seats, lanes] = mixed[at * spare : (at + 1) * spare].astype(jnp.bfloat16)

    def some_groups(step, carry):
        groups = [step * UNROLL + at for at in range(UNROLL)]
        for at in range(UNROLL + 2):
            if at < UNROLL:
                score(groups[at], score_refs[at])
            if 0 <= at - 1 < UNROLL:
                weigh(groups[at - 1], score_refs[at - 1], weight_refs[at - 1], total_refs[at - 1])
            if 0 <= at - 2 < UNROLL:
                mix(groups[at - 2], weight_refs[at - 2], total_refs[at - 2])
        return carry

    lax.fori_loop(0, ranks // UNROLL, some_groups, 0)
    seats = one_hot_rows(mixed_ref.shape[0], seat_ref[...])
    result_ref[...] = contract(seats, mixed_ref[...], 0, 0).astype(jnp.bfloat16)
    lanes = pl.ds((first_head + place) * HEAD_GROUPS * HEAD_SIZE, HEAD_GROUPS * HEAD_SIZE)
    leave = pltpu.make_async_copy(result_ref, out_ref.at[:, lanes], done.at[2 * len(pieces)])
    leave.start()
    leave.wait()


def spread(block, ranks, held):
    ring = [(rank, (rank + PLANE) % ranks) for rank in range(ranks)]
    across = [(rank, rank ^ 2) for rank in range(ranks)]
    beside = [(rank, rank ^ 1) for rank in range(ranks)]
    steps = ranks // PLANE
    half = block.shape[0] // 32 * 16

    def keep(source, first, array):
        held.setdefault(source, []).append((first, array))
        held.setdefault(source + 2 * steps, []).append((first, lax.ppermute(array, "dp", beside)))

    lane, other = block, None
    for step in range(steps - 1):
        following = lax.ppermute(lane, "dp", ring), lax.ppermute(lane, "dp", across)
        keep(step, 0, lane)
        if step:
            keep(steps + step - 1, 0, other)
        extra = yield
        lane, other, extra = lax.optimization_barrier((*following, extra))
        yield extra
    over = lax.ppermute(lane[:half], "dp", across)
    around = lax.ppermute(other[half:], "dp", ring)
    keep(steps - 1, 0, lane)
    keep(2 * steps - 2, 0, other)
    extra = yield other
    over, around, extra = lax.optimization_barrier((over, around, extra))
    keep(2 * steps - 1, 0, over)
    keep(2 * steps - 1, half, around)
    yield extra


def source_order(ranks):
    me = lax.axis_index("dp")
    lane, plane = me % PLANE, me // PLANE
    steps = ranks // PLANE
    planes = (plane - jnp.arange(steps, dtype=jnp.int32)) % steps
    return jnp.concatenate([planes * PLANE + (lane ^ flip) for flip in (0, 2, 1, 3)])


def gather_plan(
    hidden,
    queries,
    route,
    positions,
    key_matrix,
    value_matrix,
    key_projection_bias,
    value_projection_bias,
):
    ranks = lax.axis_size("dp")
    rows = hidden.shape[0]
    slots = positions.shape[0]
    share, extra = rows // ranks, 2
    spare = share + extra
    listed = ranks * extra
    stride = -(-spare // 16) * 16
    packed = -(-HEAD_GROUPS * spare // 16) * 16
    key_count = ranks * (share + extra)
    query_width = queries.shape[1]
    shape = jax.ShapeDtypeStruct

    def columns(array, chunk):
        first, heads = chunk
        return array[..., first * HEAD_SIZE : (first + heads) * HEAD_SIZE]

    matrices = {}
    sending = spread(jnp.concatenate([key_matrix, value_matrix], axis=1), ranks, matrices)
    next(sending)
    bucket, seat, sorted_route, more = pl.pallas_call(
        functools.partial(order_kernel, ranks, slots, extra, stride),
        out_shape=(
            shape((1, rows), jnp.int32),
            shape((1, rows), jnp.int32),
            shape((1, rows), jnp.int32),
            shape((2, listed), jnp.int32),
        ),
        in_specs=[VMEM],
        out_specs=(VMEM,) * 4,
        compiler_params=grant(16),
        name="order",
    )(route.reshape(1, rows))
    width = rows + 2 * listed
    plan = jnp.concatenate([sorted_route.reshape(rows), more.reshape(2 * listed), positions])
    plan = lax.all_to_all(
        jnp.broadcast_to(plan, (ranks, width + slots)), "dp", split_axis=0, concat_axis=0, tiled=True
    )
    sending.send(())
    next(sending)
    plan, bucket, seat = sending.send((plan, bucket, seat))
    next(sending)
    all_positions = plan[:, width:].reshape(-1, HEAD_SIZE)
    owners = source_order(ranks)
    sources = plan[:, :width][owners]
    key_routes = jnp.concatenate(
        [
            sources[:, :rows].reshape(ranks, ranks, share).transpose(1, 0, 2).reshape(ranks, -1),
            sources[:, rows : rows + listed]
            .reshape(ranks, ranks, extra)
            .transpose(1, 0, 2)
            .reshape(ranks, -1),
        ],
        axis=1,
    ).reshape(ranks, 1, key_count)
    more_places = sources[:, rows + listed :].reshape(ranks * listed, 1)

    half = HEAD_SIZE // 2
    frequency = 1000000.0 ** (-(jnp.arange(half, dtype=jnp.float32) * 2.0 / HEAD_SIZE))
    turned, bounds, cosine, sine = pl.pallas_call(
        functools.partial(query_kernel, ranks, spare, stride, packed),
        out_shape=(
            shape((KEY_VALUE_HEADS, ranks * packed, HEAD_SIZE), jnp.bfloat16),
            shape((ranks * packed, HEAD_SIZE), jnp.int32),
            shape((rows, HEAD_SIZE), jnp.float32),
            shape((rows, HEAD_SIZE), jnp.float32),
        ),
        in_specs=[VMEM] * 5,
        out_specs=(VMEM,) * 4,
        scratch_shapes=[pltpu.VMEM((ranks * packed, HEAD_SIZE), jnp.float32)],
        compiler_params=grant(32),
        cost_estimate=cost(4 * stride * ranks * rows * query_width, 4 * rows * query_width),
        name="turn_queries",
    )(
        route.reshape(rows, 1),
        seat,
        all_positions,
        jnp.concatenate([frequency, frequency]).reshape(1, HEAD_SIZE),
        queries,
    )

    shard, wide = key_matrix.shape[0], 2 * key_matrix.shape[1]
    planes = ranks // PLANE

    def chip_parts(sources):
        chips, arrays = [], []
        for source in sources:
            chip = []
            for one in (source, source + 2 * planes):
                for first, array in matrices[one]:
                    chip.append((one, first))
                    arrays.append(array)
            chips.append(tuple(chip))
        return chips, arrays

    def scratch(chips, arrays):
        return [
            pltpu.VMEM((len(chips), rows, 2 * shard), jnp.bfloat16),
            pltpu.VMEM((len(chips), 2 * shard, wide), jnp.bfloat16),
            pltpu.SemaphoreType.DMA((len(chips) + len(arrays),)),
        ]

    def product_cost(chips):
        depth = 2 * shard * len(chips)
        return cost(2 * rows * depth * wide, 2 * depth * (rows + wide) + 8 * rows * wide)

    def add_part(total, sources):
        chips, arrays = chip_parts(sources)
        more = [] if total is None else [total]
        return pl.pallas_call(
            functools.partial(part_kernel, chips, bool(more)),
            out_shape=shape((rows, wide), jnp.float32),
            in_specs=[SMEM] + [HBM] * (1 + len(arrays)) + [VMEM] * len(more),
            out_specs=VMEM,
            scratch_shapes=scratch(chips, arrays),
            compiler_params=grant(28),
            cost_estimate=product_cost(chips),
            name="add_part",
        )(owners, hidden, *arrays, *more)

    total = add_part(None, (0, 1, planes))
    turned, bounds, cosine, sine, key_routes, more_places, total = sending.send(
        (turned, bounds, cosine, sine, key_routes, more_places, total)
    )
    next(sending)
    (total,) = sending.send((add_part(total, (2, planes + 1)),))
    total = add_part(total, (3, planes + 2))
    chips, arrays = chip_parts((planes + 3,))
    bias = jnp.concatenate([key_projection_bias, value_projection_bias])
    pairs = pl.pallas_call(
        functools.partial(finish_kernel, chips),
        out_shape=tuple(
            shape((rows, 2 * heads * HEAD_SIZE), jnp.bfloat16) for _, heads in CHUNKS
        ),
        in_specs=[SMEM, HBM] + [VMEM] * 4 + [HBM] * len(arrays) + [VMEM],
        out_specs=(VMEM,) * len(CHUNKS),
        scratch_shapes=scratch(chips, arrays),
        compiler_params=grant(28),
        cost_estimate=product_cost(chips),
        name="finish",
    )(
        owners,
        hidden,
        bias.astype(jnp.float32).reshape(1, wide),
        cosine,
        sine,
        bucket,
        *arrays,
        total,
    )

    def attend(out, chunk, held, place):
        first_head, heads = CHUNKS[chunk]
        pieces = [(source, first) for source in held for first, _ in held[source]]
        arrays = [array for source in held for _, array in held[source]]
        taken = [] if out is None else [out]
        fixed = [turned, bounds, key_routes, seat, more_places]
        span = HEAD_GROUPS * HEAD_SIZE
        query_block = pl.BlockSpec(
            (1, ranks * packed, HEAD_SIZE), lambda i, h=first_head + place: (h, 0, 0)
        )
        return pl.pallas_call(
            functools.partial(
                attend_kernel, (first_head, place), heads, pieces, extra, stride, packed
            ),
            grid=(1,),
            out_shape=shape((rows, query_width), jnp.bfloat16),
            in_specs=[query_block] + [VMEM] * 4 + [HBM] * (len(pieces) + len(taken)),
            out_specs=HBM,
            scratch_shapes=[
                pltpu.VMEM((2, ranks, rows, HEAD_SIZE), jnp.bfloat16),
                pltpu.VMEM((2, ranks * listed, HEAD_SIZE), jnp.bfloat16),
                pltpu.VMEM((ranks * stride, span), jnp.bfloat16),
                pltpu.VMEM((rows, span), jnp.bfloat16),
                pltpu.SemaphoreType.DMA((2 * len(pieces) + 1,)),
            ]
            + [pltpu.VMEM((packed, key_count), jnp.float32)] * UNROLL
            + [pltpu.VMEM((packed, key_count), jnp.bfloat16)] * UNROLL
            + [pltpu.VMEM((packed, HEAD_SIZE), jnp.float32)] * UNROLL,
            input_output_aliases={len(fixed) + len(pieces): 0} if taken else {},
            compiler_params=grant(28),
            cost_estimate=cost(
                16 * rows * stride * ranks * span, 4 * ranks * rows * HEAD_SIZE
            ),
            name="attend",
        )(*fixed, *arrays, *taken)

    early, late = {}, {}
    sending = spread(pairs[0], ranks, early)
    for _ in range(planes - 1):
        next(sending)
        sending.send(())
    mark = next(sending)
    sending.send(())
    last, _ = lax.optimization_barrier((pairs[1], mark))
    sending = spread(last, ranks, late)
    out = None
    next(sending)
    sending.send(())
    for place in range(2):
        next(sending)
        out = attend(out, 0, early, place)
        (out,) = sending.send((out,))
    next(sending)
    (out,) = sending.send((attend(out, 0, early, 2),))
    return attend(out, 1, late, 0)


def apply_rotary(rows, slot_offset, heads):
    block_count = rows.shape[0]
    half = HEAD_SIZE // 2
    frequency = 1000000.0 ** (-(jnp.arange(half, dtype=jnp.float32) * 2.0 / HEAD_SIZE))
    angle = slot_offset.astype(jnp.float32)[:, None] * frequency[None, :]
    cosine = jnp.cos(angle)[:, None, :]
    sine = jnp.sin(angle)[:, None, :]
    grid = rows.astype(jnp.float32).reshape(block_count, heads, HEAD_SIZE)
    first = grid[:, :, :half]
    second = grid[:, :, half:]
    turned = jnp.concatenate(
        [first * cosine - second * sine, second * cosine + first * sine], axis=2
    )
    return turned.reshape(block_count, heads * HEAD_SIZE).astype(jnp.bfloat16)


def causal_block_attention(pieces):
    query_tile_rows, key_tile_rows, value_tile_rows, spot_block = pieces
    block_count = query_tile_rows.shape[0]
    head_groups = QUERY_HEADS // KEY_VALUE_HEADS
    query_block_grid = query_tile_rows.reshape(block_count, KEY_VALUE_HEADS, head_groups, HEAD_SIZE)
    key_block_grid = key_tile_rows.reshape(block_count, KEY_VALUE_HEADS, HEAD_SIZE)
    value_block_grid = value_tile_rows.reshape(block_count, KEY_VALUE_HEADS, HEAD_SIZE)
    scores = jnp.einsum(
        "qhgd,khd->hgqk", query_block_grid, key_block_grid, preferred_element_type=jnp.float32
    ) / math.sqrt(HEAD_SIZE)
    inner = jnp.arange(block_count, dtype=jnp.int32)
    visible = (inner[None, :] <= inner[:, None]) & (
        inner[None, :] >= inner[:, None] - spot_block[:, None]
    )
    scores = jnp.where(visible, scores, -jnp.inf)
    top = jnp.max(scores, axis=3, keepdims=True)
    weights = jnp.exp(scores - top)
    totals = jnp.sum(weights, axis=3)
    probs = weights.astype(jnp.bfloat16)
    mixed = jnp.einsum(
        "hgqk,khd->qhgd", probs, value_block_grid, preferred_element_type=jnp.float32
    )
    mixed = mixed / jnp.transpose(totals, (2, 0, 1))[:, :, :, None]
    return mixed.reshape(block_count, QUERY_HEADS * HEAD_SIZE).astype(jnp.bfloat16)


def add_projection(left, pieces):
    return (
        jnp.dot(left, pieces[0], preferred_element_type=jnp.float32),
        jnp.dot(left, pieces[1], preferred_element_type=jnp.float32),
    )


def project_own(hidden, key_matrix, value_matrix, key_projection_bias, value_projection_bias):
    totals = add_projection(
        hidden,
        (
            lax.all_gather(key_matrix, "dp", axis=0, tiled=True),
            lax.all_gather(value_matrix, "dp", axis=0, tiled=True),
        ),
    )
    key_rows = (totals[0] + key_projection_bias.astype(jnp.float32)).astype(jnp.bfloat16)
    value_rows = (totals[1] + value_projection_bias.astype(jnp.float32)).astype(jnp.bfloat16)
    return jnp.concatenate([key_rows, value_rows], axis=1)


def send_plan(
    hidden,
    queries,
    route,
    positions,
    key_matrix,
    value_matrix,
    key_projection_bias,
    value_projection_bias,
):
    ranks = lax.axis_size("dp")
    rows = hidden.shape[0]
    slots = positions.shape[0]
    spare = rows // ranks + 2
    width = ranks * spare
    paired_width = key_matrix.shape[1]
    target = route // slots
    place = route - target * slots
    member = (target[:, None] == jnp.arange(ranks, dtype=jnp.int32)[None, :]).astype(jnp.int32)
    order = jnp.sum(jnp.cumsum(member, axis=0) * member, axis=1) - 1
    bucket = target * spare + order
    outgoing = jnp.full((width,), slots, jnp.int32).at[bucket].set(place)
    arrived = lax.all_to_all(
        outgoing.reshape(ranks, spare), "dp", split_axis=0, concat_axis=0, tiled=True
    ).reshape(width)
    query_buf = jnp.zeros((width, queries.shape[1]), jnp.bfloat16).at[bucket].set(queries)
    own_pairs = project_own(
        hidden, key_matrix, value_matrix, key_projection_bias, value_projection_bias
    )
    pair_buf = jnp.zeros((width, 2 * paired_width), jnp.bfloat16).at[bucket].set(own_pairs)
    got_query, got_pairs = (
        lax.all_to_all(
            query_buf.reshape(ranks, spare, -1), "dp", split_axis=0, concat_axis=0, tiled=True
        ),
        lax.all_to_all(
            pair_buf.reshape(ranks, spare, -1), "dp", split_axis=0, concat_axis=0, tiled=True
        ),
    )
    got_query = got_query.reshape(width, -1)
    got_pairs = got_pairs.reshape(width, -1)
    query_slot_rows = (
        jnp.zeros((slots, got_query.shape[1]), jnp.bfloat16).at[arrived].set(got_query, mode="drop")
    )
    paired_slot_rows = (
        jnp.zeros((slots, 2 * paired_width), jnp.bfloat16).at[arrived].set(got_pairs, mode="drop")
    )
    query_turned = apply_rotary(query_slot_rows, positions, QUERY_HEADS)
    key_rotated = apply_rotary(paired_slot_rows[:, :paired_width], positions, KEY_VALUE_HEADS)
    block_list = slots // BLOCK_SLOTS
    attended = lax.map(
        causal_block_attention,
        (
            query_turned.reshape(block_list, BLOCK_SLOTS, -1),
            key_rotated.reshape(block_list, BLOCK_SLOTS, -1),
            paired_slot_rows[:, paired_width:].reshape(block_list, BLOCK_SLOTS, -1),
            positions.reshape(block_list, BLOCK_SLOTS),
        ),
    )
    attended = attended.reshape(slots, -1)
    leaving = attended[jnp.minimum(arrived, slots - 1)]
    returned = lax.all_to_all(
        leaving.reshape(ranks, spare, -1), "dp", split_axis=0, concat_axis=0, tiled=True
    ).reshape(width, -1)
    return returned[bucket]


def local(*args):
    hidden, queries, _, positions, key_matrix = args[:5]
    ranks = lax.axis_size("dp")
    rows = hidden.shape[0]
    gathered = ranks * ranks * (rows // ranks + 2) * 4 * key_matrix.shape[1]
    chip_rows = 2 * key_matrix.shape[0]
    fits = rows % (16 * ranks) == 0 and chip_rows % HEAD_SIZE == 0 and gathered <= GATHER_LIMIT
    if ranks == PLANES * PLANE and fits:
        return gather_plan(*args)
    return send_plan(*args)


def solution(mesh):
    placed = (
        P(("groups", "dp"), None),
        P(("groups", "dp"), None),
        P(("groups", "dp")),
        P(("groups", "dp")),
        P("dp", None),
        P("dp", None),
        P(),
        P(),
    )
    return jax.shard_map(
        local, mesh=mesh, in_specs=placed, out_specs=P(("groups", "dp"), None), check_vma=False
    )
```

```python
import functools
import math

import jax
import jax.numpy as jnp
from jax import lax
from jax.experimental import pallas as pl
from jax.experimental.pallas import tpu as pltpu
from jax.sharding import PartitionSpec as P

QUERY_HEADS = 20
KEY_VALUE_HEADS = 4
HEAD_SIZE = 128
BLOCK_SLOTS = 512
HEAD_GROUPS = QUERY_HEADS // KEY_VALUE_HEADS
CHUNKS = ((0, 3), (3, 1))
PLANE = 4
PLANES = 4
UNROLL = 4
GATHER_LIMIT = 40 * 2**20
MASKED = -1e30
VMEM = pl.BlockSpec(memory_space=pltpu.VMEM)
SMEM = pl.BlockSpec(memory_space=pltpu.SMEM)
HBM = pl.BlockSpec(memory_space=pltpu.HBM)


def grant(mebibytes):
    return pltpu.CompilerParams(vmem_limit_bytes=mebibytes * 2**20)


def cost(flops, moved):
    return pl.CostEstimate(flops=flops, bytes_accessed=moved, transcendentals=0)


def one_hot_rows(count, index_row):
    rows = lax.broadcasted_iota(jnp.int32, (count, index_row.shape[1]), 0)
    return (rows == index_row).astype(jnp.float32).astype(jnp.bfloat16)


def split(number):
    high = lax.shift_right_logical(number, HEAD_SIZE.bit_length() - 1)
    return high, number - high * HEAD_SIZE


def contract(left, right, left_dim, right_dim):
    return lax.dot_general(
        left, right, (((left_dim,), (right_dim,)), ((), ())), preferred_element_type=jnp.float32
    )


def turn(rows, cosine, sine):
    return (rows * cosine + pltpu.roll(rows, HEAD_SIZE // 2, 1) * sine).astype(jnp.bfloat16)


def order_kernel(
    ranks, slots, extra, stride, route_ref, bucket_ref, seat_ref, sorted_ref, more_ref
):
    route = route_ref[...]
    count = route.shape[1]
    share = count // ranks
    target = lax.div(route, slots)
    member = (lax.broadcasted_iota(jnp.int32, (ranks, count), 0) == target).astype(jnp.float32)
    before = lax.broadcasted_iota(jnp.int32, (count, count), 0) < lax.broadcasted_iota(
        jnp.int32, (count, count), 1
    )
    before = before.astype(jnp.float32).astype(jnp.bfloat16)
    ahead = contract(member.astype(jnp.bfloat16), before, 1, 0)
    order = jnp.sum(member * ahead, axis=0, keepdims=True).astype(jnp.int32)
    beyond = order >= share
    beyond_rows = jnp.broadcast_to(beyond.astype(jnp.float32), (8, count)).astype(jnp.bfloat16)
    number = contract(beyond_rows, before, 1, 0)[0:1]
    counts = jnp.sum(member, axis=1, keepdims=True)
    free = jnp.maximum(share - counts, 0.0)
    group = lax.broadcasted_iota(jnp.int32, (ranks, ranks), 0)
    lower = (group > lax.broadcasted_iota(jnp.int32, (ranks, ranks), 1)).astype(jnp.float32)
    free_rows = jnp.broadcast_to(free, (ranks, HEAD_SIZE)).astype(jnp.bfloat16)
    free_before = contract(lower.astype(jnp.bfloat16), free_rows, 1, 0)[:, 0:1]
    inside = (number >= free_before) & (number < free_before + free)
    base = lax.broadcasted_iota(jnp.int32, (ranks, 1), 0).astype(jnp.float32) * share + counts
    hole = jnp.sum(jnp.where(inside, base + number - free_before, 0.0), axis=0, keepdims=True)
    bucket = jnp.where(beyond, hole.astype(jnp.int32), target * share + order)
    bucket_ref[...] = bucket
    seat_ref[...] = target * stride + order
    high, low = split(route)
    place_high, place_low = split(bucket)
    line = lax.broadcasted_iota(jnp.int32, (8, count), 0)
    digits = jnp.where(line == 0, high, 0)
    digits = jnp.where(line == 1, low, digits)
    digits = jnp.where(line == 2, place_high, digits)
    digits = jnp.where(line == 3, place_low, digits)
    digits = jnp.where(line == 4, 1, digits).astype(jnp.float32).astype(jnp.bfloat16)
    placed = contract(digits, one_hot_rows(count, bucket), 1, 1)
    sorted_ref[...] = (placed[0:1] * HEAD_SIZE + placed[1:2]).astype(jnp.int32)
    listed = jnp.where(beyond, target * extra + order - share, -1)
    found = contract(digits, one_hot_rows(ranks * extra, listed), 1, 1)
    none = found[4:5] - 1.0
    more_ref[0:1] = (found[0:1] * HEAD_SIZE + found[1:2] + none).astype(jnp.int32)
    more_ref[1:2] = (found[2:3] * HEAD_SIZE + found[3:4] + none).astype(jnp.int32)


def query_kernel(
    ranks, spare, stride, packed, route_ref, seat_ref, positions_ref, frequency_ref, queries_ref, *refs
):
    turned_ref, bounds_ref, cosine_ref, sine_ref, rows_ref = refs
    route = route_ref[...]
    count = route.shape[0]
    lines = positions_ref.shape[0]
    line, lane = split(route)
    pick = (lax.broadcasted_iota(jnp.int32, (count, lines), 1) == line).astype(jnp.float32)
    pick = pick.astype(jnp.bfloat16)
    positions = positions_ref[...]
    half = lax.shift_right_logical(positions, 1)
    rest = positions - half * 2
    rows = 2.0 * contract(pick, half.astype(jnp.float32).astype(jnp.bfloat16), 1, 0) + contract(
        pick, rest.astype(jnp.float32).astype(jnp.bfloat16), 1, 0
    )
    lanes = lax.broadcasted_iota(jnp.int32, (count, HEAD_SIZE), 1)
    spot = jnp.sum(jnp.where(lanes == lane, rows, 0.0), axis=1, keepdims=True)
    angle = spot * frequency_ref[...]
    cosine = jnp.cos(angle)
    sine = jnp.sin(angle)
    sine = jnp.where(lanes < HEAD_SIZE // 2, -sine, sine)
    cosine_ref[...] = cosine
    sine_ref[...] = sine
    seats = one_hot_rows(ranks * stride, seat_ref[...])
    first = route - spot.astype(jnp.int32)
    first_line, first_lane = split(first)
    digits = jnp.where(lanes == 0, line, 0)
    digits = jnp.where(lanes == 1, lane, digits)
    digits = jnp.where(lanes == 2, first_line, digits)
    digits = jnp.where(lanes == 3, first_lane, digits)
    digits = jnp.where(lanes == 4, 1, digits)
    placed = contract(seats, digits.astype(jnp.float32).astype(jnp.bfloat16), 1, 0)
    live = placed[:, 4:5] - 1.0
    last = placed[:, 0:1] * HEAD_SIZE + placed[:, 1:2] + live
    start = placed[:, 2:3] * HEAD_SIZE + placed[:, 3:4] + live
    seat_lanes = lax.broadcasted_iota(jnp.int32, placed.shape, 1)
    bounds = jnp.where(seat_lanes == 0, last, start).astype(jnp.int32)
    bounds_ref[...] = jnp.full(bounds_ref.shape, -1, jnp.int32)
    rows_ref[...] = jnp.zeros(rows_ref.shape, jnp.float32)
    for group in range(ranks):
        for place in range(HEAD_GROUPS):
            at = group * packed + place * spare
            bounds_ref[at : at + spare] = bounds[group * stride : group * stride + spare]
    for head in range(KEY_VALUE_HEADS):
        for place in range(HEAD_GROUPS):
            at = (head * HEAD_GROUPS + place) * HEAD_SIZE
            one = queries_ref[:, at : at + HEAD_SIZE].astype(jnp.float32)
            rows = contract(seats, turn(one, cosine, sine), 1, 0)
            for group in range(ranks):
                at = group * packed + place * spare
                rows_ref[at : at + spare] = rows[group * stride : group * stride + spare]
        turned_ref[head] = rows_ref[...].astype(jnp.bfloat16)


def add_products(chips, owners_ref, hidden_ref, refs, columns, matrix, done):
    shard = matrix.shape[1] // 2
    copies, at, taken = [], 0, 0
    for place, chip in enumerate(chips):
        first = pl.multiple_of(lax.div(owners_ref[chip[0][0]], 2) * (2 * shard), HEAD_SIZE)
        copies.append(
            (hidden_ref.at[:, pl.ds(first, 2 * shard)], columns.at[place])
        )
        for source, row in chip:
            core = lax.rem(owners_ref[source], 2)
            rows = pl.ds(pl.multiple_of(core * shard + row, 16), refs[taken].shape[0])
            copies.append((refs[taken], matrix.at[place, rows]))
            taken += 1
    copies = [pltpu.make_async_copy(*pair, done.at[at]) for at, pair in enumerate(copies)]
    for copy in copies:
        copy.start()

    def product(span):
        total = contract(columns[0], matrix[0, :, span], 1, 0)
        for place in range(1, len(chips)):
            total = total + contract(columns[place], matrix[place, :, span], 1, 0)
        return total

    return copies, product


def part_kernel(chips, more, owners_ref, hidden_ref, *refs):
    count = sum(len(chip) for chip in chips)
    parts, refs = refs[:count], refs[count:]
    if more:
        total_ref, refs = refs[0], refs[1:]
    out_ref, columns, matrix, done = refs
    copies, product = add_products(chips, owners_ref, hidden_ref, parts, columns, matrix, done)
    for copy in copies:
        copy.wait()
    for first in range(0, out_ref.shape[1], 2 * HEAD_SIZE):
        span = slice(first, first + 2 * HEAD_SIZE)
        if more:
            out_ref[:, span] = total_ref[:, span] + product(span)
        else:
            out_ref[:, span] = product(span)


def finish_kernel(
    chips, owners_ref, hidden_ref, bias_ref, cosine_ref, sine_ref, bucket_ref, *refs
):
    count = sum(len(chip) for chip in chips)
    parts, total_ref = refs[:count], refs[count]
    outs, (columns, matrix, done) = refs[count + 1 : -3], refs[-3:]
    copies, product = add_products(chips, owners_ref, hidden_ref, parts, columns, matrix, done)
    places = one_hot_rows(outs[0].shape[0], bucket_ref[...])
    for copy in copies:
        copy.wait()
    wide = KEY_VALUE_HEADS * HEAD_SIZE
    for first in range(0, 2 * wide, 2 * HEAD_SIZE):
        span = slice(first, first + 2 * HEAD_SIZE)
        rows = (total_ref[:, span] + product(span) + bias_ref[:, span]).astype(jnp.bfloat16)
        if first < wide:
            cosine, sine = cosine_ref[...], sine_ref[...]
            halves = [
                turn(rows[:, at : at + HEAD_SIZE].astype(jnp.float32), cosine, sine)
                for at in (0, HEAD_SIZE)
            ]
            rows = jnp.concatenate(halves, axis=1)
        rows = contract(places, rows, 1, 0).astype(jnp.bfloat16)
        for half in range(2):
            head = first % wide // HEAD_SIZE + half
            for (first_head, heads), out_ref in zip(CHUNKS, outs):
                if first_head <= head < first_head + heads:
                    at = (head - first_head + first // wide * heads) * HEAD_SIZE
                    out_ref[:, at : at + HEAD_SIZE] = rows[
                        :, half * HEAD_SIZE : (half + 1) * HEAD_SIZE
                    ]


def attend_kernel(
    head, heads, pieces, extra, stride, packed,
    queries_ref, bounds_ref, routes_ref, seat_ref, more_ref, *refs
):
    first_head, place = head
    ranks = routes_ref.shape[0]
    parts, refs = refs[: len(pieces)], refs[-(6 + 3 * UNROLL) :]
    out_ref, blocks, more, mixed_ref, result_ref, done = refs[:6]
    score_refs, weight_refs, total_refs = (
        refs[6 + at * UNROLL : 6 + (at + 1) * UNROLL] for at in range(3)
    )
    count = blocks.shape[2]
    share = count // ranks
    spare = share + extra
    copies = []
    for at, ((source, first), ref) in enumerate(zip(pieces, parts)):
        for part in range(2):
            lanes = pl.ds((part * heads + place) * HEAD_SIZE, HEAD_SIZE)
            copies.append(
                pltpu.make_async_copy(
                    ref.at[:, lanes],
                    blocks.at[part, source, pl.ds(first, ref.shape[0])],
                    done.at[2 * at + part],
                )
            )
            copies[-1].start()
    mixed_ref[...] = jnp.zeros(mixed_ref.shape, jnp.bfloat16)
    listed = ranks * extra
    lines = lax.broadcasted_iota(jnp.int32, (listed, count), 1)
    picks = [
        (lines == more_ref[j * listed : (j + 1) * listed]).astype(jnp.float32).astype(jnp.bfloat16)
        for j in range(ranks)
    ]
    column = lax.broadcasted_iota(jnp.int32, (1, ranks * listed), 1)
    source, rest = lax.div(column, listed), lax.rem(column, listed)
    group, index = lax.div(rest, extra), lax.rem(rest, extra)
    regroup = one_hot_rows(ranks * listed, group * listed + source * extra + index)
    for copy in copies:
        copy.wait()
    for part in range(2):
        found = [
            contract(picks[j], blocks[part, j], 1, 0).astype(jnp.bfloat16) for j in range(ranks)
        ]
        more[part] = contract(regroup, jnp.concatenate(found, axis=0), 1, 0).astype(jnp.bfloat16)
    scale = math.log2(math.e) / math.sqrt(HEAD_SIZE)

    def rows_of(part, group):
        window = pl.ds(pl.multiple_of(group * share, 16), share)
        rows = [blocks[part, j, window] for j in range(ranks)]
        rows.append(more[part, pl.ds(pl.multiple_of(group * listed, 16), listed)])
        return jnp.concatenate(rows, axis=0)

    def score(group, score_ref):
        query = queries_ref[0, pl.ds(pl.multiple_of(group * packed, 16), packed)]
        score_ref[...] = contract(query, rows_of(0, group), 1, 1)

    def weigh(group, score_ref, weight_ref, total_ref):
        routes = routes_ref[group]
        for first in range(0, packed, 16):
            at = pl.ds(pl.multiple_of(group * packed + first, 16), 16)
            visible = (routes <= bounds_ref[at, 0:1]) & (routes >= bounds_ref[at, 1:2])
            scores = jnp.where(visible, score_ref[first : first + 16], MASKED)
            top = jnp.max(scores, axis=1, keepdims=True)
            weights = jnp.exp2((scores - top) * scale)
            total = jnp.sum(weights, axis=1, keepdims=True)
            weight_ref[first : first + 16] = weights.astype(jnp.bfloat16)
            total_ref[first : first + 16] = jnp.broadcast_to(1.0 / total, (16, HEAD_SIZE))

    def mix(group, weight_ref, total_ref):
        mixed = contract(weight_ref[...], rows_of(1, group), 1, 0) * total_ref[...]
        seats = pl.ds(pl.multiple_of(group * stride, 16), spare)
        for at in range(HEAD_GROUPS):
            lanes = slice(at * HEAD_SIZE, (at + 1) * HEAD_SIZE)
            mixed_ref[seats, lanes] = mixed[at * spare : (at + 1) * spare].astype(jnp.bfloat16)

    def some_groups(step, carry):
        groups = [step * UNROLL + at for at in range(UNROLL)]
        for at in range(UNROLL + 2):
            if at < UNROLL:
                score(groups[at], score_refs[at])
            if 0 <= at - 1 < UNROLL:
                weigh(groups[at - 1], score_refs[at - 1], weight_refs[at - 1], total_refs[at - 1])
            if 0 <= at - 2 < UNROLL:
                mix(groups[at - 2], weight_refs[at - 2], total_refs[at - 2])
        return carry

    lax.fori_loop(0, ranks // UNROLL, some_groups, 0)
    seats = one_hot_rows(mixed_ref.shape[0], seat_ref[...])
    result_ref[...] = contract(seats, mixed_ref[...], 0, 0).astype(jnp.bfloat16)
    lanes = pl.ds((first_head + place) * HEAD_GROUPS * HEAD_SIZE, HEAD_GROUPS * HEAD_SIZE)
    leave = pltpu.make_async_copy(result_ref, out_ref.at[:, lanes], done.at[2 * len(pieces)])
    leave.start()
    leave.wait()


def spread(block, ranks, held):
    ring = [(rank, (rank + PLANE) % ranks) for rank in range(ranks)]
    across = [(rank, rank ^ 2) for rank in range(ranks)]
    beside = [(rank, rank ^ 1) for rank in range(ranks)]
    steps = ranks // PLANE
    half = block.shape[0] // 32 * 16

    def keep(source, first, array):
        held.setdefault(source, []).append((first, array))
        held.setdefault(source + 2 * steps, []).append((first, lax.ppermute(array, "dp", beside)))

    lane, other = block, None
    for step in range(steps - 1):
        following = lax.ppermute(lane, "dp", ring), lax.ppermute(lane, "dp", across)
        keep(step, 0, lane)
        if step:
            keep(steps + step - 1, 0, other)
        extra = yield
        lane, other, extra = lax.optimization_barrier((*following, extra))
        yield extra
    over = lax.ppermute(lane[:half], "dp", across)
    around = lax.ppermute(other[half:], "dp", ring)
    keep(steps - 1, 0, lane)
    keep(2 * steps - 2, 0, other)
    extra = yield other
    over, around, extra = lax.optimization_barrier((over, around, extra))
    keep(2 * steps - 1, 0, over)
    keep(2 * steps - 1, half, around)
    yield extra


def source_order(ranks):
    me = lax.axis_index("dp")
    lane, plane = me % PLANE, me // PLANE
    steps = ranks // PLANE
    planes = (plane - jnp.arange(steps, dtype=jnp.int32)) % steps
    return jnp.concatenate([planes * PLANE + (lane ^ flip) for flip in (0, 2, 1, 3)])


def gather_plan(
    hidden,
    queries,
    route,
    positions,
    key_matrix,
    value_matrix,
    key_projection_bias,
    value_projection_bias,
):
    ranks = lax.axis_size("dp")
    rows = hidden.shape[0]
    slots = positions.shape[0]
    share, extra = rows // ranks, 2
    spare = share + extra
    listed = ranks * extra
    stride = -(-spare // 16) * 16
    packed = -(-HEAD_GROUPS * spare // 16) * 16
    key_count = ranks * (share + extra)
    query_width = queries.shape[1]
    shape = jax.ShapeDtypeStruct

    def columns(array, chunk):
        first, heads = chunk
        return array[..., first * HEAD_SIZE : (first + heads) * HEAD_SIZE]

    matrices = {}
    sending = spread(jnp.concatenate([key_matrix, value_matrix], axis=1), ranks, matrices)
    next(sending)
    bucket, seat, sorted_route, more = pl.pallas_call(
        functools.partial(order_kernel, ranks, slots, extra, stride),
        out_shape=(
            shape((1, rows), jnp.int32),
            shape((1, rows), jnp.int32),
            shape((1, rows), jnp.int32),
            shape((2, listed), jnp.int32),
        ),
        in_specs=[VMEM],
        out_specs=(VMEM,) * 4,
        compiler_params=grant(16),
        name="order",
    )(route.reshape(1, rows))
    width = rows + 2 * listed
    plan = jnp.concatenate([sorted_route.reshape(rows), more.reshape(2 * listed), positions])
    plan = lax.all_to_all(
        jnp.broadcast_to(plan, (ranks, width + slots)), "dp", split_axis=0, concat_axis=0, tiled=True
    )
    sending.send(())
    next(sending)
    all_positions = plan[:, width:].reshape(-1, HEAD_SIZE)
    owners = source_order(ranks)
    sources = plan[:, :width][owners]
    key_routes = jnp.concatenate(
        [
            sources[:, :rows].reshape(ranks, ranks, share).transpose(1, 0, 2).reshape(ranks, -1),
            sources[:, rows : rows + listed]
            .reshape(ranks, ranks, extra)
            .transpose(1, 0, 2)
            .reshape(ranks, -1),
        ],
        axis=1,
    ).reshape(ranks, 1, key_count)
    more_places = sources[:, rows + listed :].reshape(ranks * listed, 1)

    half = HEAD_SIZE // 2
    frequency = 1000000.0 ** (-(jnp.arange(half, dtype=jnp.float32) * 2.0 / HEAD_SIZE))
    turned, bounds, cosine, sine = pl.pallas_call(
        functools.partial(query_kernel, ranks, spare, stride, packed),
        out_shape=(
            shape((KEY_VALUE_HEADS, ranks * packed, HEAD_SIZE), jnp.bfloat16),
            shape((ranks * packed, HEAD_SIZE), jnp.int32),
            shape((rows, HEAD_SIZE), jnp.float32),
            shape((rows, HEAD_SIZE), jnp.float32),
        ),
        in_specs=[VMEM] * 5,
        out_specs=(VMEM,) * 4,
        scratch_shapes=[pltpu.VMEM((ranks * packed, HEAD_SIZE), jnp.float32)],
        compiler_params=grant(20),
        cost_estimate=cost(4 * stride * ranks * rows * query_width, 4 * rows * query_width),
        name="turn_queries",
    )(
        route.reshape(rows, 1),
        seat,
        all_positions,
        jnp.concatenate([frequency, frequency]).reshape(1, HEAD_SIZE),
        queries,
    )

    shard, wide = key_matrix.shape[0], 2 * key_matrix.shape[1]
    planes = ranks // PLANE

    def chip_parts(sources):
        chips, arrays = [], []
        for source in sources:
            chip = []
            for one in (source, source + 2 * planes):
                for first, array in matrices[one]:
                    chip.append((one, first))
                    arrays.append(array)
            chips.append(tuple(chip))
        return chips, arrays

    def scratch(chips, arrays):
        return [
            pltpu.VMEM((len(chips), rows, 2 * shard), jnp.bfloat16),
            pltpu.VMEM((len(chips), 2 * shard, wide), jnp.bfloat16),
            pltpu.SemaphoreType.DMA((len(chips) + len(arrays),)),
        ]

    def product_cost(chips):
        depth = 2 * shard * len(chips)
        return cost(2 * rows * depth * wide, 2 * depth * (rows + wide) + 8 * rows * wide)

    def add_part(total, sources):
        chips, arrays = chip_parts(sources)
        more = [] if total is None else [total]
        return pl.pallas_call(
            functools.partial(part_kernel, chips, bool(more)),
            out_shape=shape((rows, wide), jnp.float32),
            in_specs=[SMEM] + [HBM] * (1 + len(arrays)) + [VMEM] * len(more),
            out_specs=VMEM,
            scratch_shapes=scratch(chips, arrays),
            compiler_params=grant(16),
            cost_estimate=product_cost(chips),
            name="add_part",
        )(owners, hidden, *arrays, *more)

    turned, bounds, cosine, sine, key_routes, more_places = sending.send(
        (turned, bounds, cosine, sine, key_routes, more_places)
    )
    next(sending)
    (total,) = sending.send((add_part(None, (0, 1, planes)),))
    next(sending)
    (total,) = sending.send((add_part(total, (2, planes + 1)),))
    total = add_part(total, (3, planes + 2))
    chips, arrays = chip_parts((planes + 3,))
    bias = jnp.concatenate([key_projection_bias, value_projection_bias])
    pairs = pl.pallas_call(
        functools.partial(finish_kernel, chips),
        out_shape=tuple(
            shape((rows, 2 * heads * HEAD_SIZE), jnp.bfloat16) for _, heads in CHUNKS
        ),
        in_specs=[SMEM, HBM] + [VMEM] * 4 + [HBM] * len(arrays) + [VMEM],
        out_specs=(VMEM,) * len(CHUNKS),
        scratch_shapes=scratch(chips, arrays),
        compiler_params=grant(16),
        cost_estimate=product_cost(chips),
        name="finish",
    )(
        owners,
        hidden,
        bias.astype(jnp.float32).reshape(1, wide),
        cosine,
        sine,
        bucket,
        *arrays,
        total,
    )

    def attend(out, chunk, held, place):
        first_head, heads = CHUNKS[chunk]
        pieces = [(source, first) for source in held for first, _ in held[source]]
        arrays = [array for source in held for _, array in held[source]]
        taken = [] if out is None else [out]
        fixed = [turned, bounds, key_routes, seat, more_places]
        span = HEAD_GROUPS * HEAD_SIZE
        query_block = pl.BlockSpec(
            (1, ranks * packed, HEAD_SIZE), lambda i, h=first_head + place: (h, 0, 0)
        )
        return pl.pallas_call(
            functools.partial(
                attend_kernel, (first_head, place), heads, pieces, extra, stride, packed
            ),
            grid=(1,),
            out_shape=shape((rows, query_width), jnp.bfloat16),
            in_specs=[query_block] + [VMEM] * 4 + [HBM] * (len(pieces) + len(taken)),
            out_specs=HBM,
            scratch_shapes=[
                pltpu.VMEM((2, ranks, rows, HEAD_SIZE), jnp.bfloat16),
                pltpu.VMEM((2, ranks * listed, HEAD_SIZE), jnp.bfloat16),
                pltpu.VMEM((ranks * stride, span), jnp.bfloat16),
                pltpu.VMEM((rows, span), jnp.bfloat16),
                pltpu.SemaphoreType.DMA((2 * len(pieces) + 1,)),
            ]
            + [pltpu.VMEM((packed, key_count), jnp.float32)] * UNROLL
            + [pltpu.VMEM((packed, key_count), jnp.bfloat16)] * UNROLL
            + [pltpu.VMEM((packed, HEAD_SIZE), jnp.float32)] * UNROLL,
            input_output_aliases={len(fixed) + len(pieces): 0} if taken else {},
            compiler_params=grant(16),
            cost_estimate=cost(
                16 * rows * stride * ranks * span, 4 * ranks * rows * HEAD_SIZE
            ),
            name="attend",
        )(*fixed, *arrays, *taken)

    early, late = {}, {}
    sending = spread(pairs[0], ranks, early)
    for _ in range(planes - 1):
        next(sending)
        sending.send(())
    mark = next(sending)
    sending.send(())
    last, _ = lax.optimization_barrier((pairs[1], mark))
    sending = spread(last, ranks, late)
    out = None
    next(sending)
    sending.send(())
    for place in range(2):
        next(sending)
        out = attend(out, 0, early, place)
        (out,) = sending.send((out,))
    next(sending)
    (out,) = sending.send((attend(out, 0, early, 2),))
    return attend(out, 1, late, 0)


def apply_rotary(rows, slot_offset, heads):
    block_count = rows.shape[0]
    half = HEAD_SIZE // 2
    frequency = 1000000.0 ** (-(jnp.arange(half, dtype=jnp.float32) * 2.0 / HEAD_SIZE))
    angle = slot_offset.astype(jnp.float32)[:, None] * frequency[None, :]
    cosine = jnp.cos(angle)[:, None, :]
    sine = jnp.sin(angle)[:, None, :]
    grid = rows.astype(jnp.float32).reshape(block_count, heads, HEAD_SIZE)
    first = grid[:, :, :half]
    second = grid[:, :, half:]
    turned = jnp.concatenate(
        [first * cosine - second * sine, second * cosine + first * sine], axis=2
    )
    return turned.reshape(block_count, heads * HEAD_SIZE).astype(jnp.bfloat16)


def causal_block_attention(pieces):
    query_tile_rows, key_tile_rows, value_tile_rows, spot_block = pieces
    block_count = query_tile_rows.shape[0]
    head_groups = QUERY_HEADS // KEY_VALUE_HEADS
    query_block_grid = query_tile_rows.reshape(block_count, KEY_VALUE_HEADS, head_groups, HEAD_SIZE)
    key_block_grid = key_tile_rows.reshape(block_count, KEY_VALUE_HEADS, HEAD_SIZE)
    value_block_grid = value_tile_rows.reshape(block_count, KEY_VALUE_HEADS, HEAD_SIZE)
    scores = jnp.einsum(
        "qhgd,khd->hgqk", query_block_grid, key_block_grid, preferred_element_type=jnp.float32
    ) / math.sqrt(HEAD_SIZE)
    inner = jnp.arange(block_count, dtype=jnp.int32)
    visible = (inner[None, :] <= inner[:, None]) & (
        inner[None, :] >= inner[:, None] - spot_block[:, None]
    )
    scores = jnp.where(visible, scores, -jnp.inf)
    top = jnp.max(scores, axis=3, keepdims=True)
    weights = jnp.exp(scores - top)
    totals = jnp.sum(weights, axis=3)
    probs = weights.astype(jnp.bfloat16)
    mixed = jnp.einsum(
        "hgqk,khd->qhgd", probs, value_block_grid, preferred_element_type=jnp.float32
    )
    mixed = mixed / jnp.transpose(totals, (2, 0, 1))[:, :, :, None]
    return mixed.reshape(block_count, QUERY_HEADS * HEAD_SIZE).astype(jnp.bfloat16)


def add_projection(left, pieces):
    return (
        jnp.dot(left, pieces[0], preferred_element_type=jnp.float32),
        jnp.dot(left, pieces[1], preferred_element_type=jnp.float32),
    )


def project_own(hidden, key_matrix, value_matrix, key_projection_bias, value_projection_bias):
    totals = add_projection(
        hidden,
        (
            lax.all_gather(key_matrix, "dp", axis=0, tiled=True),
            lax.all_gather(value_matrix, "dp", axis=0, tiled=True),
        ),
    )
    key_rows = (totals[0] + key_projection_bias.astype(jnp.float32)).astype(jnp.bfloat16)
    value_rows = (totals[1] + value_projection_bias.astype(jnp.float32)).astype(jnp.bfloat16)
    return jnp.concatenate([key_rows, value_rows], axis=1)


def send_plan(
    hidden,
    queries,
    route,
    positions,
    key_matrix,
    value_matrix,
    key_projection_bias,
    value_projection_bias,
):
    ranks = lax.axis_size("dp")
    rows = hidden.shape[0]
    slots = positions.shape[0]
    spare = rows // ranks + 2
    width = ranks * spare
    paired_width = key_matrix.shape[1]
    target = route // slots
    place = route - target * slots
    member = (target[:, None] == jnp.arange(ranks, dtype=jnp.int32)[None, :]).astype(jnp.int32)
    order = jnp.sum(jnp.cumsum(member, axis=0) * member, axis=1) - 1
    bucket = target * spare + order
    outgoing = jnp.full((width,), slots, jnp.int32).at[bucket].set(place)
    arrived = lax.all_to_all(
        outgoing.reshape(ranks, spare), "dp", split_axis=0, concat_axis=0, tiled=True
    ).reshape(width)
    query_buf = jnp.zeros((width, queries.shape[1]), jnp.bfloat16).at[bucket].set(queries)
    own_pairs = project_own(
        hidden, key_matrix, value_matrix, key_projection_bias, value_projection_bias
    )
    pair_buf = jnp.zeros((width, 2 * paired_width), jnp.bfloat16).at[bucket].set(own_pairs)
    got_query, got_pairs = (
        lax.all_to_all(
            query_buf.reshape(ranks, spare, -1), "dp", split_axis=0, concat_axis=0, tiled=True
        ),
        lax.all_to_all(
            pair_buf.reshape(ranks, spare, -1), "dp", split_axis=0, concat_axis=0, tiled=True
        ),
    )
    got_query = got_query.reshape(width, -1)
    got_pairs = got_pairs.reshape(width, -1)
    query_slot_rows = (
        jnp.zeros((slots, got_query.shape[1]), jnp.bfloat16).at[arrived].set(got_query, mode="drop")
    )
    paired_slot_rows = (
        jnp.zeros((slots, 2 * paired_width), jnp.bfloat16).at[arrived].set(got_pairs, mode="drop")
    )
    query_turned = apply_rotary(query_slot_rows, positions, QUERY_HEADS)
    key_rotated = apply_rotary(paired_slot_rows[:, :paired_width], positions, KEY_VALUE_HEADS)
    block_list = slots // BLOCK_SLOTS
    attended = lax.map(
        causal_block_attention,
        (
            query_turned.reshape(block_list, BLOCK_SLOTS, -1),
            key_rotated.reshape(block_list, BLOCK_SLOTS, -1),
            paired_slot_rows[:, paired_width:].reshape(block_list, BLOCK_SLOTS, -1),
            positions.reshape(block_list, BLOCK_SLOTS),
        ),
    )
    attended = attended.reshape(slots, -1)
    leaving = attended[jnp.minimum(arrived, slots - 1)]
    returned = lax.all_to_all(
        leaving.reshape(ranks, spare, -1), "dp", split_axis=0, concat_axis=0, tiled=True
    ).reshape(width, -1)
    return returned[bucket]


def local(*args):
    hidden, queries, _, positions, key_matrix = args[:5]
    ranks = lax.axis_size("dp")
    rows = hidden.shape[0]
    gathered = ranks * ranks * (rows // ranks + 2) * 4 * key_matrix.shape[1]
    chip_rows = 2 * key_matrix.shape[0]
    fits = rows % (16 * ranks) == 0 and chip_rows % HEAD_SIZE == 0 and gathered <= GATHER_LIMIT
    if ranks == PLANES * PLANE and fits:
        return gather_plan(*args)
    return send_plan(*args)


def solution(mesh):
    placed = (
        P(("groups", "dp"), None),
        P(("groups", "dp"), None),
        P(("groups", "dp")),
        P(("groups", "dp")),
        P("dp", None),
        P("dp", None),
        P(),
        P(),
    )
    return jax.shard_map(
        local, mesh=mesh, in_specs=placed, out_specs=P(("groups", "dp"), None), check_vma=False
    )
```

```python
import functools
import math

import jax
import jax.numpy as jnp
from jax import lax
from jax.experimental import pallas as pl
from jax.experimental.pallas import tpu as pltpu
from jax.sharding import PartitionSpec as P

QUERY_HEADS = 20
KEY_VALUE_HEADS = 4
HEAD_SIZE = 128
BLOCK_SLOTS = 512
HEAD_GROUPS = QUERY_HEADS // KEY_VALUE_HEADS
CHUNKS = ((0, 3), (3, 1))
PLANE = 4
PLANES = 4
UNROLL = 2
GATHER_LIMIT = 40 * 2**20
MASKED = -1e30
VMEM = pl.BlockSpec(memory_space=pltpu.VMEM)
SMEM = pl.BlockSpec(memory_space=pltpu.SMEM)
HBM = pl.BlockSpec(memory_space=pltpu.HBM)


def grant(mebibytes):
    return pltpu.CompilerParams(vmem_limit_bytes=mebibytes * 2**20)


def cost(flops, moved):
    return pl.CostEstimate(flops=flops, bytes_accessed=moved, transcendentals=0)


def one_hot_rows(count, index_row):
    rows = lax.broadcasted_iota(jnp.int32, (count, index_row.shape[1]), 0)
    return (rows == index_row).astype(jnp.float32).astype(jnp.bfloat16)


def split(number):
    high = lax.shift_right_logical(number, HEAD_SIZE.bit_length() - 1)
    return high, number - high * HEAD_SIZE


def contract(left, right, left_dim, right_dim):
    return lax.dot_general(
        left, right, (((left_dim,), (right_dim,)), ((), ())), preferred_element_type=jnp.float32
    )


def turn(rows, cosine, sine):
    return (rows * cosine + pltpu.roll(rows, HEAD_SIZE // 2, 1) * sine).astype(jnp.bfloat16)


def order_kernel(
    ranks, slots, extra, stride, route_ref, bucket_ref, seat_ref, sorted_ref, more_ref
):
    route = route_ref[...]
    count = route.shape[1]
    share = count // ranks
    target = lax.div(route, slots)
    member = (lax.broadcasted_iota(jnp.int32, (ranks, count), 0) == target).astype(jnp.float32)
    before = lax.broadcasted_iota(jnp.int32, (count, count), 0) < lax.broadcasted_iota(
        jnp.int32, (count, count), 1
    )
    before = before.astype(jnp.float32).astype(jnp.bfloat16)
    ahead = contract(member.astype(jnp.bfloat16), before, 1, 0)
    order = jnp.sum(member * ahead, axis=0, keepdims=True).astype(jnp.int32)
    beyond = order >= share
    beyond_rows = jnp.broadcast_to(beyond.astype(jnp.float32), (8, count)).astype(jnp.bfloat16)
    number = contract(beyond_rows, before, 1, 0)[0:1]
    counts = jnp.sum(member, axis=1, keepdims=True)
    free = jnp.maximum(share - counts, 0.0)
    group = lax.broadcasted_iota(jnp.int32, (ranks, ranks), 0)
    lower = (group > lax.broadcasted_iota(jnp.int32, (ranks, ranks), 1)).astype(jnp.float32)
    free_rows = jnp.broadcast_to(free, (ranks, HEAD_SIZE)).astype(jnp.bfloat16)
    free_before = contract(lower.astype(jnp.bfloat16), free_rows, 1, 0)[:, 0:1]
    inside = (number >= free_before) & (number < free_before + free)
    base = lax.broadcasted_iota(jnp.int32, (ranks, 1), 0).astype(jnp.float32) * share + counts
    hole = jnp.sum(jnp.where(inside, base + number - free_before, 0.0), axis=0, keepdims=True)
    bucket = jnp.where(beyond, hole.astype(jnp.int32), target * share + order)
    bucket_ref[...] = bucket
    seat_ref[...] = target * stride + order
    high, low = split(route)
    place_high, place_low = split(bucket)
    line = lax.broadcasted_iota(jnp.int32, (8, count), 0)
    digits = jnp.where(line == 0, high, 0)
    digits = jnp.where(line == 1, low, digits)
    digits = jnp.where(line == 2, place_high, digits)
    digits = jnp.where(line == 3, place_low, digits)
    digits = jnp.where(line == 4, 1, digits).astype(jnp.float32).astype(jnp.bfloat16)
    placed = contract(digits, one_hot_rows(count, bucket), 1, 1)
    sorted_ref[...] = (placed[0:1] * HEAD_SIZE + placed[1:2]).astype(jnp.int32)
    listed = jnp.where(beyond, target * extra + order - share, -1)
    found = contract(digits, one_hot_rows(ranks * extra, listed), 1, 1)
    none = found[4:5] - 1.0
    more_ref[0:1] = (found[0:1] * HEAD_SIZE + found[1:2] + none).astype(jnp.int32)
    more_ref[1:2] = (found[2:3] * HEAD_SIZE + found[3:4] + none).astype(jnp.int32)


def query_kernel(
    ranks, spare, stride, packed, route_ref, seat_ref, positions_ref, frequency_ref, queries_ref, *refs
):
    turned_ref, bounds_ref, cosine_ref, sine_ref, rows_ref = refs
    route = route_ref[...]
    count = route.shape[0]
    lines = positions_ref.shape[0]
    line, lane = split(route)
    pick = (lax.broadcasted_iota(jnp.int32, (count, lines), 1) == line).astype(jnp.float32)
    pick = pick.astype(jnp.bfloat16)
    positions = positions_ref[...]
    half = lax.shift_right_logical(positions, 1)
    rest = positions - half * 2
    rows = 2.0 * contract(pick, half.astype(jnp.float32).astype(jnp.bfloat16), 1, 0) + contract(
        pick, rest.astype(jnp.float32).astype(jnp.bfloat16), 1, 0
    )
    lanes = lax.broadcasted_iota(jnp.int32, (count, HEAD_SIZE), 1)
    spot = jnp.sum(jnp.where(lanes == lane, rows, 0.0), axis=1, keepdims=True)
    angle = spot * frequency_ref[...]
    cosine = jnp.cos(angle)
    sine = jnp.sin(angle)
    sine = jnp.where(lanes < HEAD_SIZE // 2, -sine, sine)
    cosine_ref[...] = cosine
    sine_ref[...] = sine
    seats = one_hot_rows(ranks * stride, seat_ref[...])
    first = route - spot.astype(jnp.int32)
    first_line, first_lane = split(first)
    digits = jnp.where(lanes == 0, line, 0)
    digits = jnp.where(lanes == 1, lane, digits)
    digits = jnp.where(lanes == 2, first_line, digits)
    digits = jnp.where(lanes == 3, first_lane, digits)
    digits = jnp.where(lanes == 4, 1, digits)
    placed = contract(seats, digits.astype(jnp.float32).astype(jnp.bfloat16), 1, 0)
    live = placed[:, 4:5] - 1.0
    last = placed[:, 0:1] * HEAD_SIZE + placed[:, 1:2] + live
    start = placed[:, 2:3] * HEAD_SIZE + placed[:, 3:4] + live
    seat_lanes = lax.broadcasted_iota(jnp.int32, placed.shape, 1)
    bounds_ref[...] = jnp.where(seat_lanes == 0, last, start).astype(jnp.int32)
    rows_ref[...] = jnp.zeros(rows_ref.shape, jnp.float32)
    for head in range(KEY_VALUE_HEADS):
        for place in range(HEAD_GROUPS):
            at = (head * HEAD_GROUPS + place) * HEAD_SIZE
            one = queries_ref[:, at : at + HEAD_SIZE].astype(jnp.float32)
            rows = contract(seats, turn(one, cosine, sine), 1, 0)
            for group in range(ranks):
                at = group * packed + place * spare
                rows_ref[at : at + spare] = rows[group * stride : group * stride + spare]
        turned_ref[head] = rows_ref[...].astype(jnp.bfloat16)


def add_products(chips, owners_ref, hidden_ref, refs, columns, matrix, done):
    shard = matrix.shape[1] // 2
    copies, at, taken = [], 0, 0
    for place, chip in enumerate(chips):
        first = pl.multiple_of(lax.div(owners_ref[chip[0][0]], 2) * (2 * shard), HEAD_SIZE)
        copies.append(
            (hidden_ref.at[:, pl.ds(first, 2 * shard)], columns.at[place])
        )
        for source, row in chip:
            core = lax.rem(owners_ref[source], 2)
            rows = pl.ds(pl.multiple_of(core * shard + row, 16), refs[taken].shape[0])
            copies.append((refs[taken], matrix.at[place, rows]))
            taken += 1
    copies = [pltpu.make_async_copy(*pair, done.at[at]) for at, pair in enumerate(copies)]
    for copy in copies:
        copy.start()

    def product(span):
        total = contract(columns[0], matrix[0, :, span], 1, 0)
        for place in range(1, len(chips)):
            total = total + contract(columns[place], matrix[place, :, span], 1, 0)
        return total

    return copies, product


def part_kernel(chips, more, owners_ref, hidden_ref, *refs):
    count = sum(len(chip) for chip in chips)
    parts, refs = refs[:count], refs[count:]
    if more:
        total_ref, refs = refs[0], refs[1:]
    out_ref, columns, matrix, done = refs
    copies, product = add_products(chips, owners_ref, hidden_ref, parts, columns, matrix, done)
    for copy in copies:
        copy.wait()
    for first in range(0, out_ref.shape[1], 2 * HEAD_SIZE):
        span = slice(first, first + 2 * HEAD_SIZE)
        if more:
            out_ref[:, span] = total_ref[:, span] + product(span)
        else:
            out_ref[:, span] = product(span)


def finish_kernel(
    chips, owners_ref, hidden_ref, bias_ref, cosine_ref, sine_ref, bucket_ref, *refs
):
    count = sum(len(chip) for chip in chips)
    parts, total_ref = refs[:count], refs[count]
    outs, (columns, matrix, done) = refs[count + 1 : -3], refs[-3:]
    copies, product = add_products(chips, owners_ref, hidden_ref, parts, columns, matrix, done)
    places = one_hot_rows(outs[0].shape[0], bucket_ref[...])
    for copy in copies:
        copy.wait()
    wide = KEY_VALUE_HEADS * HEAD_SIZE
    for first in range(0, 2 * wide, 2 * HEAD_SIZE):
        span = slice(first, first + 2 * HEAD_SIZE)
        rows = (total_ref[:, span] + product(span) + bias_ref[:, span]).astype(jnp.bfloat16)
        if first < wide:
            cosine, sine = cosine_ref[...], sine_ref[...]
            halves = [
                turn(rows[:, at : at + HEAD_SIZE].astype(jnp.float32), cosine, sine)
                for at in (0, HEAD_SIZE)
            ]
            rows = jnp.concatenate(halves, axis=1)
        rows = contract(places, rows, 1, 0).astype(jnp.bfloat16)
        for half in range(2):
            head = first % wide // HEAD_SIZE + half
            for (first_head, heads), out_ref in zip(CHUNKS, outs):
                if first_head <= head < first_head + heads:
                    at = (head - first_head + first // wide * heads) * HEAD_SIZE
                    out_ref[:, at : at + HEAD_SIZE] = rows[
                        :, half * HEAD_SIZE : (half + 1) * HEAD_SIZE
                    ]


def veil_kernel(stride, bounds_ref, routes_ref, veil_ref):
    groups, keys = veil_ref.shape[0], veil_ref.shape[1]

    def one_group(group, carry):
        seats = pl.ds(pl.multiple_of(group * stride, 16), stride)
        routes = routes_ref[group]
        visible = (routes <= bounds_ref[seats, 0:1]) & (routes >= bounds_ref[seats, 1:2])
        veil = jnp.where(visible, 0.0, MASKED)
        rest = jnp.zeros((HEAD_SIZE - stride, veil.shape[1]), jnp.float32)
        turned = jnp.transpose(jnp.concatenate([veil, rest], axis=0))
        veil_ref[group] = turned[:keys].astype(jnp.bfloat16)
        return carry

    lax.fori_loop(0, groups, one_group, 0)


def attend_kernel(
    head, heads, pieces, extra, stride, seat_ref, more_ref, queries_ref, veil_ref, *refs
):
    first_head, place = head
    parts, refs = refs[: len(pieces)], refs[-9:]
    out_ref, blocks, more, query, veil, seen_by, mixed_ref, result_ref, done = refs
    ranks, count = blocks.shape[1], blocks.shape[2]
    packed = query.shape[0] // ranks
    share = count // ranks
    spare = share + extra
    copies = [
        pltpu.make_async_copy(queries_ref.at[first_head + place], query, done.at[0]),
        pltpu.make_async_copy(veil_ref, veil, done.at[1]),
    ]
    for part in range(2):
        lanes = pl.ds((part * heads + place) * HEAD_SIZE, HEAD_SIZE)
        for (source, first), ref in zip(pieces, parts):
            rows = pl.ds(first, ref.shape[0])
            copies.append(
                pltpu.make_async_copy(
                    ref.at[:, lanes], blocks.at[part, source, rows], done.at[len(copies)]
                )
            )
    for copy in copies:
        copy.start()
    mixed_ref[...] = jnp.zeros(mixed_ref.shape, jnp.bfloat16)
    token = lax.broadcasted_iota(jnp.int32, (packed, HEAD_SIZE), 0)
    lane = lax.broadcasted_iota(jnp.int32, (packed, HEAD_SIZE), 1)
    own = lane < 0
    for at in range(HEAD_GROUPS):
        own = own | ((token == lane + at * spare) & (lane < spare))
    seen_by[...] = own.astype(jnp.float32).astype(jnp.bfloat16)
    listed = ranks * extra
    lines = lax.broadcasted_iota(jnp.int32, (listed, count), 1)
    picks = [
        (lines == more_ref[j * listed : (j + 1) * listed]).astype(jnp.float32).astype(jnp.bfloat16)
        for j in range(ranks)
    ]
    column = lax.broadcasted_iota(jnp.int32, (1, ranks * listed), 1)
    source, rest = lax.div(column, listed), lax.rem(column, listed)
    group, index = lax.div(rest, extra), lax.rem(rest, extra)
    regroup = one_hot_rows(ranks * listed, group * listed + source * extra + index)
    for copy in copies:
        copy.wait()
    for part in range(2):
        found = [
            contract(picks[j], blocks[part, j], 1, 0).astype(jnp.bfloat16) for j in range(ranks)
        ]
        more[part] = contract(regroup, jnp.concatenate(found, axis=0), 1, 0).astype(jnp.bfloat16)
    scale = math.log2(math.e) / math.sqrt(HEAD_SIZE)

    def rows_of(part, group):
        window = pl.ds(pl.multiple_of(group * share, 16), share)
        rows = [blocks[part, j, window] for j in range(ranks)]
        rows.append(more[part, pl.ds(pl.multiple_of(group * listed, 16), listed)])
        return jnp.concatenate(rows, axis=0)

    def some_groups(step, carry):
        groups = [step * UNROLL + at for at in range(UNROLL)]
        scores = []
        for group in groups:
            tokens = pl.ds(pl.multiple_of(group * packed, 16), packed)
            left = jnp.concatenate([query[tokens], seen_by[...]], axis=1)
            right = jnp.concatenate([rows_of(0, group), veil[group]], axis=1)
            scores.append(contract(left, right, 1, 1))
        weights = []
        for one in scores:
            top = jnp.max(one, axis=1, keepdims=True)
            weights.append(jnp.exp2((one - top) * scale).astype(jnp.bfloat16))
        for group, weight in zip(groups, weights):
            values = rows_of(1, group)
            values = jnp.concatenate([values, jnp.ones_like(values)], axis=1)
            mixed = contract(weight, values, 1, 0)
            mixed = mixed[:, :HEAD_SIZE] / mixed[:, HEAD_SIZE:]
            seats = pl.ds(pl.multiple_of(group * stride, 16), spare)
            for at in range(HEAD_GROUPS):
                lanes = slice(at * HEAD_SIZE, (at + 1) * HEAD_SIZE)
                rows = mixed[at * spare : (at + 1) * spare]
                mixed_ref[seats, lanes] = rows.astype(jnp.bfloat16)
        return carry

    lax.fori_loop(0, ranks // UNROLL, some_groups, 0)
    seat_lanes = lax.broadcasted_iota(jnp.int32, (count, mixed_ref.shape[0]), 1)
    seats = (seat_lanes == seat_ref[...]).astype(jnp.float32).astype(jnp.bfloat16)
    result_ref[...] = contract(seats, mixed_ref[...], 1, 0).astype(jnp.bfloat16)
    lanes = pl.ds((first_head + place) * HEAD_GROUPS * HEAD_SIZE, HEAD_GROUPS * HEAD_SIZE)
    leave = pltpu.make_async_copy(result_ref, out_ref.at[:, lanes], done.at[len(copies)])
    leave.start()
    leave.wait()


def spread(block, ranks, held):
    ring = [(rank, (rank + PLANE) % ranks) for rank in range(ranks)]
    across = [(rank, rank ^ 2) for rank in range(ranks)]
    beside = [(rank, rank ^ 1) for rank in range(ranks)]
    steps = ranks // PLANE
    half = block.shape[0] // 32 * 16

    def keep(source, first, array):
        held.setdefault(source, []).append((first, array))
        held.setdefault(source + 2 * steps, []).append((first, lax.ppermute(array, "dp", beside)))

    lane, other = block, None
    for step in range(steps - 1):
        following = lax.ppermute(lane, "dp", ring), lax.ppermute(lane, "dp", across)
        keep(step, 0, lane)
        if step:
            keep(steps + step - 1, 0, other)
        extra = yield
        lane, other, extra = lax.optimization_barrier((*following, extra))
        yield extra
    over = lax.ppermute(lane[:half], "dp", across)
    around = lax.ppermute(other[half:], "dp", ring)
    keep(steps - 1, 0, lane)
    keep(2 * steps - 2, 0, other)
    extra = yield other
    over, around, extra = lax.optimization_barrier((over, around, extra))
    keep(2 * steps - 1, 0, over)
    keep(2 * steps - 1, half, around)
    yield extra


def source_order(ranks):
    me = lax.axis_index("dp")
    lane, plane = me % PLANE, me // PLANE
    steps = ranks // PLANE
    planes = (plane - jnp.arange(steps, dtype=jnp.int32)) % steps
    return jnp.concatenate([planes * PLANE + (lane ^ flip) for flip in (0, 2, 1, 3)])


def gather_plan(
    hidden,
    queries,
    route,
    positions,
    key_matrix,
    value_matrix,
    key_projection_bias,
    value_projection_bias,
):
    ranks = lax.axis_size("dp")
    rows = hidden.shape[0]
    slots = positions.shape[0]
    share, extra = rows // ranks, 2
    spare = share + extra
    listed = ranks * extra
    stride = -(-spare // 16) * 16
    packed = -(-HEAD_GROUPS * spare // 16) * 16
    key_count = ranks * (share + extra)
    query_width = queries.shape[1]
    shape = jax.ShapeDtypeStruct

    def columns(array, chunk):
        first, heads = chunk
        return array[..., first * HEAD_SIZE : (first + heads) * HEAD_SIZE]

    matrices = {}
    sending = spread(jnp.concatenate([key_matrix, value_matrix], axis=1), ranks, matrices)
    next(sending)
    bucket, seat, sorted_route, more = pl.pallas_call(
        functools.partial(order_kernel, ranks, slots, extra, stride),
        out_shape=(
            shape((1, rows), jnp.int32),
            shape((1, rows), jnp.int32),
            shape((1, rows), jnp.int32),
            shape((2, listed), jnp.int32),
        ),
        in_specs=[VMEM],
        out_specs=(VMEM,) * 4,
        compiler_params=grant(16),
        name="order",
    )(route.reshape(1, rows))
    width = rows + 2 * listed
    plan = jnp.concatenate([sorted_route.reshape(rows), more.reshape(2 * listed), positions])
    plan = lax.all_to_all(
        jnp.broadcast_to(plan, (ranks, width + slots)), "dp", split_axis=0, concat_axis=0, tiled=True
    )
    sending.send(())
    next(sending)
    all_positions = plan[:, width:].reshape(-1, HEAD_SIZE)
    owners = source_order(ranks)
    sources = plan[:, :width][owners]
    key_routes = jnp.concatenate(
        [
            sources[:, :rows].reshape(ranks, ranks, share).transpose(1, 0, 2).reshape(ranks, -1),
            sources[:, rows : rows + listed]
            .reshape(ranks, ranks, extra)
            .transpose(1, 0, 2)
            .reshape(ranks, -1),
        ],
        axis=1,
    ).reshape(ranks, 1, key_count)
    wide_keys = -(-key_count // HEAD_SIZE) * HEAD_SIZE
    key_routes = jnp.pad(
        key_routes, ((0, 0), (0, 0), (0, wide_keys - key_count)), constant_values=-1
    )
    more_places = sources[:, rows + listed :].reshape(ranks * listed, 1)

    half = HEAD_SIZE // 2
    frequency = 1000000.0 ** (-(jnp.arange(half, dtype=jnp.float32) * 2.0 / HEAD_SIZE))
    turned, bounds, cosine, sine = pl.pallas_call(
        functools.partial(query_kernel, ranks, spare, stride, packed),
        out_shape=(
            shape((KEY_VALUE_HEADS, ranks * packed, HEAD_SIZE), jnp.bfloat16),
            shape((ranks * stride, HEAD_SIZE), jnp.int32),
            shape((rows, HEAD_SIZE), jnp.float32),
            shape((rows, HEAD_SIZE), jnp.float32),
        ),
        in_specs=[VMEM] * 5,
        out_specs=(VMEM,) * 4,
        scratch_shapes=[pltpu.VMEM((ranks * packed, HEAD_SIZE), jnp.float32)],
        compiler_params=grant(20),
        cost_estimate=cost(4 * stride * ranks * rows * query_width, 4 * rows * query_width),
        name="turn_queries",
    )(
        route.reshape(rows, 1),
        seat,
        all_positions,
        jnp.concatenate([frequency, frequency]).reshape(1, HEAD_SIZE),
        queries,
    )

    shard, wide = key_matrix.shape[0], 2 * key_matrix.shape[1]
    planes = ranks // PLANE

    def chip_parts(sources):
        chips, arrays = [], []
        for source in sources:
            chip = []
            for one in (source, source + 2 * planes):
                for first, array in matrices[one]:
                    chip.append((one, first))
                    arrays.append(array)
            chips.append(tuple(chip))
        return chips, arrays

    def scratch(chips, arrays):
        return [
            pltpu.VMEM((len(chips), rows, 2 * shard), jnp.bfloat16),
            pltpu.VMEM((len(chips), 2 * shard, wide), jnp.bfloat16),
            pltpu.SemaphoreType.DMA((len(chips) + len(arrays),)),
        ]

    def product_cost(chips):
        depth = 2 * shard * len(chips)
        return cost(2 * rows * depth * wide, 2 * depth * (rows + wide) + 8 * rows * wide)

    def add_part(total, sources):
        chips, arrays = chip_parts(sources)
        more = [] if total is None else [total]
        return pl.pallas_call(
            functools.partial(part_kernel, chips, bool(more)),
            out_shape=shape((rows, wide), jnp.float32),
            in_specs=[SMEM] + [HBM] * (1 + len(arrays)) + [VMEM] * len(more),
            out_specs=VMEM,
            scratch_shapes=scratch(chips, arrays),
            compiler_params=grant(16),
            cost_estimate=product_cost(chips),
            name="add_part",
        )(owners, hidden, *arrays, *more)

    turned, bounds, cosine, sine, key_routes, more_places = sending.send(
        (turned, bounds, cosine, sine, key_routes, more_places)
    )
    next(sending)
    (total,) = sending.send((add_part(None, (0, 1, planes)),))
    next(sending)
    (total,) = sending.send((add_part(total, (2, planes + 1)),))
    total = add_part(total, (3, planes + 2))
    chips, arrays = chip_parts((planes + 3,))
    bias = jnp.concatenate([key_projection_bias, value_projection_bias])
    pairs = pl.pallas_call(
        functools.partial(finish_kernel, chips),
        out_shape=tuple(
            shape((rows, 2 * heads * HEAD_SIZE), jnp.bfloat16) for _, heads in CHUNKS
        ),
        in_specs=[SMEM, HBM] + [VMEM] * 4 + [HBM] * len(arrays) + [VMEM],
        out_specs=(VMEM,) * len(CHUNKS),
        scratch_shapes=scratch(chips, arrays),
        compiler_params=grant(16),
        cost_estimate=product_cost(chips),
        name="finish",
    )(
        owners,
        hidden,
        bias.astype(jnp.float32).reshape(1, wide),
        cosine,
        sine,
        bucket,
        *arrays,
        total,
    )

    def attend(out, chunk, held, place):
        first_head, heads = CHUNKS[chunk]
        pieces = [(source, first) for source in held for first, _ in held[source]]
        arrays = [array for source in held for _, array in held[source]]
        taken = [] if out is None else [out]
        fixed = [seat.reshape(rows, 1), more_places, turned, veil]
        span = HEAD_GROUPS * HEAD_SIZE
        return pl.pallas_call(
            functools.partial(attend_kernel, (first_head, place), heads, pieces, extra, stride),
            out_shape=shape((rows, query_width), jnp.bfloat16),
            in_specs=[VMEM] * 2 + [HBM] * (2 + len(pieces) + len(taken)),
            out_specs=HBM,
            scratch_shapes=[
                pltpu.VMEM((2, ranks, rows, HEAD_SIZE), jnp.bfloat16),
                pltpu.VMEM((2, ranks * listed, HEAD_SIZE), jnp.bfloat16),
                pltpu.VMEM((ranks * packed, HEAD_SIZE), jnp.bfloat16),
                pltpu.VMEM(veil.shape, jnp.bfloat16),
                pltpu.VMEM((packed, HEAD_SIZE), jnp.bfloat16),
                pltpu.VMEM((ranks * stride, span), jnp.bfloat16),
                pltpu.VMEM((rows, span), jnp.bfloat16),
                pltpu.SemaphoreType.DMA((2 * len(pieces) + 3,)),
            ],
            input_output_aliases={len(fixed) + len(pieces): 0} if taken else {},
            compiler_params=grant(24),
            cost_estimate=cost(
                16 * rows * stride * ranks * span, 4 * ranks * rows * HEAD_SIZE
            ),
            name="attend",
        )(*fixed, *arrays, *taken)

    early, late = {}, {}
    sending = spread(pairs[0], ranks, early)
    next(sending)
    veil = pl.pallas_call(
        functools.partial(veil_kernel, stride),
        out_shape=shape((ranks, key_count, HEAD_SIZE), jnp.bfloat16),
        in_specs=[VMEM] * 2,
        out_specs=VMEM,
        compiler_params=grant(16),
        cost_estimate=cost(2 * 10**9, 4 * ranks * key_count * HEAD_SIZE),
        name="veil",
    )(bounds, key_routes)
    (veil,) = sending.send((veil,))
    for _ in range(planes - 2):
        next(sending)
        sending.send(())
    mark = next(sending)
    sending.send(())
    last, _ = lax.optimization_barrier((pairs[1], mark))
    sending = spread(last, ranks, late)
    out = None
    next(sending)
    sending.send(())
    for place in range(2):
        next(sending)
        out = attend(out, 0, early, place)
        (out,) = sending.send((out,))
    next(sending)
    (out,) = sending.send((attend(out, 0, early, 2),))
    return attend(out, 1, late, 0)


def apply_rotary(rows, slot_offset, heads):
    block_count = rows.shape[0]
    half = HEAD_SIZE // 2
    frequency = 1000000.0 ** (-(jnp.arange(half, dtype=jnp.float32) * 2.0 / HEAD_SIZE))
    angle = slot_offset.astype(jnp.float32)[:, None] * frequency[None, :]
    cosine = jnp.cos(angle)[:, None, :]
    sine = jnp.sin(angle)[:, None, :]
    grid = rows.astype(jnp.float32).reshape(block_count, heads, HEAD_SIZE)
    first = grid[:, :, :half]
    second = grid[:, :, half:]
    turned = jnp.concatenate(
        [first * cosine - second * sine, second * cosine + first * sine], axis=2
    )
    return turned.reshape(block_count, heads * HEAD_SIZE).astype(jnp.bfloat16)


def causal_block_attention(pieces):
    query_tile_rows, key_tile_rows, value_tile_rows, spot_block = pieces
    block_count = query_tile_rows.shape[0]
    head_groups = QUERY_HEADS // KEY_VALUE_HEADS
    query_block_grid = query_tile_rows.reshape(block_count, KEY_VALUE_HEADS, head_groups, HEAD_SIZE)
    key_block_grid = key_tile_rows.reshape(block_count, KEY_VALUE_HEADS, HEAD_SIZE)
    value_block_grid = value_tile_rows.reshape(block_count, KEY_VALUE_HEADS, HEAD_SIZE)
    scores = jnp.einsum(
        "qhgd,khd->hgqk", query_block_grid, key_block_grid, preferred_element_type=jnp.float32
    ) / math.sqrt(HEAD_SIZE)
    inner = jnp.arange(block_count, dtype=jnp.int32)
    visible = (inner[None, :] <= inner[:, None]) & (
        inner[None, :] >= inner[:, None] - spot_block[:, None]
    )
    scores = jnp.where(visible, scores, -jnp.inf)
    top = jnp.max(scores, axis=3, keepdims=True)
    weights = jnp.exp(scores - top)
    totals = jnp.sum(weights, axis=3)
    probs = weights.astype(jnp.bfloat16)
    mixed = jnp.einsum(
        "hgqk,khd->qhgd", probs, value_block_grid, preferred_element_type=jnp.float32
    )
    mixed = mixed / jnp.transpose(totals, (2, 0, 1))[:, :, :, None]
    return mixed.reshape(block_count, QUERY_HEADS * HEAD_SIZE).astype(jnp.bfloat16)


def add_projection(left, pieces):
    return (
        jnp.dot(left, pieces[0], preferred_element_type=jnp.float32),
        jnp.dot(left, pieces[1], preferred_element_type=jnp.float32),
    )


def project_own(hidden, key_matrix, value_matrix, key_projection_bias, value_projection_bias):
    totals = add_projection(
        hidden,
        (
            lax.all_gather(key_matrix, "dp", axis=0, tiled=True),
            lax.all_gather(value_matrix, "dp", axis=0, tiled=True),
        ),
    )
    key_rows = (totals[0] + key_projection_bias.astype(jnp.float32)).astype(jnp.bfloat16)
    value_rows = (totals[1] + value_projection_bias.astype(jnp.float32)).astype(jnp.bfloat16)
    return jnp.concatenate([key_rows, value_rows], axis=1)


def send_plan(
    hidden,
    queries,
    route,
    positions,
    key_matrix,
    value_matrix,
    key_projection_bias,
    value_projection_bias,
):
    ranks = lax.axis_size("dp")
    rows = hidden.shape[0]
    slots = positions.shape[0]
    spare = rows // ranks + 2
    width = ranks * spare
    paired_width = key_matrix.shape[1]
    target = route // slots
    place = route - target * slots
    member = (target[:, None] == jnp.arange(ranks, dtype=jnp.int32)[None, :]).astype(jnp.int32)
    order = jnp.sum(jnp.cumsum(member, axis=0) * member, axis=1) - 1
    bucket = target * spare + order
    outgoing = jnp.full((width,), slots, jnp.int32).at[bucket].set(place)
    arrived = lax.all_to_all(
        outgoing.reshape(ranks, spare), "dp", split_axis=0, concat_axis=0, tiled=True
    ).reshape(width)
    query_buf = jnp.zeros((width, queries.shape[1]), jnp.bfloat16).at[bucket].set(queries)
    own_pairs = project_own(
        hidden, key_matrix, value_matrix, key_projection_bias, value_projection_bias
    )
    pair_buf = jnp.zeros((width, 2 * paired_width), jnp.bfloat16).at[bucket].set(own_pairs)
    got_query, got_pairs = (
        lax.all_to_all(
            query_buf.reshape(ranks, spare, -1), "dp", split_axis=0, concat_axis=0, tiled=True
        ),
        lax.all_to_all(
            pair_buf.reshape(ranks, spare, -1), "dp", split_axis=0, concat_axis=0, tiled=True
        ),
    )
    got_query = got_query.reshape(width, -1)
    got_pairs = got_pairs.reshape(width, -1)
    query_slot_rows = (
        jnp.zeros((slots, got_query.shape[1]), jnp.bfloat16).at[arrived].set(got_query, mode="drop")
    )
    paired_slot_rows = (
        jnp.zeros((slots, 2 * paired_width), jnp.bfloat16).at[arrived].set(got_pairs, mode="drop")
    )
    query_turned = apply_rotary(query_slot_rows, positions, QUERY_HEADS)
    key_rotated = apply_rotary(paired_slot_rows[:, :paired_width], positions, KEY_VALUE_HEADS)
    block_list = slots // BLOCK_SLOTS
    attended = lax.map(
        causal_block_attention,
        (
            query_turned.reshape(block_list, BLOCK_SLOTS, -1),
            key_rotated.reshape(block_list, BLOCK_SLOTS, -1),
            paired_slot_rows[:, paired_width:].reshape(block_list, BLOCK_SLOTS, -1),
            positions.reshape(block_list, BLOCK_SLOTS),
        ),
    )
    attended = attended.reshape(slots, -1)
    leaving = attended[jnp.minimum(arrived, slots - 1)]
    returned = lax.all_to_all(
        leaving.reshape(ranks, spare, -1), "dp", split_axis=0, concat_axis=0, tiled=True
    ).reshape(width, -1)
    return returned[bucket]


def local(*args):
    hidden, queries, _, positions, key_matrix = args[:5]
    ranks = lax.axis_size("dp")
    rows = hidden.shape[0]
    gathered = ranks * ranks * (rows // ranks + 2) * 4 * key_matrix.shape[1]
    chip_rows = 2 * key_matrix.shape[0]
    fits = rows % (16 * ranks) == 0 and chip_rows % HEAD_SIZE == 0 and gathered <= GATHER_LIMIT
    if ranks == PLANES * PLANE and fits:
        return gather_plan(*args)
    return send_plan(*args)


def solution(mesh):
    placed = (
        P(("groups", "dp"), None),
        P(("groups", "dp"), None),
        P(("groups", "dp")),
        P(("groups", "dp")),
        P("dp", None),
        P("dp", None),
        P(),
        P(),
    )
    return jax.shard_map(
        local, mesh=mesh, in_specs=placed, out_specs=P(("groups", "dp"), None), check_vma=False
    )
```

```python
import functools
import math

import jax
import jax.numpy as jnp
from jax import lax
from jax.experimental import pallas as pl
from jax.experimental.pallas import tpu as pltpu
from jax.sharding import PartitionSpec as P

QUERY_HEADS = 20
KEY_VALUE_HEADS = 4
HEAD_SIZE = 128
BLOCK_SLOTS = 512
HEAD_GROUPS = QUERY_HEADS // KEY_VALUE_HEADS
CHUNKS = ((0, KEY_VALUE_HEADS),)
PLANE = 4
PLANES = 4
UNROLL = 2
GATHER_LIMIT = 40 * 2**20
MASKED = -1e30
VMEM = pl.BlockSpec(memory_space=pltpu.VMEM)
SMEM = pl.BlockSpec(memory_space=pltpu.SMEM)
HBM = pl.BlockSpec(memory_space=pltpu.HBM)


def grant(mebibytes):
    return pltpu.CompilerParams(vmem_limit_bytes=mebibytes * 2**20)


def cost(flops, moved):
    return pl.CostEstimate(flops=flops, bytes_accessed=moved, transcendentals=0)


def one_hot_rows(count, index_row):
    rows = lax.broadcasted_iota(jnp.int32, (count, index_row.shape[1]), 0)
    return (rows == index_row).astype(jnp.float32).astype(jnp.bfloat16)


def split(number):
    high = lax.shift_right_logical(number, HEAD_SIZE.bit_length() - 1)
    return high, number - high * HEAD_SIZE


def contract(left, right, left_dim, right_dim):
    return lax.dot_general(
        left, right, (((left_dim,), (right_dim,)), ((), ())), preferred_element_type=jnp.float32
    )


def turn(rows, cosine, sine):
    return (rows * cosine + pltpu.roll(rows, HEAD_SIZE // 2, 1) * sine).astype(jnp.bfloat16)


def order_kernel(
    ranks, slots, extra, stride, route_ref, bucket_ref, seat_ref, sorted_ref, more_ref
):
    route = route_ref[...]
    count = route.shape[1]
    share = count // ranks
    target = lax.div(route, slots)
    member = (lax.broadcasted_iota(jnp.int32, (ranks, count), 0) == target).astype(jnp.float32)
    before = lax.broadcasted_iota(jnp.int32, (count, count), 0) < lax.broadcasted_iota(
        jnp.int32, (count, count), 1
    )
    before = before.astype(jnp.float32).astype(jnp.bfloat16)
    ahead = contract(member.astype(jnp.bfloat16), before, 1, 0)
    order = jnp.sum(member * ahead, axis=0, keepdims=True).astype(jnp.int32)
    beyond = order >= share
    beyond_rows = jnp.broadcast_to(beyond.astype(jnp.float32), (8, count)).astype(jnp.bfloat16)
    number = contract(beyond_rows, before, 1, 0)[0:1]
    counts = jnp.sum(member, axis=1, keepdims=True)
    free = jnp.maximum(share - counts, 0.0)
    group = lax.broadcasted_iota(jnp.int32, (ranks, ranks), 0)
    lower = (group > lax.broadcasted_iota(jnp.int32, (ranks, ranks), 1)).astype(jnp.float32)
    free_rows = jnp.broadcast_to(free, (ranks, HEAD_SIZE)).astype(jnp.bfloat16)
    free_before = contract(lower.astype(jnp.bfloat16), free_rows, 1, 0)[:, 0:1]
    inside = (number >= free_before) & (number < free_before + free)
    base = lax.broadcasted_iota(jnp.int32, (ranks, 1), 0).astype(jnp.float32) * share + counts
    hole = jnp.sum(jnp.where(inside, base + number - free_before, 0.0), axis=0, keepdims=True)
    bucket = jnp.where(beyond, hole.astype(jnp.int32), target * share + order)
    bucket_ref[...] = bucket
    seat_ref[...] = target * stride + order
    high, low = split(route)
    place_high, place_low = split(bucket)
    line = lax.broadcasted_iota(jnp.int32, (8, count), 0)
    digits = jnp.where(line == 0, high, 0)
    digits = jnp.where(line == 1, low, digits)
    digits = jnp.where(line == 2, place_high, digits)
    digits = jnp.where(line == 3, place_low, digits)
    digits = jnp.where(line == 4, 1, digits).astype(jnp.float32).astype(jnp.bfloat16)
    placed = contract(digits, one_hot_rows(count, bucket), 1, 1)
    sorted_ref[...] = (placed[0:1] * HEAD_SIZE + placed[1:2]).astype(jnp.int32)
    listed = jnp.where(beyond, target * extra + order - share, -1)
    found = contract(digits, one_hot_rows(ranks * extra, listed), 1, 1)
    none = found[4:5] - 1.0
    more_ref[0:1] = (found[0:1] * HEAD_SIZE + found[1:2] + none).astype(jnp.int32)
    more_ref[1:2] = (found[2:3] * HEAD_SIZE + found[3:4] + none).astype(jnp.int32)


def query_kernel(
    ranks, spare, stride, packed, route_ref, seat_ref, positions_ref, frequency_ref, queries_ref, *refs
):
    turned_ref, bounds_ref, cosine_ref, sine_ref, rows_ref = refs
    route = route_ref[...]
    count = route.shape[0]
    lines = positions_ref.shape[0]
    line, lane = split(route)
    pick = (lax.broadcasted_iota(jnp.int32, (count, lines), 1) == line).astype(jnp.float32)
    pick = pick.astype(jnp.bfloat16)
    positions = positions_ref[...]
    half = lax.shift_right_logical(positions, 1)
    rest = positions - half * 2
    rows = 2.0 * contract(pick, half.astype(jnp.float32).astype(jnp.bfloat16), 1, 0) + contract(
        pick, rest.astype(jnp.float32).astype(jnp.bfloat16), 1, 0
    )
    lanes = lax.broadcasted_iota(jnp.int32, (count, HEAD_SIZE), 1)
    spot = jnp.sum(jnp.where(lanes == lane, rows, 0.0), axis=1, keepdims=True)
    angle = spot * frequency_ref[...]
    cosine = jnp.cos(angle)
    sine = jnp.sin(angle)
    sine = jnp.where(lanes < HEAD_SIZE // 2, -sine, sine)
    cosine_ref[...] = cosine
    sine_ref[...] = sine
    seats = one_hot_rows(ranks * stride, seat_ref[...])
    first = route - spot.astype(jnp.int32)
    first_line, first_lane = split(first)
    digits = jnp.where(lanes == 0, line, 0)
    digits = jnp.where(lanes == 1, lane, digits)
    digits = jnp.where(lanes == 2, first_line, digits)
    digits = jnp.where(lanes == 3, first_lane, digits)
    digits = jnp.where(lanes == 4, 1, digits)
    placed = contract(seats, digits.astype(jnp.float32).astype(jnp.bfloat16), 1, 0)
    live = placed[:, 4:5] - 1.0
    last = placed[:, 0:1] * HEAD_SIZE + placed[:, 1:2] + live
    start = placed[:, 2:3] * HEAD_SIZE + placed[:, 3:4] + live
    seat_lanes = lax.broadcasted_iota(jnp.int32, placed.shape, 1)
    bounds_ref[...] = jnp.where(seat_lanes == 0, last, start).astype(jnp.int32)
    rows_ref[...] = jnp.zeros(rows_ref.shape, jnp.float32)
    for head in range(KEY_VALUE_HEADS):
        for place in range(HEAD_GROUPS):
            at = (head * HEAD_GROUPS + place) * HEAD_SIZE
            one = queries_ref[:, at : at + HEAD_SIZE].astype(jnp.float32)
            rows = contract(seats, turn(one, cosine, sine), 1, 0)
            for group in range(ranks):
                at = group * packed + place * spare
                rows_ref[at : at + spare] = rows[group * stride : group * stride + spare]
        turned_ref[head] = rows_ref[...].astype(jnp.bfloat16)


def add_products(chips, owners_ref, hidden_ref, refs, columns, matrix, done):
    shard = matrix.shape[1] // 2
    copies, at, taken = [], 0, 0
    for place, chip in enumerate(chips):
        first = pl.multiple_of(lax.div(owners_ref[chip[0][0]], 2) * (2 * shard), HEAD_SIZE)
        copies.append(
            (hidden_ref.at[:, pl.ds(first, 2 * shard)], columns.at[place])
        )
        for source, row in chip:
            core = lax.rem(owners_ref[source], 2)
            rows = pl.ds(pl.multiple_of(core * shard + row, 16), refs[taken].shape[0])
            copies.append((refs[taken], matrix.at[place, rows]))
            taken += 1
    copies = [pltpu.make_async_copy(*pair, done.at[at]) for at, pair in enumerate(copies)]
    for copy in copies:
        copy.start()

    def product(span):
        total = contract(columns[0], matrix[0, :, span], 1, 0)
        for place in range(1, len(chips)):
            total = total + contract(columns[place], matrix[place, :, span], 1, 0)
        return total

    return copies, product


def part_kernel(chips, more, owners_ref, hidden_ref, *refs):
    count = sum(len(chip) for chip in chips)
    parts, refs = refs[:count], refs[count:]
    if more:
        total_ref, refs = refs[0], refs[1:]
    out_ref, columns, matrix, done = refs
    copies, product = add_products(chips, owners_ref, hidden_ref, parts, columns, matrix, done)
    for copy in copies:
        copy.wait()
    for first in range(0, out_ref.shape[1], 2 * HEAD_SIZE):
        span = slice(first, first + 2 * HEAD_SIZE)
        if more:
            out_ref[:, span] = total_ref[:, span] + product(span)
        else:
            out_ref[:, span] = product(span)


def finish_kernel(
    chips, owners_ref, hidden_ref, bias_ref, cosine_ref, sine_ref, bucket_ref, *refs
):
    count = sum(len(chip) for chip in chips)
    parts, total_ref = refs[:count], refs[count]
    outs, (columns, matrix, done) = refs[count + 1 : -3], refs[-3:]
    copies, product = add_products(chips, owners_ref, hidden_ref, parts, columns, matrix, done)
    places = one_hot_rows(outs[0].shape[0], bucket_ref[...])
    for copy in copies:
        copy.wait()
    wide = KEY_VALUE_HEADS * HEAD_SIZE
    for first in range(0, 2 * wide, 2 * HEAD_SIZE):
        span = slice(first, first + 2 * HEAD_SIZE)
        rows = (total_ref[:, span] + product(span) + bias_ref[:, span]).astype(jnp.bfloat16)
        if first < wide:
            cosine, sine = cosine_ref[...], sine_ref[...]
            halves = [
                turn(rows[:, at : at + HEAD_SIZE].astype(jnp.float32), cosine, sine)
                for at in (0, HEAD_SIZE)
            ]
            rows = jnp.concatenate(halves, axis=1)
        rows = contract(places, rows, 1, 0).astype(jnp.bfloat16)
        for half in range(2):
            head = first % wide // HEAD_SIZE + half
            for (first_head, heads), out_ref in zip(CHUNKS, outs):
                if first_head <= head < first_head + heads:
                    at = (head - first_head + first // wide * heads) * HEAD_SIZE
                    out_ref[:, at : at + HEAD_SIZE] = rows[
                        :, half * HEAD_SIZE : (half + 1) * HEAD_SIZE
                    ]


def veil_kernel(sets, stride, bounds_ref, routes_ref, more_ref, *veil_refs):
    rest = jnp.zeros((HEAD_SIZE - stride, more_ref.shape[1]), jnp.float32)
    share = routes_ref.shape[2] // routes_ref.shape[0]

    def one_group(group, carry):
        seats = pl.ds(pl.multiple_of(group * stride, 16), stride)
        last, start = bounds_ref[seats, 0:1], bounds_ref[seats, 1:2]
        both = []
        for routes in (routes_ref[group], more_ref[...]):
            veil = jnp.where((routes <= last) & (routes >= start), 0.0, MASKED)
            veil = jnp.transpose(jnp.concatenate([veil, rest], axis=0))
            both.append(veil.astype(jnp.bfloat16))
        first = 0
        for sources, veil_ref in zip(sets, veil_refs):
            end = first + len(sources) * share
            veil_ref[group] = jnp.concatenate([veil[first:end] for veil in both], axis=0)
            first = end
        return carry

    lax.fori_loop(0, routes_ref.shape[0], one_group, 0)


def attend_kernel(starts, before, spare, stride, more, last, *refs):
    more_ref, queries_ref, veil_ref = refs[:3]
    refs = refs[3:]
    blocks = []
    for first_rows in starts:
        blocks.append(dict(zip(first_rows, refs)))
        refs = refs[len(first_rows) :]
    if more:
        top_ref, sum_ref, total_ref = refs[:3]
        refs = refs[3:]
    if last:
        seat_ref, out_ref, listed_rows, seen_by, mixed_ref, result_ref, done = refs
        mixed_ref[...] = jnp.zeros(mixed_ref.shape, jnp.bfloat16)
    else:
        new_top_ref, new_sum_ref, new_total_ref, listed_rows, seen_by = refs
    heads, ranks = queries_ref.shape[0], veil_ref.shape[0]
    packed = queries_ref.shape[1] // ranks
    wide = heads * HEAD_SIZE
    share = listed_rows.shape[0] // len(starts)
    count = share * ranks

    token = lax.broadcasted_iota(jnp.int32, (packed, HEAD_SIZE), 0)
    lane = lax.broadcasted_iota(jnp.int32, (packed, HEAD_SIZE), 1)
    own = lane < 0
    for at in range(HEAD_GROUPS):
        own = own | ((token == lane + at * spare) & (lane < spare))
    seen_by[...] = own.astype(jnp.float32).astype(jnp.bfloat16)
    lines = lax.broadcasted_iota(jnp.int32, (share, count), 1)
    for at, block in enumerate(blocks):
        places = more_ref[(before + at) * share : (before + at + 1) * share]
        pick = (lines == places).astype(jnp.float32).astype(jnp.bfloat16)
        for first in range(0, 2 * wide, 2 * HEAD_SIZE):
            lanes = slice(first, first + 2 * HEAD_SIZE)
            found = [
                contract(pick[:, row : row + ref.shape[0]], ref[:, lanes], 1, 0)
                for row, ref in block.items()
            ]
            listed_rows[at * share : (at + 1) * share, lanes] = sum(found).astype(jnp.bfloat16)
    scale = math.log2(math.e) / math.sqrt(HEAD_SIZE)

    def rows_of(group, row, first):
        lanes = slice(first, first + HEAD_SIZE)
        window = pl.ds(pl.multiple_of(group * share - row, 16), share)
        rows = [block[row][window, lanes] for block in blocks]
        return jnp.concatenate(rows + [listed_rows[:, lanes]], axis=0)

    def add_heads(group, row, some):
        tokens = pl.ds(pl.multiple_of(group * packed, 16), packed)
        scores = []
        for head in some:
            left = jnp.concatenate([queries_ref[head, tokens], seen_by[...]], axis=1)
            keys = rows_of(group, row, head * HEAD_SIZE)
            right = jnp.concatenate([keys, veil_ref[group]], axis=1)
            scores.append(contract(left, right, 1, 1))
        tops, weights = [], []
        for head, score in zip(some, scores):
            top = jnp.max(score, axis=1, keepdims=True)
            if more:
                top = jnp.maximum(top_ref[head, tokens], top)
            else:
                top = jnp.broadcast_to(top, (packed, HEAD_SIZE))
            tops.append(top)
            tiled = jnp.concatenate([top] * (score.shape[1] // HEAD_SIZE), axis=1)
            weights.append(jnp.exp2((score - tiled) * scale).astype(jnp.bfloat16))
        for head, top, weight in zip(some, tops, weights):
            values = rows_of(group, row, wide + head * HEAD_SIZE)
            values = jnp.concatenate([values, jnp.ones_like(values)], axis=1)
            mixed = contract(weight, values, 1, 0)
            total, weight_sum = mixed[:, :HEAD_SIZE], mixed[:, HEAD_SIZE:]
            if more:
                fade = jnp.exp2((top_ref[head, tokens] - top) * scale)
                total = total + fade * total_ref[head, tokens]
                weight_sum = weight_sum + fade * sum_ref[head, tokens]
            if last:
                mixed = total / weight_sum
                seats = pl.ds(pl.multiple_of(group * stride, 16), spare)
                for at in range(HEAD_GROUPS):
                    place = (head * HEAD_GROUPS + at) * HEAD_SIZE
                    rows = mixed[at * spare : (at + 1) * spare]
                    mixed_ref[seats, place : place + HEAD_SIZE] = rows.astype(jnp.bfloat16)
            else:
                new_top_ref[head, tokens] = top
                new_sum_ref[head, tokens] = weight_sum
                new_total_ref[head, tokens] = total

    rows = sorted({row for first_rows in starts for row in first_rows})
    for row, end in zip(rows, rows[1:] + [count]):

        def one_group(group, carry, row=row):
            for head in range(0, heads, UNROLL):
                add_heads(group, row, range(head, head + UNROLL))
            return carry

        lax.fori_loop(row // share, end // share, one_group, 0)
    if last:
        seat_lanes = lax.broadcasted_iota(jnp.int32, (count, mixed_ref.shape[0]), 1)
        seats = (seat_lanes == seat_ref[...]).astype(jnp.float32).astype(jnp.bfloat16)
        span = HEAD_GROUPS * HEAD_SIZE
        leaving = []
        for head in range(heads):
            lanes = slice(head * span, (head + 1) * span)
            rows = contract(seats, mixed_ref[:, lanes], 1, 0)
            result_ref[:, lanes] = rows.astype(jnp.bfloat16)
            lanes = pl.ds(head * span, span)
            leaving.append(
                pltpu.make_async_copy(
                    result_ref.at[:, lanes], out_ref.at[:, lanes], done.at[head]
                )
            )
            leaving[-1].start()
        for one in leaving:
            one.wait()


def spread(block, ranks, held):
    ring = [(rank, (rank + PLANE) % ranks) for rank in range(ranks)]
    across = [(rank, rank ^ 2) for rank in range(ranks)]
    beside = [(rank, rank ^ 1) for rank in range(ranks)]
    steps = ranks // PLANE
    half = block.shape[0] // 32 * 16

    def keep(source, first, array):
        held.setdefault(source, []).append((first, array))
        held.setdefault(source + 2 * steps, []).append((first, lax.ppermute(array, "dp", beside)))

    lane, other = block, None
    for step in range(steps - 1):
        following = lax.ppermute(lane, "dp", ring), lax.ppermute(lane, "dp", across)
        keep(step, 0, lane)
        if step:
            keep(steps + step - 1, 0, other)
        extra = yield
        lane, other, extra = lax.optimization_barrier((*following, extra))
        yield extra
    over = lax.ppermute(lane[:half], "dp", across)
    around = lax.ppermute(other[half:], "dp", ring)
    keep(steps - 1, 0, lane)
    keep(2 * steps - 2, 0, other)
    extra = yield other
    over, around, extra = lax.optimization_barrier((over, around, extra))
    keep(2 * steps - 1, 0, over)
    keep(2 * steps - 1, half, around)
    yield extra


def source_order(ranks):
    me = lax.axis_index("dp")
    lane, plane = me % PLANE, me // PLANE
    steps = ranks // PLANE
    planes = (plane - jnp.arange(steps, dtype=jnp.int32)) % steps
    return jnp.concatenate([planes * PLANE + (lane ^ flip) for flip in (0, 2, 1, 3)])


def gather_plan(
    hidden,
    queries,
    route,
    positions,
    key_matrix,
    value_matrix,
    key_projection_bias,
    value_projection_bias,
):
    ranks = lax.axis_size("dp")
    rows = hidden.shape[0]
    slots = positions.shape[0]
    share, extra = rows // ranks, 2
    spare = share + extra
    listed = ranks * extra
    stride = -(-spare // 16) * 16
    packed = -(-HEAD_GROUPS * spare // 16) * 16
    query_width = queries.shape[1]
    shape = jax.ShapeDtypeStruct

    def columns(array, chunk):
        first, heads = chunk
        return array[..., first * HEAD_SIZE : (first + heads) * HEAD_SIZE]

    matrices = {}
    sending = spread(jnp.concatenate([key_matrix, value_matrix], axis=1), ranks, matrices)
    next(sending)
    bucket, seat, sorted_route, more = pl.pallas_call(
        functools.partial(order_kernel, ranks, slots, extra, stride),
        out_shape=(
            shape((1, rows), jnp.int32),
            shape((1, rows), jnp.int32),
            shape((1, rows), jnp.int32),
            shape((2, listed), jnp.int32),
        ),
        in_specs=[VMEM],
        out_specs=(VMEM,) * 4,
        compiler_params=grant(16),
        name="order",
    )(route.reshape(1, rows))
    width = rows + 2 * listed
    plan = jnp.concatenate([sorted_route.reshape(rows), more.reshape(2 * listed), positions])
    plan = lax.all_to_all(
        jnp.broadcast_to(plan, (ranks, width + slots)), "dp", split_axis=0, concat_axis=0, tiled=True
    )
    sending.send(())
    next(sending)
    all_positions = plan[:, width:].reshape(-1, HEAD_SIZE)
    owners = source_order(ranks)
    planes = ranks // PLANE
    sets = [(0, 2 * planes)] + [
        (step, step + 2 * planes, step + planes - 1, step + 3 * planes - 1)
        for step in range(1, planes)
    ]
    sets.append((2 * planes - 1, 4 * planes - 1))

    half = HEAD_SIZE // 2
    frequency = 1000000.0 ** (-(jnp.arange(half, dtype=jnp.float32) * 2.0 / HEAD_SIZE))
    turned, bounds, cosine, sine = pl.pallas_call(
        functools.partial(query_kernel, ranks, spare, stride, packed),
        out_shape=(
            shape((KEY_VALUE_HEADS, ranks * packed, HEAD_SIZE), jnp.bfloat16),
            shape((ranks * stride, HEAD_SIZE), jnp.int32),
            shape((rows, HEAD_SIZE), jnp.float32),
            shape((rows, HEAD_SIZE), jnp.float32),
        ),
        in_specs=[VMEM] * 5,
        out_specs=(VMEM,) * 4,
        scratch_shapes=[pltpu.VMEM((ranks * packed, HEAD_SIZE), jnp.float32)],
        compiler_params=grant(20),
        cost_estimate=cost(4 * stride * ranks * rows * query_width, 4 * rows * query_width),
        name="turn_queries",
    )(
        route.reshape(rows, 1),
        seat,
        all_positions,
        jnp.concatenate([frequency, frequency]).reshape(1, HEAD_SIZE),
        queries,
    )

    shard, wide = key_matrix.shape[0], 2 * key_matrix.shape[1]

    def chip_parts(sources):
        chips, arrays = [], []
        for source in sources:
            chip = []
            for one in (source, source + 2 * planes):
                for first, array in matrices[one]:
                    chip.append((one, first))
                    arrays.append(array)
            chips.append(tuple(chip))
        return chips, arrays

    def scratch(chips, arrays):
        return [
            pltpu.VMEM((len(chips), rows, 2 * shard), jnp.bfloat16),
            pltpu.VMEM((len(chips), 2 * shard, wide), jnp.bfloat16),
            pltpu.SemaphoreType.DMA((len(chips) + len(arrays),)),
        ]

    def product_cost(chips):
        depth = 2 * shard * len(chips)
        return cost(2 * rows * depth * wide, 2 * depth * (rows + wide) + 8 * rows * wide)

    def add_part(total, sources):
        chips, arrays = chip_parts(sources)
        more = [] if total is None else [total]
        return pl.pallas_call(
            functools.partial(part_kernel, chips, bool(more)),
            out_shape=shape((rows, wide), jnp.float32),
            in_specs=[SMEM] + [HBM] * (1 + len(arrays)) + [VMEM] * len(more),
            out_specs=VMEM,
            scratch_shapes=scratch(chips, arrays),
            compiler_params=grant(16),
            cost_estimate=product_cost(chips),
            name="add_part",
        )(owners, hidden, *arrays, *more)

    turned, bounds, cosine, sine = sending.send((turned, bounds, cosine, sine))
    next(sending)
    (total,) = sending.send((add_part(None, (0, 1, planes)),))
    next(sending)
    (total,) = sending.send((add_part(total, (2, planes + 1)),))
    total = add_part(total, (3, planes + 2))
    chips, arrays = chip_parts((planes + 3,))
    bias = jnp.concatenate([key_projection_bias, value_projection_bias])
    (pairs,) = pl.pallas_call(
        functools.partial(finish_kernel, chips),
        out_shape=tuple(
            shape((rows, 2 * heads * HEAD_SIZE), jnp.bfloat16) for _, heads in CHUNKS
        ),
        in_specs=[SMEM, HBM] + [VMEM] * 4 + [HBM] * len(arrays) + [VMEM],
        out_specs=(VMEM,) * len(CHUNKS),
        scratch_shapes=scratch(chips, arrays),
        compiler_params=grant(16),
        cost_estimate=product_cost(chips),
        name="finish",
    )(
        owners,
        hidden,
        bias.astype(jnp.float32).reshape(1, wide),
        cosine,
        sine,
        bucket,
        *arrays,
        total,
    )

    blocks = {}
    sending = spread(pairs, ranks, blocks)
    next(sending)
    order = [source for sources in sets for source in sources]
    ordered = plan[:, :width][jnp.stack([owners[source] for source in order])]
    key_routes = ordered[:, :rows].reshape(ranks, ranks, share).transpose(1, 0, 2)
    more_places = ordered[:, rows + listed :].reshape(ranks * listed, 1)
    veils = pl.pallas_call(
        functools.partial(veil_kernel, sets, stride),
        out_shape=tuple(
            shape((ranks, 2 * share * len(sources), HEAD_SIZE), jnp.bfloat16) for sources in sets
        ),
        in_specs=[VMEM] * 3,
        out_specs=(VMEM,) * len(sets),
        compiler_params=grant(16),
        cost_estimate=cost(3 * 10**9, 4 * ranks * rows * HEAD_SIZE),
        name="veil",
    )(
        bounds,
        key_routes.reshape(ranks, 1, rows),
        ordered[:, rows : rows + listed].reshape(1, ranks * listed),
    )

    def attend(state, index):
        sources, last = sets[index], index == len(sets) - 1
        starts = [tuple(first for first, _ in blocks[source]) for source in sources]
        arrays = [array for source in sources for _, array in blocks[source]]
        fixed = [more_places, turned, veils[index], *arrays, *state]
        kept = shape((KEY_VALUE_HEADS, ranks * packed, HEAD_SIZE), jnp.float32)
        scratch_shapes = [
            pltpu.VMEM((len(sources) * share, wide), jnp.bfloat16),
            pltpu.VMEM((packed, HEAD_SIZE), jnp.bfloat16),
        ]
        if last:
            fixed.append(seat.reshape(rows, 1))
            scratch_shapes += [
                pltpu.VMEM((ranks * stride, query_width), jnp.bfloat16),
                pltpu.VMEM((rows, query_width), jnp.bfloat16),
                pltpu.SemaphoreType.DMA((KEY_VALUE_HEADS,)),
            ]
        keys = 2 * share * len(sources)
        return pl.pallas_call(
            functools.partial(
                attend_kernel,
                starts,
                sum(len(one) for one in sets[:index]),
                spare,
                stride,
                bool(state),
                last,
            ),
            out_shape=shape((rows, query_width), jnp.bfloat16) if last else (kept,) * 3,
            in_specs=[VMEM] * len(fixed),
            out_specs=HBM if last else (VMEM,) * 3,
            scratch_shapes=scratch_shapes,
            input_output_aliases={}
            if last or not state
            else {len(fixed) - 3 + at: at for at in range(3)},
            compiler_params=grant(20),
            cost_estimate=cost(
                8 * ranks * KEY_VALUE_HEADS * packed * (keys + 256) * HEAD_SIZE,
                2 * keys * rows * HEAD_SIZE,
            ),
            name="attend",
        )(*fixed)

    state = ()
    for step in range(planes - 1):
        if step:
            next(sending)
        state = sending.send(tuple(attend(state, step)))
    next(sending)
    state = sending.send(tuple(attend(state, planes - 1)))
    return attend(state, planes)


def apply_rotary(rows, slot_offset, heads):
    block_count = rows.shape[0]
    half = HEAD_SIZE // 2
    frequency = 1000000.0 ** (-(jnp.arange(half, dtype=jnp.float32) * 2.0 / HEAD_SIZE))
    angle = slot_offset.astype(jnp.float32)[:, None] * frequency[None, :]
    cosine = jnp.cos(angle)[:, None, :]
    sine = jnp.sin(angle)[:, None, :]
    grid = rows.astype(jnp.float32).reshape(block_count, heads, HEAD_SIZE)
    first = grid[:, :, :half]
    second = grid[:, :, half:]
    turned = jnp.concatenate(
        [first * cosine - second * sine, second * cosine + first * sine], axis=2
    )
    return turned.reshape(block_count, heads * HEAD_SIZE).astype(jnp.bfloat16)


def causal_block_attention(pieces):
    query_tile_rows, key_tile_rows, value_tile_rows, spot_block = pieces
    block_count = query_tile_rows.shape[0]
    head_groups = QUERY_HEADS // KEY_VALUE_HEADS
    query_block_grid = query_tile_rows.reshape(block_count, KEY_VALUE_HEADS, head_groups, HEAD_SIZE)
    key_block_grid = key_tile_rows.reshape(block_count, KEY_VALUE_HEADS, HEAD_SIZE)
    value_block_grid = value_tile_rows.reshape(block_count, KEY_VALUE_HEADS, HEAD_SIZE)
    scores = jnp.einsum(
        "qhgd,khd->hgqk", query_block_grid, key_block_grid, preferred_element_type=jnp.float32
    ) / math.sqrt(HEAD_SIZE)
    inner = jnp.arange(block_count, dtype=jnp.int32)
    visible = (inner[None, :] <= inner[:, None]) & (
        inner[None, :] >= inner[:, None] - spot_block[:, None]
    )
    scores = jnp.where(visible, scores, -jnp.inf)
    top = jnp.max(scores, axis=3, keepdims=True)
    weights = jnp.exp(scores - top)
    totals = jnp.sum(weights, axis=3)
    probs = weights.astype(jnp.bfloat16)
    mixed = jnp.einsum(
        "hgqk,khd->qhgd", probs, value_block_grid, preferred_element_type=jnp.float32
    )
    mixed = mixed / jnp.transpose(totals, (2, 0, 1))[:, :, :, None]
    return mixed.reshape(block_count, QUERY_HEADS * HEAD_SIZE).astype(jnp.bfloat16)


def add_projection(left, pieces):
    return (
        jnp.dot(left, pieces[0], preferred_element_type=jnp.float32),
        jnp.dot(left, pieces[1], preferred_element_type=jnp.float32),
    )


def project_own(hidden, key_matrix, value_matrix, key_projection_bias, value_projection_bias):
    totals = add_projection(
        hidden,
        (
            lax.all_gather(key_matrix, "dp", axis=0, tiled=True),
            lax.all_gather(value_matrix, "dp", axis=0, tiled=True),
        ),
    )
    key_rows = (totals[0] + key_projection_bias.astype(jnp.float32)).astype(jnp.bfloat16)
    value_rows = (totals[1] + value_projection_bias.astype(jnp.float32)).astype(jnp.bfloat16)
    return jnp.concatenate([key_rows, value_rows], axis=1)


def send_plan(
    hidden,
    queries,
    route,
    positions,
    key_matrix,
    value_matrix,
    key_projection_bias,
    value_projection_bias,
):
    ranks = lax.axis_size("dp")
    rows = hidden.shape[0]
    slots = positions.shape[0]
    spare = rows // ranks + 2
    width = ranks * spare
    paired_width = key_matrix.shape[1]
    target = route // slots
    place = route - target * slots
    member = (target[:, None] == jnp.arange(ranks, dtype=jnp.int32)[None, :]).astype(jnp.int32)
    order = jnp.sum(jnp.cumsum(member, axis=0) * member, axis=1) - 1
    bucket = target * spare + order
    outgoing = jnp.full((width,), slots, jnp.int32).at[bucket].set(place)
    arrived = lax.all_to_all(
        outgoing.reshape(ranks, spare), "dp", split_axis=0, concat_axis=0, tiled=True
    ).reshape(width)
    query_buf = jnp.zeros((width, queries.shape[1]), jnp.bfloat16).at[bucket].set(queries)
    own_pairs = project_own(
        hidden, key_matrix, value_matrix, key_projection_bias, value_projection_bias
    )
    pair_buf = jnp.zeros((width, 2 * paired_width), jnp.bfloat16).at[bucket].set(own_pairs)
    got_query, got_pairs = (
        lax.all_to_all(
            query_buf.reshape(ranks, spare, -1), "dp", split_axis=0, concat_axis=0, tiled=True
        ),
        lax.all_to_all(
            pair_buf.reshape(ranks, spare, -1), "dp", split_axis=0, concat_axis=0, tiled=True
        ),
    )
    got_query = got_query.reshape(width, -1)
    got_pairs = got_pairs.reshape(width, -1)
    query_slot_rows = (
        jnp.zeros((slots, got_query.shape[1]), jnp.bfloat16).at[arrived].set(got_query, mode="drop")
    )
    paired_slot_rows = (
        jnp.zeros((slots, 2 * paired_width), jnp.bfloat16).at[arrived].set(got_pairs, mode="drop")
    )
    query_turned = apply_rotary(query_slot_rows, positions, QUERY_HEADS)
    key_rotated = apply_rotary(paired_slot_rows[:, :paired_width], positions, KEY_VALUE_HEADS)
    block_list = slots // BLOCK_SLOTS
    attended = lax.map(
        causal_block_attention,
        (
            query_turned.reshape(block_list, BLOCK_SLOTS, -1),
            key_rotated.reshape(block_list, BLOCK_SLOTS, -1),
            paired_slot_rows[:, paired_width:].reshape(block_list, BLOCK_SLOTS, -1),
            positions.reshape(block_list, BLOCK_SLOTS),
        ),
    )
    attended = attended.reshape(slots, -1)
    leaving = attended[jnp.minimum(arrived, slots - 1)]
    returned = lax.all_to_all(
        leaving.reshape(ranks, spare, -1), "dp", split_axis=0, concat_axis=0, tiled=True
    ).reshape(width, -1)
    return returned[bucket]


def local(*args):
    hidden, queries, _, positions, key_matrix = args[:5]
    ranks = lax.axis_size("dp")
    rows = hidden.shape[0]
    gathered = ranks * ranks * (rows // ranks + 2) * 4 * key_matrix.shape[1]
    chip_rows = 2 * key_matrix.shape[0]
    fits = rows % (16 * ranks) == 0 and chip_rows % HEAD_SIZE == 0 and gathered <= GATHER_LIMIT
    if ranks == PLANES * PLANE and fits:
        return gather_plan(*args)
    return send_plan(*args)


def solution(mesh):
    placed = (
        P(("groups", "dp"), None),
        P(("groups", "dp"), None),
        P(("groups", "dp")),
        P(("groups", "dp")),
        P("dp", None),
        P("dp", None),
        P(),
        P(),
    )
    return jax.shard_map(
        local, mesh=mesh, in_specs=placed, out_specs=P(("groups", "dp"), None), check_vma=False
    )
```

```python
import functools
import math

import jax
import jax.numpy as jnp
import numpy as np
from jax import lax
from jax.experimental import pallas as pl
from jax.experimental.pallas import tpu as pltpu
from jax.sharding import PartitionSpec as P

QUERY_HEADS = 20
KEY_VALUE_HEADS = 4
HEAD_SIZE = 128
BLOCK_SLOTS = 512
HEAD_GROUPS = QUERY_HEADS // KEY_VALUE_HEADS
CHUNKS = ((0, KEY_VALUE_HEADS),)
PLANE = 4
PLANES = 4
UNROLL = 4
GATHER_LIMIT = 40 * 2**20
MASKED = -1e30
VMEM = pl.BlockSpec(memory_space=pltpu.VMEM)
SMEM = pl.BlockSpec(memory_space=pltpu.SMEM)
HBM = pl.BlockSpec(memory_space=pltpu.HBM)


def grant(mebibytes):
    return pltpu.CompilerParams(vmem_limit_bytes=mebibytes * 2**20)


def cost(flops, moved):
    return pl.CostEstimate(flops=flops, bytes_accessed=moved, transcendentals=0)


def one_hot_rows(count, index_row):
    rows = lax.broadcasted_iota(jnp.int32, (count, index_row.shape[1]), 0)
    return (rows == index_row).astype(jnp.float32).astype(jnp.bfloat16)


def split(number):
    high = lax.shift_right_logical(number, HEAD_SIZE.bit_length() - 1)
    return high, number - high * HEAD_SIZE


def contract(left, right, left_dim, right_dim):
    return lax.dot_general(
        left, right, (((left_dim,), (right_dim,)), ((), ())), preferred_element_type=jnp.float32
    )


def turn(rows, cosine, sine):
    return (rows * cosine + pltpu.roll(rows, HEAD_SIZE // 2, 1) * sine).astype(jnp.bfloat16)


def join_kernel(left_ref, right_ref, out_ref, done):
    wide = left_ref.shape[1]
    copies = [
        pltpu.make_async_copy(ref, out_ref.at[:, pl.ds(at * wide, wide)], done.at[at])
        for at, ref in enumerate((left_ref, right_ref))
    ]
    for copy in copies:
        copy.start()
    for copy in copies:
        copy.wait()


def order_kernel(
    ranks, slots, extra, stride, route_ref, bucket_ref, seat_ref, sorted_ref, more_ref
):
    route = route_ref[...]
    count = route.shape[1]
    share = count // ranks
    target = lax.div(route, slots)
    member = (lax.broadcasted_iota(jnp.int32, (ranks, count), 0) == target).astype(jnp.float32)
    before = lax.broadcasted_iota(jnp.int32, (count, count), 0) < lax.broadcasted_iota(
        jnp.int32, (count, count), 1
    )
    before = before.astype(jnp.float32).astype(jnp.bfloat16)
    ahead = contract(member.astype(jnp.bfloat16), before, 1, 0)
    order = jnp.sum(member * ahead, axis=0, keepdims=True).astype(jnp.int32)
    beyond = order >= share
    beyond_rows = jnp.broadcast_to(beyond.astype(jnp.float32), (8, count)).astype(jnp.bfloat16)
    number = contract(beyond_rows, before, 1, 0)[0:1]
    counts = jnp.sum(member, axis=1, keepdims=True)
    free = jnp.maximum(share - counts, 0.0)
    group = lax.broadcasted_iota(jnp.int32, (ranks, ranks), 0)
    lower = (group > lax.broadcasted_iota(jnp.int32, (ranks, ranks), 1)).astype(jnp.float32)
    free_rows = jnp.broadcast_to(free, (ranks, HEAD_SIZE)).astype(jnp.bfloat16)
    free_before = contract(lower.astype(jnp.bfloat16), free_rows, 1, 0)[:, 0:1]
    inside = (number >= free_before) & (number < free_before + free)
    base = lax.broadcasted_iota(jnp.int32, (ranks, 1), 0).astype(jnp.float32) * share + counts
    hole = jnp.sum(jnp.where(inside, base + number - free_before, 0.0), axis=0, keepdims=True)
    bucket = jnp.where(beyond, hole.astype(jnp.int32), target * share + order)
    bucket_ref[...] = bucket
    seat_ref[...] = target * stride + order
    high, low = split(route)
    place_high, place_low = split(bucket)
    line = lax.broadcasted_iota(jnp.int32, (8, count), 0)
    digits = jnp.where(line == 0, high, 0)
    digits = jnp.where(line == 1, low, digits)
    digits = jnp.where(line == 2, place_high, digits)
    digits = jnp.where(line == 3, place_low, digits)
    digits = jnp.where(line == 4, 1, digits).astype(jnp.float32).astype(jnp.bfloat16)
    placed = contract(digits, one_hot_rows(count, bucket), 1, 1)
    sorted_ref[...] = (placed[0:1] * HEAD_SIZE + placed[1:2]).astype(jnp.int32)
    listed = jnp.where(beyond, target * extra + order - share, -1)
    found = contract(digits, one_hot_rows(ranks * extra, listed), 1, 1)
    none = found[4:5] - 1.0
    more_ref[0:1] = (found[0:1] * HEAD_SIZE + found[1:2] + none).astype(jnp.int32)
    more_ref[1:2] = (found[2:3] * HEAD_SIZE + found[3:4] + none).astype(jnp.int32)


def query_kernel(
    ranks, spare, stride, packed, route_ref, seat_ref, positions_ref, frequency_ref, queries_ref, *refs
):
    turned_ref, bounds_ref, cosine_ref, sine_ref, rows_ref = refs
    route = route_ref[...]
    count = route.shape[0]
    lines = positions_ref.shape[0]
    line, lane = split(route)
    pick = (lax.broadcasted_iota(jnp.int32, (count, lines), 1) == line).astype(jnp.float32)
    pick = pick.astype(jnp.bfloat16)
    positions = positions_ref[...]
    half = lax.shift_right_logical(positions, 1)
    rest = positions - half * 2
    rows = 2.0 * contract(pick, half.astype(jnp.float32).astype(jnp.bfloat16), 1, 0) + contract(
        pick, rest.astype(jnp.float32).astype(jnp.bfloat16), 1, 0
    )
    lanes = lax.broadcasted_iota(jnp.int32, (count, HEAD_SIZE), 1)
    spot = jnp.sum(jnp.where(lanes == lane, rows, 0.0), axis=1, keepdims=True)
    angle = spot * frequency_ref[...]
    cosine = jnp.cos(angle)
    sine = jnp.sin(angle)
    sine = jnp.where(lanes < HEAD_SIZE // 2, -sine, sine)
    cosine_ref[...] = cosine
    sine_ref[...] = sine
    seats = one_hot_rows(ranks * stride, seat_ref[...])
    first = route - spot.astype(jnp.int32)
    first_line, first_lane = split(first)
    digits = jnp.where(lanes == 0, line, 0)
    digits = jnp.where(lanes == 1, lane, digits)
    digits = jnp.where(lanes == 2, first_line, digits)
    digits = jnp.where(lanes == 3, first_lane, digits)
    digits = jnp.where(lanes == 4, 1, digits)
    placed = contract(seats, digits.astype(jnp.float32).astype(jnp.bfloat16), 1, 0)
    live = placed[:, 4:5] - 1.0
    last = placed[:, 0:1] * HEAD_SIZE + placed[:, 1:2] + live
    start = placed[:, 2:3] * HEAD_SIZE + placed[:, 3:4] + live
    seat_lanes = lax.broadcasted_iota(jnp.int32, placed.shape, 1)
    bounds_ref[...] = jnp.where(seat_lanes == 0, last, start).astype(jnp.int32)
    rows_ref[...] = jnp.zeros(rows_ref.shape, jnp.float32)
    for head in range(KEY_VALUE_HEADS):
        for place in range(HEAD_GROUPS):
            at = (head * HEAD_GROUPS + place) * HEAD_SIZE
            one = queries_ref[:, at : at + HEAD_SIZE].astype(jnp.float32)
            rows = contract(seats, turn(one, cosine, sine), 1, 0)
            for group in range(ranks):
                at = group * packed + place * spare
                rows_ref[at : at + spare] = rows[group * stride : group * stride + spare]
        turned_ref[head] = rows_ref[...].astype(jnp.bfloat16)


def add_products(chips, owners_ref, hidden_ref, refs, columns, matrix, done):
    shard = matrix.shape[1] // 2
    copies, at, taken = [], 0, 0
    for place, chip in enumerate(chips):
        first = pl.multiple_of(lax.div(owners_ref[chip[0][0]], 2) * (2 * shard), HEAD_SIZE)
        copies.append(
            (hidden_ref.at[:, pl.ds(first, 2 * shard)], columns.at[place])
        )
        for source, row in chip:
            core = lax.rem(owners_ref[source], 2)
            rows = pl.ds(pl.multiple_of(core * shard + row, 16), refs[taken].shape[0])
            copies.append((refs[taken], matrix.at[place, rows]))
            taken += 1
    copies = [pltpu.make_async_copy(*pair, done.at[at]) for at, pair in enumerate(copies)]
    for copy in copies:
        copy.start()

    def product(span):
        total = contract(columns[0], matrix[0, :, span], 1, 0)
        for place in range(1, len(chips)):
            total = total + contract(columns[place], matrix[place, :, span], 1, 0)
        return total

    return copies, product


def part_kernel(chips, more, owners_ref, hidden_ref, *refs):
    count = sum(len(chip) for chip in chips)
    parts, refs = refs[:count], refs[count:]
    if more:
        total_ref, refs = refs[0], refs[1:]
    out_ref, columns, matrix, done = refs
    copies, product = add_products(chips, owners_ref, hidden_ref, parts, columns, matrix, done)
    for copy in copies:
        copy.wait()
    for first in range(0, out_ref.shape[1], 2 * HEAD_SIZE):
        span = slice(first, first + 2 * HEAD_SIZE)
        if more:
            out_ref[:, span] = total_ref[:, span] + product(span)
        else:
            out_ref[:, span] = product(span)


def finish_kernel(
    chips, owners_ref, hidden_ref, bias_ref, cosine_ref, sine_ref, bucket_ref, *refs
):
    count = sum(len(chip) for chip in chips)
    parts, total_ref = refs[:count], refs[count]
    outs, (columns, matrix, done) = refs[count + 1 : -3], refs[-3:]
    copies, product = add_products(chips, owners_ref, hidden_ref, parts, columns, matrix, done)
    places = one_hot_rows(outs[0].shape[0], bucket_ref[...])
    for copy in copies:
        copy.wait()
    wide = KEY_VALUE_HEADS * HEAD_SIZE
    for first in range(0, 2 * wide, 2 * HEAD_SIZE):
        span = slice(first, first + 2 * HEAD_SIZE)
        rows = (total_ref[:, span] + product(span) + bias_ref[:, span]).astype(jnp.bfloat16)
        if first < wide:
            cosine, sine = cosine_ref[...], sine_ref[...]
            halves = [
                turn(rows[:, at : at + HEAD_SIZE].astype(jnp.float32), cosine, sine)
                for at in (0, HEAD_SIZE)
            ]
            rows = jnp.concatenate(halves, axis=1)
        rows = contract(places, rows, 1, 0).astype(jnp.bfloat16)
        for half in range(2):
            head = first % wide // HEAD_SIZE + half
            for (first_head, heads), out_ref in zip(CHUNKS, outs):
                if first_head <= head < first_head + heads:
                    at = (head - first_head + first // wide * heads) * HEAD_SIZE
                    out_ref[:, at : at + HEAD_SIZE] = rows[
                        :, half * HEAD_SIZE : (half + 1) * HEAD_SIZE
                    ]


def veil_kernel(sets, stride, bounds_ref, routes_ref, more_ref, *veil_refs):
    rest = jnp.zeros((HEAD_SIZE - stride, more_ref.shape[1]), jnp.float32)
    share = routes_ref.shape[2] // routes_ref.shape[0]

    def one_group(group, carry):
        seats = pl.ds(pl.multiple_of(group * stride, 16), stride)
        last, start = bounds_ref[seats, 0:1], bounds_ref[seats, 1:2]
        both = []
        for routes in (routes_ref[group], more_ref[...]):
            veil = jnp.where((routes <= last) & (routes >= start), 0.0, MASKED)
            veil = jnp.transpose(jnp.concatenate([veil, rest], axis=0))
            both.append(veil.astype(jnp.bfloat16))
        first = 0
        for sources, veil_ref in zip(sets, veil_refs):
            end = first + len(sources) * share
            veil_ref[group] = jnp.concatenate([veil[first:end] for veil in both], axis=0)
            first = end
        return carry

    lax.fori_loop(0, routes_ref.shape[0], one_group, 0)


def attend_kernel(starts, before, spare, stride, more, last, *refs):
    more_ref, queries_ref, veil_ref = refs[:3]
    refs = refs[3:]
    blocks = []
    for first_rows in starts:
        blocks.append(dict(zip(first_rows, refs)))
        refs = refs[len(first_rows) :]
    if more:
        stats_ref, total_ref = refs[:2]
        refs = refs[2:]
    if last:
        seat_ref, out_ref, listed_rows, seen_by, mixed_ref, result_ref, done = refs
        mixed_ref[...] = jnp.zeros(mixed_ref.shape, jnp.bfloat16)
    else:
        new_stats_ref, new_total_ref, listed_rows, seen_by = refs
    heads, ranks = queries_ref.shape[0], veil_ref.shape[0]
    packed = queries_ref.shape[1] // ranks
    wide = heads * HEAD_SIZE
    share = listed_rows.shape[0] // len(starts)
    count = share * ranks

    token = lax.broadcasted_iota(jnp.int32, (packed, HEAD_SIZE), 0)
    lane = lax.broadcasted_iota(jnp.int32, (packed, HEAD_SIZE), 1)
    own = lane < 0
    for at in range(HEAD_GROUPS):
        own = own | ((token == lane + at * spare) & (lane < spare))
    seen_by[...] = own.astype(jnp.float32).astype(jnp.bfloat16)
    lines = lax.broadcasted_iota(jnp.int32, (share, count), 1)
    for at, block in enumerate(blocks):
        places = more_ref[(before + at) * share : (before + at + 1) * share]
        pick = (lines == places).astype(jnp.float32).astype(jnp.bfloat16)
        for first in range(0, 2 * wide, 2 * HEAD_SIZE):
            lanes = slice(first, first + 2 * HEAD_SIZE)
            found = [
                contract(pick[:, row : row + ref.shape[0]], ref[:, lanes], 1, 0)
                for row, ref in block.items()
            ]
            listed_rows[at * share : (at + 1) * share, lanes] = sum(found).astype(jnp.bfloat16)
    scale = math.log2(math.e) / math.sqrt(HEAD_SIZE)

    def rows_of(group, row, first):
        lanes = slice(first, first + HEAD_SIZE)
        window = pl.ds(pl.multiple_of(group * share - row, 16), share)
        rows = [block[row][window, lanes] for block in blocks]
        return jnp.concatenate(rows + [listed_rows[:, lanes]], axis=0)

    def add_heads(group, row, some):
        tokens = pl.ds(pl.multiple_of(group * packed, 16), packed)
        scores = []
        for head in some:
            left = jnp.concatenate([queries_ref[head, tokens], seen_by[...]], axis=1)
            keys = rows_of(group, row, head * HEAD_SIZE)
            right = jnp.concatenate([keys, veil_ref[group]], axis=1)
            scores.append(contract(left, right, 1, 1))
        tops, weights, fades, sums = [], [], [], []
        for head, score in zip(some, scores):
            top = jnp.max(score, axis=1, keepdims=True)
            if more:
                stats = stats_ref[head, tokens]
                other = pltpu.roll(stats, HEAD_SIZE // 2, 1)
                old_top = jnp.where(lane < HEAD_SIZE // 2, stats, other)
                sums.append(jnp.where(lane < HEAD_SIZE // 2, other, stats))
                top = jnp.maximum(old_top, top)
                fades.append(jnp.exp2((old_top - top) * scale))
            else:
                top = jnp.broadcast_to(top, (packed, HEAD_SIZE))
            tops.append(top)
            tiled = jnp.concatenate([top] * (score.shape[1] // HEAD_SIZE), axis=1)
            weights.append(jnp.exp2((score - tiled) * scale).astype(jnp.bfloat16))
        for at_head, (head, top, weight) in enumerate(zip(some, tops, weights)):
            values = rows_of(group, row, wide + head * HEAD_SIZE)
            values = jnp.concatenate([values, jnp.ones_like(values)], axis=1)
            mixed = contract(weight, values, 1, 0)
            total, weight_sum = mixed[:, :HEAD_SIZE], mixed[:, HEAD_SIZE:]
            if more:
                total = total + fades[at_head] * total_ref[head, tokens]
                weight_sum = weight_sum + fades[at_head] * sums[at_head]
            if last:
                mixed = total / weight_sum
                seats = pl.ds(pl.multiple_of(group * stride, 16), spare)
                for at in range(HEAD_GROUPS):
                    place = (head * HEAD_GROUPS + at) * HEAD_SIZE
                    rows = mixed[at * spare : (at + 1) * spare]
                    mixed_ref[seats, place : place + HEAD_SIZE] = rows.astype(jnp.bfloat16)
            else:
                new_stats_ref[head, tokens] = jnp.where(lane < HEAD_SIZE // 2, top, weight_sum)
                new_total_ref[head, tokens] = total

    rows = sorted({row for first_rows in starts for row in first_rows})
    for row, end in zip(rows, rows[1:] + [count]):

        def one_group(group, carry, row=row):
            for head in range(0, heads, UNROLL):
                add_heads(group, row, range(head, head + UNROLL))
            return carry

        lax.fori_loop(row // share, end // share, one_group, 0)
    if last:
        seat_lanes = lax.broadcasted_iota(jnp.int32, (count, mixed_ref.shape[0]), 1)
        seats = (seat_lanes == seat_ref[...]).astype(jnp.float32).astype(jnp.bfloat16)
        span = HEAD_GROUPS * HEAD_SIZE
        leaving = []
        for head in range(heads):
            lanes = slice(head * span, (head + 1) * span)
            rows = contract(seats, mixed_ref[:, lanes], 1, 0)
            result_ref[:, lanes] = rows.astype(jnp.bfloat16)
            lanes = pl.ds(head * span, span)
            leaving.append(
                pltpu.make_async_copy(
                    result_ref.at[:, lanes], out_ref.at[:, lanes], done.at[head]
                )
            )
            leaving[-1].start()
        for one in leaving:
            one.wait()


def spread(block, ranks, held):
    ring = [(rank, (rank + PLANE) % ranks) for rank in range(ranks)]
    across = [(rank, rank ^ 2) for rank in range(ranks)]
    beside = [(rank, rank ^ 1) for rank in range(ranks)]
    steps = ranks // PLANE
    half = block.shape[0] // 32 * 16

    def keep(source, first, array):
        held.setdefault(source, []).append((first, array))
        held.setdefault(source + 2 * steps, []).append((first, lax.ppermute(array, "dp", beside)))

    lane, other = block, None
    for step in range(steps - 1):
        following = lax.ppermute(lane, "dp", ring), lax.ppermute(lane, "dp", across)
        keep(step, 0, lane)
        if step:
            keep(steps + step - 1, 0, other)
        extra = yield
        lane, other, extra = lax.optimization_barrier((*following, extra))
        yield extra
    over = lax.ppermute(lane[:half], "dp", across)
    around = lax.ppermute(other[half:], "dp", ring)
    keep(steps - 1, 0, lane)
    keep(2 * steps - 2, 0, other)
    extra = yield other
    over, around, extra = lax.optimization_barrier((over, around, extra))
    keep(2 * steps - 1, 0, over)
    keep(2 * steps - 1, half, around)
    yield extra


def source_order(ranks, sources):
    me = lax.axis_index("dp")
    lane, plane = lax.rem(me, PLANE), lax.div(me, PLANE)
    planes = ranks // PLANE
    steps = np.array([source % planes for source in sources], np.int32)
    flips = np.array([(0, 2, 1, 3)[source // planes] for source in sources], np.int32)
    return lax.rem(plane + (planes - steps), planes) * PLANE + (lane ^ flips)


def gather_plan(
    hidden,
    queries,
    route,
    positions,
    key_matrix,
    value_matrix,
    key_projection_bias,
    value_projection_bias,
):
    ranks = lax.axis_size("dp")
    rows = hidden.shape[0]
    slots = positions.shape[0]
    share, extra = rows // ranks, 2
    spare = share + extra
    listed = ranks * extra
    stride = -(-spare // 16) * 16
    packed = -(-HEAD_GROUPS * spare // 16) * 16
    query_width = queries.shape[1]
    shape = jax.ShapeDtypeStruct

    def columns(array, chunk):
        first, heads = chunk
        return array[..., first * HEAD_SIZE : (first + heads) * HEAD_SIZE]

    matrices = {}
    joined = pl.pallas_call(
        join_kernel,
        out_shape=shape((key_matrix.shape[0], 2 * key_matrix.shape[1]), jnp.bfloat16),
        in_specs=[HBM] * 2,
        out_specs=VMEM,
        scratch_shapes=[pltpu.SemaphoreType.DMA((2,))],
        compiler_params=grant(14),
        name="join",
    )(key_matrix, value_matrix)
    sending = spread(joined, ranks, matrices)
    next(sending)
    bucket, seat, sorted_route, more = pl.pallas_call(
        functools.partial(order_kernel, ranks, slots, extra, stride),
        out_shape=(
            shape((1, rows), jnp.int32),
            shape((1, rows), jnp.int32),
            shape((1, rows), jnp.int32),
            shape((2, listed), jnp.int32),
        ),
        in_specs=[VMEM],
        out_specs=(VMEM,) * 4,
        compiler_params=grant(14),
        name="order",
    )(route.reshape(1, rows))
    width = rows + 2 * listed
    plan = jnp.concatenate([sorted_route.reshape(rows), more.reshape(2 * listed), positions])
    plan = lax.all_to_all(
        jnp.broadcast_to(plan, (ranks, width + slots)), "dp", split_axis=0, concat_axis=0, tiled=True
    )
    plan, bucket, seat = sending.send((plan, bucket, seat))
    next(sending)
    all_positions = plan[:, width:].reshape(-1, HEAD_SIZE)
    planes = ranks // PLANE
    sets = [(0, 2 * planes)] + [
        (step, step + 2 * planes, step + planes - 1, step + 3 * planes - 1)
        for step in range(1, planes)
    ]
    sets.append((2 * planes - 1, 4 * planes - 1))
    owners = source_order(ranks, range(ranks))

    half = HEAD_SIZE // 2
    frequency = 1000000.0 ** (-(jnp.arange(half, dtype=jnp.float32) * 2.0 / HEAD_SIZE))
    turned, bounds, cosine, sine = pl.pallas_call(
        functools.partial(query_kernel, ranks, spare, stride, packed),
        out_shape=(
            shape((KEY_VALUE_HEADS, ranks * packed, HEAD_SIZE), jnp.bfloat16),
            shape((ranks * stride, HEAD_SIZE), jnp.int32),
            shape((rows, HEAD_SIZE), jnp.float32),
            shape((rows, HEAD_SIZE), jnp.float32),
        ),
        in_specs=[VMEM] * 5,
        out_specs=(VMEM,) * 4,
        scratch_shapes=[pltpu.VMEM((ranks * packed, HEAD_SIZE), jnp.float32)],
        compiler_params=grant(14),
        cost_estimate=cost(4 * stride * ranks * rows * query_width, 4 * rows * query_width),
        name="turn_queries",
    )(
        route.reshape(rows, 1),
        seat,
        all_positions,
        jnp.concatenate([frequency, frequency]).reshape(1, HEAD_SIZE),
        queries,
    )

    shard, wide = key_matrix.shape[0], 2 * key_matrix.shape[1]

    def chip_parts(sources):
        chips, arrays = [], []
        for source in sources:
            chip = []
            for one in (source, source + 2 * planes):
                for first, array in matrices[one]:
                    chip.append((one, first))
                    arrays.append(array)
            chips.append(tuple(chip))
        return chips, arrays

    def scratch(chips, arrays):
        return [
            pltpu.VMEM((len(chips), rows, 2 * shard), jnp.bfloat16),
            pltpu.VMEM((len(chips), 2 * shard, wide), jnp.bfloat16),
            pltpu.SemaphoreType.DMA((len(chips) + len(arrays),)),
        ]

    def product_cost(chips):
        depth = 2 * shard * len(chips)
        return cost(2 * rows * depth * wide, 2 * depth * (rows + wide) + 8 * rows * wide)

    def add_part(total, sources):
        chips, arrays = chip_parts(sources)
        more = [] if total is None else [total]
        return pl.pallas_call(
            functools.partial(part_kernel, chips, bool(more)),
            out_shape=shape((rows, wide), jnp.float32),
            in_specs=[SMEM] + [HBM] * (1 + len(arrays)) + [VMEM] * len(more),
            out_specs=VMEM,
            scratch_shapes=scratch(chips, arrays),
            compiler_params=grant(14),
            cost_estimate=product_cost(chips),
            name="add_part",
        )(owners, hidden, *arrays, *more)

    turned, bounds, cosine, sine = sending.send((turned, bounds, cosine, sine))
    next(sending)
    (total,) = sending.send((add_part(None, (0, 1, planes)),))
    next(sending)
    total = add_part(total, (2, planes + 1))
    (total,) = sending.send((add_part(total, (3, planes + 2)),))
    chips, arrays = chip_parts((planes + 3,))
    bias = jnp.concatenate([key_projection_bias, value_projection_bias])
    (pairs,) = pl.pallas_call(
        functools.partial(finish_kernel, chips),
        out_shape=tuple(
            shape((rows, 2 * heads * HEAD_SIZE), jnp.bfloat16) for _, heads in CHUNKS
        ),
        in_specs=[SMEM, HBM] + [VMEM] * 4 + [HBM] * len(arrays) + [VMEM],
        out_specs=(VMEM,) * len(CHUNKS),
        scratch_shapes=scratch(chips, arrays),
        compiler_params=grant(14),
        cost_estimate=product_cost(chips),
        name="finish",
    )(
        owners,
        hidden,
        bias.astype(jnp.float32).reshape(1, wide),
        cosine,
        sine,
        bucket,
        *arrays,
        total,
    )

    blocks = {}
    sending = spread(pairs, ranks, blocks)
    next(sending)
    order = [source for sources in sets for source in sources]
    ordered = plan[:, :width][source_order(ranks, order)]
    key_routes = ordered[:, :rows].reshape(ranks, ranks, share).transpose(1, 0, 2)
    more_places = ordered[:, rows + listed :].reshape(ranks * listed, 1)
    veils = pl.pallas_call(
        functools.partial(veil_kernel, sets, stride),
        out_shape=tuple(
            shape((ranks, 2 * share * len(sources), HEAD_SIZE), jnp.bfloat16) for sources in sets
        ),
        in_specs=[VMEM] * 3,
        out_specs=(VMEM,) * len(sets),
        compiler_params=grant(14),
        cost_estimate=cost(3 * 10**9, 4 * ranks * rows * HEAD_SIZE),
        name="veil",
    )(
        bounds,
        key_routes.reshape(ranks, 1, rows),
        ordered[:, rows : rows + listed].reshape(1, ranks * listed),
    )

    def attend(state, index):
        sources, last = sets[index], index == len(sets) - 1
        starts = [tuple(first for first, _ in blocks[source]) for source in sources]
        arrays = [array for source in sources for _, array in blocks[source]]
        fixed = [more_places, turned, veils[index], *arrays, *state]
        kept = shape((KEY_VALUE_HEADS, ranks * packed, HEAD_SIZE), jnp.float32)
        scratch_shapes = [
            pltpu.VMEM((len(sources) * share, wide), jnp.bfloat16),
            pltpu.VMEM((packed, HEAD_SIZE), jnp.bfloat16),
        ]
        if last:
            fixed.append(seat.reshape(rows, 1))
            scratch_shapes += [
                pltpu.VMEM((ranks * stride, query_width), jnp.bfloat16),
                pltpu.VMEM((rows, query_width), jnp.bfloat16),
                pltpu.SemaphoreType.DMA((KEY_VALUE_HEADS,)),
            ]
        keys = 2 * share * len(sources)
        return pl.pallas_call(
            functools.partial(
                attend_kernel,
                starts,
                sum(len(one) for one in sets[:index]),
                spare,
                stride,
                bool(state),
                last,
            ),
            out_shape=shape((rows, query_width), jnp.bfloat16) if last else (kept,) * 2,
            in_specs=[VMEM] * len(fixed),
            out_specs=HBM if last else (VMEM,) * 2,
            scratch_shapes=scratch_shapes,
            input_output_aliases={}
            if last or not state
            else {len(fixed) - 2 + at: at for at in range(2)},
            compiler_params=grant(14),
            cost_estimate=cost(
                8 * ranks * KEY_VALUE_HEADS * packed * (keys + 256) * HEAD_SIZE,
                2 * keys * rows * HEAD_SIZE,
            ),
            name="attend",
        )(*fixed)

    state = ()
    for step in range(planes - 1):
        if step:
            next(sending)
        state = sending.send(tuple(attend(state, step)))
    next(sending)
    state = sending.send(tuple(attend(state, planes - 1)))
    return attend(state, planes)


def apply_rotary(rows, slot_offset, heads):
    block_count = rows.shape[0]
    half = HEAD_SIZE // 2
    frequency = 1000000.0 ** (-(jnp.arange(half, dtype=jnp.float32) * 2.0 / HEAD_SIZE))
    angle = slot_offset.astype(jnp.float32)[:, None] * frequency[None, :]
    cosine = jnp.cos(angle)[:, None, :]
    sine = jnp.sin(angle)[:, None, :]
    grid = rows.astype(jnp.float32).reshape(block_count, heads, HEAD_SIZE)
    first = grid[:, :, :half]
    second = grid[:, :, half:]
    turned = jnp.concatenate(
        [first * cosine - second * sine, second * cosine + first * sine], axis=2
    )
    return turned.reshape(block_count, heads * HEAD_SIZE).astype(jnp.bfloat16)


def causal_block_attention(pieces):
    query_tile_rows, key_tile_rows, value_tile_rows, spot_block = pieces
    block_count = query_tile_rows.shape[0]
    head_groups = QUERY_HEADS // KEY_VALUE_HEADS
    query_block_grid = query_tile_rows.reshape(block_count, KEY_VALUE_HEADS, head_groups, HEAD_SIZE)
    key_block_grid = key_tile_rows.reshape(block_count, KEY_VALUE_HEADS, HEAD_SIZE)
    value_block_grid = value_tile_rows.reshape(block_count, KEY_VALUE_HEADS, HEAD_SIZE)
    scores = jnp.einsum(
        "qhgd,khd->hgqk", query_block_grid, key_block_grid, preferred_element_type=jnp.float32
    ) / math.sqrt(HEAD_SIZE)
    inner = jnp.arange(block_count, dtype=jnp.int32)
    visible = (inner[None, :] <= inner[:, None]) & (
        inner[None, :] >= inner[:, None] - spot_block[:, None]
    )
    scores = jnp.where(visible, scores, -jnp.inf)
    top = jnp.max(scores, axis=3, keepdims=True)
    weights = jnp.exp(scores - top)
    totals = jnp.sum(weights, axis=3)
    probs = weights.astype(jnp.bfloat16)
    mixed = jnp.einsum(
        "hgqk,khd->qhgd", probs, value_block_grid, preferred_element_type=jnp.float32
    )
    mixed = mixed / jnp.transpose(totals, (2, 0, 1))[:, :, :, None]
    return mixed.reshape(block_count, QUERY_HEADS * HEAD_SIZE).astype(jnp.bfloat16)


def add_projection(left, pieces):
    return (
        jnp.dot(left, pieces[0], preferred_element_type=jnp.float32),
        jnp.dot(left, pieces[1], preferred_element_type=jnp.float32),
    )


def project_own(hidden, key_matrix, value_matrix, key_projection_bias, value_projection_bias):
    totals = add_projection(
        hidden,
        (
            lax.all_gather(key_matrix, "dp", axis=0, tiled=True),
            lax.all_gather(value_matrix, "dp", axis=0, tiled=True),
        ),
    )
    key_rows = (totals[0] + key_projection_bias.astype(jnp.float32)).astype(jnp.bfloat16)
    value_rows = (totals[1] + value_projection_bias.astype(jnp.float32)).astype(jnp.bfloat16)
    return jnp.concatenate([key_rows, value_rows], axis=1)


def send_plan(
    hidden,
    queries,
    route,
    positions,
    key_matrix,
    value_matrix,
    key_projection_bias,
    value_projection_bias,
):
    ranks = lax.axis_size("dp")
    rows = hidden.shape[0]
    slots = positions.shape[0]
    spare = rows // ranks + 2
    width = ranks * spare
    paired_width = key_matrix.shape[1]
    target = route // slots
    place = route - target * slots
    member = (target[:, None] == jnp.arange(ranks, dtype=jnp.int32)[None, :]).astype(jnp.int32)
    order = jnp.sum(jnp.cumsum(member, axis=0) * member, axis=1) - 1
    bucket = target * spare + order
    outgoing = jnp.full((width,), slots, jnp.int32).at[bucket].set(place)
    arrived = lax.all_to_all(
        outgoing.reshape(ranks, spare), "dp", split_axis=0, concat_axis=0, tiled=True
    ).reshape(width)
    query_buf = jnp.zeros((width, queries.shape[1]), jnp.bfloat16).at[bucket].set(queries)
    own_pairs = project_own(
        hidden, key_matrix, value_matrix, key_projection_bias, value_projection_bias
    )
    pair_buf = jnp.zeros((width, 2 * paired_width), jnp.bfloat16).at[bucket].set(own_pairs)
    got_query, got_pairs = (
        lax.all_to_all(
            query_buf.reshape(ranks, spare, -1), "dp", split_axis=0, concat_axis=0, tiled=True
        ),
        lax.all_to_all(
            pair_buf.reshape(ranks, spare, -1), "dp", split_axis=0, concat_axis=0, tiled=True
        ),
    )
    got_query = got_query.reshape(width, -1)
    got_pairs = got_pairs.reshape(width, -1)
    query_slot_rows = (
        jnp.zeros((slots, got_query.shape[1]), jnp.bfloat16).at[arrived].set(got_query, mode="drop")
    )
    paired_slot_rows = (
        jnp.zeros((slots, 2 * paired_width), jnp.bfloat16).at[arrived].set(got_pairs, mode="drop")
    )
    query_turned = apply_rotary(query_slot_rows, positions, QUERY_HEADS)
    key_rotated = apply_rotary(paired_slot_rows[:, :paired_width], positions, KEY_VALUE_HEADS)
    block_list = slots // BLOCK_SLOTS
    attended = lax.map(
        causal_block_attention,
        (
            query_turned.reshape(block_list, BLOCK_SLOTS, -1),
            key_rotated.reshape(block_list, BLOCK_SLOTS, -1),
            paired_slot_rows[:, paired_width:].reshape(block_list, BLOCK_SLOTS, -1),
            positions.reshape(block_list, BLOCK_SLOTS),
        ),
    )
    attended = attended.reshape(slots, -1)
    leaving = attended[jnp.minimum(arrived, slots - 1)]
    returned = lax.all_to_all(
        leaving.reshape(ranks, spare, -1), "dp", split_axis=0, concat_axis=0, tiled=True
    ).reshape(width, -1)
    return returned[bucket]


def local(*args):
    hidden, queries, _, positions, key_matrix = args[:5]
    ranks = lax.axis_size("dp")
    rows = hidden.shape[0]
    gathered = ranks * ranks * (rows // ranks + 2) * 4 * key_matrix.shape[1]
    chip_rows = 2 * key_matrix.shape[0]
    fits = rows % (16 * ranks) == 0 and chip_rows % HEAD_SIZE == 0 and gathered <= GATHER_LIMIT
    if ranks == PLANES * PLANE and fits:
        return gather_plan(*args)
    return send_plan(*args)


def solution(mesh):
    placed = (
        P(("groups", "dp"), None),
        P(("groups", "dp"), None),
        P(("groups", "dp")),
        P(("groups", "dp")),
        P("dp", None),
        P("dp", None),
        P(),
        P(),
    )
    return jax.shard_map(
        local, mesh=mesh, in_specs=placed, out_specs=P(("groups", "dp"), None), check_vma=False
    )
```

```python
import functools
import math

import jax
import jax.numpy as jnp
import numpy as np
from jax import lax
from jax.experimental import pallas as pl
from jax.experimental.pallas import tpu as pltpu
from jax.sharding import PartitionSpec as P

QUERY_HEADS = 20
KEY_VALUE_HEADS = 4
HEAD_SIZE = 128
BLOCK_SLOTS = 512
HEAD_GROUPS = QUERY_HEADS // KEY_VALUE_HEADS
CHUNKS = ((0, KEY_VALUE_HEADS),)
PLANE = 4
PLANES = 4
SAFE_POWER = 64.0
GATHER_LIMIT = 40 * 2**20
MASKED = -1e30
VMEM = pl.BlockSpec(memory_space=pltpu.VMEM)
SMEM = pl.BlockSpec(memory_space=pltpu.SMEM)
HBM = pl.BlockSpec(memory_space=pltpu.HBM)


def grant(mebibytes):
    return pltpu.CompilerParams(vmem_limit_bytes=mebibytes * 2**20)


def cost(flops, moved):
    return pl.CostEstimate(flops=flops, bytes_accessed=moved, transcendentals=0)


def one_hot_rows(count, index_row):
    rows = lax.broadcasted_iota(jnp.int32, (count, index_row.shape[1]), 0)
    return (rows == index_row).astype(jnp.float32).astype(jnp.bfloat16)


def split(number):
    high = lax.shift_right_logical(number, HEAD_SIZE.bit_length() - 1)
    return high, number - high * HEAD_SIZE


def contract(left, right, left_dim, right_dim):
    return lax.dot_general(
        left, right, (((left_dim,), (right_dim,)), ((), ())), preferred_element_type=jnp.float32
    )


def turn(rows, cosine, sine):
    return (rows * cosine + pltpu.roll(rows, HEAD_SIZE // 2, 1) * sine).astype(jnp.bfloat16)


def join_kernel(left_ref, right_ref, out_ref, done):
    wide = left_ref.shape[1]
    copies = [
        pltpu.make_async_copy(ref, out_ref.at[:, pl.ds(at * wide, wide)], done.at[at])
        for at, ref in enumerate((left_ref, right_ref))
    ]
    for copy in copies:
        copy.start()
    for copy in copies:
        copy.wait()


def order_kernel(
    ranks, slots, extra, stride, route_ref, bucket_ref, seat_ref, sorted_ref, more_ref
):
    route = route_ref[...]
    count = route.shape[1]
    share = count // ranks
    target = lax.div(route, slots)
    member = (lax.broadcasted_iota(jnp.int32, (ranks, count), 0) == target).astype(jnp.float32)
    before = lax.broadcasted_iota(jnp.int32, (count, count), 0) < lax.broadcasted_iota(
        jnp.int32, (count, count), 1
    )
    before = before.astype(jnp.float32).astype(jnp.bfloat16)
    ahead = contract(member.astype(jnp.bfloat16), before, 1, 0)
    order = jnp.sum(member * ahead, axis=0, keepdims=True).astype(jnp.int32)
    beyond = order >= share
    beyond_rows = jnp.broadcast_to(beyond.astype(jnp.float32), (8, count)).astype(jnp.bfloat16)
    number = contract(beyond_rows, before, 1, 0)[0:1]
    counts = jnp.sum(member, axis=1, keepdims=True)
    free = jnp.maximum(share - counts, 0.0)
    group = lax.broadcasted_iota(jnp.int32, (ranks, ranks), 0)
    lower = (group > lax.broadcasted_iota(jnp.int32, (ranks, ranks), 1)).astype(jnp.float32)
    free_rows = jnp.broadcast_to(free, (ranks, HEAD_SIZE)).astype(jnp.bfloat16)
    free_before = contract(lower.astype(jnp.bfloat16), free_rows, 1, 0)[:, 0:1]
    inside = (number >= free_before) & (number < free_before + free)
    base = lax.broadcasted_iota(jnp.int32, (ranks, 1), 0).astype(jnp.float32) * share + counts
    hole = jnp.sum(jnp.where(inside, base + number - free_before, 0.0), axis=0, keepdims=True)
    bucket = jnp.where(beyond, hole.astype(jnp.int32), target * share + order)
    bucket_ref[...] = bucket
    seat_ref[...] = target * stride + order
    high, low = split(route)
    place_high, place_low = split(bucket)
    line = lax.broadcasted_iota(jnp.int32, (8, count), 0)
    digits = jnp.where(line == 0, high, 0)
    digits = jnp.where(line == 1, low, digits)
    digits = jnp.where(line == 2, place_high, digits)
    digits = jnp.where(line == 3, place_low, digits)
    digits = jnp.where(line == 4, 1, digits).astype(jnp.float32).astype(jnp.bfloat16)
    placed = contract(digits, one_hot_rows(count, bucket), 1, 1)
    sorted_ref[...] = (placed[0:1] * HEAD_SIZE + placed[1:2]).astype(jnp.int32)
    listed = jnp.where(beyond, target * extra + order - share, -1)
    found = contract(digits, one_hot_rows(ranks * extra, listed), 1, 1)
    none = found[4:5] - 1.0
    more_ref[0:1] = (found[0:1] * HEAD_SIZE + found[1:2] + none).astype(jnp.int32)
    more_ref[1:2] = (found[2:3] * HEAD_SIZE + found[3:4] + none).astype(jnp.int32)


def query_kernel(
    ranks, row_step, stride, packed, route_ref, seat_ref, positions_ref, frequency_ref, queries_ref, *refs
):
    turned_ref, bounds_ref, cosine_ref, sine_ref, rows_ref = refs
    route = route_ref[...]
    count = route.shape[0]
    lines = positions_ref.shape[0]
    line, lane = split(route)
    pick = (lax.broadcasted_iota(jnp.int32, (count, lines), 1) == line).astype(jnp.float32)
    pick = pick.astype(jnp.bfloat16)
    positions = positions_ref[...]
    half = lax.shift_right_logical(positions, 1)
    rest = positions - half * 2
    rows = 2.0 * contract(pick, half.astype(jnp.float32).astype(jnp.bfloat16), 1, 0) + contract(
        pick, rest.astype(jnp.float32).astype(jnp.bfloat16), 1, 0
    )
    lanes = lax.broadcasted_iota(jnp.int32, (count, HEAD_SIZE), 1)
    spot = jnp.sum(jnp.where(lanes == lane, rows, 0.0), axis=1, keepdims=True)
    angle = spot * frequency_ref[...]
    cosine = jnp.cos(angle)
    sine = jnp.sin(angle)
    sine = jnp.where(lanes < HEAD_SIZE // 2, -sine, sine)
    cosine_ref[...] = cosine
    sine_ref[...] = sine
    seats = one_hot_rows(ranks * stride, seat_ref[...])
    first = route - spot.astype(jnp.int32)
    first_line, first_lane = split(first)
    digits = jnp.where(lanes == 0, line, 0)
    digits = jnp.where(lanes == 1, lane, digits)
    digits = jnp.where(lanes == 2, first_line, digits)
    digits = jnp.where(lanes == 3, first_lane, digits)
    digits = jnp.where(lanes == 4, 1, digits)
    placed = contract(seats, digits.astype(jnp.float32).astype(jnp.bfloat16), 1, 0)
    live = placed[:, 4:5] - 1.0
    last = placed[:, 0:1] * HEAD_SIZE + placed[:, 1:2] + live
    start = placed[:, 2:3] * HEAD_SIZE + placed[:, 3:4] - live * 2.0**20
    seat_lanes = lax.broadcasted_iota(jnp.int32, placed.shape, 1)
    bounds_ref[...] = jnp.where(seat_lanes == 0, last, start).astype(jnp.int32)
    rows_ref[...] = jnp.zeros(rows_ref.shape, jnp.float32)
    for head in range(KEY_VALUE_HEADS):
        for place in range(HEAD_GROUPS):
            at = (head * HEAD_GROUPS + place) * HEAD_SIZE
            one = queries_ref[:, at : at + HEAD_SIZE].astype(jnp.float32)
            rows = contract(seats, turn(one, cosine, sine), 1, 0)
            for group in range(ranks):
                at = group * packed + place * row_step
                rows_ref[at : at + row_step] = rows[group * stride : group * stride + row_step]
        turned_ref[head] = rows_ref[...].astype(jnp.bfloat16)


def add_products(chips, owners_ref, hidden_ref, refs, columns, matrix, done):
    shard = matrix.shape[1] // 2
    copies, at, taken = [], 0, 0
    for place, chip in enumerate(chips):
        first = pl.multiple_of(lax.div(owners_ref[chip[0][0]], 2) * (2 * shard), HEAD_SIZE)
        copies.append(
            (hidden_ref.at[:, pl.ds(first, 2 * shard)], columns.at[place])
        )
        for source, row in chip:
            core = lax.rem(owners_ref[source], 2)
            rows = pl.ds(pl.multiple_of(core * shard + row, 16), refs[taken].shape[0])
            copies.append((refs[taken], matrix.at[place, rows]))
            taken += 1
    copies = [pltpu.make_async_copy(*pair, done.at[at]) for at, pair in enumerate(copies)]
    for copy in copies:
        copy.start()

    def product(span):
        total = contract(columns[0], matrix[0, :, span], 1, 0)
        for place in range(1, len(chips)):
            total = total + contract(columns[place], matrix[place, :, span], 1, 0)
        return total

    return copies, product


def part_kernel(chips, more, owners_ref, hidden_ref, *refs):
    count = sum(len(chip) for chip in chips)
    parts, refs = refs[:count], refs[count:]
    if more:
        total_ref, refs = refs[0], refs[1:]
    out_ref, columns, matrix, done = refs
    copies, product = add_products(chips, owners_ref, hidden_ref, parts, columns, matrix, done)
    for copy in copies:
        copy.wait()
    for first in range(0, out_ref.shape[1], 2 * HEAD_SIZE):
        span = slice(first, first + 2 * HEAD_SIZE)
        if more:
            out_ref[:, span] = total_ref[:, span] + product(span)
        else:
            out_ref[:, span] = product(span)


def finish_kernel(
    chips, owners_ref, hidden_ref, bias_ref, cosine_ref, sine_ref, bucket_ref, *refs
):
    count = sum(len(chip) for chip in chips)
    parts, total_ref = refs[:count], refs[count]
    outs, (columns, matrix, done) = refs[count + 1 : -3], refs[-3:]
    copies, product = add_products(chips, owners_ref, hidden_ref, parts, columns, matrix, done)
    places = one_hot_rows(outs[0].shape[0], bucket_ref[...])
    for copy in copies:
        copy.wait()
    wide = KEY_VALUE_HEADS * HEAD_SIZE
    for first in range(0, 2 * wide, 2 * HEAD_SIZE):
        span = slice(first, first + 2 * HEAD_SIZE)
        rows = (total_ref[:, span] + product(span) + bias_ref[:, span]).astype(jnp.bfloat16)
        if first < wide:
            cosine, sine = cosine_ref[...], sine_ref[...]
            halves = [
                turn(rows[:, at : at + HEAD_SIZE].astype(jnp.float32), cosine, sine)
                for at in (0, HEAD_SIZE)
            ]
            rows = jnp.concatenate(halves, axis=1)
        rows = contract(places, rows, 1, 0).astype(jnp.bfloat16)
        for half in range(2):
            head = first % wide // HEAD_SIZE + half
            for (first_head, heads), out_ref in zip(CHUNKS, outs):
                if first_head <= head < first_head + heads:
                    at = (head - first_head + first // wide * heads) * HEAD_SIZE
                    out_ref[:, at : at + HEAD_SIZE] = rows[
                        :, half * HEAD_SIZE : (half + 1) * HEAD_SIZE
                    ]


def veil_kernel(sets, stride, bounds_ref, routes_ref, more_ref, *veil_refs):
    rest = jnp.zeros((HEAD_SIZE - stride, more_ref.shape[1]), jnp.float32)
    share = routes_ref.shape[2] // routes_ref.shape[0]

    def one_group(group, carry):
        seats = pl.ds(pl.multiple_of(group * stride, 16), stride)
        last, start = bounds_ref[seats, 0:1], bounds_ref[seats, 1:2]
        both = []
        for routes in (routes_ref[group], more_ref[...]):
            veil = jnp.where((routes <= last) & (routes >= start), 0.0, MASKED)
            veil = jnp.transpose(jnp.concatenate([veil, rest], axis=0))
            both.append(veil.astype(jnp.bfloat16))
        first = 0
        for sources, veil_ref in zip(sets, veil_refs):
            end = first + len(sources) * share
            veil_ref[group] = jnp.concatenate([veil[first:end] for veil in both], axis=0)
            first = end
        return carry

    lax.fori_loop(0, routes_ref.shape[0], one_group, 0)


def attend_kernel(starts, before, spare, row_step, stride, more, last, *refs):
    more_ref, queries_ref, veil_ref = refs[:3]
    refs = refs[3:]
    blocks = []
    for first_rows in starts:
        blocks.append(dict(zip(first_rows, refs)))
        refs = refs[len(first_rows) :]
    if more:
        top_ref, sum_ref, total_ref = refs[:3]
        refs = refs[3:]
    if last:
        seat_ref, out_ref, mixed_ref, result_ref, leave = refs[0], refs[1], *refs[-3:]
        refs = refs[:-3]
        mixed_ref[...] = jnp.zeros(mixed_ref.shape, jnp.bfloat16)
    else:
        new_top_ref, new_sum_ref, new_total_ref = refs[:3]
    listed_rows, seen_by, veil, veil_in = refs[-4:]
    fetch_veil = pltpu.make_async_copy(veil_ref, veil, veil_in)
    fetch_veil.start()
    heads, ranks = queries_ref.shape[0], veil_ref.shape[0]
    packed = queries_ref.shape[1] // ranks
    wide = heads * HEAD_SIZE
    share = listed_rows.shape[0] // len(starts)
    count = share * ranks

    token = lax.broadcasted_iota(jnp.int32, (packed, HEAD_SIZE), 0)
    lane = lax.broadcasted_iota(jnp.int32, (packed, HEAD_SIZE), 1)
    own = lane < 0
    for at in range(HEAD_GROUPS):
        own = own | ((token == lane + at * row_step) & (lane < spare))
    seen_by[...] = own.astype(jnp.float32).astype(jnp.bfloat16)
    lines = lax.broadcasted_iota(jnp.int32, (share, count), 1)
    for at, block in enumerate(blocks):
        places = more_ref[(before + at) * share : (before + at + 1) * share]
        pick = (lines == places).astype(jnp.float32).astype(jnp.bfloat16)
        for first in range(0, 2 * wide, 2 * HEAD_SIZE):
            lanes = slice(first, first + 2 * HEAD_SIZE)
            found = [
                contract(pick[:, row : row + ref.shape[0]], ref[:, lanes], 1, 0)
                for row, ref in block.items()
            ]
            listed_rows[at * share : (at + 1) * share, lanes] = sum(found).astype(jnp.bfloat16)
    fetch_veil.wait()
    scale = math.log2(math.e) / math.sqrt(HEAD_SIZE)

    def rows_of(group, row, first):
        lanes = slice(first, first + HEAD_SIZE)
        window = pl.ds(pl.multiple_of(group * share - row, 16), share)
        rows = [block[row][window, lanes] for block in blocks]
        return jnp.concatenate(rows + [listed_rows[:, lanes]], axis=0)

    def scores_of(group, row, head, tokens):
        left = jnp.concatenate([queries_ref[head, tokens], seen_by[...]], axis=1)
        keys = rows_of(group, row, head * HEAD_SIZE)
        return contract(left, jnp.concatenate([keys, veil[group]], axis=1), 1, 1)

    def products_of(group, row, head, weight):
        values = rows_of(group, row, wide + head * HEAD_SIZE)
        values = jnp.concatenate([values, jnp.ones_like(values)], axis=1)
        mixed = contract(weight, values, 1, 0)
        return mixed[:, :HEAD_SIZE], mixed[:, HEAD_SIZE:]

    def tile(top, keys):
        return jnp.concatenate([top] * (keys // HEAD_SIZE), axis=1)

    def finish_head(group, head, total, weight_sum):
        mixed = total / weight_sum
        seats = pl.ds(pl.multiple_of(group * stride, 16), row_step)
        for at in range(HEAD_GROUPS):
            place = (head * HEAD_GROUPS + at) * HEAD_SIZE
            rows = mixed[at * row_step : (at + 1) * row_step]
            mixed_ref[seats, place : place + HEAD_SIZE] = rows.astype(jnp.bfloat16)

    def add_heads(group, row, some):
        tokens = pl.ds(pl.multiple_of(group * packed, 16), packed)
        scores = [scores_of(group, row, head, tokens) for head in some]
        tops, weights = [], []
        for head, score in zip(some, scores):
            top = jnp.max(score, axis=1, keepdims=True)
            if more:
                top = jnp.maximum(top_ref[head, tokens], top)
            else:
                top = jnp.broadcast_to(top, (packed, HEAD_SIZE))
            tops.append(top)
            weight = jnp.exp2((score - tile(top, score.shape[1])) * scale)
            weights.append(weight.astype(jnp.bfloat16))
        for head, top, weight in zip(some, tops, weights):
            total, weight_sum = products_of(group, row, head, weight)
            if more:
                fade = jnp.exp2((top_ref[head, tokens] - top) * scale)
                total = total + fade * total_ref[head, tokens]
                weight_sum = weight_sum + fade * sum_ref[head, tokens]
            if last:
                finish_head(group, head, total, weight_sum)
            else:
                new_top_ref[head, tokens] = top
                new_sum_ref[head, tokens] = weight_sum
                new_total_ref[head, tokens] = total

    def add_heads_as_before(group, row, worst):
        tokens = pl.ds(pl.multiple_of(group * packed, 16), packed)
        scores = [scores_of(group, row, head, tokens) for head in range(heads)]
        weights = []
        for head, score in enumerate(scores):
            above = score - tile(top_ref[head, tokens], score.shape[1])
            for first in range(0, score.shape[1], HEAD_SIZE):
                part = above[:, first : first + HEAD_SIZE].reshape(packed // 8, 8, HEAD_SIZE)
                worst = jnp.maximum(worst, jnp.max(part, axis=0))
            weights.append(jnp.exp2(above * scale).astype(jnp.bfloat16))
        for head, weight in enumerate(weights):
            total, weight_sum = products_of(group, row, head, weight)
            total = total + total_ref[head, tokens]
            weight_sum = weight_sum + sum_ref[head, tokens]
            finish_head(group, head, total, weight_sum)
        return worst

    firsts = sorted({row for first_rows in starts for row in first_rows})
    spans = [
        (row, row // share, end // share) for row, end in zip(firsts, firsts[1:] + [count])
    ]

    def add_all(together):
        for row, first, end in spans:

            def one_group(group, carry, row=row):
                for head in range(0, heads, together):
                    add_heads(group, row, range(head, head + together))
                return carry

            lax.fori_loop(first, end, one_group, 0)

    if not last:
        add_all(2 if more else 4)
        return
    worst = jnp.full((8, HEAD_SIZE), MASKED, jnp.float32)
    for row, first, end in spans:
        worst = lax.fori_loop(
            first,
            end,
            lambda group, worst, row=row: add_heads_as_before(group, row, worst),
            worst,
        )

    @pl.when(jnp.max(worst) * scale > SAFE_POWER)
    def _():
        add_all(2)

    seat_lanes = lax.broadcasted_iota(jnp.int32, (count, mixed_ref.shape[0]), 1)
    seats = (seat_lanes == seat_ref[...]).astype(jnp.float32).astype(jnp.bfloat16)
    span = HEAD_GROUPS * HEAD_SIZE
    leaving = []
    for head in range(heads):
        lanes = slice(head * span, (head + 1) * span)
        rows = contract(seats, mixed_ref[:, lanes], 1, 0)
        result_ref[:, lanes] = rows.astype(jnp.bfloat16)
        lanes = pl.ds(head * span, span)
        leaving.append(
            pltpu.make_async_copy(result_ref.at[:, lanes], out_ref.at[:, lanes], leave.at[head])
        )
        leaving[-1].start()
    for one in leaving:
        one.wait()


def spread(block, ranks, held):
    ring = [(rank, (rank + PLANE) % ranks) for rank in range(ranks)]
    across = [(rank, rank ^ 2) for rank in range(ranks)]
    beside = [(rank, rank ^ 1) for rank in range(ranks)]
    steps = ranks // PLANE
    half = block.shape[0] // 32 * 16

    def keep(source, first, array):
        held.setdefault(source, []).append((first, array))
        held.setdefault(source + 2 * steps, []).append((first, lax.ppermute(array, "dp", beside)))

    lane, other = block, None
    for step in range(steps - 1):
        following = lax.ppermute(lane, "dp", ring), lax.ppermute(lane, "dp", across)
        keep(step, 0, lane)
        if step:
            keep(steps + step - 1, 0, other)
        extra = yield
        lane, other, extra = lax.optimization_barrier((*following, extra))
        yield extra
    over = lax.ppermute(lane[:half], "dp", across)
    around = lax.ppermute(other[half:], "dp", ring)
    keep(steps - 1, 0, lane)
    keep(2 * steps - 2, 0, other)
    extra = yield other
    over, around, extra = lax.optimization_barrier((over, around, extra))
    keep(2 * steps - 1, 0, over)
    keep(2 * steps - 1, half, around)
    yield extra


def source_order(ranks, sources):
    me = lax.axis_index("dp")
    lane, plane = lax.rem(me, PLANE), lax.div(me, PLANE)
    planes = ranks // PLANE
    steps = np.array([source % planes for source in sources], np.int32)
    flips = np.array([(0, 2, 1, 3)[source // planes] for source in sources], np.int32)
    return lax.rem(plane + (planes - steps), planes) * PLANE + (lane ^ flips)


def weight_order(ranks):
    me = lax.axis_index("dp")
    lane, plane = lax.rem(me, PLANE), lax.div(me, PLANE)
    planes = ranks // PLANE
    turn_back = lax.axis_index("groups") == 1
    up = np.array([0, 1, 0, planes - 1, 2, 1, 2, planes - 1] * 2, np.int32)
    steps = jnp.where(turn_back, (planes - up) % planes, up)
    flips = np.array([0, 0, 2, 0, 0, 2, 2, 2], np.int32)
    flips = np.concatenate([flips, flips ^ 1])
    return lax.rem(plane + (planes - steps), planes) * PLANE + (lane ^ flips)


def gather_plan(
    hidden,
    queries,
    route,
    positions,
    key_matrix,
    value_matrix,
    key_projection_bias,
    value_projection_bias,
):
    ranks = lax.axis_size("dp")
    rows = hidden.shape[0]
    slots = positions.shape[0]
    share, extra = rows // ranks, 2
    spare = share + extra
    listed = ranks * extra
    stride = -(-spare // 16) * 16
    row_step = -(-spare // 8) * 8
    packed = -(-HEAD_GROUPS * row_step // 16) * 16
    query_width = queries.shape[1]
    shape = jax.ShapeDtypeStruct

    def columns(array, chunk):
        first, heads = chunk
        return array[..., first * HEAD_SIZE : (first + heads) * HEAD_SIZE]

    joined = pl.pallas_call(
        join_kernel,
        out_shape=shape((key_matrix.shape[0], 2 * key_matrix.shape[1]), jnp.bfloat16),
        in_specs=[HBM] * 2,
        out_specs=VMEM,
        scratch_shapes=[pltpu.SemaphoreType.DMA((2,))],
        compiler_params=grant(14),
        name="join",
    )(key_matrix, value_matrix)
    every = [(group, rank) for group in range(2) for rank in range(ranks)]
    ring = [
        (group * ranks + rank, group * ranks + (rank + (1 - 2 * group) * PLANE) % ranks)
        for group, rank in every
    ]
    across = [(group * ranks + rank, group * ranks + (rank ^ 2)) for group, rank in every]
    beside = [(group * ranks + rank, group * ranks + (rank ^ 1)) for group, rank in every]
    swap = [(group * ranks + rank, (1 - group) * ranks + rank) for group, rank in every]

    def send(array, pairs):
        return lax.ppermute(array, ("groups", "dp"), pairs)

    near_lane, other_row = send(joined, ring), send(joined, across)
    matrices = {0: (joined, send(joined, beside))}
    bucket, seat, sorted_route, more = pl.pallas_call(
        functools.partial(order_kernel, ranks, slots, extra, stride),
        out_shape=(
            shape((1, rows), jnp.int32),
            shape((1, rows), jnp.int32),
            shape((1, rows), jnp.int32),
            shape((2, listed), jnp.int32),
        ),
        in_specs=[VMEM],
        out_specs=(VMEM,) * 4,
        compiler_params=grant(14),
        name="order",
    )(route.reshape(1, rows))
    width = rows + 2 * listed
    plan = jnp.concatenate([sorted_route.reshape(rows), more.reshape(2 * listed), positions])
    plan = lax.all_to_all(
        jnp.broadcast_to(plan, (ranks, width + slots)), "dp", split_axis=0, concat_axis=0, tiled=True
    )
    near_lane, other_row, plan, bucket, seat = lax.optimization_barrier(
        (near_lane, other_row, plan, bucket, seat)
    )
    far_lane, next_lane = send(near_lane, swap), send(near_lane, ring)
    near_other = send(near_lane, across)
    matrices[1] = (near_lane, send(near_lane, beside))
    matrices[2] = (other_row, send(other_row, beside))
    all_positions = plan[:, width:].reshape(-1, HEAD_SIZE)
    planes = ranks // PLANE
    sets = [(0, 2 * planes)] + [
        (step, step + 2 * planes, step + planes - 1, step + 3 * planes - 1)
        for step in range(1, planes)
    ]
    sets.append((2 * planes - 1, 4 * planes - 1))
    owners = weight_order(ranks)

    half = HEAD_SIZE // 2
    frequency = 1000000.0 ** (-(jnp.arange(half, dtype=jnp.float32) * 2.0 / HEAD_SIZE))
    turned, bounds, cosine, sine = pl.pallas_call(
        functools.partial(query_kernel, ranks, row_step, stride, packed),
        out_shape=(
            shape((KEY_VALUE_HEADS, ranks * packed, HEAD_SIZE), jnp.bfloat16),
            shape((ranks * stride, HEAD_SIZE), jnp.int32),
            shape((rows, HEAD_SIZE), jnp.float32),
            shape((rows, HEAD_SIZE), jnp.float32),
        ),
        in_specs=[VMEM] * 5,
        out_specs=(VMEM,) * 4,
        scratch_shapes=[pltpu.VMEM((ranks * packed, HEAD_SIZE), jnp.float32)],
        compiler_params=grant(14),
        cost_estimate=cost(4 * stride * ranks * rows * query_width, 4 * rows * query_width),
        name="turn_queries",
    )(
        route.reshape(rows, 1),
        seat,
        all_positions,
        jnp.concatenate([frequency, frequency]).reshape(1, HEAD_SIZE),
        queries,
    )

    shard, wide = key_matrix.shape[0], 2 * key_matrix.shape[1]

    def chip_parts(sources):
        chips = [((source, 0), (source + ranks // 2, 0)) for source in sources]
        return chips, [array for source in sources for array in matrices[source]]

    def scratch(chips, arrays):
        return [
            pltpu.VMEM((len(chips), rows, 2 * shard), jnp.bfloat16),
            pltpu.VMEM((len(chips), 2 * shard, wide), jnp.bfloat16),
            pltpu.SemaphoreType.DMA((len(chips) + len(arrays),)),
        ]

    def product_cost(chips):
        depth = 2 * shard * len(chips)
        return cost(2 * rows * depth * wide, 2 * depth * (rows + wide) + 8 * rows * wide)

    def add_part(total, sources):
        chips, arrays = chip_parts(sources)
        more = [] if total is None else [total]
        return pl.pallas_call(
            functools.partial(part_kernel, chips, bool(more)),
            out_shape=shape((rows, wide), jnp.float32),
            in_specs=[SMEM] + [HBM] * (1 + len(arrays)) + [VMEM] * len(more),
            out_specs=VMEM,
            scratch_shapes=scratch(chips, arrays),
            compiler_params=grant(14),
            cost_estimate=product_cost(chips),
            name="add_part",
        )(owners, hidden, *arrays, *more)

    far_lane, next_lane, near_other, turned, bounds, cosine, sine = lax.optimization_barrier(
        (far_lane, next_lane, near_other, turned, bounds, cosine, sine)
    )
    next_other, far_other = send(next_lane, across), send(near_other, swap)
    matrices[3] = (far_lane, send(far_lane, beside))
    matrices[4] = (next_lane, send(next_lane, beside))
    matrices[5] = (near_other, send(near_other, beside))
    total = add_part(add_part(None, (0, 1, 2)), (3, 4, 5))
    next_other, far_other, total = lax.optimization_barrier((next_other, far_other, total))
    matrices[6] = (next_other, send(next_other, beside))
    matrices[7] = (far_other, send(far_other, beside))
    chips, arrays = chip_parts((6, 7))
    bias = jnp.concatenate([key_projection_bias, value_projection_bias])
    (pairs,) = pl.pallas_call(
        functools.partial(finish_kernel, chips),
        out_shape=tuple(
            shape((rows, 2 * heads * HEAD_SIZE), jnp.bfloat16) for _, heads in CHUNKS
        ),
        in_specs=[SMEM, HBM] + [VMEM] * 4 + [HBM] * len(arrays) + [VMEM],
        out_specs=(VMEM,) * len(CHUNKS),
        scratch_shapes=scratch(chips, arrays),
        compiler_params=grant(14),
        cost_estimate=product_cost(chips),
        name="finish",
    )(
        owners,
        hidden,
        bias.astype(jnp.float32).reshape(1, wide),
        cosine,
        sine,
        bucket,
        *arrays,
        total,
    )

    blocks = {}
    sending = spread(pairs, ranks, blocks)
    next(sending)
    order = [source for sources in sets for source in sources]
    ordered = plan[:, :width][source_order(ranks, order)]
    key_routes = ordered[:, :rows].reshape(ranks, ranks, share).transpose(1, 0, 2)
    more_places = ordered[:, rows + listed :].reshape(ranks * listed, 1)
    veils = pl.pallas_call(
        functools.partial(veil_kernel, sets, stride),
        out_shape=tuple(
            shape((ranks, 2 * share * len(sources), HEAD_SIZE), jnp.bfloat16) for sources in sets
        ),
        in_specs=[VMEM] * 3,
        out_specs=(VMEM,) * len(sets),
        compiler_params=grant(14),
        cost_estimate=cost(3 * 10**9, 4 * ranks * rows * HEAD_SIZE),
        name="veil",
    )(
        bounds,
        key_routes.reshape(ranks, 1, rows),
        ordered[:, rows : rows + listed].reshape(1, ranks * listed),
    )

    def attend(state, index):
        sources, last = sets[index], index == len(sets) - 1
        starts = [tuple(first for first, _ in blocks[source]) for source in sources]
        arrays = [array for source in sources for _, array in blocks[source]]
        keys = 2 * share * len(sources)
        fixed = [more_places, turned, veils[index], *arrays, *state]
        kept = shape((KEY_VALUE_HEADS, ranks * packed, HEAD_SIZE), jnp.float32)
        outs = [kept] * 3
        out_specs = [VMEM] * 3
        in_specs = [VMEM, VMEM, HBM] + [VMEM] * (len(fixed) - 3)
        handed = {len(fixed) - 3 + at: at + last for at in range(3)} if state else {}
        scratch_shapes = [
            pltpu.VMEM((len(sources) * share, wide), jnp.bfloat16),
            pltpu.VMEM((packed, HEAD_SIZE), jnp.bfloat16),
            pltpu.VMEM((ranks, keys, HEAD_SIZE), jnp.bfloat16),
            pltpu.SemaphoreType.DMA,
        ]
        if last:
            fixed.append(seat.reshape(rows, 1))
            in_specs.append(VMEM)
            outs.insert(0, shape((rows, query_width), jnp.bfloat16))
            out_specs.insert(0, HBM)
            scratch_shapes += [
                pltpu.VMEM((ranks * stride, query_width), jnp.bfloat16),
                pltpu.VMEM((rows, query_width), jnp.bfloat16),
                pltpu.SemaphoreType.DMA((KEY_VALUE_HEADS,)),
            ]
        return pl.pallas_call(
            functools.partial(
                attend_kernel,
                starts,
                sum(len(one) for one in sets[:index]),
                spare,
                row_step,
                stride,
                bool(state),
                last,
            ),
            out_shape=tuple(outs),
            in_specs=in_specs,
            out_specs=tuple(out_specs),
            scratch_shapes=scratch_shapes,
            input_output_aliases=handed,
            compiler_params=grant(18 if last else 14),
            cost_estimate=cost(
                8 * ranks * KEY_VALUE_HEADS * packed * (keys + 256) * HEAD_SIZE,
                2 * keys * rows * HEAD_SIZE,
            ),
            name="attend",
        )(*fixed)

    state = ()
    for step in range(planes - 1):
        if step:
            next(sending)
        state = sending.send(tuple(attend(state, step)))
    next(sending)
    state = sending.send(tuple(attend(state, planes - 1)))
    return attend(state, planes)[0]


def apply_rotary(rows, slot_offset, heads):
    block_count = rows.shape[0]
    half = HEAD_SIZE // 2
    frequency = 1000000.0 ** (-(jnp.arange(half, dtype=jnp.float32) * 2.0 / HEAD_SIZE))
    angle = slot_offset.astype(jnp.float32)[:, None] * frequency[None, :]
    cosine = jnp.cos(angle)[:, None, :]
    sine = jnp.sin(angle)[:, None, :]
    grid = rows.astype(jnp.float32).reshape(block_count, heads, HEAD_SIZE)
    first = grid[:, :, :half]
    second = grid[:, :, half:]
    turned = jnp.concatenate(
        [first * cosine - second * sine, second * cosine + first * sine], axis=2
    )
    return turned.reshape(block_count, heads * HEAD_SIZE).astype(jnp.bfloat16)


def causal_block_attention(pieces):
    query_tile_rows, key_tile_rows, value_tile_rows, spot_block = pieces
    block_count = query_tile_rows.shape[0]
    head_groups = QUERY_HEADS // KEY_VALUE_HEADS
    query_block_grid = query_tile_rows.reshape(block_count, KEY_VALUE_HEADS, head_groups, HEAD_SIZE)
    key_block_grid = key_tile_rows.reshape(block_count, KEY_VALUE_HEADS, HEAD_SIZE)
    value_block_grid = value_tile_rows.reshape(block_count, KEY_VALUE_HEADS, HEAD_SIZE)
    scores = jnp.einsum(
        "qhgd,khd->hgqk", query_block_grid, key_block_grid, preferred_element_type=jnp.float32
    ) / math.sqrt(HEAD_SIZE)
    inner = jnp.arange(block_count, dtype=jnp.int32)
    visible = (inner[None, :] <= inner[:, None]) & (
        inner[None, :] >= inner[:, None] - spot_block[:, None]
    )
    scores = jnp.where(visible, scores, -jnp.inf)
    top = jnp.max(scores, axis=3, keepdims=True)
    weights = jnp.exp(scores - top)
    totals = jnp.sum(weights, axis=3)
    probs = weights.astype(jnp.bfloat16)
    mixed = jnp.einsum(
        "hgqk,khd->qhgd", probs, value_block_grid, preferred_element_type=jnp.float32
    )
    mixed = mixed / jnp.transpose(totals, (2, 0, 1))[:, :, :, None]
    return mixed.reshape(block_count, QUERY_HEADS * HEAD_SIZE).astype(jnp.bfloat16)


def add_projection(left, pieces):
    return (
        jnp.dot(left, pieces[0], preferred_element_type=jnp.float32),
        jnp.dot(left, pieces[1], preferred_element_type=jnp.float32),
    )


def project_own(hidden, key_matrix, value_matrix, key_projection_bias, value_projection_bias):
    totals = add_projection(
        hidden,
        (
            lax.all_gather(key_matrix, "dp", axis=0, tiled=True),
            lax.all_gather(value_matrix, "dp", axis=0, tiled=True),
        ),
    )
    key_rows = (totals[0] + key_projection_bias.astype(jnp.float32)).astype(jnp.bfloat16)
    value_rows = (totals[1] + value_projection_bias.astype(jnp.float32)).astype(jnp.bfloat16)
    return jnp.concatenate([key_rows, value_rows], axis=1)


def send_plan(
    hidden,
    queries,
    route,
    positions,
    key_matrix,
    value_matrix,
    key_projection_bias,
    value_projection_bias,
):
    ranks = lax.axis_size("dp")
    rows = hidden.shape[0]
    slots = positions.shape[0]
    spare = rows // ranks + 2
    width = ranks * spare
    paired_width = key_matrix.shape[1]
    target = route // slots
    place = route - target * slots
    member = (target[:, None] == jnp.arange(ranks, dtype=jnp.int32)[None, :]).astype(jnp.int32)
    order = jnp.sum(jnp.cumsum(member, axis=0) * member, axis=1) - 1
    bucket = target * spare + order
    outgoing = jnp.full((width,), slots, jnp.int32).at[bucket].set(place)
    arrived = lax.all_to_all(
        outgoing.reshape(ranks, spare), "dp", split_axis=0, concat_axis=0, tiled=True
    ).reshape(width)
    query_buf = jnp.zeros((width, queries.shape[1]), jnp.bfloat16).at[bucket].set(queries)
    own_pairs = project_own(
        hidden, key_matrix, value_matrix, key_projection_bias, value_projection_bias
    )
    pair_buf = jnp.zeros((width, 2 * paired_width), jnp.bfloat16).at[bucket].set(own_pairs)
    got_query, got_pairs = (
        lax.all_to_all(
            query_buf.reshape(ranks, spare, -1), "dp", split_axis=0, concat_axis=0, tiled=True
        ),
        lax.all_to_all(
            pair_buf.reshape(ranks, spare, -1), "dp", split_axis=0, concat_axis=0, tiled=True
        ),
    )
    got_query = got_query.reshape(width, -1)
    got_pairs = got_pairs.reshape(width, -1)
    query_slot_rows = (
        jnp.zeros((slots, got_query.shape[1]), jnp.bfloat16).at[arrived].set(got_query, mode="drop")
    )
    paired_slot_rows = (
        jnp.zeros((slots, 2 * paired_width), jnp.bfloat16).at[arrived].set(got_pairs, mode="drop")
    )
    query_turned = apply_rotary(query_slot_rows, positions, QUERY_HEADS)
    key_rotated = apply_rotary(paired_slot_rows[:, :paired_width], positions, KEY_VALUE_HEADS)
    block_list = slots // BLOCK_SLOTS
    attended = lax.map(
        causal_block_attention,
        (
            query_turned.reshape(block_list, BLOCK_SLOTS, -1),
            key_rotated.reshape(block_list, BLOCK_SLOTS, -1),
            paired_slot_rows[:, paired_width:].reshape(block_list, BLOCK_SLOTS, -1),
            positions.reshape(block_list, BLOCK_SLOTS),
        ),
    )
    attended = attended.reshape(slots, -1)
    leaving = attended[jnp.minimum(arrived, slots - 1)]
    returned = lax.all_to_all(
        leaving.reshape(ranks, spare, -1), "dp", split_axis=0, concat_axis=0, tiled=True
    ).reshape(width, -1)
    return returned[bucket]


def local(*args):
    hidden, queries, _, positions, key_matrix = args[:5]
    ranks = lax.axis_size("dp")
    rows = hidden.shape[0]
    gathered = ranks * ranks * (rows // ranks + 2) * 4 * key_matrix.shape[1]
    chip_rows = 2 * key_matrix.shape[0]
    fits = rows % (16 * ranks) == 0 and chip_rows % HEAD_SIZE == 0 and gathered <= GATHER_LIMIT
    if ranks == PLANES * PLANE and lax.axis_size("groups") == 2 and fits:
        return gather_plan(*args)
    return send_plan(*args)


def solution(mesh):
    placed = (
        P(("groups", "dp"), None),
        P(("groups", "dp"), None),
        P(("groups", "dp")),
        P(("groups", "dp")),
        P("dp", None),
        P("dp", None),
        P(),
        P(),
    )
    return jax.shard_map(
        local, mesh=mesh, in_specs=placed, out_specs=P(("groups", "dp"), None), check_vma=False
    )
```

```python
import functools
import math

import jax
import jax.numpy as jnp
import numpy as np
from jax import lax
from jax.experimental import pallas as pl
from jax.experimental.pallas import tpu as pltpu
from jax.sharding import PartitionSpec as P

QUERY_HEADS = 20
KEY_VALUE_HEADS = 4
HEAD_SIZE = 128
BLOCK_SLOTS = 512
HEAD_GROUPS = QUERY_HEADS // KEY_VALUE_HEADS
CHUNKS = ((0, KEY_VALUE_HEADS),)
PLANE = 4
PLANES = 4
SAFE_POWER = 64.0
GATHER_LIMIT = 40 * 2**20
MASKED = -1e30
VMEM = pl.BlockSpec(memory_space=pltpu.VMEM)
SMEM = pl.BlockSpec(memory_space=pltpu.SMEM)
HBM = pl.BlockSpec(memory_space=pltpu.HBM)


def grant(mebibytes):
    return pltpu.CompilerParams(vmem_limit_bytes=mebibytes * 2**20)


def cost(flops, moved):
    return pl.CostEstimate(flops=flops, bytes_accessed=moved, transcendentals=0)


def one_hot_rows(count, index_row):
    rows = lax.broadcasted_iota(jnp.int32, (count, index_row.shape[1]), 0)
    return (rows == index_row).astype(jnp.float32).astype(jnp.bfloat16)


def split(number):
    high = lax.shift_right_logical(number, HEAD_SIZE.bit_length() - 1)
    return high, number - high * HEAD_SIZE


def contract(left, right, left_dim, right_dim):
    return lax.dot_general(
        left, right, (((left_dim,), (right_dim,)), ((), ())), preferred_element_type=jnp.float32
    )


def turn(rows, cosine, sine):
    return (rows * cosine + pltpu.roll(rows, HEAD_SIZE // 2, 1) * sine).astype(jnp.bfloat16)


def join_kernel(left_ref, right_ref, out_ref, done):
    wide = left_ref.shape[1]
    copies = [
        pltpu.make_async_copy(ref, out_ref.at[:, pl.ds(at * wide, wide)], done.at[at])
        for at, ref in enumerate((left_ref, right_ref))
    ]
    for copy in copies:
        copy.start()
    for copy in copies:
        copy.wait()


def order_kernel(
    ranks, slots, extra, stride, route_ref, bucket_ref, seat_ref, sorted_ref, more_ref
):
    route = route_ref[...]
    count = route.shape[1]
    share = count // ranks
    target = lax.div(route, slots)
    member = (lax.broadcasted_iota(jnp.int32, (ranks, count), 0) == target).astype(jnp.float32)
    before = lax.broadcasted_iota(jnp.int32, (count, count), 0) < lax.broadcasted_iota(
        jnp.int32, (count, count), 1
    )
    before = before.astype(jnp.float32).astype(jnp.bfloat16)
    ahead = contract(member.astype(jnp.bfloat16), before, 1, 0)
    order = jnp.sum(member * ahead, axis=0, keepdims=True).astype(jnp.int32)
    beyond = order >= share
    beyond_rows = jnp.broadcast_to(beyond.astype(jnp.float32), (8, count)).astype(jnp.bfloat16)
    number = contract(beyond_rows, before, 1, 0)[0:1]
    counts = jnp.sum(member, axis=1, keepdims=True)
    free = jnp.maximum(share - counts, 0.0)
    group = lax.broadcasted_iota(jnp.int32, (ranks, ranks), 0)
    lower = (group > lax.broadcasted_iota(jnp.int32, (ranks, ranks), 1)).astype(jnp.float32)
    free_rows = jnp.broadcast_to(free, (ranks, HEAD_SIZE)).astype(jnp.bfloat16)
    free_before = contract(lower.astype(jnp.bfloat16), free_rows, 1, 0)[:, 0:1]
    inside = (number >= free_before) & (number < free_before + free)
    base = lax.broadcasted_iota(jnp.int32, (ranks, 1), 0).astype(jnp.float32) * share + counts
    hole = jnp.sum(jnp.where(inside, base + number - free_before, 0.0), axis=0, keepdims=True)
    bucket = jnp.where(beyond, hole.astype(jnp.int32), target * share + order)
    bucket_ref[...] = bucket
    seat_ref[...] = target * stride + order
    high, low = split(route)
    place_high, place_low = split(bucket)
    line = lax.broadcasted_iota(jnp.int32, (8, count), 0)
    digits = jnp.where(line == 0, high, 0)
    digits = jnp.where(line == 1, low, digits)
    digits = jnp.where(line == 2, place_high, digits)
    digits = jnp.where(line == 3, place_low, digits)
    digits = jnp.where(line == 4, 1, digits).astype(jnp.float32).astype(jnp.bfloat16)
    placed = contract(digits, one_hot_rows(count, bucket), 1, 1)
    sorted_ref[...] = (placed[0:1] * HEAD_SIZE + placed[1:2]).astype(jnp.int32)
    listed = jnp.where(beyond, target * extra + order - share, -1)
    found = contract(digits, one_hot_rows(ranks * extra, listed), 1, 1)
    none = found[4:5] - 1.0
    more_ref[0:1] = (found[0:1] * HEAD_SIZE + found[1:2] + none).astype(jnp.int32)
    more_ref[1:2] = (found[2:3] * HEAD_SIZE + found[3:4] + none).astype(jnp.int32)


def query_kernel(
    ranks, row_step, stride, packed, route_ref, seat_ref, positions_ref, frequency_ref, queries_ref, *refs
):
    turned_ref, bounds_ref, cosine_ref, sine_ref, rows_ref = refs
    route = route_ref[...]
    count = route.shape[0]
    lines = positions_ref.shape[0]
    line, lane = split(route)
    pick = (lax.broadcasted_iota(jnp.int32, (count, lines), 1) == line).astype(jnp.float32)
    pick = pick.astype(jnp.bfloat16)
    positions = positions_ref[...]
    half = lax.shift_right_logical(positions, 1)
    rest = positions - half * 2
    rows = 2.0 * contract(pick, half.astype(jnp.float32).astype(jnp.bfloat16), 1, 0) + contract(
        pick, rest.astype(jnp.float32).astype(jnp.bfloat16), 1, 0
    )
    lanes = lax.broadcasted_iota(jnp.int32, (count, HEAD_SIZE), 1)
    spot = jnp.sum(jnp.where(lanes == lane, rows, 0.0), axis=1, keepdims=True)
    angle = spot * frequency_ref[...]
    cosine = jnp.cos(angle)
    sine = jnp.sin(angle)
    sine = jnp.where(lanes < HEAD_SIZE // 2, -sine, sine)
    cosine_ref[...] = cosine
    sine_ref[...] = sine
    seats = one_hot_rows(ranks * stride, seat_ref[...])
    first = route - spot.astype(jnp.int32)
    first_line, first_lane = split(first)
    digits = jnp.where(lanes == 0, line, 0)
    digits = jnp.where(lanes == 1, lane, digits)
    digits = jnp.where(lanes == 2, first_line, digits)
    digits = jnp.where(lanes == 3, first_lane, digits)
    digits = jnp.where(lanes == 4, 1, digits)
    placed = contract(seats, digits.astype(jnp.float32).astype(jnp.bfloat16), 1, 0)
    live = placed[:, 4:5] - 1.0
    last = placed[:, 0:1] * HEAD_SIZE + placed[:, 1:2] + live
    start = placed[:, 2:3] * HEAD_SIZE + placed[:, 3:4] - live * 2.0**20
    seat_lanes = lax.broadcasted_iota(jnp.int32, placed.shape, 1)
    bounds_ref[...] = jnp.where(seat_lanes == 0, last, start).astype(jnp.int32)
    rows_ref[...] = jnp.zeros(rows_ref.shape, jnp.float32)
    for head in range(KEY_VALUE_HEADS):
        for place in range(HEAD_GROUPS):
            at = (head * HEAD_GROUPS + place) * HEAD_SIZE
            one = queries_ref[:, at : at + HEAD_SIZE].astype(jnp.float32)
            rows = contract(seats, turn(one, cosine, sine), 1, 0)
            for group in range(ranks):
                at = group * packed + place * row_step
                rows_ref[at : at + row_step] = rows[group * stride : group * stride + row_step]
        turned_ref[head] = rows_ref[...].astype(jnp.bfloat16)


def add_products(chips, owners_ref, hidden_ref, refs, columns, matrix, done):
    shard = matrix.shape[1] // 2
    copies, at, taken = [], 0, 0
    for place, chip in enumerate(chips):
        first = pl.multiple_of(lax.div(owners_ref[chip[0][0]], 2) * (2 * shard), HEAD_SIZE)
        copies.append(
            (hidden_ref.at[:, pl.ds(first, 2 * shard)], columns.at[place])
        )
        for source, row in chip:
            core = lax.rem(owners_ref[source], 2)
            rows = pl.ds(pl.multiple_of(core * shard + row, 16), refs[taken].shape[0])
            copies.append((refs[taken], matrix.at[place, rows]))
            taken += 1
    copies = [pltpu.make_async_copy(*pair, done.at[at]) for at, pair in enumerate(copies)]
    for copy in copies:
        copy.start()

    def product(span):
        total = contract(columns[0], matrix[0, :, span], 1, 0)
        for place in range(1, len(chips)):
            total = total + contract(columns[place], matrix[place, :, span], 1, 0)
        return total

    return copies, product


def part_kernel(chips, more, owners_ref, hidden_ref, *refs):
    count = sum(len(chip) for chip in chips)
    parts, refs = refs[:count], refs[count:]
    if more:
        total_ref, refs = refs[0], refs[1:]
    out_ref, columns, matrix, done = refs
    copies, product = add_products(chips, owners_ref, hidden_ref, parts, columns, matrix, done)
    for copy in copies:
        copy.wait()
    for first in range(0, out_ref.shape[1], 2 * HEAD_SIZE):
        span = slice(first, first + 2 * HEAD_SIZE)
        if more:
            out_ref[:, span] = total_ref[:, span] + product(span)
        else:
            out_ref[:, span] = product(span)


def finish_kernel(
    chips, owners_ref, hidden_ref, bias_ref, cosine_ref, sine_ref, bucket_ref, *refs
):
    count = sum(len(chip) for chip in chips)
    parts, total_ref = refs[:count], refs[count]
    outs, (columns, matrix, done) = refs[count + 1 : -3], refs[-3:]
    copies, product = add_products(chips, owners_ref, hidden_ref, parts, columns, matrix, done)
    places = one_hot_rows(outs[0].shape[0], bucket_ref[...])
    for copy in copies:
        copy.wait()
    wide = KEY_VALUE_HEADS * HEAD_SIZE
    for first in range(0, 2 * wide, 2 * HEAD_SIZE):
        span = slice(first, first + 2 * HEAD_SIZE)
        rows = (total_ref[:, span] + product(span) + bias_ref[:, span]).astype(jnp.bfloat16)
        if first < wide:
            cosine, sine = cosine_ref[...], sine_ref[...]
            halves = [
                turn(rows[:, at : at + HEAD_SIZE].astype(jnp.float32), cosine, sine)
                for at in (0, HEAD_SIZE)
            ]
            rows = jnp.concatenate(halves, axis=1)
        rows = contract(places, rows, 1, 0).astype(jnp.bfloat16)
        for half in range(2):
            head = first % wide // HEAD_SIZE + half
            for (first_head, heads), out_ref in zip(CHUNKS, outs):
                if first_head <= head < first_head + heads:
                    at = (head - first_head + first // wide * heads) * HEAD_SIZE
                    out_ref[:, at : at + HEAD_SIZE] = rows[
                        :, half * HEAD_SIZE : (half + 1) * HEAD_SIZE
                    ]


def veil_kernel(sets, stride, bounds_ref, routes_ref, more_ref, *veil_refs):
    rest = jnp.zeros((HEAD_SIZE - stride, more_ref.shape[1]), jnp.float32)
    share = routes_ref.shape[2] // routes_ref.shape[0]

    def one_group(group, carry):
        seats = pl.ds(pl.multiple_of(group * stride, 16), stride)
        last, start = bounds_ref[seats, 0:1], bounds_ref[seats, 1:2]
        both = []
        for routes in (routes_ref[group], more_ref[...]):
            veil = jnp.where((routes <= last) & (routes >= start), 0.0, MASKED)
            veil = jnp.transpose(jnp.concatenate([veil, rest], axis=0))
            both.append(veil.astype(jnp.bfloat16))
        first = 0
        for sources, veil_ref in zip(sets, veil_refs):
            end = first + len(sources) * share
            veil_ref[group] = jnp.concatenate([veil[first:end] for veil in both], axis=0)
            first = end
        return carry

    lax.fori_loop(0, routes_ref.shape[0], one_group, 0)


def attend_kernel(starts, before, spare, row_step, stride, more, last, *refs):
    more_ref, queries_ref, veil_ref = refs[:3]
    refs = refs[3:]
    blocks = []
    for first_rows in starts:
        blocks.append(dict(zip(first_rows, refs)))
        refs = refs[len(first_rows) :]
    if more:
        top_ref, sum_ref, total_ref = refs[:3]
        refs = refs[3:]
    if last:
        seat_ref, out_ref, mixed_ref, result_ref, leave = refs[0], refs[1], *refs[-3:]
        refs = refs[:-3]
        mixed_ref[...] = jnp.zeros(mixed_ref.shape, jnp.bfloat16)
    else:
        new_top_ref, new_sum_ref, new_total_ref = refs[:3]
    listed_rows, seen_by, veil, veil_in = refs[-4:]
    fetch_veil = pltpu.make_async_copy(veil_ref, veil, veil_in)
    fetch_veil.start()
    heads, ranks = queries_ref.shape[0], veil_ref.shape[0]
    packed = queries_ref.shape[1] // ranks
    wide = heads * HEAD_SIZE
    share = listed_rows.shape[0] // len(starts)
    count = share * ranks

    token = lax.broadcasted_iota(jnp.int32, (packed, HEAD_SIZE), 0)
    lane = lax.broadcasted_iota(jnp.int32, (packed, HEAD_SIZE), 1)
    own = lane < 0
    for at in range(HEAD_GROUPS):
        own = own | ((token == lane + at * row_step) & (lane < spare))
    seen_by[...] = own.astype(jnp.float32).astype(jnp.bfloat16)
    lines = lax.broadcasted_iota(jnp.int32, (share, count), 1)
    for at, block in enumerate(blocks):
        places = more_ref[(before + at) * share : (before + at + 1) * share]
        pick = (lines == places).astype(jnp.float32).astype(jnp.bfloat16)
        for first in range(0, 2 * wide, 2 * HEAD_SIZE):
            lanes = slice(first, first + 2 * HEAD_SIZE)
            found = [
                contract(pick[:, row : row + ref.shape[0]], ref[:, lanes], 1, 0)
                for row, ref in block.items()
            ]
            listed_rows[at * share : (at + 1) * share, lanes] = sum(found).astype(jnp.bfloat16)
    fetch_veil.wait()
    scale = math.log2(math.e) / math.sqrt(HEAD_SIZE)

    def rows_of(group, row, first):
        lanes = slice(first, first + HEAD_SIZE)
        window = pl.ds(pl.multiple_of(group * share - row, 16), share)
        rows = [block[row][window, lanes] for block in blocks]
        return jnp.concatenate(rows + [listed_rows[:, lanes]], axis=0)

    def scores_of(group, row, head, tokens):
        left = jnp.concatenate([queries_ref[head, tokens], seen_by[...]], axis=1)
        keys = rows_of(group, row, head * HEAD_SIZE)
        return contract(left, jnp.concatenate([keys, veil[group]], axis=1), 1, 1)

    def products_of(group, row, head, weight):
        values = rows_of(group, row, wide + head * HEAD_SIZE)
        values = jnp.concatenate([values, jnp.ones_like(values)], axis=1)
        mixed = contract(weight, values, 1, 0)
        return mixed[:, :HEAD_SIZE], mixed[:, HEAD_SIZE:]

    def tile(top, keys):
        return jnp.concatenate([top] * (keys // HEAD_SIZE), axis=1)

    def finish_head(group, head, total, weight_sum):
        mixed = total / weight_sum
        seats = pl.ds(pl.multiple_of(group * stride, 16), row_step)
        for at in range(HEAD_GROUPS):
            place = (head * HEAD_GROUPS + at) * HEAD_SIZE
            rows = mixed[at * row_step : (at + 1) * row_step]
            mixed_ref[seats, place : place + HEAD_SIZE] = rows.astype(jnp.bfloat16)

    def add_heads(group, row, some):
        tokens = pl.ds(pl.multiple_of(group * packed, 16), packed)
        scores = [scores_of(group, row, head, tokens) for head in some]
        tops, weights = [], []
        for head, score in zip(some, scores):
            top = jnp.max(score, axis=1, keepdims=True)
            if more:
                top = jnp.maximum(top_ref[head, tokens], top)
            else:
                top = jnp.broadcast_to(top, (packed, HEAD_SIZE))
            tops.append(top)
            weight = jnp.exp2((score - tile(top, score.shape[1])) * scale)
            weights.append(weight.astype(jnp.bfloat16))
        for head, top, weight in zip(some, tops, weights):
            total, weight_sum = products_of(group, row, head, weight)
            if more:
                fade = jnp.exp2((top_ref[head, tokens] - top) * scale)
                total = total + fade * total_ref[head, tokens]
                weight_sum = weight_sum + fade * sum_ref[head, tokens]
            if last:
                finish_head(group, head, total, weight_sum)
            else:
                new_top_ref[head, tokens] = top
                new_sum_ref[head, tokens] = weight_sum
                new_total_ref[head, tokens] = total

    def add_heads_as_before(group, row, worst):
        tokens = pl.ds(pl.multiple_of(group * packed, 16), packed)
        scores = [scores_of(group, row, head, tokens) for head in range(heads)]
        weights = []
        for head, score in enumerate(scores):
            above = score - tile(top_ref[head, tokens], score.shape[1])
            for first in range(0, score.shape[1], HEAD_SIZE):
                part = above[:, first : first + HEAD_SIZE].reshape(packed // 8, 8, HEAD_SIZE)
                worst = jnp.maximum(worst, jnp.max(part, axis=0))
            weights.append(jnp.exp2(above * scale).astype(jnp.bfloat16))
        for head, weight in enumerate(weights):
            total, weight_sum = products_of(group, row, head, weight)
            total = total + total_ref[head, tokens]
            weight_sum = weight_sum + sum_ref[head, tokens]
            finish_head(group, head, total, weight_sum)
        return worst

    firsts = sorted({row for first_rows in starts for row in first_rows})
    spans = [
        (row, row // share, end // share) for row, end in zip(firsts, firsts[1:] + [count])
    ]

    def add_all(together):
        for row, first, end in spans:

            def one_group(group, carry, row=row):
                for head in range(0, heads, together):
                    add_heads(group, row, range(head, head + together))
                return carry

            lax.fori_loop(first, end, one_group, 0)

    if not last:
        add_all(2 if more else 4)
        return
    worst = jnp.full((8, HEAD_SIZE), MASKED, jnp.float32)
    for row, first, end in spans:
        worst = lax.fori_loop(
            first,
            end,
            lambda group, worst, row=row: add_heads_as_before(group, row, worst),
            worst,
        )

    @pl.when(jnp.max(worst) * scale > SAFE_POWER)
    def _():
        add_all(2)

    seat_lanes = lax.broadcasted_iota(jnp.int32, (count, mixed_ref.shape[0]), 1)
    seats = (seat_lanes == seat_ref[...]).astype(jnp.float32).astype(jnp.bfloat16)
    span = HEAD_GROUPS * HEAD_SIZE
    leaving = []
    for head in range(heads):
        lanes = slice(head * span, (head + 1) * span)
        rows = contract(seats, mixed_ref[:, lanes], 1, 0)
        result_ref[:, lanes] = rows.astype(jnp.bfloat16)
        lanes = pl.ds(head * span, span)
        leaving.append(
            pltpu.make_async_copy(result_ref.at[:, lanes], out_ref.at[:, lanes], leave.at[head])
        )
        leaving[-1].start()
    for one in leaving:
        one.wait()


def spread(block, ranks, held):
    ring = [(rank, (rank + PLANE) % ranks) for rank in range(ranks)]
    across = [(rank, rank ^ 2) for rank in range(ranks)]
    beside = [(rank, rank ^ 1) for rank in range(ranks)]
    steps = ranks // PLANE
    half = block.shape[0] // 32 * 16

    def keep(source, first, array):
        held.setdefault(source, []).append((first, array))
        held.setdefault(source + 2 * steps, []).append((first, lax.ppermute(array, "dp", beside)))

    lane, other = block, None
    for step in range(steps - 1):
        following = lax.ppermute(lane, "dp", ring), lax.ppermute(lane, "dp", across)
        keep(step, 0, lane)
        if step:
            keep(steps + step - 1, 0, other)
        extra = yield
        lane, other, extra = lax.optimization_barrier((*following, extra))
        yield extra
    over = lax.ppermute(lane[:half], "dp", across)
    around = lax.ppermute(other[half:], "dp", ring)
    keep(steps - 1, 0, lane)
    keep(2 * steps - 2, 0, other)
    extra = yield other
    over, around, extra = lax.optimization_barrier((over, around, extra))
    keep(2 * steps - 1, 0, over)
    keep(2 * steps - 1, half, around)
    yield extra


def source_order(ranks, sources):
    me = lax.axis_index("dp")
    lane, plane = lax.rem(me, PLANE), lax.div(me, PLANE)
    planes = ranks // PLANE
    steps = np.array([source % planes for source in sources], np.int32)
    flips = np.array([(0, 2, 1, 3)[source // planes] for source in sources], np.int32)
    return lax.rem(plane + (planes - steps), planes) * PLANE + (lane ^ flips)


def weight_order(ranks):
    me = lax.axis_index("dp")
    lane, plane = lax.rem(me, PLANE), lax.div(me, PLANE)
    planes = ranks // PLANE
    turn_back = lax.axis_index("groups") == 1
    up = np.array([0, 1, 0, planes - 1, 2, 1, 2, planes - 1] * 2, np.int32)
    steps = jnp.where(turn_back, (planes - up) % planes, up)
    flips = np.array([0, 0, 2, 0, 0, 2, 2, 2], np.int32)
    flips = np.concatenate([flips, flips ^ 1])
    return lax.rem(plane + (planes - steps), planes) * PLANE + (lane ^ flips)


def gather_plan(
    hidden,
    queries,
    route,
    positions,
    key_matrix,
    value_matrix,
    key_projection_bias,
    value_projection_bias,
):
    ranks = lax.axis_size("dp")
    rows = hidden.shape[0]
    slots = positions.shape[0]
    share, extra = rows // ranks, 2
    spare = share + extra
    listed = ranks * extra
    stride = -(-spare // 16) * 16
    row_step = -(-spare // 8) * 8
    packed = -(-HEAD_GROUPS * row_step // 16) * 16
    query_width = queries.shape[1]
    shape = jax.ShapeDtypeStruct

    def columns(array, chunk):
        first, heads = chunk
        return array[..., first * HEAD_SIZE : (first + heads) * HEAD_SIZE]

    joined = pl.pallas_call(
        join_kernel,
        out_shape=shape((key_matrix.shape[0], 2 * key_matrix.shape[1]), jnp.bfloat16),
        in_specs=[HBM] * 2,
        out_specs=VMEM,
        scratch_shapes=[pltpu.SemaphoreType.DMA((2,))],
        compiler_params=grant(14),
        name="join",
    )(key_matrix, value_matrix)
    every = [(group, rank) for group in range(2) for rank in range(ranks)]
    ring = [
        (group * ranks + rank, group * ranks + (rank + (1 - 2 * group) * PLANE) % ranks)
        for group, rank in every
    ]
    across = [(group * ranks + rank, group * ranks + (rank ^ 2)) for group, rank in every]
    beside = [(group * ranks + rank, group * ranks + (rank ^ 1)) for group, rank in every]
    swap = [(group * ranks + rank, (1 - group) * ranks + rank) for group, rank in every]

    def send(array, pairs):
        return lax.ppermute(array, ("groups", "dp"), pairs)

    near_lane, other_row = send(joined, ring), send(joined, across)
    joined_swap = send(joined, beside)
    bucket, seat, sorted_route, more = pl.pallas_call(
        functools.partial(order_kernel, ranks, slots, extra, stride),
        out_shape=(
            shape((1, rows), jnp.int32),
            shape((1, rows), jnp.int32),
            shape((1, rows), jnp.int32),
            shape((2, listed), jnp.int32),
        ),
        in_specs=[VMEM],
        out_specs=(VMEM,) * 4,
        compiler_params=grant(14),
        name="order",
    )(route.reshape(1, rows))
    width = rows + 2 * listed
    plan = jnp.concatenate([sorted_route.reshape(rows), more.reshape(2 * listed), positions])
    plan = lax.all_to_all(
        jnp.broadcast_to(plan, (ranks, width + slots)), "dp", split_axis=0, concat_axis=0, tiled=True
    )
    near_lane, other_row, joined_swap, plan, bucket, seat = lax.optimization_barrier(
        (near_lane, other_row, joined_swap, plan, bucket, seat)
    )
    matrices = {0: (joined, joined_swap)}
    far_lane, next_lane = send(near_lane, swap), send(near_lane, ring)
    near_other = send(near_lane, across)
    swaps = send(near_lane, beside), send(other_row, beside)
    all_positions = plan[:, width:].reshape(-1, HEAD_SIZE)
    planes = ranks // PLANE
    sets = [(0, 2 * planes)] + [
        (step, step + 2 * planes, step + planes - 1, step + 3 * planes - 1)
        for step in range(1, planes)
    ]
    sets.append((2 * planes - 1, 4 * planes - 1))
    owners = weight_order(ranks)

    half = HEAD_SIZE // 2
    frequency = 1000000.0 ** (-(jnp.arange(half, dtype=jnp.float32) * 2.0 / HEAD_SIZE))
    turned, bounds, cosine, sine = pl.pallas_call(
        functools.partial(query_kernel, ranks, row_step, stride, packed),
        out_shape=(
            shape((KEY_VALUE_HEADS, ranks * packed, HEAD_SIZE), jnp.bfloat16),
            shape((ranks * stride, HEAD_SIZE), jnp.int32),
            shape((rows, HEAD_SIZE), jnp.float32),
            shape((rows, HEAD_SIZE), jnp.float32),
        ),
        in_specs=[VMEM] * 5,
        out_specs=(VMEM,) * 4,
        scratch_shapes=[pltpu.VMEM((ranks * packed, HEAD_SIZE), jnp.float32)],
        compiler_params=grant(14),
        cost_estimate=cost(4 * stride * ranks * rows * query_width, 4 * rows * query_width),
        name="turn_queries",
    )(
        route.reshape(rows, 1),
        seat,
        all_positions,
        jnp.concatenate([frequency, frequency]).reshape(1, HEAD_SIZE),
        queries,
    )

    shard, wide = key_matrix.shape[0], 2 * key_matrix.shape[1]

    def chip_parts(sources):
        chips = [((source, 0), (source + ranks // 2, 0)) for source in sources]
        return chips, [array for source in sources for array in matrices[source]]

    def scratch(chips, arrays):
        return [
            pltpu.VMEM((len(chips), rows, 2 * shard), jnp.bfloat16),
            pltpu.VMEM((len(chips), 2 * shard, wide), jnp.bfloat16),
            pltpu.SemaphoreType.DMA((len(chips) + len(arrays),)),
        ]

    def product_cost(chips):
        depth = 2 * shard * len(chips)
        return cost(2 * rows * depth * wide, 2 * depth * (rows + wide) + 8 * rows * wide)

    def add_part(total, sources):
        chips, arrays = chip_parts(sources)
        more = [] if total is None else [total]
        return pl.pallas_call(
            functools.partial(part_kernel, chips, bool(more)),
            out_shape=shape((rows, wide), jnp.float32),
            in_specs=[SMEM] + [HBM] * (1 + len(arrays)) + [VMEM] * len(more),
            out_specs=VMEM,
            scratch_shapes=scratch(chips, arrays),
            compiler_params=grant(14),
            cost_estimate=product_cost(chips),
            name="add_part",
        )(owners, hidden, *arrays, *more)

    bias = jnp.concatenate([key_projection_bias, value_projection_bias])
    bias = bias.astype(jnp.float32).reshape(1, -1)
    seat = seat.reshape(rows, 1)
    far_lane, next_lane, near_other, swaps, turned, bounds, cosine, sine, bias, owners, seat = (
        lax.optimization_barrier(
            (
                far_lane, next_lane, near_other, swaps,
                turned, bounds, cosine, sine, bias, owners, seat,
            )
        )
    )
    matrices[1], matrices[2] = (near_lane, swaps[0]), (other_row, swaps[1])
    next_other, far_other = send(next_lane, across), send(near_other, swap)
    matrices[3] = (far_lane, send(far_lane, beside))
    matrices[4] = (next_lane, send(next_lane, beside))
    matrices[5] = (near_other, send(near_other, beside))
    total = add_part(add_part(None, (0, 1, 2)), (3, 4, 5))
    next_other, far_other, total = lax.optimization_barrier((next_other, far_other, total))
    matrices[6] = (next_other, send(next_other, beside))
    matrices[7] = (far_other, send(far_other, beside))
    chips, arrays = chip_parts((6, 7))
    (pairs,) = pl.pallas_call(
        functools.partial(finish_kernel, chips),
        out_shape=tuple(
            shape((rows, 2 * heads * HEAD_SIZE), jnp.bfloat16) for _, heads in CHUNKS
        ),
        in_specs=[SMEM, HBM] + [VMEM] * 4 + [HBM] * len(arrays) + [VMEM],
        out_specs=(VMEM,) * len(CHUNKS),
        scratch_shapes=scratch(chips, arrays),
        compiler_params=grant(14),
        cost_estimate=product_cost(chips),
        name="finish",
    )(
        owners,
        hidden,
        bias,
        cosine,
        sine,
        bucket,
        *arrays,
        total,
    )

    blocks = {}
    sending = spread(pairs, ranks, blocks)
    next(sending)
    order = [source for sources in sets for source in sources]
    ordered = plan[:, :width][source_order(ranks, order)]
    key_routes = ordered[:, :rows].reshape(ranks, ranks, share).transpose(1, 0, 2)
    more_places = ordered[:, rows + listed :].reshape(ranks * listed, 1)
    veils = pl.pallas_call(
        functools.partial(veil_kernel, sets, stride),
        out_shape=tuple(
            shape((ranks, 2 * share * len(sources), HEAD_SIZE), jnp.bfloat16) for sources in sets
        ),
        in_specs=[VMEM] * 3,
        out_specs=(VMEM,) * len(sets),
        compiler_params=grant(14),
        cost_estimate=cost(3 * 10**9, 4 * ranks * rows * HEAD_SIZE),
        name="veil",
    )(
        bounds,
        key_routes.reshape(ranks, 1, rows),
        ordered[:, rows : rows + listed].reshape(1, ranks * listed),
    )

    def attend(state, index):
        sources, last = sets[index], index == len(sets) - 1
        starts = [tuple(first for first, _ in blocks[source]) for source in sources]
        arrays = [array for source in sources for _, array in blocks[source]]
        keys = 2 * share * len(sources)
        fixed = [more_places, turned, veils[index], *arrays, *state]
        kept = shape((KEY_VALUE_HEADS, ranks * packed, HEAD_SIZE), jnp.float32)
        outs = [kept] * 3
        out_specs = [VMEM] * 3
        in_specs = [VMEM, VMEM, HBM] + [VMEM] * (len(fixed) - 3)
        handed = {len(fixed) - 3 + at: at + last for at in range(3)} if state else {}
        scratch_shapes = [
            pltpu.VMEM((len(sources) * share, wide), jnp.bfloat16),
            pltpu.VMEM((packed, HEAD_SIZE), jnp.bfloat16),
            pltpu.VMEM((ranks, keys, HEAD_SIZE), jnp.bfloat16),
            pltpu.SemaphoreType.DMA,
        ]
        if last:
            fixed.append(seat)
            in_specs.append(VMEM)
            outs.insert(0, shape((rows, query_width), jnp.bfloat16))
            out_specs.insert(0, HBM)
            scratch_shapes += [
                pltpu.VMEM((ranks * stride, query_width), jnp.bfloat16),
                pltpu.VMEM((rows, query_width), jnp.bfloat16),
                pltpu.SemaphoreType.DMA((KEY_VALUE_HEADS,)),
            ]
        return pl.pallas_call(
            functools.partial(
                attend_kernel,
                starts,
                sum(len(one) for one in sets[:index]),
                spare,
                row_step,
                stride,
                bool(state),
                last,
            ),
            out_shape=tuple(outs),
            in_specs=in_specs,
            out_specs=tuple(out_specs),
            scratch_shapes=scratch_shapes,
            input_output_aliases=handed,
            compiler_params=grant(18 if last else 14),
            cost_estimate=cost(
                8 * ranks * KEY_VALUE_HEADS * packed * (keys + 256) * HEAD_SIZE,
                2 * keys * rows * HEAD_SIZE,
            ),
            name="attend",
        )(*fixed)

    state = ()
    for step in range(planes - 1):
        if step:
            next(sending)
        state = sending.send(tuple(attend(state, step)))
    next(sending)
    state = sending.send(tuple(attend(state, planes - 1)))
    return attend(state, planes)[0]


def apply_rotary(rows, slot_offset, heads):
    block_count = rows.shape[0]
    half = HEAD_SIZE // 2
    frequency = 1000000.0 ** (-(jnp.arange(half, dtype=jnp.float32) * 2.0 / HEAD_SIZE))
    angle = slot_offset.astype(jnp.float32)[:, None] * frequency[None, :]
    cosine = jnp.cos(angle)[:, None, :]
    sine = jnp.sin(angle)[:, None, :]
    grid = rows.astype(jnp.float32).reshape(block_count, heads, HEAD_SIZE)
    first = grid[:, :, :half]
    second = grid[:, :, half:]
    turned = jnp.concatenate(
        [first * cosine - second * sine, second * cosine + first * sine], axis=2
    )
    return turned.reshape(block_count, heads * HEAD_SIZE).astype(jnp.bfloat16)


def causal_block_attention(pieces):
    query_tile_rows, key_tile_rows, value_tile_rows, spot_block = pieces
    block_count = query_tile_rows.shape[0]
    head_groups = QUERY_HEADS // KEY_VALUE_HEADS
    query_block_grid = query_tile_rows.reshape(block_count, KEY_VALUE_HEADS, head_groups, HEAD_SIZE)
    key_block_grid = key_tile_rows.reshape(block_count, KEY_VALUE_HEADS, HEAD_SIZE)
    value_block_grid = value_tile_rows.reshape(block_count, KEY_VALUE_HEADS, HEAD_SIZE)
    scores = jnp.einsum(
        "qhgd,khd->hgqk", query_block_grid, key_block_grid, preferred_element_type=jnp.float32
    ) / math.sqrt(HEAD_SIZE)
    inner = jnp.arange(block_count, dtype=jnp.int32)
    visible = (inner[None, :] <= inner[:, None]) & (
        inner[None, :] >= inner[:, None] - spot_block[:, None]
    )
    scores = jnp.where(visible, scores, -jnp.inf)
    top = jnp.max(scores, axis=3, keepdims=True)
    weights = jnp.exp(scores - top)
    totals = jnp.sum(weights, axis=3)
    probs = weights.astype(jnp.bfloat16)
    mixed = jnp.einsum(
        "hgqk,khd->qhgd", probs, value_block_grid, preferred_element_type=jnp.float32
    )
    mixed = mixed / jnp.transpose(totals, (2, 0, 1))[:, :, :, None]
    return mixed.reshape(block_count, QUERY_HEADS * HEAD_SIZE).astype(jnp.bfloat16)


def add_projection(left, pieces):
    return (
        jnp.dot(left, pieces[0], preferred_element_type=jnp.float32),
        jnp.dot(left, pieces[1], preferred_element_type=jnp.float32),
    )


def project_own(hidden, key_matrix, value_matrix, key_projection_bias, value_projection_bias):
    totals = add_projection(
        hidden,
        (
            lax.all_gather(key_matrix, "dp", axis=0, tiled=True),
            lax.all_gather(value_matrix, "dp", axis=0, tiled=True),
        ),
    )
    key_rows = (totals[0] + key_projection_bias.astype(jnp.float32)).astype(jnp.bfloat16)
    value_rows = (totals[1] + value_projection_bias.astype(jnp.float32)).astype(jnp.bfloat16)
    return jnp.concatenate([key_rows, value_rows], axis=1)


def send_plan(
    hidden,
    queries,
    route,
    positions,
    key_matrix,
    value_matrix,
    key_projection_bias,
    value_projection_bias,
):
    ranks = lax.axis_size("dp")
    rows = hidden.shape[0]
    slots = positions.shape[0]
    spare = rows // ranks + 2
    width = ranks * spare
    paired_width = key_matrix.shape[1]
    target = route // slots
    place = route - target * slots
    member = (target[:, None] == jnp.arange(ranks, dtype=jnp.int32)[None, :]).astype(jnp.int32)
    order = jnp.sum(jnp.cumsum(member, axis=0) * member, axis=1) - 1
    bucket = target * spare + order
    outgoing = jnp.full((width,), slots, jnp.int32).at[bucket].set(place)
    arrived = lax.all_to_all(
        outgoing.reshape(ranks, spare), "dp", split_axis=0, concat_axis=0, tiled=True
    ).reshape(width)
    query_buf = jnp.zeros((width, queries.shape[1]), jnp.bfloat16).at[bucket].set(queries)
    own_pairs = project_own(
        hidden, key_matrix, value_matrix, key_projection_bias, value_projection_bias
    )
    pair_buf = jnp.zeros((width, 2 * paired_width), jnp.bfloat16).at[bucket].set(own_pairs)
    got_query, got_pairs = (
        lax.all_to_all(
            query_buf.reshape(ranks, spare, -1), "dp", split_axis=0, concat_axis=0, tiled=True
        ),
        lax.all_to_all(
            pair_buf.reshape(ranks, spare, -1), "dp", split_axis=0, concat_axis=0, tiled=True
        ),
    )
    got_query = got_query.reshape(width, -1)
    got_pairs = got_pairs.reshape(width, -1)
    query_slot_rows = (
        jnp.zeros((slots, got_query.shape[1]), jnp.bfloat16).at[arrived].set(got_query, mode="drop")
    )
    paired_slot_rows = (
        jnp.zeros((slots, 2 * paired_width), jnp.bfloat16).at[arrived].set(got_pairs, mode="drop")
    )
    query_turned = apply_rotary(query_slot_rows, positions, QUERY_HEADS)
    key_rotated = apply_rotary(paired_slot_rows[:, :paired_width], positions, KEY_VALUE_HEADS)
    block_list = slots // BLOCK_SLOTS
    attended = lax.map(
        causal_block_attention,
        (
            query_turned.reshape(block_list, BLOCK_SLOTS, -1),
            key_rotated.reshape(block_list, BLOCK_SLOTS, -1),
            paired_slot_rows[:, paired_width:].reshape(block_list, BLOCK_SLOTS, -1),
            positions.reshape(block_list, BLOCK_SLOTS),
        ),
    )
    attended = attended.reshape(slots, -1)
    leaving = attended[jnp.minimum(arrived, slots - 1)]
    returned = lax.all_to_all(
        leaving.reshape(ranks, spare, -1), "dp", split_axis=0, concat_axis=0, tiled=True
    ).reshape(width, -1)
    return returned[bucket]


def local(*args):
    hidden, queries, _, positions, key_matrix = args[:5]
    ranks = lax.axis_size("dp")
    rows = hidden.shape[0]
    gathered = ranks * ranks * (rows // ranks + 2) * 4 * key_matrix.shape[1]
    chip_rows = 2 * key_matrix.shape[0]
    fits = rows % (16 * ranks) == 0 and chip_rows % HEAD_SIZE == 0 and gathered <= GATHER_LIMIT
    if ranks == PLANES * PLANE and lax.axis_size("groups") == 2 and fits:
        return gather_plan(*args)
    return send_plan(*args)


def solution(mesh):
    placed = (
        P(("groups", "dp"), None),
        P(("groups", "dp"), None),
        P(("groups", "dp")),
        P(("groups", "dp")),
        P("dp", None),
        P("dp", None),
        P(),
        P(),
    )
    return jax.shard_map(
        local, mesh=mesh, in_specs=placed, out_specs=P(("groups", "dp"), None), check_vma=False
    )
```

```python
import functools
import math

import jax
import jax.numpy as jnp
import numpy as np
from jax import lax
from jax.experimental import pallas as pl
from jax.experimental.pallas import tpu as pltpu
from jax.sharding import PartitionSpec as P

QUERY_HEADS = 20
KEY_VALUE_HEADS = 4
HEAD_SIZE = 128
BLOCK_SLOTS = 512
HEAD_GROUPS = QUERY_HEADS // KEY_VALUE_HEADS
CHUNKS = ((0, KEY_VALUE_HEADS),)
PLANE = 4
PLANES = 4
SAFE_POWER = 64.0
GATHER_LIMIT = 40 * 2**20
MASKED = -1e30
VMEM = pl.BlockSpec(memory_space=pltpu.VMEM)
SMEM = pl.BlockSpec(memory_space=pltpu.SMEM)
HBM = pl.BlockSpec(memory_space=pltpu.HBM)


def grant(mebibytes):
    return pltpu.CompilerParams(vmem_limit_bytes=mebibytes * 2**20)


def cost(flops, moved):
    return pl.CostEstimate(flops=flops, bytes_accessed=moved, transcendentals=0)


def one_hot_rows(count, index_row):
    rows = lax.broadcasted_iota(jnp.int32, (count, index_row.shape[1]), 0)
    return (rows == index_row).astype(jnp.float32).astype(jnp.bfloat16)


def split(number):
    high = lax.shift_right_logical(number, HEAD_SIZE.bit_length() - 1)
    return high, number - high * HEAD_SIZE


def contract(left, right, left_dim, right_dim):
    return lax.dot_general(
        left, right, (((left_dim,), (right_dim,)), ((), ())), preferred_element_type=jnp.float32
    )


def turn(rows, cosine, sine):
    return (rows * cosine + pltpu.roll(rows, HEAD_SIZE // 2, 1) * sine).astype(jnp.bfloat16)


def join_kernel(left_ref, right_ref, out_ref, done):
    wide = left_ref.shape[1]
    copies = [
        pltpu.make_async_copy(ref, out_ref.at[:, pl.ds(at * wide, wide)], done.at[at])
        for at, ref in enumerate((left_ref, right_ref))
    ]
    for copy in copies:
        copy.start()
    for copy in copies:
        copy.wait()


def order_kernel(
    ranks, slots, extra, stride, route_ref, bucket_ref, seat_ref, sorted_ref, more_ref
):
    route = route_ref[...]
    count = route.shape[1]
    share = count // ranks
    target = lax.div(route, slots)
    member = (lax.broadcasted_iota(jnp.int32, (ranks, count), 0) == target).astype(jnp.float32)
    before = lax.broadcasted_iota(jnp.int32, (count, count), 0) < lax.broadcasted_iota(
        jnp.int32, (count, count), 1
    )
    before = before.astype(jnp.float32).astype(jnp.bfloat16)
    ahead = contract(member.astype(jnp.bfloat16), before, 1, 0)
    order = jnp.sum(member * ahead, axis=0, keepdims=True).astype(jnp.int32)
    beyond = order >= share
    beyond_rows = jnp.broadcast_to(beyond.astype(jnp.float32), (8, count)).astype(jnp.bfloat16)
    number = contract(beyond_rows, before, 1, 0)[0:1]
    counts = jnp.sum(member, axis=1, keepdims=True)
    free = jnp.maximum(share - counts, 0.0)
    group = lax.broadcasted_iota(jnp.int32, (ranks, ranks), 0)
    lower = (group > lax.broadcasted_iota(jnp.int32, (ranks, ranks), 1)).astype(jnp.float32)
    free_rows = jnp.broadcast_to(free, (ranks, HEAD_SIZE)).astype(jnp.bfloat16)
    free_before = contract(lower.astype(jnp.bfloat16), free_rows, 1, 0)[:, 0:1]
    inside = (number >= free_before) & (number < free_before + free)
    base = lax.broadcasted_iota(jnp.int32, (ranks, 1), 0).astype(jnp.float32) * share + counts
    hole = jnp.sum(jnp.where(inside, base + number - free_before, 0.0), axis=0, keepdims=True)
    bucket = jnp.where(beyond, hole.astype(jnp.int32), target * share + order)
    bucket_ref[...] = bucket
    seat_ref[...] = target * stride + order
    high, low = split(route)
    place_high, place_low = split(bucket)
    line = lax.broadcasted_iota(jnp.int32, (8, count), 0)
    digits = jnp.where(line == 0, high, 0)
    digits = jnp.where(line == 1, low, digits)
    digits = jnp.where(line == 2, place_high, digits)
    digits = jnp.where(line == 3, place_low, digits)
    digits = jnp.where(line == 4, 1, digits).astype(jnp.float32).astype(jnp.bfloat16)
    placed = contract(digits, one_hot_rows(count, bucket), 1, 1)
    sorted_ref[...] = (placed[0:1] * HEAD_SIZE + placed[1:2]).astype(jnp.int32)
    listed = jnp.where(beyond, target * extra + order - share, -1)
    found = contract(digits, one_hot_rows(ranks * extra, listed), 1, 1)
    none = found[4:5] - 1.0
    more_ref[0:1] = (found[0:1] * HEAD_SIZE + found[1:2] + none).astype(jnp.int32)
    more_ref[1:2] = (found[2:3] * HEAD_SIZE + found[3:4] + none).astype(jnp.int32)


def query_kernel(
    ranks, spare, stride, packed, route_ref, seat_ref, positions_ref, frequency_ref, queries_ref, *refs
):
    turned_ref, bounds_ref, cosine_ref, sine_ref, column_ref, rows_ref = refs
    route = route_ref[...]
    count = route.shape[0]
    lines = positions_ref.shape[0]
    line, lane = split(route)
    pick = (lax.broadcasted_iota(jnp.int32, (count, lines), 1) == line).astype(jnp.float32)
    pick = pick.astype(jnp.bfloat16)
    positions = positions_ref[...]
    half = lax.shift_right_logical(positions, 1)
    rest = positions - half * 2
    rows = 2.0 * contract(pick, half.astype(jnp.float32).astype(jnp.bfloat16), 1, 0) + contract(
        pick, rest.astype(jnp.float32).astype(jnp.bfloat16), 1, 0
    )
    lanes = lax.broadcasted_iota(jnp.int32, (count, HEAD_SIZE), 1)
    spot = jnp.sum(jnp.where(lanes == lane, rows, 0.0), axis=1, keepdims=True)
    angle = spot * frequency_ref[...]
    cosine = jnp.cos(angle)
    sine = jnp.sin(angle)
    sine = jnp.where(lanes < HEAD_SIZE // 2, -sine, sine)
    cosine_ref[...] = cosine
    sine_ref[...] = sine
    seats = one_hot_rows(ranks * stride, seat_ref[...])
    seat_line, seat_lane = split(seat_ref[...])
    digit = lax.broadcasted_iota(jnp.int32, (8, count), 0)
    digits = jnp.where(digit == 0, seat_line, jnp.where(digit == 1, seat_lane, 0))
    same = one_hot_rows(count, lax.broadcasted_iota(jnp.int32, (1, count), 1))
    column = contract(same, digits.astype(jnp.float32).astype(jnp.bfloat16), 1, 1)
    column_ref[...] = (column[:, 0:1] * HEAD_SIZE + column[:, 1:2]).astype(jnp.int32)
    first = route - spot.astype(jnp.int32)
    first_line, first_lane = split(first)
    digits = jnp.where(lanes == 0, line, 0)
    digits = jnp.where(lanes == 1, lane, digits)
    digits = jnp.where(lanes == 2, first_line, digits)
    digits = jnp.where(lanes == 3, first_lane, digits)
    digits = jnp.where(lanes == 4, 1, digits)
    placed = contract(seats, digits.astype(jnp.float32).astype(jnp.bfloat16), 1, 0)
    live = placed[:, 4:5] - 1.0
    last = placed[:, 0:1] * HEAD_SIZE + placed[:, 1:2] + live
    start = placed[:, 2:3] * HEAD_SIZE + placed[:, 3:4] - live * 2.0**20
    seat_lanes = lax.broadcasted_iota(jnp.int32, placed.shape, 1)
    bounds_ref[...] = jnp.where(seat_lanes == 0, last, start).astype(jnp.int32)
    rows_ref[...] = jnp.zeros(rows_ref.shape, jnp.float32)
    for head in range(KEY_VALUE_HEADS):
        for place in range(HEAD_GROUPS):
            at = (head * HEAD_GROUPS + place) * HEAD_SIZE
            one = queries_ref[:, at : at + HEAD_SIZE].astype(jnp.float32)
            rows = contract(seats, turn(one, cosine, sine), 1, 0)
            for group in range(ranks):
                at = group * packed + place * spare
                rows_ref[at : at + spare] = rows[group * stride : group * stride + spare]
        turned_ref[head] = rows_ref[...].astype(jnp.bfloat16)


def add_products(chips, owners_ref, hidden_ref, refs, columns, matrix, done):
    shard = matrix.shape[1] // 2
    copies, at, taken = [], 0, 0
    for place, chip in enumerate(chips):
        first = pl.multiple_of(lax.div(owners_ref[chip[0][0]], 2) * (2 * shard), HEAD_SIZE)
        copies.append(
            (hidden_ref.at[:, pl.ds(first, 2 * shard)], columns.at[place])
        )
        for source, row in chip:
            core = lax.rem(owners_ref[source], 2)
            rows = pl.ds(pl.multiple_of(core * shard + row, 16), refs[taken].shape[0])
            copies.append((refs[taken], matrix.at[place, rows]))
            taken += 1
    copies = [pltpu.make_async_copy(*pair, done.at[at]) for at, pair in enumerate(copies)]
    for copy in copies:
        copy.start()

    def product(span):
        total = contract(columns[0], matrix[0, :, span], 1, 0)
        for place in range(1, len(chips)):
            total = total + contract(columns[place], matrix[place, :, span], 1, 0)
        return total

    return copies, product


def part_kernel(chips, more, owners_ref, hidden_ref, *refs):
    count = sum(len(chip) for chip in chips)
    parts, refs = refs[:count], refs[count:]
    if more:
        total_ref, refs = refs[0], refs[1:]
    out_ref, columns, matrix, done = refs
    copies, product = add_products(chips, owners_ref, hidden_ref, parts, columns, matrix, done)
    for copy in copies:
        copy.wait()
    for first in range(0, out_ref.shape[1], 2 * HEAD_SIZE):
        span = slice(first, first + 2 * HEAD_SIZE)
        if more:
            out_ref[:, span] = total_ref[:, span] + product(span)
        else:
            out_ref[:, span] = product(span)


def finish_kernel(
    chips, owners_ref, hidden_ref, bias_ref, cosine_ref, sine_ref, bucket_ref, *refs
):
    count = sum(len(chip) for chip in chips)
    parts, total_ref = refs[:count], refs[count]
    outs, (columns, matrix, done) = refs[count + 1 : -3], refs[-3:]
    copies, product = add_products(chips, owners_ref, hidden_ref, parts, columns, matrix, done)
    places = one_hot_rows(outs[0].shape[0], bucket_ref[...])
    for copy in copies:
        copy.wait()
    wide = KEY_VALUE_HEADS * HEAD_SIZE
    for first in range(0, 2 * wide, 2 * HEAD_SIZE):
        span = slice(first, first + 2 * HEAD_SIZE)
        rows = (total_ref[:, span] + product(span) + bias_ref[:, span]).astype(jnp.bfloat16)
        if first < wide:
            cosine, sine = cosine_ref[...], sine_ref[...]
            halves = [
                turn(rows[:, at : at + HEAD_SIZE].astype(jnp.float32), cosine, sine)
                for at in (0, HEAD_SIZE)
            ]
            rows = jnp.concatenate(halves, axis=1)
        rows = contract(places, rows, 1, 0).astype(jnp.bfloat16)
        for half in range(2):
            head = first % wide // HEAD_SIZE + half
            for (first_head, heads), out_ref in zip(CHUNKS, outs):
                if first_head <= head < first_head + heads:
                    at = (head - first_head + first // wide * heads) * HEAD_SIZE
                    out_ref[:, at : at + HEAD_SIZE] = rows[
                        :, half * HEAD_SIZE : (half + 1) * HEAD_SIZE
                    ]


def veil_kernel(sets, stride, bounds_ref, routes_ref, more_ref, *veil_refs):
    rest = jnp.zeros((HEAD_SIZE - stride, more_ref.shape[1]), jnp.float32)
    share = routes_ref.shape[2] // routes_ref.shape[0]

    def one_group(group, carry):
        seats = pl.ds(pl.multiple_of(group * stride, 16), stride)
        last, start = bounds_ref[seats, 0:1], bounds_ref[seats, 1:2]
        both = []
        for routes in (routes_ref[group], more_ref[...]):
            veil = jnp.where((routes <= last) & (routes >= start), 0.0, MASKED)
            veil = jnp.transpose(jnp.concatenate([veil, rest], axis=0))
            both.append(veil.astype(jnp.bfloat16))
        first = 0
        for sources, veil_ref in zip(sets, veil_refs):
            end = first + len(sources) * share
            veil_ref[group] = jnp.concatenate([veil[first:end] for veil in both], axis=0)
            first = end
        return carry

    lax.fori_loop(0, routes_ref.shape[0], one_group, 0)


def attend_kernel(starts, before, spare, stride, more, last, *refs):
    more_ref, queries_ref, veil_ref = refs[:3]
    refs = refs[3:]
    blocks = []
    for first_rows in starts:
        blocks.append(dict(zip(first_rows, refs)))
        refs = refs[len(first_rows) :]
    if more:
        top_ref, sum_ref, total_ref = refs[:3]
        refs = refs[3:]
    if last:
        seat_ref, out_ref, mixed_ref, result_ref, leave = refs[0], refs[1], *refs[-3:]
        refs = refs[:-3]
        mixed_ref[...] = jnp.zeros(mixed_ref.shape, jnp.bfloat16)
    else:
        new_top_ref, new_sum_ref, new_total_ref = refs[:3]
    listed_rows, seen_by, veil, veil_in = refs[-4:]
    fetch_veil = pltpu.make_async_copy(veil_ref, veil, veil_in)
    fetch_veil.start()
    heads, ranks = queries_ref.shape[0], veil_ref.shape[0]
    packed = queries_ref.shape[1] // ranks
    wide = heads * HEAD_SIZE
    share = listed_rows.shape[0] // len(starts)
    count = share * ranks

    token = lax.broadcasted_iota(jnp.int32, (packed, HEAD_SIZE), 0)
    lane = lax.broadcasted_iota(jnp.int32, (packed, HEAD_SIZE), 1)
    own = lane < 0
    for at in range(HEAD_GROUPS):
        own = own | ((token == lane + at * spare) & (lane < spare))
    seen_by[...] = own.astype(jnp.float32).astype(jnp.bfloat16)
    lines = lax.broadcasted_iota(jnp.int32, (share, count), 1)
    for at, block in enumerate(blocks):
        places = more_ref[(before + at) * share : (before + at + 1) * share]
        pick = (lines == places).astype(jnp.float32).astype(jnp.bfloat16)
        for first in range(0, 2 * wide, 2 * HEAD_SIZE):
            lanes = slice(first, first + 2 * HEAD_SIZE)
            found = [
                contract(pick[:, row : row + ref.shape[0]], ref[:, lanes], 1, 0)
                for row, ref in block.items()
            ]
            listed_rows[at * share : (at + 1) * share, lanes] = sum(found).astype(jnp.bfloat16)
    fetch_veil.wait()
    scale = math.log2(math.e) / math.sqrt(HEAD_SIZE)

    def rows_of(group, row, first):
        lanes = slice(first, first + HEAD_SIZE)
        window = pl.ds(pl.multiple_of(group * share - row, 16), share)
        rows = [block[row][window, lanes] for block in blocks]
        return jnp.concatenate(rows + [listed_rows[:, lanes]], axis=0)

    def scores_of(group, row, head, tokens):
        left = jnp.concatenate([queries_ref[head, tokens], seen_by[...]], axis=1)
        keys = rows_of(group, row, head * HEAD_SIZE)
        return contract(left, jnp.concatenate([keys, veil[group]], axis=1), 1, 1)

    def products_of(group, row, head, weight):
        values = rows_of(group, row, wide + head * HEAD_SIZE)
        values = jnp.concatenate([values, jnp.ones_like(values)], axis=1)
        mixed = contract(weight, values, 1, 0)
        return mixed[:, :HEAD_SIZE], mixed[:, HEAD_SIZE:]

    def tile(top, keys):
        return jnp.concatenate([top] * (keys // HEAD_SIZE), axis=1)

    def finish_head(group, head, total, weight_sum):
        mixed = total / weight_sum
        seats = pl.ds(pl.multiple_of(group * stride, 16), spare)
        for at in range(HEAD_GROUPS):
            place = (head * HEAD_GROUPS + at) * HEAD_SIZE
            rows = mixed[at * spare : (at + 1) * spare]
            mixed_ref[seats, place : place + HEAD_SIZE] = rows.astype(jnp.bfloat16)

    def add_heads(group, row, some):
        tokens = pl.ds(pl.multiple_of(group * packed, 16), packed)
        scores = [scores_of(group, row, head, tokens) for head in some]
        tops, weights = [], []
        for head, score in zip(some, scores):
            top = jnp.max(score, axis=1, keepdims=True)
            if more:
                top = jnp.maximum(top_ref[head, tokens], top)
            else:
                top = jnp.broadcast_to(top, (packed, HEAD_SIZE))
            tops.append(top)
            weight = jnp.exp2((score - tile(top, score.shape[1])) * scale)
            weights.append(weight.astype(jnp.bfloat16))
        for head, top, weight in zip(some, tops, weights):
            total, weight_sum = products_of(group, row, head, weight)
            if more:
                fade = jnp.exp2((top_ref[head, tokens] - top) * scale)
                total = total + fade * total_ref[head, tokens]
                weight_sum = weight_sum + fade * sum_ref[head, tokens]
            if last:
                finish_head(group, head, total, weight_sum)
            else:
                new_top_ref[head, tokens] = top
                new_sum_ref[head, tokens] = weight_sum
                new_total_ref[head, tokens] = total

    def add_heads_as_before(group, row, worst):
        tokens = pl.ds(pl.multiple_of(group * packed, 16), packed)
        scores = [scores_of(group, row, head, tokens) for head in range(heads)]
        weights = []
        for head, score in enumerate(scores):
            above = score - tile(top_ref[head, tokens], score.shape[1])
            for first in range(0, score.shape[1], HEAD_SIZE):
                part = above[:, first : first + HEAD_SIZE].reshape(packed // 8, 8, HEAD_SIZE)
                worst = jnp.maximum(worst, jnp.max(part, axis=0))
            weights.append(jnp.exp2(above * scale).astype(jnp.bfloat16))
        for head, weight in enumerate(weights):
            total, weight_sum = products_of(group, row, head, weight)
            total = total + total_ref[head, tokens]
            weight_sum = weight_sum + sum_ref[head, tokens]
            finish_head(group, head, total, weight_sum)
        return worst

    firsts = sorted({row for first_rows in starts for row in first_rows})
    spans = [
        (row, row // share, end // share) for row, end in zip(firsts, firsts[1:] + [count])
    ]

    def add_all(together):
        for row, first, end in spans:

            def one_group(group, carry, row=row):
                for head in range(0, heads, together):
                    add_heads(group, row, range(head, head + together))
                return carry

            lax.fori_loop(first, end, one_group, 0)

    if not last:
        add_all(2 if more else 4)
        return
    worst = jnp.full((8, HEAD_SIZE), MASKED, jnp.float32)
    for row, first, end in spans:
        worst = lax.fori_loop(
            first,
            end,
            lambda group, worst, row=row: add_heads_as_before(group, row, worst),
            worst,
        )

    @pl.when(jnp.max(worst) * scale > SAFE_POWER)
    def _():
        add_all(2)

    seat_lanes = lax.broadcasted_iota(jnp.int32, (count, mixed_ref.shape[0]), 1)
    seats = (seat_lanes == seat_ref[...]).astype(jnp.float32).astype(jnp.bfloat16)
    span = HEAD_GROUPS * HEAD_SIZE
    leaving = []
    for head in range(heads):
        lanes = slice(head * span, (head + 1) * span)
        rows = contract(seats, mixed_ref[:, lanes], 1, 0)
        result_ref[:, lanes] = rows.astype(jnp.bfloat16)
        lanes = pl.ds(head * span, span)
        leaving.append(
            pltpu.make_async_copy(result_ref.at[:, lanes], out_ref.at[:, lanes], leave.at[head])
        )
        leaving[-1].start()
    for one in leaving:
        one.wait()


def spread(block, ranks, held):
    ring = [(rank, (rank + PLANE) % ranks) for rank in range(ranks)]
    across = [(rank, rank ^ 2) for rank in range(ranks)]
    beside = [(rank, rank ^ 1) for rank in range(ranks)]
    steps = ranks // PLANE
    half = block.shape[0] // 32 * 16

    def keep(source, first, array):
        held.setdefault(source, []).append((first, array))
        held.setdefault(source + 2 * steps, []).append((first, lax.ppermute(array, "dp", beside)))

    lane, other = block, None
    for step in range(steps - 1):
        following = lax.ppermute(lane, "dp", ring), lax.ppermute(lane, "dp", across)
        keep(step, 0, lane)
        if step:
            keep(steps + step - 1, 0, other)
        extra = yield
        lane, other, extra = lax.optimization_barrier((*following, extra))
        yield extra
    over = lax.ppermute(lane[:half], "dp", across)
    around = lax.ppermute(other[half:], "dp", ring)
    keep(steps - 1, 0, lane)
    keep(2 * steps - 2, 0, other)
    extra = yield other
    over, around, extra = lax.optimization_barrier((over, around, extra))
    keep(2 * steps - 1, 0, over)
    keep(2 * steps - 1, half, around)
    yield extra


def source_order(ranks, sources):
    me = lax.axis_index("dp")
    lane, plane = lax.rem(me, PLANE), lax.div(me, PLANE)
    planes = ranks // PLANE
    steps = np.array([source % planes for source in sources], np.int32)
    flips = np.array([(0, 2, 1, 3)[source // planes] for source in sources], np.int32)
    return lax.rem(plane + (planes - steps), planes) * PLANE + (lane ^ flips)


def weight_order(ranks):
    me = lax.axis_index("dp")
    lane, plane = lax.rem(me, PLANE), lax.div(me, PLANE)
    planes = ranks // PLANE
    turn_back = lax.axis_index("groups") == 1
    up = np.array([0, 1, 0, planes - 1, 2, 1, 2, planes - 1] * 2, np.int32)
    steps = jnp.where(turn_back, (planes - up) % planes, up)
    flips = np.array([0, 0, 2, 0, 0, 2, 2, 2], np.int32)
    flips = np.concatenate([flips, flips ^ 1])
    return lax.rem(plane + (planes - steps), planes) * PLANE + (lane ^ flips)


def gather_plan(
    hidden,
    queries,
    route,
    positions,
    key_matrix,
    value_matrix,
    key_projection_bias,
    value_projection_bias,
):
    ranks = lax.axis_size("dp")
    rows = hidden.shape[0]
    slots = positions.shape[0]
    share, extra = rows // ranks, 2
    spare = share + extra
    listed = ranks * extra
    stride = -(-spare // 16) * 16
    packed = -(-HEAD_GROUPS * spare // 16) * 16
    query_width = queries.shape[1]
    shape = jax.ShapeDtypeStruct

    def columns(array, chunk):
        first, heads = chunk
        return array[..., first * HEAD_SIZE : (first + heads) * HEAD_SIZE]

    joined = pl.pallas_call(
        join_kernel,
        out_shape=shape((key_matrix.shape[0], 2 * key_matrix.shape[1]), jnp.bfloat16),
        in_specs=[HBM] * 2,
        out_specs=VMEM,
        scratch_shapes=[pltpu.SemaphoreType.DMA((2,))],
        compiler_params=grant(56),
        name="join",
    )(key_matrix, value_matrix)
    every = [(group, rank) for group in range(2) for rank in range(ranks)]
    ring = [
        (group * ranks + rank, group * ranks + (rank + (1 - 2 * group) * PLANE) % ranks)
        for group, rank in every
    ]
    across = [(group * ranks + rank, group * ranks + (rank ^ 2)) for group, rank in every]
    beside = [(group * ranks + rank, group * ranks + (rank ^ 1)) for group, rank in every]
    swap = [(group * ranks + rank, (1 - group) * ranks + rank) for group, rank in every]

    def send(array, pairs):
        return lax.ppermute(array, ("groups", "dp"), pairs)

    near_lane, other_row = send(joined, ring), send(joined, across)
    joined_swap = send(joined, beside)
    bucket, seat, sorted_route, more = pl.pallas_call(
        functools.partial(order_kernel, ranks, slots, extra, stride),
        out_shape=(
            shape((1, rows), jnp.int32),
            shape((1, rows), jnp.int32),
            shape((1, rows), jnp.int32),
            shape((2, listed), jnp.int32),
        ),
        in_specs=[VMEM],
        out_specs=(VMEM,) * 4,
        compiler_params=grant(14),
        name="order",
    )(route.reshape(1, rows))
    width = rows + 2 * listed
    plan = jnp.concatenate([sorted_route.reshape(rows), more.reshape(2 * listed), positions])
    plan = lax.all_to_all(
        jnp.broadcast_to(plan, (ranks, width + slots)), "dp", split_axis=0, concat_axis=0, tiled=True
    )
    near_lane, other_row, joined_swap, plan, bucket, seat = lax.optimization_barrier(
        (near_lane, other_row, joined_swap, plan, bucket, seat)
    )
    matrices = {0: (joined, joined_swap)}
    far_lane, next_lane = send(near_lane, swap), send(near_lane, ring)
    near_other = send(near_lane, across)
    swaps = send(near_lane, beside), send(other_row, beside)
    all_positions = plan[:, width:].reshape(-1, HEAD_SIZE)
    planes = ranks // PLANE
    sets = [(0, 2 * planes)] + [
        (step, step + 2 * planes, step + planes - 1, step + 3 * planes - 1)
        for step in range(1, planes)
    ]
    sets.append((2 * planes - 1, 4 * planes - 1))
    owners = weight_order(ranks)

    half = HEAD_SIZE // 2
    frequency = 1000000.0 ** (-(jnp.arange(half, dtype=jnp.float32) * 2.0 / HEAD_SIZE))
    turned, bounds, cosine, sine, seat_column = pl.pallas_call(
        functools.partial(query_kernel, ranks, spare, stride, packed),
        out_shape=(
            shape((KEY_VALUE_HEADS, ranks * packed, HEAD_SIZE), jnp.bfloat16),
            shape((ranks * stride, HEAD_SIZE), jnp.int32),
            shape((rows, HEAD_SIZE), jnp.float32),
            shape((rows, HEAD_SIZE), jnp.float32),
            shape((rows, 1), jnp.int32),
        ),
        in_specs=[VMEM] * 5,
        out_specs=(VMEM,) * 5,
        scratch_shapes=[pltpu.VMEM((ranks * packed, HEAD_SIZE), jnp.float32)],
        compiler_params=grant(14),
        cost_estimate=cost(4 * stride * ranks * rows * query_width, 4 * rows * query_width),
        name="turn_queries",
    )(
        route.reshape(rows, 1),
        seat,
        all_positions,
        jnp.concatenate([frequency, frequency]).reshape(1, HEAD_SIZE),
        queries,
    )

    shard, wide = key_matrix.shape[0], 2 * key_matrix.shape[1]

    def chip_parts(sources):
        chips = [((source, 0), (source + ranks // 2, 0)) for source in sources]
        return chips, [array for source in sources for array in matrices[source]]

    def scratch(chips, arrays):
        return [
            pltpu.VMEM((len(chips), rows, 2 * shard), jnp.bfloat16),
            pltpu.VMEM((len(chips), 2 * shard, wide), jnp.bfloat16),
            pltpu.SemaphoreType.DMA((len(chips) + len(arrays),)),
        ]

    def product_cost(chips):
        depth = 2 * shard * len(chips)
        return cost(2 * rows * depth * wide, 2 * depth * (rows + wide) + 8 * rows * wide)

    def add_part(total, sources):
        chips, arrays = chip_parts(sources)
        more = [] if total is None else [total]
        return pl.pallas_call(
            functools.partial(part_kernel, chips, bool(more)),
            out_shape=shape((rows, wide), jnp.float32),
            in_specs=[SMEM] + [HBM] * (1 + len(arrays)) + [VMEM] * len(more),
            out_specs=VMEM,
            scratch_shapes=scratch(chips, arrays),
            compiler_params=grant(14),
            cost_estimate=product_cost(chips),
            name="add_part",
        )(owners, hidden, *arrays, *more)

    bias = jnp.concatenate([key_projection_bias, value_projection_bias])
    bias = bias.astype(jnp.float32).reshape(1, -1)
    step = (far_lane, next_lane, near_other, swaps)
    step, turned, bounds, cosine, sine, seat_column, bias, owners = lax.optimization_barrier(
        (step, turned, bounds, cosine, sine, seat_column, bias, owners)
    )
    far_lane, next_lane, near_other, swaps = step
    matrices[1], matrices[2] = (near_lane, swaps[0]), (other_row, swaps[1])
    next_other, far_other = send(next_lane, across), send(near_other, swap)
    matrices[3] = (far_lane, send(far_lane, beside))
    matrices[4] = (next_lane, send(next_lane, beside))
    matrices[5] = (near_other, send(near_other, beside))
    total = add_part(add_part(None, (0, 1, 2)), (3, 4, 5))
    next_other, far_other, total = lax.optimization_barrier((next_other, far_other, total))
    matrices[6] = (next_other, send(next_other, beside))
    matrices[7] = (far_other, send(far_other, beside))
    chips, arrays = chip_parts((6, 7))
    (pairs,) = pl.pallas_call(
        functools.partial(finish_kernel, chips),
        out_shape=tuple(
            shape((rows, 2 * heads * HEAD_SIZE), jnp.bfloat16) for _, heads in CHUNKS
        ),
        in_specs=[SMEM, HBM] + [VMEM] * 4 + [HBM] * len(arrays) + [VMEM],
        out_specs=(VMEM,) * len(CHUNKS),
        scratch_shapes=scratch(chips, arrays),
        compiler_params=grant(14),
        cost_estimate=product_cost(chips),
        name="finish",
    )(
        owners,
        hidden,
        bias,
        cosine,
        sine,
        bucket,
        *arrays,
        total,
    )

    blocks = {}
    sending = spread(pairs, ranks, blocks)
    next(sending)
    order = [source for sources in sets for source in sources]
    ordered = plan[:, :width][source_order(ranks, order)]
    key_routes = ordered[:, :rows].reshape(ranks, ranks, share).transpose(1, 0, 2)
    more_places = ordered[:, rows + listed :].reshape(ranks * listed, 1)
    veils = pl.pallas_call(
        functools.partial(veil_kernel, sets, stride),
        out_shape=tuple(
            shape((ranks, 2 * share * len(sources), HEAD_SIZE), jnp.bfloat16) for sources in sets
        ),
        in_specs=[VMEM] * 3,
        out_specs=(VMEM,) * len(sets),
        compiler_params=grant(14),
        cost_estimate=cost(3 * 10**9, 4 * ranks * rows * HEAD_SIZE),
        name="veil",
    )(
        bounds,
        key_routes.reshape(ranks, 1, rows),
        ordered[:, rows : rows + listed].reshape(1, ranks * listed),
    )

    def attend(state, index):
        sources, last = sets[index], index == len(sets) - 1
        starts = [tuple(first for first, _ in blocks[source]) for source in sources]
        arrays = [array for source in sources for _, array in blocks[source]]
        keys = 2 * share * len(sources)
        fixed = [more_places, turned, veils[index], *arrays, *state]
        kept = shape((KEY_VALUE_HEADS, ranks * packed, HEAD_SIZE), jnp.float32)
        outs = [kept] * 3
        out_specs = [VMEM] * 3
        in_specs = [VMEM, VMEM, HBM] + [VMEM] * (len(fixed) - 3)
        handed = {len(fixed) - 3 + at: at + last for at in range(3)} if state else {}
        scratch_shapes = [
            pltpu.VMEM((len(sources) * share, wide), jnp.bfloat16),
            pltpu.VMEM((packed, HEAD_SIZE), jnp.bfloat16),
            pltpu.VMEM((ranks, keys, HEAD_SIZE), jnp.bfloat16),
            pltpu.SemaphoreType.DMA,
        ]
        if last:
            fixed.append(seat_column)
            in_specs.append(VMEM)
            outs.insert(0, shape((rows, query_width), jnp.bfloat16))
            out_specs.insert(0, HBM)
            scratch_shapes += [
                pltpu.VMEM((ranks * stride, query_width), jnp.bfloat16),
                pltpu.VMEM((rows, query_width), jnp.bfloat16),
                pltpu.SemaphoreType.DMA((KEY_VALUE_HEADS,)),
            ]
        return pl.pallas_call(
            functools.partial(
                attend_kernel,
                starts,
                sum(len(one) for one in sets[:index]),
                spare,
                stride,
                bool(state),
                last,
            ),
            out_shape=tuple(outs),
            in_specs=in_specs,
            out_specs=tuple(out_specs),
            scratch_shapes=scratch_shapes,
            input_output_aliases=handed,
            compiler_params=grant(18 if last else 14),
            cost_estimate=cost(
                8 * ranks * KEY_VALUE_HEADS * packed * (keys + 256) * HEAD_SIZE,
                2 * keys * rows * HEAD_SIZE,
            ),
            name="attend",
        )(*fixed)

    state = ()
    for step in range(planes - 1):
        if step:
            next(sending)
        state = sending.send(tuple(attend(state, step)))
    next(sending)
    state = sending.send(tuple(attend(state, planes - 1)))
    return attend(state, planes)[0]


def apply_rotary(rows, slot_offset, heads):
    block_count = rows.shape[0]
    half = HEAD_SIZE // 2
    frequency = 1000000.0 ** (-(jnp.arange(half, dtype=jnp.float32) * 2.0 / HEAD_SIZE))
    angle = slot_offset.astype(jnp.float32)[:, None] * frequency[None, :]
    cosine = jnp.cos(angle)[:, None, :]
    sine = jnp.sin(angle)[:, None, :]
    grid = rows.astype(jnp.float32).reshape(block_count, heads, HEAD_SIZE)
    first = grid[:, :, :half]
    second = grid[:, :, half:]
    turned = jnp.concatenate(
        [first * cosine - second * sine, second * cosine + first * sine], axis=2
    )
    return turned.reshape(block_count, heads * HEAD_SIZE).astype(jnp.bfloat16)


def causal_block_attention(pieces):
    query_tile_rows, key_tile_rows, value_tile_rows, spot_block = pieces
    block_count = query_tile_rows.shape[0]
    head_groups = QUERY_HEADS // KEY_VALUE_HEADS
    query_block_grid = query_tile_rows.reshape(block_count, KEY_VALUE_HEADS, head_groups, HEAD_SIZE)
    key_block_grid = key_tile_rows.reshape(block_count, KEY_VALUE_HEADS, HEAD_SIZE)
    value_block_grid = value_tile_rows.reshape(block_count, KEY_VALUE_HEADS, HEAD_SIZE)
    scores = jnp.einsum(
        "qhgd,khd->hgqk", query_block_grid, key_block_grid, preferred_element_type=jnp.float32
    ) / math.sqrt(HEAD_SIZE)
    inner = jnp.arange(block_count, dtype=jnp.int32)
    visible = (inner[None, :] <= inner[:, None]) & (
        inner[None, :] >= inner[:, None] - spot_block[:, None]
    )
    scores = jnp.where(visible, scores, -jnp.inf)
    top = jnp.max(scores, axis=3, keepdims=True)
    weights = jnp.exp(scores - top)
    totals = jnp.sum(weights, axis=3)
    probs = weights.astype(jnp.bfloat16)
    mixed = jnp.einsum(
        "hgqk,khd->qhgd", probs, value_block_grid, preferred_element_type=jnp.float32
    )
    mixed = mixed / jnp.transpose(totals, (2, 0, 1))[:, :, :, None]
    return mixed.reshape(block_count, QUERY_HEADS * HEAD_SIZE).astype(jnp.bfloat16)


def add_projection(left, pieces):
    return (
        jnp.dot(left, pieces[0], preferred_element_type=jnp.float32),
        jnp.dot(left, pieces[1], preferred_element_type=jnp.float32),
    )


def project_own(hidden, key_matrix, value_matrix, key_projection_bias, value_projection_bias):
    totals = add_projection(
        hidden,
        (
            lax.all_gather(key_matrix, "dp", axis=0, tiled=True),
            lax.all_gather(value_matrix, "dp", axis=0, tiled=True),
        ),
    )
    key_rows = (totals[0] + key_projection_bias.astype(jnp.float32)).astype(jnp.bfloat16)
    value_rows = (totals[1] + value_projection_bias.astype(jnp.float32)).astype(jnp.bfloat16)
    return jnp.concatenate([key_rows, value_rows], axis=1)


def send_plan(
    hidden,
    queries,
    route,
    positions,
    key_matrix,
    value_matrix,
    key_projection_bias,
    value_projection_bias,
):
    ranks = lax.axis_size("dp")
    rows = hidden.shape[0]
    slots = positions.shape[0]
    spare = rows // ranks + 2
    width = ranks * spare
    paired_width = key_matrix.shape[1]
    target = route // slots
    place = route - target * slots
    member = (target[:, None] == jnp.arange(ranks, dtype=jnp.int32)[None, :]).astype(jnp.int32)
    order = jnp.sum(jnp.cumsum(member, axis=0) * member, axis=1) - 1
    bucket = target * spare + order
    outgoing = jnp.full((width,), slots, jnp.int32).at[bucket].set(place)
    arrived = lax.all_to_all(
        outgoing.reshape(ranks, spare), "dp", split_axis=0, concat_axis=0, tiled=True
    ).reshape(width)
    query_buf = jnp.zeros((width, queries.shape[1]), jnp.bfloat16).at[bucket].set(queries)
    own_pairs = project_own(
        hidden, key_matrix, value_matrix, key_projection_bias, value_projection_bias
    )
    pair_buf = jnp.zeros((width, 2 * paired_width), jnp.bfloat16).at[bucket].set(own_pairs)
    got_query, got_pairs = (
        lax.all_to_all(
            query_buf.reshape(ranks, spare, -1), "dp", split_axis=0, concat_axis=0, tiled=True
        ),
        lax.all_to_all(
            pair_buf.reshape(ranks, spare, -1), "dp", split_axis=0, concat_axis=0, tiled=True
        ),
    )
    got_query = got_query.reshape(width, -1)
    got_pairs = got_pairs.reshape(width, -1)
    query_slot_rows = (
        jnp.zeros((slots, got_query.shape[1]), jnp.bfloat16).at[arrived].set(got_query, mode="drop")
    )
    paired_slot_rows = (
        jnp.zeros((slots, 2 * paired_width), jnp.bfloat16).at[arrived].set(got_pairs, mode="drop")
    )
    query_turned = apply_rotary(query_slot_rows, positions, QUERY_HEADS)
    key_rotated = apply_rotary(paired_slot_rows[:, :paired_width], positions, KEY_VALUE_HEADS)
    block_list = slots // BLOCK_SLOTS
    attended = lax.map(
        causal_block_attention,
        (
            query_turned.reshape(block_list, BLOCK_SLOTS, -1),
            key_rotated.reshape(block_list, BLOCK_SLOTS, -1),
            paired_slot_rows[:, paired_width:].reshape(block_list, BLOCK_SLOTS, -1),
            positions.reshape(block_list, BLOCK_SLOTS),
        ),
    )
    attended = attended.reshape(slots, -1)
    leaving = attended[jnp.minimum(arrived, slots - 1)]
    returned = lax.all_to_all(
        leaving.reshape(ranks, spare, -1), "dp", split_axis=0, concat_axis=0, tiled=True
    ).reshape(width, -1)
    return returned[bucket]


def local(*args):
    hidden, queries, _, positions, key_matrix = args[:5]
    ranks = lax.axis_size("dp")
    rows = hidden.shape[0]
    gathered = ranks * ranks * (rows // ranks + 2) * 4 * key_matrix.shape[1]
    chip_rows = 2 * key_matrix.shape[0]
    fits = rows % (16 * ranks) == 0 and chip_rows % HEAD_SIZE == 0 and gathered <= GATHER_LIMIT
    if ranks == PLANES * PLANE and lax.axis_size("groups") == 2 and fits:
        return gather_plan(*args)
    return send_plan(*args)


def solution(mesh):
    placed = (
        P(("groups", "dp"), None),
        P(("groups", "dp"), None),
        P(("groups", "dp")),
        P(("groups", "dp")),
        P("dp", None),
        P("dp", None),
        P(),
        P(),
    )
    return jax.shard_map(
        local, mesh=mesh, in_specs=placed, out_specs=P(("groups", "dp"), None), check_vma=False
    )
```

```python
import functools
import math

import jax
import jax.numpy as jnp
import numpy as np
from jax import lax
from jax.experimental import pallas as pl
from jax.experimental.pallas import tpu as pltpu
from jax.sharding import PartitionSpec as P

QUERY_HEADS = 20
KEY_VALUE_HEADS = 4
HEAD_SIZE = 128
BLOCK_SLOTS = 512
HEAD_GROUPS = QUERY_HEADS // KEY_VALUE_HEADS
CHUNKS = ((0, KEY_VALUE_HEADS),)
PLANE = 4
PLANES = 4
SAFE_POWER = 64.0
GATHER_LIMIT = 40 * 2**20
MASKED = -1e30
VMEM = pl.BlockSpec(memory_space=pltpu.VMEM)
SMEM = pl.BlockSpec(memory_space=pltpu.SMEM)
HBM = pl.BlockSpec(memory_space=pltpu.HBM)


def grant(mebibytes):
    return pltpu.CompilerParams(vmem_limit_bytes=mebibytes * 2**20)


def cost(flops, moved):
    return pl.CostEstimate(flops=flops, bytes_accessed=moved, transcendentals=0)


def one_hot_rows(count, index_row):
    rows = lax.broadcasted_iota(jnp.int32, (count, index_row.shape[1]), 0)
    return (rows == index_row).astype(jnp.float32).astype(jnp.bfloat16)


def split(number):
    high = lax.shift_right_logical(number, HEAD_SIZE.bit_length() - 1)
    return high, number - high * HEAD_SIZE


def contract(left, right, left_dim, right_dim):
    return lax.dot_general(
        left, right, (((left_dim,), (right_dim,)), ((), ())), preferred_element_type=jnp.float32
    )


def turn(rows, cosine, sine):
    return (rows * cosine + pltpu.roll(rows, HEAD_SIZE // 2, 1) * sine).astype(jnp.bfloat16)


def join_kernel(left_ref, right_ref, out_ref, done):
    wide = left_ref.shape[1]
    copies = [
        pltpu.make_async_copy(ref, out_ref.at[:, pl.ds(at * wide, wide)], done.at[at])
        for at, ref in enumerate((left_ref, right_ref))
    ]
    for copy in copies:
        copy.start()
    for copy in copies:
        copy.wait()


def order_kernel(
    ranks, slots, extra, stride, route_ref, bucket_ref, seat_ref, sorted_ref, more_ref
):
    route = route_ref[...]
    count = route.shape[1]
    share = count // ranks
    target = lax.div(route, slots)
    member = (lax.broadcasted_iota(jnp.int32, (ranks, count), 0) == target).astype(jnp.float32)
    before = lax.broadcasted_iota(jnp.int32, (count, count), 0) < lax.broadcasted_iota(
        jnp.int32, (count, count), 1
    )
    before = before.astype(jnp.float32).astype(jnp.bfloat16)
    ahead = contract(member.astype(jnp.bfloat16), before, 1, 0)
    order = jnp.sum(member * ahead, axis=0, keepdims=True).astype(jnp.int32)
    beyond = order >= share
    beyond_rows = jnp.broadcast_to(beyond.astype(jnp.float32), (8, count)).astype(jnp.bfloat16)
    number = contract(beyond_rows, before, 1, 0)[0:1]
    counts = jnp.sum(member, axis=1, keepdims=True)
    free = jnp.maximum(share - counts, 0.0)
    group = lax.broadcasted_iota(jnp.int32, (ranks, ranks), 0)
    lower = (group > lax.broadcasted_iota(jnp.int32, (ranks, ranks), 1)).astype(jnp.float32)
    free_rows = jnp.broadcast_to(free, (ranks, HEAD_SIZE)).astype(jnp.bfloat16)
    free_before = contract(lower.astype(jnp.bfloat16), free_rows, 1, 0)[:, 0:1]
    inside = (number >= free_before) & (number < free_before + free)
    base = lax.broadcasted_iota(jnp.int32, (ranks, 1), 0).astype(jnp.float32) * share + counts
    hole = jnp.sum(jnp.where(inside, base + number - free_before, 0.0), axis=0, keepdims=True)
    bucket = jnp.where(beyond, hole.astype(jnp.int32), target * share + order)
    bucket_ref[...] = bucket
    seat_ref[...] = target * stride + order
    high, low = split(route)
    place_high, place_low = split(bucket)
    line = lax.broadcasted_iota(jnp.int32, (8, count), 0)
    digits = jnp.where(line == 0, high, 0)
    digits = jnp.where(line == 1, low, digits)
    digits = jnp.where(line == 2, place_high, digits)
    digits = jnp.where(line == 3, place_low, digits)
    digits = jnp.where(line == 4, 1, digits).astype(jnp.float32).astype(jnp.bfloat16)
    placed = contract(digits, one_hot_rows(count, bucket), 1, 1)
    sorted_ref[...] = (placed[0:1] * HEAD_SIZE + placed[1:2]).astype(jnp.int32)
    listed = jnp.where(beyond, target * extra + order - share, -1)
    found = contract(digits, one_hot_rows(ranks * extra, listed), 1, 1)
    none = found[4:5] - 1.0
    more_ref[0:1] = (found[0:1] * HEAD_SIZE + found[1:2] + none).astype(jnp.int32)
    more_ref[1:2] = (found[2:3] * HEAD_SIZE + found[3:4] + none).astype(jnp.int32)


def query_kernel(
    ranks, spare, stride, packed, route_ref, seat_ref, positions_ref, frequency_ref, queries_ref, *refs
):
    turned_ref, bounds_ref, cosine_ref, sine_ref, column_ref, rows_ref = refs
    route = route_ref[...]
    count = route.shape[0]
    lines = positions_ref.shape[0]
    line, lane = split(route)
    pick = (lax.broadcasted_iota(jnp.int32, (count, lines), 1) == line).astype(jnp.float32)
    pick = pick.astype(jnp.bfloat16)
    positions = positions_ref[...]
    half = lax.shift_right_logical(positions, 1)
    rest = positions - half * 2
    rows = 2.0 * contract(pick, half.astype(jnp.float32).astype(jnp.bfloat16), 1, 0) + contract(
        pick, rest.astype(jnp.float32).astype(jnp.bfloat16), 1, 0
    )
    lanes = lax.broadcasted_iota(jnp.int32, (count, HEAD_SIZE), 1)
    spot = jnp.sum(jnp.where(lanes == lane, rows, 0.0), axis=1, keepdims=True)
    angle = spot * frequency_ref[...]
    cosine = jnp.cos(angle)
    sine = jnp.sin(angle)
    sine = jnp.where(lanes < HEAD_SIZE // 2, -sine, sine)
    cosine_ref[...] = cosine
    sine_ref[...] = sine
    seats = one_hot_rows(ranks * stride, seat_ref[...])
    seat_line, seat_lane = split(seat_ref[...])
    digit = lax.broadcasted_iota(jnp.int32, (8, count), 0)
    digits = jnp.where(digit == 0, seat_line, jnp.where(digit == 1, seat_lane, 0))
    same = one_hot_rows(count, lax.broadcasted_iota(jnp.int32, (1, count), 1))
    column = contract(same, digits.astype(jnp.float32).astype(jnp.bfloat16), 1, 1)
    column_ref[...] = (column[:, 0:1] * HEAD_SIZE + column[:, 1:2]).astype(jnp.int32)
    first = route - spot.astype(jnp.int32)
    first_line, first_lane = split(first)
    digits = jnp.where(lanes == 0, line, 0)
    digits = jnp.where(lanes == 1, lane, digits)
    digits = jnp.where(lanes == 2, first_line, digits)
    digits = jnp.where(lanes == 3, first_lane, digits)
    digits = jnp.where(lanes == 4, 1, digits)
    placed = contract(seats, digits.astype(jnp.float32).astype(jnp.bfloat16), 1, 0)
    live = placed[:, 4:5] - 1.0
    last = placed[:, 0:1] * HEAD_SIZE + placed[:, 1:2] + live
    start = placed[:, 2:3] * HEAD_SIZE + placed[:, 3:4] - live * 2.0**20
    seat_lanes = lax.broadcasted_iota(jnp.int32, placed.shape, 1)
    bounds_ref[...] = jnp.where(seat_lanes == 0, last, start).astype(jnp.int32)
    rows_ref[...] = jnp.zeros(rows_ref.shape, jnp.float32)
    for head in range(KEY_VALUE_HEADS):
        for place in range(HEAD_GROUPS):
            at = (head * HEAD_GROUPS + place) * HEAD_SIZE
            one = queries_ref[:, at : at + HEAD_SIZE].astype(jnp.float32)
            rows = contract(seats, turn(one, cosine, sine), 1, 0)
            for group in range(ranks):
                at = group * packed + place * spare
                rows_ref[at : at + spare] = rows[group * stride : group * stride + spare]
        turned_ref[head] = rows_ref[...].astype(jnp.bfloat16)


def fetch_columns(chips, owners_ref, hidden_ref, columns, done):
    deep = columns.shape[1] // len(chips)
    copies = []
    for place, chip in enumerate(chips):
        first = pl.multiple_of(lax.div(owners_ref[chip[0]], 2) * deep, HEAD_SIZE)
        copies.append(
            pltpu.make_async_copy(
                hidden_ref.at[:, pl.ds(first, deep)],
                columns.at[:, pl.ds(place * deep, deep)],
                done.at[place],
            )
        )
        copies[-1].start()
    return copies


def place_rows(owners_ref, chips, matrix):
    shard = matrix.shape[0] // len(chips) // 2
    return [
        pl.ds(pl.multiple_of((2 * place + lax.rem(owners_ref[source], 2)) * shard, 16), shard)
        for place, chip in enumerate(chips)
        for source in chip
    ]


def part_kernel(chips, more, owners_ref, hidden_ref, *refs):
    count = 2 * len(chips)
    parts, refs = refs[:count], refs[count:]
    if more:
        total_ref, refs = refs[0], refs[1:]
    out_ref, columns, matrix, done = refs
    copies = fetch_columns(chips, owners_ref, hidden_ref, columns, done)
    for at, (ref, rows) in enumerate(zip(parts, place_rows(owners_ref, chips, matrix))):
        copies.append(pltpu.make_async_copy(ref, matrix.at[rows], done.at[len(chips) + at]))
        copies[-1].start()
    for copy in copies:
        copy.wait()
    for first in range(0, out_ref.shape[1], 2 * HEAD_SIZE):
        span = slice(first, first + 2 * HEAD_SIZE)
        product = contract(columns[...], matrix[:, span], 1, 0)
        out_ref[:, span] = total_ref[:, span] + product if more else product


def finish_kernel(
    chips, owners_ref, hidden_ref, bias_ref, cosine_ref, sine_ref, bucket_ref, *refs
):
    count = 2 * len(chips)
    parts, total_ref = refs[:count], refs[count]
    outs, (columns, matrix, done) = refs[count + 1 : -3], refs[-3:]
    copies = fetch_columns(chips, owners_ref, hidden_ref, columns, done)
    for ref, rows in zip(parts, place_rows(owners_ref, chips, matrix)):
        matrix[rows] = ref[...]
    places = one_hot_rows(outs[0].shape[0], bucket_ref[...])
    for copy in copies:
        copy.wait()
    wide = KEY_VALUE_HEADS * HEAD_SIZE
    for first in range(0, 2 * wide, 2 * HEAD_SIZE):
        span = slice(first, first + 2 * HEAD_SIZE)
        rows = contract(columns[...], matrix[:, span], 1, 0) + total_ref[:, span]
        rows = (rows + bias_ref[:, span]).astype(jnp.bfloat16)
        if first < wide:
            cosine, sine = cosine_ref[...], sine_ref[...]
            halves = [
                turn(rows[:, at : at + HEAD_SIZE].astype(jnp.float32), cosine, sine)
                for at in (0, HEAD_SIZE)
            ]
            rows = jnp.concatenate(halves, axis=1)
        rows = contract(places, rows, 1, 0).astype(jnp.bfloat16)
        for half in range(2):
            head = first % wide // HEAD_SIZE + half
            for (first_head, heads), out_ref in zip(CHUNKS, outs):
                if first_head <= head < first_head + heads:
                    at = (head - first_head + first // wide * heads) * HEAD_SIZE
                    out_ref[:, at : at + HEAD_SIZE] = rows[
                        :, half * HEAD_SIZE : (half + 1) * HEAD_SIZE
                    ]


def veil_kernel(sets, stride, bounds_ref, routes_ref, more_ref, *veil_refs):
    rest = jnp.zeros((HEAD_SIZE - stride, more_ref.shape[1]), jnp.float32)
    share = routes_ref.shape[2] // routes_ref.shape[0]

    def one_group(group, carry):
        seats = pl.ds(pl.multiple_of(group * stride, 16), stride)
        last, start = bounds_ref[seats, 0:1], bounds_ref[seats, 1:2]
        both = []
        for routes in (routes_ref[group], more_ref[...]):
            veil = jnp.where((routes <= last) & (routes >= start), 0.0, MASKED)
            veil = jnp.transpose(jnp.concatenate([veil, rest], axis=0))
            both.append(veil.astype(jnp.bfloat16))
        first = 0
        for sources, veil_ref in zip(sets, veil_refs):
            end = first + len(sources) * share
            veil_ref[group] = jnp.concatenate([veil[first:end] for veil in both], axis=0)
            first = end
        return carry

    lax.fori_loop(0, routes_ref.shape[0], one_group, 0)


def attend_kernel(starts, before, spare, stride, more, last, *refs):
    more_ref, queries_ref, veil_ref = refs[:3]
    refs = refs[3:]
    blocks = []
    for first_rows in starts:
        blocks.append(dict(zip(first_rows, refs)))
        refs = refs[len(first_rows) :]
    if more:
        top_ref, sum_ref, total_ref = refs[:3]
        refs = refs[3:]
    if last:
        seat_ref, out_ref, mixed_ref, result_ref, leave = refs[0], refs[1], *refs[-3:]
        refs = refs[:-3]
        mixed_ref[...] = jnp.zeros(mixed_ref.shape, jnp.bfloat16)
    else:
        new_top_ref, new_sum_ref, new_total_ref = refs[:3]
    listed_rows, seen_by, veil, veil_in = refs[-4:]
    fetch_veil = pltpu.make_async_copy(veil_ref, veil, veil_in)
    fetch_veil.start()
    heads, ranks = queries_ref.shape[0], veil_ref.shape[0]
    packed = queries_ref.shape[1] // ranks
    wide = heads * HEAD_SIZE
    share = listed_rows.shape[0] // len(starts)
    count = share * ranks

    token = lax.broadcasted_iota(jnp.int32, (packed, HEAD_SIZE), 0)
    lane = lax.broadcasted_iota(jnp.int32, (packed, HEAD_SIZE), 1)
    own = lane < 0
    for at in range(HEAD_GROUPS):
        own = own | ((token == lane + at * spare) & (lane < spare))
    seen_by[...] = own.astype(jnp.float32).astype(jnp.bfloat16)
    lines = lax.broadcasted_iota(jnp.int32, (share, count), 1)
    for at, block in enumerate(blocks):
        places = more_ref[(before + at) * share : (before + at + 1) * share]
        pick = (lines == places).astype(jnp.float32).astype(jnp.bfloat16)
        for first in range(0, 2 * wide, 2 * HEAD_SIZE):
            lanes = slice(first, first + 2 * HEAD_SIZE)
            found = [
                contract(pick[:, row : row + ref.shape[0]], ref[:, lanes], 1, 0)
                for row, ref in block.items()
            ]
            listed_rows[at * share : (at + 1) * share, lanes] = sum(found).astype(jnp.bfloat16)
    fetch_veil.wait()
    scale = math.log2(math.e) / math.sqrt(HEAD_SIZE)

    def rows_of(group, row, first):
        lanes = slice(first, first + HEAD_SIZE)
        window = pl.ds(pl.multiple_of(group * share - row, 16), share)
        rows = [block[row][window, lanes] for block in blocks]
        return jnp.concatenate(rows + [listed_rows[:, lanes]], axis=0)

    def scores_of(group, row, head, tokens):
        left = jnp.concatenate([queries_ref[head, tokens], seen_by[...]], axis=1)
        keys = rows_of(group, row, head * HEAD_SIZE)
        return contract(left, jnp.concatenate([keys, veil[group]], axis=1), 1, 1)

    def products_of(group, row, head, weight):
        values = rows_of(group, row, wide + head * HEAD_SIZE)
        values = jnp.concatenate([values, jnp.ones_like(values)], axis=1)
        mixed = contract(weight, values, 1, 0)
        return mixed[:, :HEAD_SIZE], mixed[:, HEAD_SIZE:]

    def tile(top, keys):
        return jnp.concatenate([top] * (keys // HEAD_SIZE), axis=1)

    def finish_head(group, head, total, weight_sum):
        mixed = total / weight_sum
        seats = pl.ds(pl.multiple_of(group * stride, 16), spare)
        for at in range(HEAD_GROUPS):
            place = (head * HEAD_GROUPS + at) * HEAD_SIZE
            rows = mixed[at * spare : (at + 1) * spare]
            mixed_ref[seats, place : place + HEAD_SIZE] = rows.astype(jnp.bfloat16)

    def add_heads(group, row, some):
        tokens = pl.ds(pl.multiple_of(group * packed, 16), packed)
        scores = [scores_of(group, row, head, tokens) for head in some]
        tops, weights = [], []
        for head, score in zip(some, scores):
            top = jnp.max(score, axis=1, keepdims=True)
            if more:
                top = jnp.maximum(top_ref[head, tokens], top)
            else:
                top = jnp.broadcast_to(top, (packed, HEAD_SIZE))
            tops.append(top)
            weight = jnp.exp2((score - tile(top, score.shape[1])) * scale)
            weights.append(weight.astype(jnp.bfloat16))
        for head, top, weight in zip(some, tops, weights):
            total, weight_sum = products_of(group, row, head, weight)
            if more:
                fade = jnp.exp2((top_ref[head, tokens] - top) * scale)
                total = total + fade * total_ref[head, tokens]
                weight_sum = weight_sum + fade * sum_ref[head, tokens]
            if last:
                finish_head(group, head, total, weight_sum)
            else:
                new_top_ref[head, tokens] = top
                new_sum_ref[head, tokens] = weight_sum
                new_total_ref[head, tokens] = total

    def add_heads_as_before(group, row, worst):
        tokens = pl.ds(pl.multiple_of(group * packed, 16), packed)
        scores = [scores_of(group, row, head, tokens) for head in range(heads)]
        weights = []
        for head, score in enumerate(scores):
            above = score - tile(top_ref[head, tokens], score.shape[1])
            for first in range(0, score.shape[1], HEAD_SIZE):
                part = above[:, first : first + HEAD_SIZE].reshape(packed // 8, 8, HEAD_SIZE)
                worst = jnp.maximum(worst, jnp.max(part, axis=0))
            weights.append(jnp.exp2(above * scale).astype(jnp.bfloat16))
        for head, weight in enumerate(weights):
            total, weight_sum = products_of(group, row, head, weight)
            total = total + total_ref[head, tokens]
            weight_sum = weight_sum + sum_ref[head, tokens]
            finish_head(group, head, total, weight_sum)
        return worst

    firsts = sorted({row for first_rows in starts for row in first_rows})
    spans = [
        (row, row // share, end // share) for row, end in zip(firsts, firsts[1:] + [count])
    ]

    def add_all(together):
        for row, first, end in spans:

            def one_group(group, carry, row=row):
                for head in range(0, heads, together):
                    add_heads(group, row, range(head, head + together))
                return carry

            lax.fori_loop(first, end, one_group, 0)

    if not last:
        add_all(heads)
        return
    worst = jnp.full((8, HEAD_SIZE), MASKED, jnp.float32)
    for row, first, end in spans:
        worst = lax.fori_loop(
            first,
            end,
            lambda group, worst, row=row: add_heads_as_before(group, row, worst),
            worst,
        )

    @pl.when(jnp.max(worst) * scale > SAFE_POWER)
    def _():
        add_all(1)

    seat_lanes = lax.broadcasted_iota(jnp.int32, (count, mixed_ref.shape[0]), 1)
    seats = (seat_lanes == seat_ref[...]).astype(jnp.float32).astype(jnp.bfloat16)
    span = HEAD_GROUPS * HEAD_SIZE
    leaving = []
    for head in range(heads):
        lanes = slice(head * span, (head + 1) * span)
        rows = contract(seats, mixed_ref[:, lanes], 1, 0)
        result_ref[:, lanes] = rows.astype(jnp.bfloat16)
        lanes = pl.ds(head * span, span)
        leaving.append(
            pltpu.make_async_copy(result_ref.at[:, lanes], out_ref.at[:, lanes], leave.at[head])
        )
        leaving[-1].start()
    for one in leaving:
        one.wait()


def spread(block, ranks, held):
    ring = [(rank, (rank + PLANE) % ranks) for rank in range(ranks)]
    across = [(rank, rank ^ 2) for rank in range(ranks)]
    beside = [(rank, rank ^ 1) for rank in range(ranks)]
    steps = ranks // PLANE
    half = block.shape[0] // 32 * 16

    def keep(source, first, array):
        held.setdefault(source, []).append((first, array))
        held.setdefault(source + 2 * steps, []).append((first, lax.ppermute(array, "dp", beside)))

    lane, other = block, None
    for step in range(steps - 1):
        following = lax.ppermute(lane, "dp", ring), lax.ppermute(lane, "dp", across)
        keep(step, 0, lane)
        if step:
            keep(steps + step - 1, 0, other)
        extra = yield
        lane, other, extra = lax.optimization_barrier((*following, extra))
        yield extra
    over = lax.ppermute(lane[:half], "dp", across)
    around = lax.ppermute(other[half:], "dp", ring)
    keep(steps - 1, 0, lane)
    keep(2 * steps - 2, 0, other)
    extra = yield other
    over, around, extra = lax.optimization_barrier((over, around, extra))
    keep(2 * steps - 1, 0, over)
    keep(2 * steps - 1, half, around)
    yield extra


def source_order(ranks, sources):
    me = lax.axis_index("dp")
    lane, plane = lax.rem(me, PLANE), lax.div(me, PLANE)
    planes = ranks // PLANE
    steps = np.array([source % planes for source in sources], np.int32)
    flips = np.array([(0, 2, 1, 3)[source // planes] for source in sources], np.int32)
    return lax.rem(plane + (planes - steps), planes) * PLANE + (lane ^ flips)


def weight_order(ranks):
    me = lax.axis_index("dp")
    lane, plane = lax.rem(me, PLANE), lax.div(me, PLANE)
    planes = ranks // PLANE
    turn_back = lax.axis_index("groups") == 1
    up = np.array([0, 1, 0, planes - 1, 2, 1, 2, planes - 1] * 2, np.int32)
    steps = jnp.where(turn_back, (planes - up) % planes, up)
    flips = np.array([0, 0, 2, 0, 0, 2, 2, 2], np.int32)
    flips = np.concatenate([flips, flips ^ 1])
    return lax.rem(plane + (planes - steps), planes) * PLANE + (lane ^ flips)


def gather_plan(
    hidden,
    queries,
    route,
    positions,
    key_matrix,
    value_matrix,
    key_projection_bias,
    value_projection_bias,
):
    ranks = lax.axis_size("dp")
    rows = hidden.shape[0]
    slots = positions.shape[0]
    share, extra = rows // ranks, 2
    spare = share + extra
    listed = ranks * extra
    stride = -(-spare // 16) * 16
    packed = -(-HEAD_GROUPS * spare // 16) * 16
    query_width = queries.shape[1]
    shape = jax.ShapeDtypeStruct

    def columns(array, chunk):
        first, heads = chunk
        return array[..., first * HEAD_SIZE : (first + heads) * HEAD_SIZE]

    joined = pl.pallas_call(
        join_kernel,
        out_shape=shape((key_matrix.shape[0], 2 * key_matrix.shape[1]), jnp.bfloat16),
        in_specs=[HBM] * 2,
        out_specs=VMEM,
        scratch_shapes=[pltpu.SemaphoreType.DMA((2,))],
        compiler_params=grant(56),
        name="join",
    )(key_matrix, value_matrix)
    every = [(group, rank) for group in range(2) for rank in range(ranks)]
    ring = [
        (group * ranks + rank, group * ranks + (rank + (1 - 2 * group) * PLANE) % ranks)
        for group, rank in every
    ]
    across = [(group * ranks + rank, group * ranks + (rank ^ 2)) for group, rank in every]
    beside = [(group * ranks + rank, group * ranks + (rank ^ 1)) for group, rank in every]
    swap = [(group * ranks + rank, (1 - group) * ranks + rank) for group, rank in every]

    def send(array, pairs):
        return lax.ppermute(array, ("groups", "dp"), pairs)

    near_lane, other_row = send(joined, ring), send(joined, across)
    joined_swap = send(joined, beside)
    bucket, seat, sorted_route, more = pl.pallas_call(
        functools.partial(order_kernel, ranks, slots, extra, stride),
        out_shape=(
            shape((1, rows), jnp.int32),
            shape((1, rows), jnp.int32),
            shape((1, rows), jnp.int32),
            shape((2, listed), jnp.int32),
        ),
        in_specs=[VMEM],
        out_specs=(VMEM,) * 4,
        compiler_params=grant(14),
        name="order",
    )(route.reshape(1, rows))
    width = rows + 2 * listed
    plan = jnp.concatenate([sorted_route.reshape(rows), more.reshape(2 * listed), positions])
    plan = lax.all_to_all(
        jnp.broadcast_to(plan, (ranks, width + slots)), "dp", split_axis=0, concat_axis=0, tiled=True
    )
    near_lane, other_row, joined_swap, plan, bucket, seat = lax.optimization_barrier(
        (near_lane, other_row, joined_swap, plan, bucket, seat)
    )
    matrices = {0: (joined, joined_swap)}
    far_lane, next_lane = send(near_lane, swap), send(near_lane, ring)
    near_other = send(near_lane, across)
    swaps = send(near_lane, beside), send(other_row, beside)
    all_positions = plan[:, width:].reshape(-1, HEAD_SIZE)
    planes = ranks // PLANE
    sets = [(0, 2 * planes)] + [
        (step, step + 2 * planes, step + planes - 1, step + 3 * planes - 1)
        for step in range(1, planes)
    ]
    sets.append((2 * planes - 1, 4 * planes - 1))
    owners = weight_order(ranks)

    half = HEAD_SIZE // 2
    frequency = 1000000.0 ** (-(jnp.arange(half, dtype=jnp.float32) * 2.0 / HEAD_SIZE))
    turned, bounds, cosine, sine, seat_column = pl.pallas_call(
        functools.partial(query_kernel, ranks, spare, stride, packed),
        out_shape=(
            shape((KEY_VALUE_HEADS, ranks * packed, HEAD_SIZE), jnp.bfloat16),
            shape((ranks * stride, HEAD_SIZE), jnp.int32),
            shape((rows, HEAD_SIZE), jnp.float32),
            shape((rows, HEAD_SIZE), jnp.float32),
            shape((rows, 1), jnp.int32),
        ),
        in_specs=[VMEM] * 5,
        out_specs=(VMEM,) * 5,
        scratch_shapes=[pltpu.VMEM((ranks * packed, HEAD_SIZE), jnp.float32)],
        compiler_params=grant(14),
        cost_estimate=cost(4 * stride * ranks * rows * query_width, 4 * rows * query_width),
        name="turn_queries",
    )(
        route.reshape(rows, 1),
        seat,
        all_positions,
        jnp.concatenate([frequency, frequency]).reshape(1, HEAD_SIZE),
        queries,
    )

    shard, wide = key_matrix.shape[0], 2 * key_matrix.shape[1]

    def chip_parts(sources):
        chips = [(source, source + ranks // 2) for source in sources]
        return chips, [array for source in sources for array in matrices[source]]

    def scratch(chips, arrays):
        return [
            pltpu.VMEM((rows, 2 * shard * len(chips)), jnp.bfloat16),
            pltpu.VMEM((2 * shard * len(chips), wide), jnp.bfloat16),
            pltpu.SemaphoreType.DMA((len(chips) + len(arrays),)),
        ]

    def product_cost(chips):
        depth = 2 * shard * len(chips)
        return cost(2 * rows * depth * wide, 2 * depth * (rows + wide) + 8 * rows * wide)

    def add_part(total, sources):
        chips, arrays = chip_parts(sources)
        more = [] if total is None else [total]
        return pl.pallas_call(
            functools.partial(part_kernel, chips, bool(more)),
            out_shape=shape((rows, wide), jnp.float32),
            in_specs=[SMEM] + [HBM] * (1 + len(arrays)) + [VMEM] * len(more),
            out_specs=VMEM,
            scratch_shapes=scratch(chips, arrays),
            compiler_params=grant(14),
            cost_estimate=product_cost(chips),
            name="add_part",
        )(owners, hidden, *arrays, *more)

    bias = jnp.concatenate([key_projection_bias, value_projection_bias])
    bias = bias.astype(jnp.float32).reshape(1, -1)
    step = (far_lane, next_lane, near_other, swaps)
    step, turned, bounds, cosine, sine, seat_column, bias, owners = lax.optimization_barrier(
        (step, turned, bounds, cosine, sine, seat_column, bias, owners)
    )
    far_lane, next_lane, near_other, swaps = step
    matrices[1], matrices[2] = (near_lane, swaps[0]), (other_row, swaps[1])
    next_other, far_other = send(next_lane, across), send(near_other, swap)
    matrices[3] = (far_lane, send(far_lane, beside))
    matrices[4] = (next_lane, send(next_lane, beside))
    matrices[5] = (near_other, send(near_other, beside))
    total = add_part(add_part(None, (0, 1, 2)), (3, 4, 5))
    next_other, far_other, total = lax.optimization_barrier((next_other, far_other, total))
    matrices[6] = (next_other, send(next_other, beside))
    matrices[7] = (far_other, send(far_other, beside))
    chips, arrays = chip_parts((6, 7))
    (pairs,) = pl.pallas_call(
        functools.partial(finish_kernel, chips),
        out_shape=tuple(
            shape((rows, 2 * heads * HEAD_SIZE), jnp.bfloat16) for _, heads in CHUNKS
        ),
        in_specs=[SMEM, HBM] + [VMEM] * (5 + len(arrays)),
        out_specs=(VMEM,) * len(CHUNKS),
        scratch_shapes=scratch(chips, arrays),
        compiler_params=grant(14),
        cost_estimate=product_cost(chips),
        name="finish",
    )(
        owners,
        hidden,
        bias,
        cosine,
        sine,
        bucket,
        *arrays,
        total,
    )

    blocks = {}
    sending = spread(pairs, ranks, blocks)
    next(sending)
    order = [source for sources in sets for source in sources]
    ordered = plan[:, :width][source_order(ranks, order)]
    key_routes = ordered[:, :rows].reshape(ranks, ranks, share).transpose(1, 0, 2)
    more_places = ordered[:, rows + listed :].reshape(ranks * listed, 1)
    veils = pl.pallas_call(
        functools.partial(veil_kernel, sets, stride),
        out_shape=tuple(
            shape((ranks, 2 * share * len(sources), HEAD_SIZE), jnp.bfloat16) for sources in sets
        ),
        in_specs=[VMEM] * 3,
        out_specs=(VMEM,) * len(sets),
        compiler_params=grant(14),
        cost_estimate=cost(3 * 10**9, 4 * ranks * rows * HEAD_SIZE),
        name="veil",
    )(
        bounds,
        key_routes.reshape(ranks, 1, rows),
        ordered[:, rows : rows + listed].reshape(1, ranks * listed),
    )

    def attend(state, index):
        sources, last = sets[index], index == len(sets) - 1
        starts = [tuple(first for first, _ in blocks[source]) for source in sources]
        arrays = [array for source in sources for _, array in blocks[source]]
        keys = 2 * share * len(sources)
        fixed = [more_places, turned, veils[index], *arrays, *state]
        kept = shape((KEY_VALUE_HEADS, ranks * packed, HEAD_SIZE), jnp.float32)
        outs = [kept] * 3
        out_specs = [VMEM] * 3
        in_specs = [VMEM, VMEM, HBM] + [VMEM] * (len(fixed) - 3)
        handed = {len(fixed) - 3 + at: at + last for at in range(3)} if state else {}
        scratch_shapes = [
            pltpu.VMEM((len(sources) * share, wide), jnp.bfloat16),
            pltpu.VMEM((packed, HEAD_SIZE), jnp.bfloat16),
            pltpu.VMEM((ranks, keys, HEAD_SIZE), jnp.bfloat16),
            pltpu.SemaphoreType.DMA,
        ]
        if last:
            fixed.append(seat_column)
            in_specs.append(VMEM)
            outs.insert(0, shape((rows, query_width), jnp.bfloat16))
            out_specs.insert(0, HBM)
            scratch_shapes += [
                pltpu.VMEM((ranks * stride, query_width), jnp.bfloat16),
                pltpu.VMEM((rows, query_width), jnp.bfloat16),
                pltpu.SemaphoreType.DMA((KEY_VALUE_HEADS,)),
            ]
        return pl.pallas_call(
            functools.partial(
                attend_kernel,
                starts,
                sum(len(one) for one in sets[:index]),
                spare,
                stride,
                bool(state),
                last,
            ),
            out_shape=tuple(outs),
            in_specs=in_specs,
            out_specs=tuple(out_specs),
            scratch_shapes=scratch_shapes,
            input_output_aliases=handed,
            compiler_params=grant(18 if last else 14),
            cost_estimate=cost(
                8 * ranks * KEY_VALUE_HEADS * packed * (keys + 256) * HEAD_SIZE,
                2 * keys * rows * HEAD_SIZE,
            ),
            name="attend",
        )(*fixed)

    state = ()
    for step in range(planes - 1):
        if step:
            next(sending)
        state = sending.send(tuple(attend(state, step)))
    next(sending)
    state = sending.send(tuple(attend(state, planes - 1)))
    return attend(state, planes)[0]


def apply_rotary(rows, slot_offset, heads):
    block_count = rows.shape[0]
    half = HEAD_SIZE // 2
    frequency = 1000000.0 ** (-(jnp.arange(half, dtype=jnp.float32) * 2.0 / HEAD_SIZE))
    angle = slot_offset.astype(jnp.float32)[:, None] * frequency[None, :]
    cosine = jnp.cos(angle)[:, None, :]
    sine = jnp.sin(angle)[:, None, :]
    grid = rows.astype(jnp.float32).reshape(block_count, heads, HEAD_SIZE)
    first = grid[:, :, :half]
    second = grid[:, :, half:]
    turned = jnp.concatenate(
        [first * cosine - second * sine, second * cosine + first * sine], axis=2
    )
    return turned.reshape(block_count, heads * HEAD_SIZE).astype(jnp.bfloat16)


def causal_block_attention(pieces):
    query_tile_rows, key_tile_rows, value_tile_rows, spot_block = pieces
    block_count = query_tile_rows.shape[0]
    head_groups = QUERY_HEADS // KEY_VALUE_HEADS
    query_block_grid = query_tile_rows.reshape(block_count, KEY_VALUE_HEADS, head_groups, HEAD_SIZE)
    key_block_grid = key_tile_rows.reshape(block_count, KEY_VALUE_HEADS, HEAD_SIZE)
    value_block_grid = value_tile_rows.reshape(block_count, KEY_VALUE_HEADS, HEAD_SIZE)
    scores = jnp.einsum(
        "qhgd,khd->hgqk", query_block_grid, key_block_grid, preferred_element_type=jnp.float32
    ) / math.sqrt(HEAD_SIZE)
    inner = jnp.arange(block_count, dtype=jnp.int32)
    visible = (inner[None, :] <= inner[:, None]) & (
        inner[None, :] >= inner[:, None] - spot_block[:, None]
    )
    scores = jnp.where(visible, scores, -jnp.inf)
    top = jnp.max(scores, axis=3, keepdims=True)
    weights = jnp.exp(scores - top)
    totals = jnp.sum(weights, axis=3)
    probs = weights.astype(jnp.bfloat16)
    mixed = jnp.einsum(
        "hgqk,khd->qhgd", probs, value_block_grid, preferred_element_type=jnp.float32
    )
    mixed = mixed / jnp.transpose(totals, (2, 0, 1))[:, :, :, None]
    return mixed.reshape(block_count, QUERY_HEADS * HEAD_SIZE).astype(jnp.bfloat16)


def add_projection(left, pieces):
    return (
        jnp.dot(left, pieces[0], preferred_element_type=jnp.float32),
        jnp.dot(left, pieces[1], preferred_element_type=jnp.float32),
    )


def project_own(hidden, key_matrix, value_matrix, key_projection_bias, value_projection_bias):
    totals = add_projection(
        hidden,
        (
            lax.all_gather(key_matrix, "dp", axis=0, tiled=True),
            lax.all_gather(value_matrix, "dp", axis=0, tiled=True),
        ),
    )
    key_rows = (totals[0] + key_projection_bias.astype(jnp.float32)).astype(jnp.bfloat16)
    value_rows = (totals[1] + value_projection_bias.astype(jnp.float32)).astype(jnp.bfloat16)
    return jnp.concatenate([key_rows, value_rows], axis=1)


def send_plan(
    hidden,
    queries,
    route,
    positions,
    key_matrix,
    value_matrix,
    key_projection_bias,
    value_projection_bias,
):
    ranks = lax.axis_size("dp")
    rows = hidden.shape[0]
    slots = positions.shape[0]
    spare = rows // ranks + 2
    width = ranks * spare
    paired_width = key_matrix.shape[1]
    target = route // slots
    place = route - target * slots
    member = (target[:, None] == jnp.arange(ranks, dtype=jnp.int32)[None, :]).astype(jnp.int32)
    order = jnp.sum(jnp.cumsum(member, axis=0) * member, axis=1) - 1
    bucket = target * spare + order
    outgoing = jnp.full((width,), slots, jnp.int32).at[bucket].set(place)
    arrived = lax.all_to_all(
        outgoing.reshape(ranks, spare), "dp", split_axis=0, concat_axis=0, tiled=True
    ).reshape(width)
    query_buf = jnp.zeros((width, queries.shape[1]), jnp.bfloat16).at[bucket].set(queries)
    own_pairs = project_own(
        hidden, key_matrix, value_matrix, key_projection_bias, value_projection_bias
    )
    pair_buf = jnp.zeros((width, 2 * paired_width), jnp.bfloat16).at[bucket].set(own_pairs)
    got_query, got_pairs = (
        lax.all_to_all(
            query_buf.reshape(ranks, spare, -1), "dp", split_axis=0, concat_axis=0, tiled=True
        ),
        lax.all_to_all(
            pair_buf.reshape(ranks, spare, -1), "dp", split_axis=0, concat_axis=0, tiled=True
        ),
    )
    got_query = got_query.reshape(width, -1)
    got_pairs = got_pairs.reshape(width, -1)
    query_slot_rows = (
        jnp.zeros((slots, got_query.shape[1]), jnp.bfloat16).at[arrived].set(got_query, mode="drop")
    )
    paired_slot_rows = (
        jnp.zeros((slots, 2 * paired_width), jnp.bfloat16).at[arrived].set(got_pairs, mode="drop")
    )
    query_turned = apply_rotary(query_slot_rows, positions, QUERY_HEADS)
    key_rotated = apply_rotary(paired_slot_rows[:, :paired_width], positions, KEY_VALUE_HEADS)
    block_list = slots // BLOCK_SLOTS
    attended = lax.map(
        causal_block_attention,
        (
            query_turned.reshape(block_list, BLOCK_SLOTS, -1),
            key_rotated.reshape(block_list, BLOCK_SLOTS, -1),
            paired_slot_rows[:, paired_width:].reshape(block_list, BLOCK_SLOTS, -1),
            positions.reshape(block_list, BLOCK_SLOTS),
        ),
    )
    attended = attended.reshape(slots, -1)
    leaving = attended[jnp.minimum(arrived, slots - 1)]
    returned = lax.all_to_all(
        leaving.reshape(ranks, spare, -1), "dp", split_axis=0, concat_axis=0, tiled=True
    ).reshape(width, -1)
    return returned[bucket]


def local(*args):
    hidden, queries, _, positions, key_matrix = args[:5]
    ranks = lax.axis_size("dp")
    rows = hidden.shape[0]
    gathered = ranks * ranks * (rows // ranks + 2) * 4 * key_matrix.shape[1]
    chip_rows = 2 * key_matrix.shape[0]
    fits = rows % (16 * ranks) == 0 and chip_rows % HEAD_SIZE == 0 and gathered <= GATHER_LIMIT
    if ranks == PLANES * PLANE and lax.axis_size("groups") == 2 and fits:
        return gather_plan(*args)
    return send_plan(*args)


def solution(mesh):
    placed = (
        P(("groups", "dp"), None),
        P(("groups", "dp"), None),
        P(("groups", "dp")),
        P(("groups", "dp")),
        P("dp", None),
        P("dp", None),
        P(),
        P(),
    )
    return jax.shard_map(
        local, mesh=mesh, in_specs=placed, out_specs=P(("groups", "dp"), None), check_vma=False
    )
```

```python
import functools
import math

import jax
import jax.numpy as jnp
import numpy as np
from jax import lax
from jax.experimental import pallas as pl
from jax.experimental.pallas import tpu as pltpu
from jax.sharding import PartitionSpec as P

QUERY_HEADS = 20
KEY_VALUE_HEADS = 4
HEAD_SIZE = 128
BLOCK_SLOTS = 512
HEAD_GROUPS = QUERY_HEADS // KEY_VALUE_HEADS
CHUNKS = ((0, KEY_VALUE_HEADS),)
PLANE = 4
PLANES = 4
SAFE_POWER = 64.0
GATHER_LIMIT = 40 * 2**20
MASKED = -1e30
VMEM = pl.BlockSpec(memory_space=pltpu.VMEM)
SMEM = pl.BlockSpec(memory_space=pltpu.SMEM)
HBM = pl.BlockSpec(memory_space=pltpu.HBM)


def grant(mebibytes):
    return pltpu.CompilerParams(vmem_limit_bytes=mebibytes * 2**20)


def cost(flops, moved):
    return pl.CostEstimate(flops=flops, bytes_accessed=moved, transcendentals=0)


def one_hot_rows(count, index_row):
    rows = lax.broadcasted_iota(jnp.int32, (count, index_row.shape[1]), 0)
    return (rows == index_row).astype(jnp.float32).astype(jnp.bfloat16)


def split(number):
    high = lax.shift_right_logical(number, HEAD_SIZE.bit_length() - 1)
    return high, number - high * HEAD_SIZE


def contract(left, right, left_dim, right_dim):
    return lax.dot_general(
        left, right, (((left_dim,), (right_dim,)), ((), ())), preferred_element_type=jnp.float32
    )


def turn(rows, cosine, sine):
    return (rows * cosine + pltpu.roll(rows, HEAD_SIZE // 2, 1) * sine).astype(jnp.bfloat16)


def join_kernel(left_ref, right_ref, out_ref, done):
    wide = left_ref.shape[1]
    copies = [
        pltpu.make_async_copy(ref, out_ref.at[:, pl.ds(at * wide, wide)], done.at[at])
        for at, ref in enumerate((left_ref, right_ref))
    ]
    for copy in copies:
        copy.start()
    for copy in copies:
        copy.wait()


def order_kernel(
    ranks, slots, extra, stride, route_ref, bucket_ref, seat_ref, sorted_ref, more_ref
):
    route = route_ref[...]
    count = route.shape[1]
    share = count // ranks
    target = lax.div(route, slots)
    member = (lax.broadcasted_iota(jnp.int32, (ranks, count), 0) == target).astype(jnp.float32)
    before = lax.broadcasted_iota(jnp.int32, (count, count), 0) < lax.broadcasted_iota(
        jnp.int32, (count, count), 1
    )
    before = before.astype(jnp.float32).astype(jnp.bfloat16)
    ahead = contract(member.astype(jnp.bfloat16), before, 1, 0)
    order = jnp.sum(member * ahead, axis=0, keepdims=True).astype(jnp.int32)
    beyond = order >= share
    beyond_rows = jnp.broadcast_to(beyond.astype(jnp.float32), (8, count)).astype(jnp.bfloat16)
    number = contract(beyond_rows, before, 1, 0)[0:1]
    counts = jnp.sum(member, axis=1, keepdims=True)
    free = jnp.maximum(share - counts, 0.0)
    group = lax.broadcasted_iota(jnp.int32, (ranks, ranks), 0)
    lower = (group > lax.broadcasted_iota(jnp.int32, (ranks, ranks), 1)).astype(jnp.float32)
    free_rows = jnp.broadcast_to(free, (ranks, HEAD_SIZE)).astype(jnp.bfloat16)
    free_before = contract(lower.astype(jnp.bfloat16), free_rows, 1, 0)[:, 0:1]
    inside = (number >= free_before) & (number < free_before + free)
    base = lax.broadcasted_iota(jnp.int32, (ranks, 1), 0).astype(jnp.float32) * share + counts
    hole = jnp.sum(jnp.where(inside, base + number - free_before, 0.0), axis=0, keepdims=True)
    bucket = jnp.where(beyond, hole.astype(jnp.int32), target * share + order)
    bucket_ref[...] = bucket
    seat_ref[...] = target * stride + order
    high, low = split(route)
    place_high, place_low = split(bucket)
    line = lax.broadcasted_iota(jnp.int32, (8, count), 0)
    digits = jnp.where(line == 0, high, 0)
    digits = jnp.where(line == 1, low, digits)
    digits = jnp.where(line == 2, place_high, digits)
    digits = jnp.where(line == 3, place_low, digits)
    digits = jnp.where(line == 4, 1, digits).astype(jnp.float32).astype(jnp.bfloat16)
    placed = contract(digits, one_hot_rows(count, bucket), 1, 1)
    sorted_ref[...] = (placed[0:1] * HEAD_SIZE + placed[1:2]).astype(jnp.int32)
    listed = jnp.where(beyond, target * extra + order - share, -1)
    found = contract(digits, one_hot_rows(ranks * extra, listed), 1, 1)
    none = found[4:5] - 1.0
    more_ref[0:1] = (found[0:1] * HEAD_SIZE + found[1:2] + none).astype(jnp.int32)
    more_ref[1:2] = (found[2:3] * HEAD_SIZE + found[3:4] + none).astype(jnp.int32)


def query_kernel(
    ranks, spare, stride, packed, route_ref, seat_ref, positions_ref, frequency_ref, queries_ref, *refs
):
    turned_ref, bounds_ref, cosine_ref, sine_ref, column_ref, rows_ref = refs
    route = route_ref[...]
    count = route.shape[0]
    lines = positions_ref.shape[0]
    line, lane = split(route)
    pick = (lax.broadcasted_iota(jnp.int32, (count, lines), 1) == line).astype(jnp.float32)
    pick = pick.astype(jnp.bfloat16)
    positions = positions_ref[...]
    half = lax.shift_right_logical(positions, 1)
    rest = positions - half * 2
    rows = 2.0 * contract(pick, half.astype(jnp.float32).astype(jnp.bfloat16), 1, 0) + contract(
        pick, rest.astype(jnp.float32).astype(jnp.bfloat16), 1, 0
    )
    lanes = lax.broadcasted_iota(jnp.int32, (count, HEAD_SIZE), 1)
    spot = jnp.sum(jnp.where(lanes == lane, rows, 0.0), axis=1, keepdims=True)
    angle = spot * frequency_ref[...]
    cosine = jnp.cos(angle)
    sine = jnp.sin(angle)
    sine = jnp.where(lanes < HEAD_SIZE // 2, -sine, sine)
    cosine_ref[...] = cosine
    sine_ref[...] = sine
    seats = one_hot_rows(ranks * stride, seat_ref[...])
    seat_line, seat_lane = split(seat_ref[...])
    digit = lax.broadcasted_iota(jnp.int32, (8, count), 0)
    digits = jnp.where(digit == 0, seat_line, jnp.where(digit == 1, seat_lane, 0))
    same = one_hot_rows(count, lax.broadcasted_iota(jnp.int32, (1, count), 1))
    column = contract(same, digits.astype(jnp.float32).astype(jnp.bfloat16), 1, 1)
    column_ref[...] = (column[:, 0:1] * HEAD_SIZE + column[:, 1:2]).astype(jnp.int32)
    first = route - spot.astype(jnp.int32)
    first_line, first_lane = split(first)
    digits = jnp.where(lanes == 0, line, 0)
    digits = jnp.where(lanes == 1, lane, digits)
    digits = jnp.where(lanes == 2, first_line, digits)
    digits = jnp.where(lanes == 3, first_lane, digits)
    digits = jnp.where(lanes == 4, 1, digits)
    placed = contract(seats, digits.astype(jnp.float32).astype(jnp.bfloat16), 1, 0)
    live = placed[:, 4:5] - 1.0
    last = placed[:, 0:1] * HEAD_SIZE + placed[:, 1:2] + live
    start = placed[:, 2:3] * HEAD_SIZE + placed[:, 3:4] - live * 2.0**20
    seat_lanes = lax.broadcasted_iota(jnp.int32, placed.shape, 1)
    bounds_ref[...] = jnp.where(seat_lanes == 0, last, start).astype(jnp.int32)
    rows_ref[...] = jnp.zeros(rows_ref.shape, jnp.float32)
    for head in range(KEY_VALUE_HEADS):
        for place in range(HEAD_GROUPS):
            at = (head * HEAD_GROUPS + place) * HEAD_SIZE
            one = queries_ref[:, at : at + HEAD_SIZE].astype(jnp.float32)
            rows = contract(seats, turn(one, cosine, sine), 1, 0)
            for group in range(ranks):
                at = group * packed + place * spare
                rows_ref[at : at + spare] = rows[group * stride : group * stride + spare]
        turned_ref[head] = rows_ref[...].astype(jnp.bfloat16)


def fetch_columns(chips, owners_ref, hidden_ref, columns, done):
    deep = columns.shape[1] // len(chips)
    copies = []
    for place, chip in enumerate(chips):
        first = pl.multiple_of(lax.div(owners_ref[chip[0]], 2) * deep, HEAD_SIZE)
        copies.append(
            pltpu.make_async_copy(
                hidden_ref.at[:, pl.ds(first, deep)],
                columns.at[:, pl.ds(place * deep, deep)],
                done.at[place],
            )
        )
        copies[-1].start()
    return copies


def place_rows(owners_ref, chips, matrix):
    shard = matrix.shape[0] // len(chips) // 2
    return [
        pl.ds(pl.multiple_of((2 * place + lax.rem(owners_ref[source], 2)) * shard, 16), shard)
        for place, chip in enumerate(chips)
        for source in chip
    ]


def part_kernel(chips, more, owners_ref, hidden_ref, *refs):
    count = 2 * len(chips)
    parts, refs = refs[:count], refs[count:]
    if more:
        total_ref, refs = refs[0], refs[1:]
    out_ref, columns, matrix, done = refs
    copies = fetch_columns(chips, owners_ref, hidden_ref, columns, done)
    for at, (ref, rows) in enumerate(zip(parts, place_rows(owners_ref, chips, matrix))):
        copies.append(pltpu.make_async_copy(ref, matrix.at[rows], done.at[len(chips) + at]))
        copies[-1].start()
    for copy in copies:
        copy.wait()
    for first in range(0, out_ref.shape[1], 2 * HEAD_SIZE):
        span = slice(first, first + 2 * HEAD_SIZE)
        product = contract(columns[...], matrix[:, span], 1, 0)
        out_ref[:, span] = total_ref[:, span] + product if more else product


def finish_kernel(
    chips, owners_ref, hidden_ref, bias_ref, cosine_ref, sine_ref, bucket_ref, *refs
):
    count = 2 * len(chips)
    parts, total_ref = refs[:count], refs[count]
    outs, (columns, matrix, done) = refs[count + 1 : -3], refs[-3:]
    copies = fetch_columns(chips, owners_ref, hidden_ref, columns, done)
    for ref, rows in zip(parts, place_rows(owners_ref, chips, matrix)):
        matrix[rows] = ref[...]
    places = one_hot_rows(outs[0].shape[0], bucket_ref[...])
    for copy in copies:
        copy.wait()
    wide = KEY_VALUE_HEADS * HEAD_SIZE
    for first in range(0, 2 * wide, 2 * HEAD_SIZE):
        span = slice(first, first + 2 * HEAD_SIZE)
        rows = contract(columns[...], matrix[:, span], 1, 0) + total_ref[:, span]
        rows = (rows + bias_ref[:, span]).astype(jnp.bfloat16)
        if first < wide:
            cosine, sine = cosine_ref[...], sine_ref[...]
            halves = [
                turn(rows[:, at : at + HEAD_SIZE].astype(jnp.float32), cosine, sine)
                for at in (0, HEAD_SIZE)
            ]
            rows = jnp.concatenate(halves, axis=1)
        rows = contract(places, rows, 1, 0).astype(jnp.bfloat16)
        for half in range(2):
            head = first % wide // HEAD_SIZE + half
            for (first_head, heads), out_ref in zip(CHUNKS, outs):
                if first_head <= head < first_head + heads:
                    at = (head - first_head + first // wide * heads) * HEAD_SIZE
                    out_ref[:, at : at + HEAD_SIZE] = rows[
                        :, half * HEAD_SIZE : (half + 1) * HEAD_SIZE
                    ]


def veil_kernel(sets, stride, bounds_ref, routes_ref, more_ref, *veil_refs):
    rest = jnp.zeros((HEAD_SIZE - stride, more_ref.shape[1]), jnp.float32)
    share = routes_ref.shape[2] // routes_ref.shape[0]

    def one_group(group, carry):
        seats = pl.ds(pl.multiple_of(group * stride, 16), stride)
        last, start = bounds_ref[seats, 0:1], bounds_ref[seats, 1:2]
        both = []
        for routes in (routes_ref[group], more_ref[...]):
            veil = jnp.where((routes <= last) & (routes >= start), 0.0, MASKED)
            veil = jnp.transpose(jnp.concatenate([veil, rest], axis=0))
            both.append(veil.astype(jnp.bfloat16))
        first = 0
        for sources, veil_ref in zip(sets, veil_refs):
            end = first + len(sources) * share
            veil_ref[group] = jnp.concatenate([veil[first:end] for veil in both], axis=0)
            first = end
        return carry

    lax.fori_loop(0, routes_ref.shape[0], one_group, 0)


def attend_kernel(starts, before, spare, stride, more, last, *refs):
    more_ref, queries_ref, veil_ref = refs[:3]
    refs = refs[3:]
    blocks = []
    for first_rows in starts:
        blocks.append(dict(zip(first_rows, refs)))
        refs = refs[len(first_rows) :]
    if more:
        top_ref, sum_ref, total_ref = refs[:3]
        refs = refs[3:]
    if last:
        seat_ref, out_ref, mixed_ref, result_ref, leave = refs[0], refs[1], *refs[-3:]
        refs = refs[:-3]
        mixed_ref[...] = jnp.zeros(mixed_ref.shape, jnp.bfloat16)
    else:
        new_top_ref, new_sum_ref, new_total_ref = refs[:3]
    listed_rows, seen_by, veil, veil_in = refs[-4:]
    fetch_veil = pltpu.make_async_copy(veil_ref, veil, veil_in)
    fetch_veil.start()
    heads, ranks = queries_ref.shape[0], veil_ref.shape[0]
    packed = queries_ref.shape[1] // ranks
    wide = heads * HEAD_SIZE
    share = listed_rows.shape[0] // len(starts)
    count = share * ranks

    token = lax.broadcasted_iota(jnp.int32, (packed, HEAD_SIZE), 0)
    lane = lax.broadcasted_iota(jnp.int32, (packed, HEAD_SIZE), 1)
    own = lane < 0
    for at in range(HEAD_GROUPS):
        own = own | ((token == lane + at * spare) & (lane < spare))
    seen_by[...] = own.astype(jnp.float32).astype(jnp.bfloat16)
    lines = lax.broadcasted_iota(jnp.int32, (share, count), 1)
    for at, block in enumerate(blocks):
        places = more_ref[(before + at) * share : (before + at + 1) * share]
        pick = (lines == places).astype(jnp.float32).astype(jnp.bfloat16)
        for first in range(0, 2 * wide, 2 * HEAD_SIZE):
            lanes = slice(first, first + 2 * HEAD_SIZE)
            found = [
                contract(pick[:, row : row + ref.shape[0]], ref[:, lanes], 1, 0)
                for row, ref in block.items()
            ]
            listed_rows[at * share : (at + 1) * share, lanes] = sum(found).astype(jnp.bfloat16)
    fetch_veil.wait()
    scale = math.log2(math.e) / math.sqrt(HEAD_SIZE)

    def rows_of(group, row, first):
        lanes = slice(first, first + HEAD_SIZE)
        window = pl.ds(pl.multiple_of(group * share - row, 16), share)
        rows = [block[row][window, lanes] for block in blocks]
        return jnp.concatenate(rows + [listed_rows[:, lanes]], axis=0)

    def scores_of(group, row, head, tokens):
        left = jnp.concatenate([queries_ref[head, tokens], seen_by[...]], axis=1)
        keys = rows_of(group, row, head * HEAD_SIZE)
        return contract(left, jnp.concatenate([keys, veil[group]], axis=1), 1, 1)

    def products_of(group, row, head, weight):
        values = rows_of(group, row, wide + head * HEAD_SIZE)
        values = jnp.concatenate([values, jnp.ones_like(values)], axis=1)
        mixed = contract(weight, values, 1, 0)
        return mixed[:, :HEAD_SIZE], mixed[:, HEAD_SIZE:]

    def tile(top, keys):
        return jnp.concatenate([top] * (keys // HEAD_SIZE), axis=1)

    def finish_head(group, head, total, weight_sum):
        mixed = total / weight_sum
        seats = pl.ds(pl.multiple_of(group * stride, 16), spare)
        for at in range(HEAD_GROUPS):
            place = (head * HEAD_GROUPS + at) * HEAD_SIZE
            rows = mixed[at * spare : (at + 1) * spare]
            mixed_ref[seats, place : place + HEAD_SIZE] = rows.astype(jnp.bfloat16)

    def add_heads(group, row, some):
        tokens = pl.ds(pl.multiple_of(group * packed, 16), packed)
        scores = [scores_of(group, row, head, tokens) for head in some]
        tops, weights = [], []
        for head, score in zip(some, scores):
            top = jnp.max(score, axis=1, keepdims=True)
            if more:
                top = jnp.maximum(top_ref[head, tokens], top)
            else:
                top = jnp.broadcast_to(top, (packed, HEAD_SIZE))
            tops.append(top)
            weight = jnp.exp2((score - tile(top, score.shape[1])) * scale)
            weights.append(weight.astype(jnp.bfloat16))
        for head, top, weight in zip(some, tops, weights):
            total, weight_sum = products_of(group, row, head, weight)
            if more:
                fade = jnp.exp2((top_ref[head, tokens] - top) * scale)
                total = total + fade * total_ref[head, tokens]
                weight_sum = weight_sum + fade * sum_ref[head, tokens]
            if last:
                finish_head(group, head, total, weight_sum)
            else:
                new_top_ref[head, tokens] = top
                new_sum_ref[head, tokens] = weight_sum
                new_total_ref[head, tokens] = total

    def add_heads_as_before(group, row, worst):
        tokens = pl.ds(pl.multiple_of(group * packed, 16), packed)
        scores = [scores_of(group, row, head, tokens) for head in range(heads)]
        weights = []
        for head, score in enumerate(scores):
            above = score - tile(top_ref[head, tokens], score.shape[1])
            for first in range(0, score.shape[1], HEAD_SIZE):
                part = above[:, first : first + HEAD_SIZE].reshape(packed // 8, 8, HEAD_SIZE)
                worst = jnp.maximum(worst, jnp.max(part, axis=0))
            weights.append(jnp.exp2(above * scale).astype(jnp.bfloat16))
        for head, weight in enumerate(weights):
            total, weight_sum = products_of(group, row, head, weight)
            total = total + total_ref[head, tokens]
            weight_sum = weight_sum + sum_ref[head, tokens]
            finish_head(group, head, total, weight_sum)
        return worst

    firsts = sorted({row for first_rows in starts for row in first_rows})
    spans = [
        (row, row // share, end // share) for row, end in zip(firsts, firsts[1:] + [count])
    ]

    def add_all(together):
        for row, first, end in spans:

            def one_group(group, carry, row=row):
                for head in range(0, heads, together):
                    add_heads(group, row, range(head, head + together))
                return carry

            lax.fori_loop(first, end, one_group, 0)

    if not last:
        add_all(heads)
        return
    worst = jnp.full((8, HEAD_SIZE), MASKED, jnp.float32)
    for row, first, end in spans:
        worst = lax.fori_loop(
            first,
            end,
            lambda group, worst, row=row: add_heads_as_before(group, row, worst),
            worst,
        )

    @pl.when(jnp.max(worst) * scale > SAFE_POWER)
    def _():
        add_all(1)

    seat_lanes = lax.broadcasted_iota(jnp.int32, (count, mixed_ref.shape[0]), 1)
    seats = (seat_lanes == seat_ref[...]).astype(jnp.float32).astype(jnp.bfloat16)
    span = HEAD_GROUPS * HEAD_SIZE
    leaving = []
    for head in range(heads):
        lanes = slice(head * span, (head + 1) * span)
        rows = contract(seats, mixed_ref[:, lanes], 1, 0)
        result_ref[:, lanes] = rows.astype(jnp.bfloat16)
        lanes = pl.ds(head * span, span)
        leaving.append(
            pltpu.make_async_copy(result_ref.at[:, lanes], out_ref.at[:, lanes], leave.at[head])
        )
        leaving[-1].start()
    for one in leaving:
        one.wait()


def spread(block, ranks, held):
    ring = [(rank, (rank + PLANE) % ranks) for rank in range(ranks)]
    across = [(rank, rank ^ 2) for rank in range(ranks)]
    beside = [(rank, rank ^ 1) for rank in range(ranks)]
    steps = ranks // PLANE
    half = block.shape[0] // 32 * 18

    def keep(source, first, array):
        held.setdefault(source, []).append((first, array))
        held.setdefault(source + 2 * steps, []).append((first, lax.ppermute(array, "dp", beside)))

    lane, other = block, None
    for step in range(steps - 1):
        keep(step, 0, lane)
        if step:
            keep(steps + step - 1, 0, other)
        following = lax.ppermute(lane, "dp", across), lax.ppermute(lane, "dp", ring)
        extra = yield
        other, lane, extra = lax.optimization_barrier((*following, extra))
        yield extra
    keep(steps - 1, 0, lane)
    keep(2 * steps - 2, 0, other)
    over = lax.ppermute(lane[:half], "dp", across)
    around = lax.ppermute(other[half:], "dp", ring)
    extra = yield other
    over, around, extra = lax.optimization_barrier((over, around, extra))
    keep(2 * steps - 1, 0, over)
    keep(2 * steps - 1, half, around)
    yield extra


def source_order(ranks, sources):
    me = lax.axis_index("dp")
    lane, plane = lax.rem(me, PLANE), lax.div(me, PLANE)
    planes = ranks // PLANE
    steps = np.array([source % planes for source in sources], np.int32)
    flips = np.array([(0, 2, 1, 3)[source // planes] for source in sources], np.int32)
    return lax.rem(plane + (planes - steps), planes) * PLANE + (lane ^ flips)


def weight_order(ranks):
    me = lax.axis_index("dp")
    lane, plane = lax.rem(me, PLANE), lax.div(me, PLANE)
    planes = ranks // PLANE
    turn_back = lax.axis_index("groups") == 1
    up = np.array([0, 1, 0, planes - 1, 2, 1, 2, planes - 1] * 2, np.int32)
    steps = jnp.where(turn_back, (planes - up) % planes, up)
    flips = np.array([0, 0, 2, 0, 0, 2, 2, 2], np.int32)
    flips = np.concatenate([flips, flips ^ 1])
    return lax.rem(plane + (planes - steps), planes) * PLANE + (lane ^ flips)


def gather_plan(
    hidden,
    queries,
    route,
    positions,
    key_matrix,
    value_matrix,
    key_projection_bias,
    value_projection_bias,
):
    ranks = lax.axis_size("dp")
    rows = hidden.shape[0]
    slots = positions.shape[0]
    share, extra = rows // ranks, 2
    spare = share + extra
    listed = ranks * extra
    stride = -(-spare // 16) * 16
    packed = -(-HEAD_GROUPS * spare // 16) * 16
    query_width = queries.shape[1]
    shape = jax.ShapeDtypeStruct

    def columns(array, chunk):
        first, heads = chunk
        return array[..., first * HEAD_SIZE : (first + heads) * HEAD_SIZE]

    joined = pl.pallas_call(
        join_kernel,
        out_shape=shape((key_matrix.shape[0], 2 * key_matrix.shape[1]), jnp.bfloat16),
        in_specs=[HBM] * 2,
        out_specs=VMEM,
        scratch_shapes=[pltpu.SemaphoreType.DMA((2,))],
        compiler_params=grant(56),
        name="join",
    )(key_matrix, value_matrix)
    every = [(group, rank) for group in range(2) for rank in range(ranks)]
    ring = [
        (group * ranks + rank, group * ranks + (rank + (1 - 2 * group) * PLANE) % ranks)
        for group, rank in every
    ]
    across = [(group * ranks + rank, group * ranks + (rank ^ 2)) for group, rank in every]
    beside = [(group * ranks + rank, group * ranks + (rank ^ 1)) for group, rank in every]
    swap = [(group * ranks + rank, (1 - group) * ranks + rank) for group, rank in every]

    def send(array, pairs):
        return lax.ppermute(array, ("groups", "dp"), pairs)

    joined_swap = send(joined, beside)
    other_row, near_lane = send(joined, across), send(joined, ring)
    bucket, seat, sorted_route, more = pl.pallas_call(
        functools.partial(order_kernel, ranks, slots, extra, stride),
        out_shape=(
            shape((1, rows), jnp.int32),
            shape((1, rows), jnp.int32),
            shape((1, rows), jnp.int32),
            shape((2, listed), jnp.int32),
        ),
        in_specs=[VMEM],
        out_specs=(VMEM,) * 4,
        compiler_params=grant(14),
        name="order",
    )(route.reshape(1, rows))
    width = rows + 2 * listed
    plan = jnp.concatenate([sorted_route.reshape(rows), more.reshape(2 * listed), positions])
    plan = lax.all_to_all(
        jnp.broadcast_to(plan, (ranks, width + slots)), "dp", split_axis=0, concat_axis=0, tiled=True
    )
    other_row, near_lane, joined_swap, plan, bucket, seat = lax.optimization_barrier(
        (other_row, near_lane, joined_swap, plan, bucket, seat)
    )
    matrices = {0: (joined, joined_swap)}
    swaps = send(near_lane, beside), send(other_row, beside)
    far_lane, near_other = send(near_lane, swap), send(near_lane, across)
    next_lane = send(near_lane, ring)
    all_positions = plan[:, width:].reshape(-1, HEAD_SIZE)
    planes = ranks // PLANE
    sets = [(0, 2 * planes)] + [
        (step, step + 2 * planes, step + planes - 1, step + 3 * planes - 1)
        for step in range(1, planes)
    ]
    sets.append((2 * planes - 1, 4 * planes - 1))
    owners = weight_order(ranks)

    half = HEAD_SIZE // 2
    frequency = 1000000.0 ** (-(jnp.arange(half, dtype=jnp.float32) * 2.0 / HEAD_SIZE))
    turned, bounds, cosine, sine, seat_column = pl.pallas_call(
        functools.partial(query_kernel, ranks, spare, stride, packed),
        out_shape=(
            shape((KEY_VALUE_HEADS, ranks * packed, HEAD_SIZE), jnp.bfloat16),
            shape((ranks * stride, HEAD_SIZE), jnp.int32),
            shape((rows, HEAD_SIZE), jnp.float32),
            shape((rows, HEAD_SIZE), jnp.float32),
            shape((rows, 1), jnp.int32),
        ),
        in_specs=[VMEM] * 5,
        out_specs=(VMEM,) * 5,
        scratch_shapes=[pltpu.VMEM((ranks * packed, HEAD_SIZE), jnp.float32)],
        compiler_params=grant(14),
        cost_estimate=cost(4 * stride * ranks * rows * query_width, 4 * rows * query_width),
        name="turn_queries",
    )(
        route.reshape(rows, 1),
        seat,
        all_positions,
        jnp.concatenate([frequency, frequency]).reshape(1, HEAD_SIZE),
        queries,
    )

    shard, wide = key_matrix.shape[0], 2 * key_matrix.shape[1]

    def chip_parts(sources):
        chips = [(source, source + ranks // 2) for source in sources]
        return chips, [array for source in sources for array in matrices[source]]

    def scratch(chips, arrays):
        return [
            pltpu.VMEM((rows, 2 * shard * len(chips)), jnp.bfloat16),
            pltpu.VMEM((2 * shard * len(chips), wide), jnp.bfloat16),
            pltpu.SemaphoreType.DMA((len(chips) + len(arrays),)),
        ]

    def product_cost(chips):
        depth = 2 * shard * len(chips)
        return cost(2 * rows * depth * wide, 2 * depth * (rows + wide) + 8 * rows * wide)

    def add_part(total, sources):
        chips, arrays = chip_parts(sources)
        more = [] if total is None else [total]
        return pl.pallas_call(
            functools.partial(part_kernel, chips, bool(more)),
            out_shape=shape((rows, wide), jnp.float32),
            in_specs=[SMEM] + [HBM] * (1 + len(arrays)) + [VMEM] * len(more),
            out_specs=VMEM,
            scratch_shapes=scratch(chips, arrays),
            compiler_params=grant(14),
            cost_estimate=product_cost(chips),
            name="add_part",
        )(owners, hidden, *arrays, *more)

    bias = jnp.concatenate([key_projection_bias, value_projection_bias])
    bias = bias.astype(jnp.float32).reshape(1, -1)
    step = (far_lane, near_other, next_lane, swaps)
    step, turned, bounds, cosine, sine, seat_column, bias, owners = lax.optimization_barrier(
        (step, turned, bounds, cosine, sine, seat_column, bias, owners)
    )
    far_lane, near_other, next_lane, swaps = step
    matrices[1], matrices[2] = (near_lane, swaps[0]), (other_row, swaps[1])
    matrices[3] = (far_lane, send(far_lane, beside))
    matrices[4] = (next_lane, send(next_lane, beside))
    matrices[5] = (near_other, send(near_other, beside))
    far_other, next_other = send(near_other, swap), send(next_lane, across)
    total = add_part(add_part(None, (0, 1, 2)), (3, 4, 5))
    next_other, far_other, total = lax.optimization_barrier((next_other, far_other, total))
    matrices[6] = (next_other, send(next_other, beside))
    matrices[7] = (far_other, send(far_other, beside))
    chips, arrays = chip_parts((6, 7))
    (pairs,) = pl.pallas_call(
        functools.partial(finish_kernel, chips),
        out_shape=tuple(
            shape((rows, 2 * heads * HEAD_SIZE), jnp.bfloat16) for _, heads in CHUNKS
        ),
        in_specs=[SMEM, HBM] + [VMEM] * (5 + len(arrays)),
        out_specs=(VMEM,) * len(CHUNKS),
        scratch_shapes=scratch(chips, arrays),
        compiler_params=grant(14),
        cost_estimate=product_cost(chips),
        name="finish",
    )(
        owners,
        hidden,
        bias,
        cosine,
        sine,
        bucket,
        *arrays,
        total,
    )

    blocks = {}
    sending = spread(pairs, ranks, blocks)
    next(sending)
    order = [source for sources in sets for source in sources]
    ordered = plan[:, :width][source_order(ranks, order)]
    key_routes = ordered[:, :rows].reshape(ranks, ranks, share).transpose(1, 0, 2)
    more_places = ordered[:, rows + listed :].reshape(ranks * listed, 1)
    veils = pl.pallas_call(
        functools.partial(veil_kernel, sets, stride),
        out_shape=tuple(
            shape((ranks, 2 * share * len(sources), HEAD_SIZE), jnp.bfloat16) for sources in sets
        ),
        in_specs=[VMEM] * 3,
        out_specs=(VMEM,) * len(sets),
        compiler_params=grant(14),
        cost_estimate=cost(3 * 10**9, 4 * ranks * rows * HEAD_SIZE),
        name="veil",
    )(
        bounds,
        key_routes.reshape(ranks, 1, rows),
        ordered[:, rows : rows + listed].reshape(1, ranks * listed),
    )

    def attend(state, index):
        sources, last = sets[index], index == len(sets) - 1
        starts = [tuple(first for first, _ in blocks[source]) for source in sources]
        arrays = [array for source in sources for _, array in blocks[source]]
        keys = 2 * share * len(sources)
        fixed = [more_places, turned, veils[index], *arrays, *state]
        kept = shape((KEY_VALUE_HEADS, ranks * packed, HEAD_SIZE), jnp.float32)
        outs = [kept] * 3
        out_specs = [VMEM] * 3
        in_specs = [VMEM, VMEM, HBM] + [VMEM] * (len(fixed) - 3)
        handed = {len(fixed) - 3 + at: at + last for at in range(3)} if state else {}
        scratch_shapes = [
            pltpu.VMEM((len(sources) * share, wide), jnp.bfloat16),
            pltpu.VMEM((packed, HEAD_SIZE), jnp.bfloat16),
            pltpu.VMEM((ranks, keys, HEAD_SIZE), jnp.bfloat16),
            pltpu.SemaphoreType.DMA,
        ]
        if last:
            fixed.append(seat_column)
            in_specs.append(VMEM)
            outs.insert(0, shape((rows, query_width), jnp.bfloat16))
            out_specs.insert(0, HBM)
            scratch_shapes += [
                pltpu.VMEM((ranks * stride, query_width), jnp.bfloat16),
                pltpu.VMEM((rows, query_width), jnp.bfloat16),
                pltpu.SemaphoreType.DMA((KEY_VALUE_HEADS,)),
            ]
        return pl.pallas_call(
            functools.partial(
                attend_kernel,
                starts,
                sum(len(one) for one in sets[:index]),
                spare,
                stride,
                bool(state),
                last,
            ),
            out_shape=tuple(outs),
            in_specs=in_specs,
            out_specs=tuple(out_specs),
            scratch_shapes=scratch_shapes,
            input_output_aliases=handed,
            compiler_params=grant(18 if last else 14),
            cost_estimate=cost(
                8 * ranks * KEY_VALUE_HEADS * packed * (keys + 256) * HEAD_SIZE,
                2 * keys * rows * HEAD_SIZE,
            ),
            name="attend",
        )(*fixed)

    state = ()
    for step in range(planes - 1):
        if step:
            next(sending)
        state = sending.send(tuple(attend(state, step)))
    next(sending)
    state = sending.send(tuple(attend(state, planes - 1)))
    return attend(state, planes)[0]


def apply_rotary(rows, slot_offset, heads):
    block_count = rows.shape[0]
    half = HEAD_SIZE // 2
    frequency = 1000000.0 ** (-(jnp.arange(half, dtype=jnp.float32) * 2.0 / HEAD_SIZE))
    angle = slot_offset.astype(jnp.float32)[:, None] * frequency[None, :]
    cosine = jnp.cos(angle)[:, None, :]
    sine = jnp.sin(angle)[:, None, :]
    grid = rows.astype(jnp.float32).reshape(block_count, heads, HEAD_SIZE)
    first = grid[:, :, :half]
    second = grid[:, :, half:]
    turned = jnp.concatenate(
        [first * cosine - second * sine, second * cosine + first * sine], axis=2
    )
    return turned.reshape(block_count, heads * HEAD_SIZE).astype(jnp.bfloat16)


def causal_block_attention(pieces):
    query_tile_rows, key_tile_rows, value_tile_rows, spot_block = pieces
    block_count = query_tile_rows.shape[0]
    head_groups = QUERY_HEADS // KEY_VALUE_HEADS
    query_block_grid = query_tile_rows.reshape(block_count, KEY_VALUE_HEADS, head_groups, HEAD_SIZE)
    key_block_grid = key_tile_rows.reshape(block_count, KEY_VALUE_HEADS, HEAD_SIZE)
    value_block_grid = value_tile_rows.reshape(block_count, KEY_VALUE_HEADS, HEAD_SIZE)
    scores = jnp.einsum(
        "qhgd,khd->hgqk", query_block_grid, key_block_grid, preferred_element_type=jnp.float32
    ) / math.sqrt(HEAD_SIZE)
    inner = jnp.arange(block_count, dtype=jnp.int32)
    visible = (inner[None, :] <= inner[:, None]) & (
        inner[None, :] >= inner[:, None] - spot_block[:, None]
    )
    scores = jnp.where(visible, scores, -jnp.inf)
    top = jnp.max(scores, axis=3, keepdims=True)
    weights = jnp.exp(scores - top)
    totals = jnp.sum(weights, axis=3)
    probs = weights.astype(jnp.bfloat16)
    mixed = jnp.einsum(
        "hgqk,khd->qhgd", probs, value_block_grid, preferred_element_type=jnp.float32
    )
    mixed = mixed / jnp.transpose(totals, (2, 0, 1))[:, :, :, None]
    return mixed.reshape(block_count, QUERY_HEADS * HEAD_SIZE).astype(jnp.bfloat16)


def add_projection(left, pieces):
    return (
        jnp.dot(left, pieces[0], preferred_element_type=jnp.float32),
        jnp.dot(left, pieces[1], preferred_element_type=jnp.float32),
    )


def project_own(hidden, key_matrix, value_matrix, key_projection_bias, value_projection_bias):
    totals = add_projection(
        hidden,
        (
            lax.all_gather(key_matrix, "dp", axis=0, tiled=True),
            lax.all_gather(value_matrix, "dp", axis=0, tiled=True),
        ),
    )
    key_rows = (totals[0] + key_projection_bias.astype(jnp.float32)).astype(jnp.bfloat16)
    value_rows = (totals[1] + value_projection_bias.astype(jnp.float32)).astype(jnp.bfloat16)
    return jnp.concatenate([key_rows, value_rows], axis=1)


def send_plan(
    hidden,
    queries,
    route,
    positions,
    key_matrix,
    value_matrix,
    key_projection_bias,
    value_projection_bias,
):
    ranks = lax.axis_size("dp")
    rows = hidden.shape[0]
    slots = positions.shape[0]
    spare = rows // ranks + 2
    width = ranks * spare
    paired_width = key_matrix.shape[1]
    target = route // slots
    place = route - target * slots
    member = (target[:, None] == jnp.arange(ranks, dtype=jnp.int32)[None, :]).astype(jnp.int32)
    order = jnp.sum(jnp.cumsum(member, axis=0) * member, axis=1) - 1
    bucket = target * spare + order
    outgoing = jnp.full((width,), slots, jnp.int32).at[bucket].set(place)
    arrived = lax.all_to_all(
        outgoing.reshape(ranks, spare), "dp", split_axis=0, concat_axis=0, tiled=True
    ).reshape(width)
    query_buf = jnp.zeros((width, queries.shape[1]), jnp.bfloat16).at[bucket].set(queries)
    own_pairs = project_own(
        hidden, key_matrix, value_matrix, key_projection_bias, value_projection_bias
    )
    pair_buf = jnp.zeros((width, 2 * paired_width), jnp.bfloat16).at[bucket].set(own_pairs)
    got_query, got_pairs = (
        lax.all_to_all(
            query_buf.reshape(ranks, spare, -1), "dp", split_axis=0, concat_axis=0, tiled=True
        ),
        lax.all_to_all(
            pair_buf.reshape(ranks, spare, -1), "dp", split_axis=0, concat_axis=0, tiled=True
        ),
    )
    got_query = got_query.reshape(width, -1)
    got_pairs = got_pairs.reshape(width, -1)
    query_slot_rows = (
        jnp.zeros((slots, got_query.shape[1]), jnp.bfloat16).at[arrived].set(got_query, mode="drop")
    )
    paired_slot_rows = (
        jnp.zeros((slots, 2 * paired_width), jnp.bfloat16).at[arrived].set(got_pairs, mode="drop")
    )
    query_turned = apply_rotary(query_slot_rows, positions, QUERY_HEADS)
    key_rotated = apply_rotary(paired_slot_rows[:, :paired_width], positions, KEY_VALUE_HEADS)
    block_list = slots // BLOCK_SLOTS
    attended = lax.map(
        causal_block_attention,
        (
            query_turned.reshape(block_list, BLOCK_SLOTS, -1),
            key_rotated.reshape(block_list, BLOCK_SLOTS, -1),
            paired_slot_rows[:, paired_width:].reshape(block_list, BLOCK_SLOTS, -1),
            positions.reshape(block_list, BLOCK_SLOTS),
        ),
    )
    attended = attended.reshape(slots, -1)
    leaving = attended[jnp.minimum(arrived, slots - 1)]
    returned = lax.all_to_all(
        leaving.reshape(ranks, spare, -1), "dp", split_axis=0, concat_axis=0, tiled=True
    ).reshape(width, -1)
    return returned[bucket]


def local(*args):
    hidden, queries, _, positions, key_matrix = args[:5]
    ranks = lax.axis_size("dp")
    rows = hidden.shape[0]
    gathered = ranks * ranks * (rows // ranks + 2) * 4 * key_matrix.shape[1]
    chip_rows = 2 * key_matrix.shape[0]
    fits = rows % (16 * ranks) == 0 and chip_rows % HEAD_SIZE == 0 and gathered <= GATHER_LIMIT
    if ranks == PLANES * PLANE and lax.axis_size("groups") == 2 and fits:
        return gather_plan(*args)
    return send_plan(*args)


def solution(mesh):
    placed = (
        P(("groups", "dp"), None),
        P(("groups", "dp"), None),
        P(("groups", "dp")),
        P(("groups", "dp")),
        P("dp", None),
        P("dp", None),
        P(),
        P(),
    )
    return jax.shard_map(
        local, mesh=mesh, in_specs=placed, out_specs=P(("groups", "dp"), None), check_vma=False
    )
```

```python
import functools
import math

import jax
import jax.numpy as jnp
import numpy as np
from jax import lax
from jax.experimental import pallas as pl
from jax.experimental.pallas import tpu as pltpu
from jax.sharding import PartitionSpec as P

QUERY_HEADS = 20
KEY_VALUE_HEADS = 4
HEAD_SIZE = 128
BLOCK_SLOTS = 512
HEAD_GROUPS = QUERY_HEADS // KEY_VALUE_HEADS
CHUNKS = ((0, KEY_VALUE_HEADS),)
PLANE = 4
PLANES = 4
CYCLE = (0, 2, 3, 1)
SAFE_POWER = 64.0
GATHER_LIMIT = 40 * 2**20
MASKED = -1e30
VMEM = pl.BlockSpec(memory_space=pltpu.VMEM)
SMEM = pl.BlockSpec(memory_space=pltpu.SMEM)
HBM = pl.BlockSpec(memory_space=pltpu.HBM)


def grant(mebibytes):
    return pltpu.CompilerParams(vmem_limit_bytes=mebibytes * 2**20)


def cost(flops, moved):
    return pl.CostEstimate(flops=flops, bytes_accessed=moved, transcendentals=0)


def one_hot_rows(count, index_row):
    rows = lax.broadcasted_iota(jnp.int32, (count, index_row.shape[1]), 0)
    return (rows == index_row).astype(jnp.float32).astype(jnp.bfloat16)


def split(number):
    high = lax.shift_right_logical(number, HEAD_SIZE.bit_length() - 1)
    return high, number - high * HEAD_SIZE


def contract(left, right, left_dim, right_dim):
    return lax.dot_general(
        left, right, (((left_dim,), (right_dim,)), ((), ())), preferred_element_type=jnp.float32
    )


def turn(rows, cosine, sine):
    return (rows * cosine + pltpu.roll(rows, HEAD_SIZE // 2, 1) * sine).astype(jnp.bfloat16)


def join_kernel(left_ref, right_ref, out_ref, done):
    wide = left_ref.shape[1]
    copies = [
        pltpu.make_async_copy(ref, out_ref.at[:, pl.ds(at * wide, wide)], done.at[at])
        for at, ref in enumerate((left_ref, right_ref))
    ]
    for copy in copies:
        copy.start()
    for copy in copies:
        copy.wait()


def order_kernel(
    ranks, slots, extra, stride, route_ref, bucket_ref, seat_ref, sorted_ref, more_ref
):
    route = route_ref[...]
    count = route.shape[1]
    share = count // ranks
    target = lax.div(route, slots)
    member = (lax.broadcasted_iota(jnp.int32, (ranks, count), 0) == target).astype(jnp.float32)
    before = lax.broadcasted_iota(jnp.int32, (count, count), 0) < lax.broadcasted_iota(
        jnp.int32, (count, count), 1
    )
    before = before.astype(jnp.float32).astype(jnp.bfloat16)
    ahead = contract(member.astype(jnp.bfloat16), before, 1, 0)
    order = jnp.sum(member * ahead, axis=0, keepdims=True).astype(jnp.int32)
    beyond = order >= share
    beyond_rows = jnp.broadcast_to(beyond.astype(jnp.float32), (8, count)).astype(jnp.bfloat16)
    number = contract(beyond_rows, before, 1, 0)[0:1]
    counts = jnp.sum(member, axis=1, keepdims=True)
    free = jnp.maximum(share - counts, 0.0)
    group = lax.broadcasted_iota(jnp.int32, (ranks, ranks), 0)
    lower = (group > lax.broadcasted_iota(jnp.int32, (ranks, ranks), 1)).astype(jnp.float32)
    free_rows = jnp.broadcast_to(free, (ranks, HEAD_SIZE)).astype(jnp.bfloat16)
    free_before = contract(lower.astype(jnp.bfloat16), free_rows, 1, 0)[:, 0:1]
    inside = (number >= free_before) & (number < free_before + free)
    base = lax.broadcasted_iota(jnp.int32, (ranks, 1), 0).astype(jnp.float32) * share + counts
    hole = jnp.sum(jnp.where(inside, base + number - free_before, 0.0), axis=0, keepdims=True)
    bucket = jnp.where(beyond, hole.astype(jnp.int32), target * share + order)
    bucket_ref[...] = bucket
    seat_ref[...] = target * stride + order
    high, low = split(route)
    place_high, place_low = split(bucket)
    line = lax.broadcasted_iota(jnp.int32, (8, count), 0)
    digits = jnp.where(line == 0, high, 0)
    digits = jnp.where(line == 1, low, digits)
    digits = jnp.where(line == 2, place_high, digits)
    digits = jnp.where(line == 3, place_low, digits)
    digits = jnp.where(line == 4, 1, digits).astype(jnp.float32).astype(jnp.bfloat16)
    placed = contract(digits, one_hot_rows(count, bucket), 1, 1)
    sorted_ref[...] = (placed[0:1] * HEAD_SIZE + placed[1:2]).astype(jnp.int32)
    listed = jnp.where(beyond, target * extra + order - share, -1)
    found = contract(digits, one_hot_rows(ranks * extra, listed), 1, 1)
    none = found[4:5] - 1.0
    more_ref[0:1] = (found[0:1] * HEAD_SIZE + found[1:2] + none).astype(jnp.int32)
    more_ref[1:2] = (found[2:3] * HEAD_SIZE + found[3:4] + none).astype(jnp.int32)


def query_kernel(
    ranks, spare, stride, packed, route_ref, seat_ref, positions_ref, frequency_ref, queries_ref, *refs
):
    turned_ref, bounds_ref, cosine_ref, sine_ref, column_ref, rows_ref = refs
    route = route_ref[...]
    count = route.shape[0]
    lines = positions_ref.shape[0]
    line, lane = split(route)
    pick = (lax.broadcasted_iota(jnp.int32, (count, lines), 1) == line).astype(jnp.float32)
    pick = pick.astype(jnp.bfloat16)
    positions = positions_ref[...]
    half = lax.shift_right_logical(positions, 1)
    rest = positions - half * 2
    rows = 2.0 * contract(pick, half.astype(jnp.float32).astype(jnp.bfloat16), 1, 0) + contract(
        pick, rest.astype(jnp.float32).astype(jnp.bfloat16), 1, 0
    )
    lanes = lax.broadcasted_iota(jnp.int32, (count, HEAD_SIZE), 1)
    spot = jnp.sum(jnp.where(lanes == lane, rows, 0.0), axis=1, keepdims=True)
    angle = spot * frequency_ref[...]
    cosine = jnp.cos(angle)
    sine = jnp.sin(angle)
    sine = jnp.where(lanes < HEAD_SIZE // 2, -sine, sine)
    cosine_ref[...] = cosine
    sine_ref[...] = sine
    seats = one_hot_rows(ranks * stride, seat_ref[...])
    seat_line, seat_lane = split(seat_ref[...])
    digit = lax.broadcasted_iota(jnp.int32, (8, count), 0)
    digits = jnp.where(digit == 0, seat_line, jnp.where(digit == 1, seat_lane, 0))
    same = one_hot_rows(count, lax.broadcasted_iota(jnp.int32, (1, count), 1))
    column = contract(same, digits.astype(jnp.float32).astype(jnp.bfloat16), 1, 1)
    column_ref[...] = (column[:, 0:1] * HEAD_SIZE + column[:, 1:2]).astype(jnp.int32)
    first = route - spot.astype(jnp.int32)
    first_line, first_lane = split(first)
    digits = jnp.where(lanes == 0, line, 0)
    digits = jnp.where(lanes == 1, lane, digits)
    digits = jnp.where(lanes == 2, first_line, digits)
    digits = jnp.where(lanes == 3, first_lane, digits)
    digits = jnp.where(lanes == 4, 1, digits)
    placed = contract(seats, digits.astype(jnp.float32).astype(jnp.bfloat16), 1, 0)
    live = placed[:, 4:5] - 1.0
    last = placed[:, 0:1] * HEAD_SIZE + placed[:, 1:2] + live
    start = placed[:, 2:3] * HEAD_SIZE + placed[:, 3:4] - live * 2.0**20
    seat_lanes = lax.broadcasted_iota(jnp.int32, placed.shape, 1)
    bounds_ref[...] = jnp.where(seat_lanes == 0, last, start).astype(jnp.int32)
    rows_ref[...] = jnp.zeros(rows_ref.shape, jnp.float32)
    for head in range(KEY_VALUE_HEADS):
        for place in range(HEAD_GROUPS):
            at = (head * HEAD_GROUPS + place) * HEAD_SIZE
            one = queries_ref[:, at : at + HEAD_SIZE].astype(jnp.float32)
            rows = contract(seats, turn(one, cosine, sine), 1, 0)
            for group in range(ranks):
                at = group * packed + place * spare
                rows_ref[at : at + spare] = rows[group * stride : group * stride + spare]
        turned_ref[head] = rows_ref[...].astype(jnp.bfloat16)


def fetch_columns(chips, owners_ref, hidden_ref, columns, done):
    deep = columns.shape[1] // len(chips)
    copies = []
    for place, chip in enumerate(chips):
        first = pl.multiple_of(lax.div(owners_ref[chip[0]], 2) * deep, HEAD_SIZE)
        copies.append(
            pltpu.make_async_copy(
                hidden_ref.at[:, pl.ds(first, deep)],
                columns.at[:, pl.ds(place * deep, deep)],
                done.at[place],
            )
        )
        copies[-1].start()
    return copies


def place_rows(owners_ref, chips, matrix):
    shard = matrix.shape[0] // len(chips) // 2
    return [
        pl.ds(pl.multiple_of((2 * place + lax.rem(owners_ref[source], 2)) * shard, 16), shard)
        for place, chip in enumerate(chips)
        for source in chip
    ]


def part_kernel(chips, more, owners_ref, hidden_ref, *refs):
    count = 2 * len(chips)
    parts, refs = refs[:count], refs[count:]
    if more:
        total_ref, refs = refs[0], refs[1:]
    out_ref, columns, matrix, done = refs
    copies = fetch_columns(chips, owners_ref, hidden_ref, columns, done)
    for at, (ref, rows) in enumerate(zip(parts, place_rows(owners_ref, chips, matrix))):
        copies.append(pltpu.make_async_copy(ref, matrix.at[rows], done.at[len(chips) + at]))
        copies[-1].start()
    for copy in copies:
        copy.wait()
    for first in range(0, out_ref.shape[1], 2 * HEAD_SIZE):
        span = slice(first, first + 2 * HEAD_SIZE)
        product = contract(columns[...], matrix[:, span], 1, 0)
        out_ref[:, span] = total_ref[:, span] + product if more else product


def finish_kernel(
    chips, owners_ref, hidden_ref, bias_ref, cosine_ref, sine_ref, bucket_ref, *refs
):
    count = 2 * len(chips)
    parts, total_ref = refs[:count], refs[count]
    outs, (columns, matrix, done) = refs[count + 1 : -3], refs[-3:]
    copies = fetch_columns(chips, owners_ref, hidden_ref, columns, done)
    for ref, rows in zip(parts, place_rows(owners_ref, chips, matrix)):
        matrix[rows] = ref[...]
    places = one_hot_rows(outs[0].shape[0], bucket_ref[...])
    for copy in copies:
        copy.wait()
    wide = KEY_VALUE_HEADS * HEAD_SIZE
    for first in range(0, 2 * wide, 2 * HEAD_SIZE):
        span = slice(first, first + 2 * HEAD_SIZE)
        rows = contract(columns[...], matrix[:, span], 1, 0) + total_ref[:, span]
        rows = (rows + bias_ref[:, span]).astype(jnp.bfloat16)
        if first < wide:
            cosine, sine = cosine_ref[...], sine_ref[...]
            halves = [
                turn(rows[:, at : at + HEAD_SIZE].astype(jnp.float32), cosine, sine)
                for at in (0, HEAD_SIZE)
            ]
            rows = jnp.concatenate(halves, axis=1)
        rows = contract(places, rows, 1, 0).astype(jnp.bfloat16)
        for half in range(2):
            head = first % wide // HEAD_SIZE + half
            for (first_head, heads), out_ref in zip(CHUNKS, outs):
                if first_head <= head < first_head + heads:
                    at = (head - first_head + first // wide * heads) * HEAD_SIZE
                    out_ref[:, at : at + HEAD_SIZE] = rows[
                        :, half * HEAD_SIZE : (half + 1) * HEAD_SIZE
                    ]


def veil_kernel(sets, stride, bounds_ref, routes_ref, more_ref, *veil_refs):
    rest = jnp.zeros((HEAD_SIZE - stride, more_ref.shape[1]), jnp.float32)
    share = routes_ref.shape[2] // routes_ref.shape[0]

    def one_group(group, carry):
        seats = pl.ds(pl.multiple_of(group * stride, 16), stride)
        last, start = bounds_ref[seats, 0:1], bounds_ref[seats, 1:2]
        both = []
        for routes in (routes_ref[group], more_ref[...]):
            veil = jnp.where((routes <= last) & (routes >= start), 0.0, MASKED)
            veil = jnp.transpose(jnp.concatenate([veil, rest], axis=0))
            both.append(veil.astype(jnp.bfloat16))
        first = 0
        for sources, veil_ref in zip(sets, veil_refs):
            end = first + len(sources) * share
            veil_ref[group] = jnp.concatenate([veil[first:end] for veil in both], axis=0)
            first = end
        return carry

    lax.fori_loop(0, routes_ref.shape[0], one_group, 0)


def attend_kernel(starts, before, spare, stride, more, last, *refs):
    more_ref, queries_ref, veil_ref = refs[:3]
    refs = refs[3:]
    blocks = []
    for first_rows in starts:
        blocks.append(dict(zip(first_rows, refs)))
        refs = refs[len(first_rows) :]
    if more:
        top_ref, sum_ref, total_ref = refs[:3]
        refs = refs[3:]
    if last:
        seat_ref, out_ref, mixed_ref, result_ref, leave = refs[0], refs[1], *refs[-3:]
        refs = refs[:-3]
        mixed_ref[...] = jnp.zeros(mixed_ref.shape, jnp.bfloat16)
    else:
        new_top_ref, new_sum_ref, new_total_ref = refs[:3]
    listed_rows, seen_by, veil, veil_in = refs[-4:]
    fetch_veil = pltpu.make_async_copy(veil_ref, veil, veil_in)
    fetch_veil.start()
    heads, ranks = queries_ref.shape[0], veil_ref.shape[0]
    packed = queries_ref.shape[1] // ranks
    wide = heads * HEAD_SIZE
    share = listed_rows.shape[0] // len(starts)
    count = share * ranks

    token = lax.broadcasted_iota(jnp.int32, (packed, HEAD_SIZE), 0)
    lane = lax.broadcasted_iota(jnp.int32, (packed, HEAD_SIZE), 1)
    own = lane < 0
    for at in range(HEAD_GROUPS):
        own = own | ((token == lane + at * spare) & (lane < spare))
    seen_by[...] = own.astype(jnp.float32).astype(jnp.bfloat16)
    lines = lax.broadcasted_iota(jnp.int32, (share, count), 1)
    for at, block in enumerate(blocks):
        places = more_ref[(before + at) * share : (before + at + 1) * share]
        pick = (lines == places).astype(jnp.float32).astype(jnp.bfloat16)
        for first in range(0, 2 * wide, 2 * HEAD_SIZE):
            lanes = slice(first, first + 2 * HEAD_SIZE)
            found = [
                contract(pick[:, row : row + ref.shape[0]], ref[:, lanes], 1, 0)
                for row, ref in block.items()
            ]
            listed_rows[at * share : (at + 1) * share, lanes] = sum(found).astype(jnp.bfloat16)
    fetch_veil.wait()
    scale = math.log2(math.e) / math.sqrt(HEAD_SIZE)

    def rows_of(group, row, first):
        lanes = slice(first, first + HEAD_SIZE)
        window = pl.ds(pl.multiple_of(group * share - row, 16), share)
        rows = [block[row][window, lanes] for block in blocks]
        return jnp.concatenate(rows + [listed_rows[:, lanes]], axis=0)

    def scores_of(group, row, head, tokens):
        left = jnp.concatenate([queries_ref[head, tokens], seen_by[...]], axis=1)
        keys = rows_of(group, row, head * HEAD_SIZE)
        return contract(left, jnp.concatenate([keys, veil[group]], axis=1), 1, 1)

    def products_of(group, row, head, weight):
        values = rows_of(group, row, wide + head * HEAD_SIZE)
        values = jnp.concatenate([values, jnp.ones_like(values)], axis=1)
        mixed = contract(weight, values, 1, 0)
        return mixed[:, :HEAD_SIZE], mixed[:, HEAD_SIZE:]

    def tile(top, keys):
        return jnp.concatenate([top] * (keys // HEAD_SIZE), axis=1)

    def finish_head(group, head, total, weight_sum):
        mixed = total / weight_sum
        seats = pl.ds(pl.multiple_of(group * stride, 16), spare)
        for at in range(HEAD_GROUPS):
            place = (head * HEAD_GROUPS + at) * HEAD_SIZE
            rows = mixed[at * spare : (at + 1) * spare]
            mixed_ref[seats, place : place + HEAD_SIZE] = rows.astype(jnp.bfloat16)

    def add_heads(group, row, some):
        tokens = pl.ds(pl.multiple_of(group * packed, 16), packed)
        scores = [scores_of(group, row, head, tokens) for head in some]
        tops, weights = [], []
        for head, score in zip(some, scores):
            top = jnp.max(score, axis=1, keepdims=True)
            if more:
                top = jnp.maximum(top_ref[head, tokens], top)
            else:
                top = jnp.broadcast_to(top, (packed, HEAD_SIZE))
            tops.append(top)
            weight = jnp.exp2((score - tile(top, score.shape[1])) * scale)
            weights.append(weight.astype(jnp.bfloat16))
        for head, top, weight in zip(some, tops, weights):
            total, weight_sum = products_of(group, row, head, weight)
            if more:
                fade = jnp.exp2((top_ref[head, tokens] - top) * scale)
                total = total + fade * total_ref[head, tokens]
                weight_sum = weight_sum + fade * sum_ref[head, tokens]
            if last:
                finish_head(group, head, total, weight_sum)
            else:
                new_top_ref[head, tokens] = top
                new_sum_ref[head, tokens] = weight_sum
                new_total_ref[head, tokens] = total

    def add_heads_as_before(group, row, worst):
        tokens = pl.ds(pl.multiple_of(group * packed, 16), packed)
        scores = [scores_of(group, row, head, tokens) for head in range(heads)]
        weights = []
        for head, score in enumerate(scores):
            above = score - tile(top_ref[head, tokens], score.shape[1])
            for first in range(0, score.shape[1], HEAD_SIZE):
                part = above[:, first : first + HEAD_SIZE].reshape(packed // 8, 8, HEAD_SIZE)
                worst = jnp.maximum(worst, jnp.max(part, axis=0))
            weights.append(jnp.exp2(above * scale).astype(jnp.bfloat16))
        for head, weight in enumerate(weights):
            total, weight_sum = products_of(group, row, head, weight)
            total = total + total_ref[head, tokens]
            weight_sum = weight_sum + sum_ref[head, tokens]
            finish_head(group, head, total, weight_sum)
        return worst

    firsts = sorted({row for first_rows in starts for row in first_rows})
    spans = [
        (row, row // share, end // share) for row, end in zip(firsts, firsts[1:] + [count])
    ]

    def add_all(together):
        for row, first, end in spans:

            def one_group(group, carry, row=row):
                for head in range(0, heads, together):
                    add_heads(group, row, range(head, head + together))
                return carry

            lax.fori_loop(first, end, one_group, 0)

    if not last:
        add_all(heads)
        return
    worst = jnp.full((8, HEAD_SIZE), MASKED, jnp.float32)
    for row, first, end in spans:
        worst = lax.fori_loop(
            first,
            end,
            lambda group, worst, row=row: add_heads_as_before(group, row, worst),
            worst,
        )

    @pl.when(jnp.max(worst) * scale > SAFE_POWER)
    def _():
        add_all(1)

    seat_lanes = lax.broadcasted_iota(jnp.int32, (count, mixed_ref.shape[0]), 1)
    seats = (seat_lanes == seat_ref[...]).astype(jnp.float32).astype(jnp.bfloat16)
    span = HEAD_GROUPS * HEAD_SIZE
    leaving = []
    for head in range(heads):
        lanes = slice(head * span, (head + 1) * span)
        rows = contract(seats, mixed_ref[:, lanes], 1, 0)
        result_ref[:, lanes] = rows.astype(jnp.bfloat16)
        lanes = pl.ds(head * span, span)
        leaving.append(
            pltpu.make_async_copy(result_ref.at[:, lanes], out_ref.at[:, lanes], leave.at[head])
        )
        leaving[-1].start()
    for one in leaving:
        one.wait()


def spread(block, ranks, held):
    ring = ring_pairs(ranks)
    across = [(rank, rank ^ 2) for rank in range(ranks)]
    beside = [(rank, rank ^ 1) for rank in range(ranks)]
    steps = ranks // PLANE
    half = block.shape[0] // 32 * 18

    def keep(source, first, array):
        held.setdefault(source, []).append((first, array))
        held.setdefault(source + 2 * steps, []).append((first, lax.ppermute(array, "dp", beside)))

    lane, other = block, None
    for step in range(steps - 1):
        keep(step, 0, lane)
        if step:
            keep(steps + step - 1, 0, other)
        following = lax.ppermute(lane, "dp", across), lax.ppermute(lane, "dp", ring)
        extra = yield
        other, lane, extra = lax.optimization_barrier((*following, extra))
        yield extra
    keep(steps - 1, 0, lane)
    keep(2 * steps - 2, 0, other)
    over = lax.ppermute(lane[:half], "dp", across)
    around = lax.ppermute(other[half:], "dp", ring)
    extra = yield other
    over, around, extra = lax.optimization_barrier((over, around, extra))
    keep(2 * steps - 1, 0, over)
    keep(2 * steps - 1, half, around)
    yield extra


def ring_pairs(ranks, back=False):
    pairs = []
    for rank in range(ranks):
        at = CYCLE.index(rank // PLANE) + (-1 if back else 1)
        pairs.append((rank, CYCLE[at % PLANES] * PLANE + rank % PLANE))
    return pairs


def pick(table, index):
    return sum(jnp.where(index == at, number, 0) for at, number in enumerate(table))


def block_owners(steps, flips):
    me = lax.axis_index("dp")
    lane, plane = lax.rem(me, PLANE), lax.div(me, PLANE)
    place = pick([CYCLE.index(at) for at in range(PLANES)], plane)
    return pick(CYCLE, (place + PLANES - steps) % PLANES) * PLANE + (lane ^ flips)


def source_order(ranks, sources):
    steps = np.array([source % PLANES for source in sources], np.int32)
    flips = np.array([(0, 2, 1, 3)[source // PLANES] for source in sources], np.int32)
    return block_owners(steps, flips)


def weight_order(ranks):
    up = np.array([0, 1, 0, PLANES - 1, 2, 1, 2, PLANES - 1] * 2, np.int32)
    steps = jnp.where(lax.axis_index("groups") == 1, (PLANES - up) % PLANES, up)
    flips = np.array([0, 0, 2, 0, 0, 2, 2, 2], np.int32)
    return block_owners(steps, np.concatenate([flips, flips ^ 1]))


def gather_plan(
    hidden,
    queries,
    route,
    positions,
    key_matrix,
    value_matrix,
    key_projection_bias,
    value_projection_bias,
):
    ranks = lax.axis_size("dp")
    rows = hidden.shape[0]
    slots = positions.shape[0]
    share, extra = rows // ranks, 2
    spare = share + extra
    listed = ranks * extra
    stride = -(-spare // 16) * 16
    packed = -(-HEAD_GROUPS * spare // 16) * 16
    query_width = queries.shape[1]
    shape = jax.ShapeDtypeStruct

    def columns(array, chunk):
        first, heads = chunk
        return array[..., first * HEAD_SIZE : (first + heads) * HEAD_SIZE]

    joined = pl.pallas_call(
        join_kernel,
        out_shape=shape((key_matrix.shape[0], 2 * key_matrix.shape[1]), jnp.bfloat16),
        in_specs=[HBM] * 2,
        out_specs=VMEM,
        scratch_shapes=[pltpu.SemaphoreType.DMA((2,))],
        compiler_params=grant(56),
        name="join",
    )(key_matrix, value_matrix)
    every = [(group, rank) for group in range(2) for rank in range(ranks)]
    ring = [
        (group * ranks + rank, group * ranks + after)
        for group in range(2)
        for rank, after in ring_pairs(ranks, group == 1)
    ]
    across = [(group * ranks + rank, group * ranks + (rank ^ 2)) for group, rank in every]
    beside = [(group * ranks + rank, group * ranks + (rank ^ 1)) for group, rank in every]
    swap = [(group * ranks + rank, (1 - group) * ranks + rank) for group, rank in every]

    def send(array, pairs):
        return lax.ppermute(array, ("groups", "dp"), pairs)

    joined_swap = send(joined, beside)
    other_row, near_lane = send(joined, across), send(joined, ring)
    bucket, seat, sorted_route, more = pl.pallas_call(
        functools.partial(order_kernel, ranks, slots, extra, stride),
        out_shape=(
            shape((1, rows), jnp.int32),
            shape((1, rows), jnp.int32),
            shape((1, rows), jnp.int32),
            shape((2, listed), jnp.int32),
        ),
        in_specs=[VMEM],
        out_specs=(VMEM,) * 4,
        compiler_params=grant(14),
        name="order",
    )(route.reshape(1, rows))
    width = rows + 2 * listed
    plan = jnp.concatenate([sorted_route.reshape(rows), more.reshape(2 * listed), positions])
    plan = lax.all_to_all(
        jnp.broadcast_to(plan, (ranks, width + slots)), "dp", split_axis=0, concat_axis=0, tiled=True
    )
    other_row, near_lane, joined_swap, plan, bucket, seat = lax.optimization_barrier(
        (other_row, near_lane, joined_swap, plan, bucket, seat)
    )
    matrices = {0: (joined, joined_swap)}
    swaps = send(near_lane, beside), send(other_row, beside)
    far_lane, near_other = send(near_lane, swap), send(near_lane, across)
    next_lane = send(near_lane, ring)
    all_positions = plan[:, width:].reshape(-1, HEAD_SIZE)
    planes = ranks // PLANE
    sets = [(0, 2 * planes)] + [
        (step, step + 2 * planes, step + planes - 1, step + 3 * planes - 1)
        for step in range(1, planes)
    ]
    sets.append((2 * planes - 1, 4 * planes - 1))
    owners = weight_order(ranks)

    half = HEAD_SIZE // 2
    frequency = 1000000.0 ** (-(jnp.arange(half, dtype=jnp.float32) * 2.0 / HEAD_SIZE))
    turned, bounds, cosine, sine, seat_column = pl.pallas_call(
        functools.partial(query_kernel, ranks, spare, stride, packed),
        out_shape=(
            shape((KEY_VALUE_HEADS, ranks * packed, HEAD_SIZE), jnp.bfloat16),
            shape((ranks * stride, HEAD_SIZE), jnp.int32),
            shape((rows, HEAD_SIZE), jnp.float32),
            shape((rows, HEAD_SIZE), jnp.float32),
            shape((rows, 1), jnp.int32),
        ),
        in_specs=[VMEM] * 5,
        out_specs=(VMEM,) * 5,
        scratch_shapes=[pltpu.VMEM((ranks * packed, HEAD_SIZE), jnp.float32)],
        compiler_params=grant(14),
        cost_estimate=cost(4 * stride * ranks * rows * query_width, 4 * rows * query_width),
        name="turn_queries",
    )(
        route.reshape(rows, 1),
        seat,
        all_positions,
        jnp.concatenate([frequency, frequency]).reshape(1, HEAD_SIZE),
        queries,
    )

    shard, wide = key_matrix.shape[0], 2 * key_matrix.shape[1]

    def chip_parts(sources):
        chips = [(source, source + ranks // 2) for source in sources]
        return chips, [array for source in sources for array in matrices[source]]

    def scratch(chips, arrays):
        return [
            pltpu.VMEM((rows, 2 * shard * len(chips)), jnp.bfloat16),
            pltpu.VMEM((2 * shard * len(chips), wide), jnp.bfloat16),
            pltpu.SemaphoreType.DMA((len(chips) + len(arrays),)),
        ]

    def product_cost(chips):
        depth = 2 * shard * len(chips)
        return cost(2 * rows * depth * wide, 2 * depth * (rows + wide) + 8 * rows * wide)

    def add_part(total, sources):
        chips, arrays = chip_parts(sources)
        more = [] if total is None else [total]
        return pl.pallas_call(
            functools.partial(part_kernel, chips, bool(more)),
            out_shape=shape((rows, wide), jnp.float32),
            in_specs=[SMEM] + [HBM] * (1 + len(arrays)) + [VMEM] * len(more),
            out_specs=VMEM,
            scratch_shapes=scratch(chips, arrays),
            compiler_params=grant(14),
            cost_estimate=product_cost(chips),
            name="add_part",
        )(owners, hidden, *arrays, *more)

    bias = jnp.concatenate([key_projection_bias, value_projection_bias])
    bias = bias.astype(jnp.float32).reshape(1, -1)
    step = (far_lane, near_other, next_lane, swaps)
    step, turned, bounds, cosine, sine, seat_column, bias, owners = lax.optimization_barrier(
        (step, turned, bounds, cosine, sine, seat_column, bias, owners)
    )
    far_lane, near_other, next_lane, swaps = step
    matrices[1], matrices[2] = (near_lane, swaps[0]), (other_row, swaps[1])
    matrices[3] = (far_lane, send(far_lane, beside))
    matrices[4] = (next_lane, send(next_lane, beside))
    matrices[5] = (near_other, send(near_other, beside))
    far_other, next_other = send(near_other, swap), send(next_lane, across)
    total = add_part(add_part(None, (0, 1, 2)), (3, 4, 5))
    next_other, far_other, total = lax.optimization_barrier((next_other, far_other, total))
    matrices[6] = (next_other, send(next_other, beside))
    matrices[7] = (far_other, send(far_other, beside))
    chips, arrays = chip_parts((6, 7))
    (pairs,) = pl.pallas_call(
        functools.partial(finish_kernel, chips),
        out_shape=tuple(
            shape((rows, 2 * heads * HEAD_SIZE), jnp.bfloat16) for _, heads in CHUNKS
        ),
        in_specs=[SMEM, HBM] + [VMEM] * (5 + len(arrays)),
        out_specs=(VMEM,) * len(CHUNKS),
        scratch_shapes=scratch(chips, arrays),
        compiler_params=grant(14),
        cost_estimate=product_cost(chips),
        name="finish",
    )(
        owners,
        hidden,
        bias,
        cosine,
        sine,
        bucket,
        *arrays,
        total,
    )

    blocks = {}
    sending = spread(pairs, ranks, blocks)
    next(sending)
    order = [source for sources in sets for source in sources]
    ordered = plan[:, :width][source_order(ranks, order)]
    key_routes = ordered[:, :rows].reshape(ranks, ranks, share).transpose(1, 0, 2)
    more_places = ordered[:, rows + listed :].reshape(ranks * listed, 1)
    veils = pl.pallas_call(
        functools.partial(veil_kernel, sets, stride),
        out_shape=tuple(
            shape((ranks, 2 * share * len(sources), HEAD_SIZE), jnp.bfloat16) for sources in sets
        ),
        in_specs=[VMEM] * 3,
        out_specs=(VMEM,) * len(sets),
        compiler_params=grant(14),
        cost_estimate=cost(3 * 10**9, 4 * ranks * rows * HEAD_SIZE),
        name="veil",
    )(
        bounds,
        key_routes.reshape(ranks, 1, rows),
        ordered[:, rows : rows + listed].reshape(1, ranks * listed),
    )

    def attend(state, index):
        sources, last = sets[index], index == len(sets) - 1
        starts = [tuple(first for first, _ in blocks[source]) for source in sources]
        arrays = [array for source in sources for _, array in blocks[source]]
        keys = 2 * share * len(sources)
        fixed = [more_places, turned, veils[index], *arrays, *state]
        kept = shape((KEY_VALUE_HEADS, ranks * packed, HEAD_SIZE), jnp.float32)
        outs = [kept] * 3
        out_specs = [VMEM] * 3
        in_specs = [VMEM, VMEM, HBM] + [VMEM] * (len(fixed) - 3)
        handed = {len(fixed) - 3 + at: at + last for at in range(3)} if state else {}
        scratch_shapes = [
            pltpu.VMEM((len(sources) * share, wide), jnp.bfloat16),
            pltpu.VMEM((packed, HEAD_SIZE), jnp.bfloat16),
            pltpu.VMEM((ranks, keys, HEAD_SIZE), jnp.bfloat16),
            pltpu.SemaphoreType.DMA,
        ]
        if last:
            fixed.append(seat_column)
            in_specs.append(VMEM)
            outs.insert(0, shape((rows, query_width), jnp.bfloat16))
            out_specs.insert(0, HBM)
            scratch_shapes += [
                pltpu.VMEM((ranks * stride, query_width), jnp.bfloat16),
                pltpu.VMEM((rows, query_width), jnp.bfloat16),
                pltpu.SemaphoreType.DMA((KEY_VALUE_HEADS,)),
            ]
        return pl.pallas_call(
            functools.partial(
                attend_kernel,
                starts,
                sum(len(one) for one in sets[:index]),
                spare,
                stride,
                bool(state),
                last,
            ),
            out_shape=tuple(outs),
            in_specs=in_specs,
            out_specs=tuple(out_specs),
            scratch_shapes=scratch_shapes,
            input_output_aliases=handed,
            compiler_params=grant(18 if last else 14),
            cost_estimate=cost(
                8 * ranks * KEY_VALUE_HEADS * packed * (keys + 256) * HEAD_SIZE,
                2 * keys * rows * HEAD_SIZE,
            ),
            name="attend",
        )(*fixed)

    state = ()
    for step in range(planes - 1):
        if step:
            next(sending)
        state = sending.send(tuple(attend(state, step)))
    next(sending)
    state = sending.send(tuple(attend(state, planes - 1)))
    return attend(state, planes)[0]


def apply_rotary(rows, slot_offset, heads):
    block_count = rows.shape[0]
    half = HEAD_SIZE // 2
    frequency = 1000000.0 ** (-(jnp.arange(half, dtype=jnp.float32) * 2.0 / HEAD_SIZE))
    angle = slot_offset.astype(jnp.float32)[:, None] * frequency[None, :]
    cosine = jnp.cos(angle)[:, None, :]
    sine = jnp.sin(angle)[:, None, :]
    grid = rows.astype(jnp.float32).reshape(block_count, heads, HEAD_SIZE)
    first = grid[:, :, :half]
    second = grid[:, :, half:]
    turned = jnp.concatenate(
        [first * cosine - second * sine, second * cosine + first * sine], axis=2
    )
    return turned.reshape(block_count, heads * HEAD_SIZE).astype(jnp.bfloat16)


def causal_block_attention(pieces):
    query_tile_rows, key_tile_rows, value_tile_rows, spot_block = pieces
    block_count = query_tile_rows.shape[0]
    head_groups = QUERY_HEADS // KEY_VALUE_HEADS
    query_block_grid = query_tile_rows.reshape(block_count, KEY_VALUE_HEADS, head_groups, HEAD_SIZE)
    key_block_grid = key_tile_rows.reshape(block_count, KEY_VALUE_HEADS, HEAD_SIZE)
    value_block_grid = value_tile_rows.reshape(block_count, KEY_VALUE_HEADS, HEAD_SIZE)
    scores = jnp.einsum(
        "qhgd,khd->hgqk", query_block_grid, key_block_grid, preferred_element_type=jnp.float32
    ) / math.sqrt(HEAD_SIZE)
    inner = jnp.arange(block_count, dtype=jnp.int32)
    visible = (inner[None, :] <= inner[:, None]) & (
        inner[None, :] >= inner[:, None] - spot_block[:, None]
    )
    scores = jnp.where(visible, scores, -jnp.inf)
    top = jnp.max(scores, axis=3, keepdims=True)
    weights = jnp.exp(scores - top)
    totals = jnp.sum(weights, axis=3)
    probs = weights.astype(jnp.bfloat16)
    mixed = jnp.einsum(
        "hgqk,khd->qhgd", probs, value_block_grid, preferred_element_type=jnp.float32
    )
    mixed = mixed / jnp.transpose(totals, (2, 0, 1))[:, :, :, None]
    return mixed.reshape(block_count, QUERY_HEADS * HEAD_SIZE).astype(jnp.bfloat16)


def add_projection(left, pieces):
    return (
        jnp.dot(left, pieces[0], preferred_element_type=jnp.float32),
        jnp.dot(left, pieces[1], preferred_element_type=jnp.float32),
    )


def project_own(hidden, key_matrix, value_matrix, key_projection_bias, value_projection_bias):
    totals = add_projection(
        hidden,
        (
            lax.all_gather(key_matrix, "dp", axis=0, tiled=True),
            lax.all_gather(value_matrix, "dp", axis=0, tiled=True),
        ),
    )
    key_rows = (totals[0] + key_projection_bias.astype(jnp.float32)).astype(jnp.bfloat16)
    value_rows = (totals[1] + value_projection_bias.astype(jnp.float32)).astype(jnp.bfloat16)
    return jnp.concatenate([key_rows, value_rows], axis=1)


def send_plan(
    hidden,
    queries,
    route,
    positions,
    key_matrix,
    value_matrix,
    key_projection_bias,
    value_projection_bias,
):
    ranks = lax.axis_size("dp")
    rows = hidden.shape[0]
    slots = positions.shape[0]
    spare = rows // ranks + 2
    width = ranks * spare
    paired_width = key_matrix.shape[1]
    target = route // slots
    place = route - target * slots
    member = (target[:, None] == jnp.arange(ranks, dtype=jnp.int32)[None, :]).astype(jnp.int32)
    order = jnp.sum(jnp.cumsum(member, axis=0) * member, axis=1) - 1
    bucket = target * spare + order
    outgoing = jnp.full((width,), slots, jnp.int32).at[bucket].set(place)
    arrived = lax.all_to_all(
        outgoing.reshape(ranks, spare), "dp", split_axis=0, concat_axis=0, tiled=True
    ).reshape(width)
    query_buf = jnp.zeros((width, queries.shape[1]), jnp.bfloat16).at[bucket].set(queries)
    own_pairs = project_own(
        hidden, key_matrix, value_matrix, key_projection_bias, value_projection_bias
    )
    pair_buf = jnp.zeros((width, 2 * paired_width), jnp.bfloat16).at[bucket].set(own_pairs)
    got_query, got_pairs = (
        lax.all_to_all(
            query_buf.reshape(ranks, spare, -1), "dp", split_axis=0, concat_axis=0, tiled=True
        ),
        lax.all_to_all(
            pair_buf.reshape(ranks, spare, -1), "dp", split_axis=0, concat_axis=0, tiled=True
        ),
    )
    got_query = got_query.reshape(width, -1)
    got_pairs = got_pairs.reshape(width, -1)
    query_slot_rows = (
        jnp.zeros((slots, got_query.shape[1]), jnp.bfloat16).at[arrived].set(got_query, mode="drop")
    )
    paired_slot_rows = (
        jnp.zeros((slots, 2 * paired_width), jnp.bfloat16).at[arrived].set(got_pairs, mode="drop")
    )
    query_turned = apply_rotary(query_slot_rows, positions, QUERY_HEADS)
    key_rotated = apply_rotary(paired_slot_rows[:, :paired_width], positions, KEY_VALUE_HEADS)
    block_list = slots // BLOCK_SLOTS
    attended = lax.map(
        causal_block_attention,
        (
            query_turned.reshape(block_list, BLOCK_SLOTS, -1),
            key_rotated.reshape(block_list, BLOCK_SLOTS, -1),
            paired_slot_rows[:, paired_width:].reshape(block_list, BLOCK_SLOTS, -1),
            positions.reshape(block_list, BLOCK_SLOTS),
        ),
    )
    attended = attended.reshape(slots, -1)
    leaving = attended[jnp.minimum(arrived, slots - 1)]
    returned = lax.all_to_all(
        leaving.reshape(ranks, spare, -1), "dp", split_axis=0, concat_axis=0, tiled=True
    ).reshape(width, -1)
    return returned[bucket]


def local(*args):
    hidden, queries, _, positions, key_matrix = args[:5]
    ranks = lax.axis_size("dp")
    rows = hidden.shape[0]
    gathered = ranks * ranks * (rows // ranks + 2) * 4 * key_matrix.shape[1]
    chip_rows = 2 * key_matrix.shape[0]
    fits = rows % (16 * ranks) == 0 and chip_rows % HEAD_SIZE == 0 and gathered <= GATHER_LIMIT
    if ranks == PLANES * PLANE and lax.axis_size("groups") == 2 and fits:
        return gather_plan(*args)
    return send_plan(*args)


def solution(mesh):
    placed = (
        P(("groups", "dp"), None),
        P(("groups", "dp"), None),
        P(("groups", "dp")),
        P(("groups", "dp")),
        P("dp", None),
        P("dp", None),
        P(),
        P(),
    )
    return jax.shard_map(
        local, mesh=mesh, in_specs=placed, out_specs=P(("groups", "dp"), None), check_vma=False
    )
```

```python
import functools
import math

import jax
import jax.numpy as jnp
import numpy as np
from jax import lax
from jax.experimental import pallas as pl
from jax.experimental.pallas import tpu as pltpu
from jax.sharding import PartitionSpec as P

QUERY_HEADS = 20
KEY_VALUE_HEADS = 4
HEAD_SIZE = 128
BLOCK_SLOTS = 512
HEAD_GROUPS = QUERY_HEADS // KEY_VALUE_HEADS
CHUNKS = ((0, KEY_VALUE_HEADS),)
PLANE = 4
PLANES = 4
CYCLE = (0, 2, 3, 1)
SAFE_POWER = 64.0
GATHER_LIMIT = 40 * 2**20
MASKED = -1e30
VMEM = pl.BlockSpec(memory_space=pltpu.VMEM)
SMEM = pl.BlockSpec(memory_space=pltpu.SMEM)
HBM = pl.BlockSpec(memory_space=pltpu.HBM)


def grant(mebibytes):
    return pltpu.CompilerParams(vmem_limit_bytes=mebibytes * 2**20)


def cost(flops, moved):
    return pl.CostEstimate(flops=flops, bytes_accessed=moved, transcendentals=0)


def one_hot_rows(count, index_row):
    rows = lax.broadcasted_iota(jnp.int32, (count, index_row.shape[1]), 0)
    return (rows == index_row).astype(jnp.float32).astype(jnp.bfloat16)


def split(number):
    high = lax.shift_right_logical(number, HEAD_SIZE.bit_length() - 1)
    return high, number - high * HEAD_SIZE


def contract(left, right, left_dim, right_dim):
    return lax.dot_general(
        left, right, (((left_dim,), (right_dim,)), ((), ())), preferred_element_type=jnp.float32
    )


def turn(rows, cosine, sine):
    return (rows * cosine + pltpu.roll(rows, HEAD_SIZE // 2, 1) * sine).astype(jnp.bfloat16)


def join_kernel(left_ref, right_ref, out_ref, done):
    wide = left_ref.shape[1]
    copies = [
        pltpu.make_async_copy(ref, out_ref.at[:, pl.ds(at * wide, wide)], done.at[at])
        for at, ref in enumerate((left_ref, right_ref))
    ]
    for copy in copies:
        copy.start()
    for copy in copies:
        copy.wait()


def cut_kernel(split_at, far_ref, next_ref, near_ref, top_ref, rest_ref, done):
    below = far_ref.shape[0] - split_at
    copies = [
        pltpu.make_async_copy(near_ref.at[pl.ds(0, split_at)], top_ref, done.at[0]),
        pltpu.make_async_copy(
            next_ref.at[pl.ds(split_at, below)], rest_ref.at[pl.ds(0, below)], done.at[1]
        ),
        pltpu.make_async_copy(
            far_ref.at[pl.ds(split_at, below)], rest_ref.at[pl.ds(below, below)], done.at[2]
        ),
    ]
    for copy in copies:
        copy.start()
    for copy in copies:
        copy.wait()


def order_kernel(
    ranks, slots, extra, stride, route_ref, bucket_ref, seat_ref, sorted_ref, more_ref
):
    route = route_ref[...]
    count = route.shape[1]
    share = count // ranks
    target = lax.div(route, slots)
    member = (lax.broadcasted_iota(jnp.int32, (ranks, count), 0) == target).astype(jnp.float32)
    before = lax.broadcasted_iota(jnp.int32, (count, count), 0) < lax.broadcasted_iota(
        jnp.int32, (count, count), 1
    )
    before = before.astype(jnp.float32).astype(jnp.bfloat16)
    ahead = contract(member.astype(jnp.bfloat16), before, 1, 0)
    order = jnp.sum(member * ahead, axis=0, keepdims=True).astype(jnp.int32)
    beyond = order >= share
    beyond_rows = jnp.broadcast_to(beyond.astype(jnp.float32), (8, count)).astype(jnp.bfloat16)
    number = contract(beyond_rows, before, 1, 0)[0:1]
    counts = jnp.sum(member, axis=1, keepdims=True)
    free = jnp.maximum(share - counts, 0.0)
    group = lax.broadcasted_iota(jnp.int32, (ranks, ranks), 0)
    lower = (group > lax.broadcasted_iota(jnp.int32, (ranks, ranks), 1)).astype(jnp.float32)
    free_rows = jnp.broadcast_to(free, (ranks, HEAD_SIZE)).astype(jnp.bfloat16)
    free_before = contract(lower.astype(jnp.bfloat16), free_rows, 1, 0)[:, 0:1]
    inside = (number >= free_before) & (number < free_before + free)
    base = lax.broadcasted_iota(jnp.int32, (ranks, 1), 0).astype(jnp.float32) * share + counts
    hole = jnp.sum(jnp.where(inside, base + number - free_before, 0.0), axis=0, keepdims=True)
    bucket = jnp.where(beyond, hole.astype(jnp.int32), target * share + order)
    bucket_ref[...] = bucket
    seat_ref[...] = target * stride + order
    high, low = split(route)
    place_high, place_low = split(bucket)
    line = lax.broadcasted_iota(jnp.int32, (8, count), 0)
    digits = jnp.where(line == 0, high, 0)
    digits = jnp.where(line == 1, low, digits)
    digits = jnp.where(line == 2, place_high, digits)
    digits = jnp.where(line == 3, place_low, digits)
    digits = jnp.where(line == 4, 1, digits).astype(jnp.float32).astype(jnp.bfloat16)
    placed = contract(digits, one_hot_rows(count, bucket), 1, 1)
    sorted_ref[...] = (placed[0:1] * HEAD_SIZE + placed[1:2]).astype(jnp.int32)
    listed = jnp.where(beyond, target * extra + order - share, -1)
    found = contract(digits, one_hot_rows(ranks * extra, listed), 1, 1)
    none = found[4:5] - 1.0
    more_ref[0:1] = (found[0:1] * HEAD_SIZE + found[1:2] + none).astype(jnp.int32)
    more_ref[1:2] = (found[2:3] * HEAD_SIZE + found[3:4] + none).astype(jnp.int32)


def query_kernel(
    ranks, spare, stride, packed, route_ref, seat_ref, positions_ref, frequency_ref, queries_ref, *refs
):
    turned_ref, bounds_ref, cosine_ref, sine_ref, column_ref, rows_ref = refs
    route = route_ref[...]
    count = route.shape[0]
    lines = positions_ref.shape[0]
    line, lane = split(route)
    pick = (lax.broadcasted_iota(jnp.int32, (count, lines), 1) == line).astype(jnp.float32)
    pick = pick.astype(jnp.bfloat16)
    positions = positions_ref[...]
    half = lax.shift_right_logical(positions, 1)
    rest = positions - half * 2
    rows = 2.0 * contract(pick, half.astype(jnp.float32).astype(jnp.bfloat16), 1, 0) + contract(
        pick, rest.astype(jnp.float32).astype(jnp.bfloat16), 1, 0
    )
    lanes = lax.broadcasted_iota(jnp.int32, (count, HEAD_SIZE), 1)
    spot = jnp.sum(jnp.where(lanes == lane, rows, 0.0), axis=1, keepdims=True)
    angle = spot * frequency_ref[...]
    cosine = jnp.cos(angle)
    sine = jnp.sin(angle)
    sine = jnp.where(lanes < HEAD_SIZE // 2, -sine, sine)
    cosine_ref[...] = cosine
    sine_ref[...] = sine
    seats = one_hot_rows(ranks * stride, seat_ref[...])
    seat_line, seat_lane = split(seat_ref[...])
    digit = lax.broadcasted_iota(jnp.int32, (8, count), 0)
    digits = jnp.where(digit == 0, seat_line, jnp.where(digit == 1, seat_lane, 0))
    same = one_hot_rows(count, lax.broadcasted_iota(jnp.int32, (1, count), 1))
    column = contract(same, digits.astype(jnp.float32).astype(jnp.bfloat16), 1, 1)
    column_ref[...] = (column[:, 0:1] * HEAD_SIZE + column[:, 1:2]).astype(jnp.int32)
    first = route - spot.astype(jnp.int32)
    first_line, first_lane = split(first)
    digits = jnp.where(lanes == 0, line, 0)
    digits = jnp.where(lanes == 1, lane, digits)
    digits = jnp.where(lanes == 2, first_line, digits)
    digits = jnp.where(lanes == 3, first_lane, digits)
    digits = jnp.where(lanes == 4, 1, digits)
    placed = contract(seats, digits.astype(jnp.float32).astype(jnp.bfloat16), 1, 0)
    live = placed[:, 4:5] - 1.0
    last = placed[:, 0:1] * HEAD_SIZE + placed[:, 1:2] + live
    start = placed[:, 2:3] * HEAD_SIZE + placed[:, 3:4] - live * 2.0**20
    seat_lanes = lax.broadcasted_iota(jnp.int32, placed.shape, 1)
    bounds_ref[...] = jnp.where(seat_lanes == 0, last, start).astype(jnp.int32)
    rows_ref[...] = jnp.zeros(rows_ref.shape, jnp.float32)
    for head in range(KEY_VALUE_HEADS):
        for place in range(HEAD_GROUPS):
            at = (head * HEAD_GROUPS + place) * HEAD_SIZE
            one = queries_ref[:, at : at + HEAD_SIZE].astype(jnp.float32)
            rows = contract(seats, turn(one, cosine, sine), 1, 0)
            for group in range(ranks):
                at = group * packed + place * spare
                rows_ref[at : at + spare] = rows[group * stride : group * stride + spare]
        turned_ref[head] = rows_ref[...].astype(jnp.bfloat16)


def fetch_columns(chips, owners_ref, hidden_ref, columns, done):
    deep = columns.shape[1] // len(chips)
    copies = []
    for place, chip in enumerate(chips):
        first = pl.multiple_of(lax.div(owners_ref[chip[0]], 2) * deep, HEAD_SIZE)
        copies.append(
            pltpu.make_async_copy(
                hidden_ref.at[:, pl.ds(first, deep)],
                columns.at[:, pl.ds(place * deep, deep)],
                done.at[place],
            )
        )
        copies[-1].start()
    return copies


def place_rows(owners_ref, chips, matrix):
    shard = matrix.shape[0] // len(chips) // 2
    return [
        pl.ds(pl.multiple_of((2 * place + lax.rem(owners_ref[source], 2)) * shard, 16), shard)
        for place, chip in enumerate(chips)
        for source in chip
    ]


def part_kernel(chips, more, owners_ref, hidden_ref, *refs):
    count = 2 * len(chips)
    parts, refs = refs[:count], refs[count:]
    if more:
        total_ref, refs = refs[0], refs[1:]
    out_ref, columns, matrix, done = refs
    copies = fetch_columns(chips, owners_ref, hidden_ref, columns, done)
    for at, (ref, rows) in enumerate(zip(parts, place_rows(owners_ref, chips, matrix))):
        copies.append(pltpu.make_async_copy(ref, matrix.at[rows], done.at[len(chips) + at]))
        copies[-1].start()
    for copy in copies:
        copy.wait()
    for first in range(0, out_ref.shape[1], 2 * HEAD_SIZE):
        span = slice(first, first + 2 * HEAD_SIZE)
        product = contract(columns[...], matrix[:, span], 1, 0)
        out_ref[:, span] = total_ref[:, span] + product if more else product


def finish_kernel(
    chips, owners_ref, hidden_ref, bias_ref, cosine_ref, sine_ref, bucket_ref, *refs
):
    count = 3 * len(chips)
    parts, total_ref = refs[:count], refs[count]
    outs, (columns, matrix, done) = refs[count + 1 : -3], refs[-3:]
    copies = fetch_columns(chips, owners_ref, hidden_ref, columns, done)
    split_at, below = parts[0].shape[0], parts[2].shape[0] // 2
    shard = split_at + below
    for side in range(2):
        rest = parts[3 * side + 2]
        for place, chip in enumerate(chips):
            first = (2 * place + lax.rem(owners_ref[chip[side]], 2)) * shard
            matrix[pl.ds(pl.multiple_of(first, 16), split_at)] = parts[3 * side + place][...]
            matrix[pl.ds(pl.multiple_of(first + split_at, 16), below)] = rest[
                place * below : (place + 1) * below
            ]
    places = one_hot_rows(outs[0].shape[0], bucket_ref[...])
    for copy in copies:
        copy.wait()
    wide = KEY_VALUE_HEADS * HEAD_SIZE
    for first in range(0, 2 * wide, 2 * HEAD_SIZE):
        span = slice(first, first + 2 * HEAD_SIZE)
        rows = contract(columns[...], matrix[:, span], 1, 0) + total_ref[:, span]
        rows = (rows + bias_ref[:, span]).astype(jnp.bfloat16)
        if first < wide:
            cosine, sine = cosine_ref[...], sine_ref[...]
            halves = [
                turn(rows[:, at : at + HEAD_SIZE].astype(jnp.float32), cosine, sine)
                for at in (0, HEAD_SIZE)
            ]
            rows = jnp.concatenate(halves, axis=1)
        rows = contract(places, rows, 1, 0).astype(jnp.bfloat16)
        for half in range(2):
            head = first % wide // HEAD_SIZE + half
            for (first_head, heads), out_ref in zip(CHUNKS, outs):
                if first_head <= head < first_head + heads:
                    at = (head - first_head + first // wide * heads) * HEAD_SIZE
                    out_ref[:, at : at + HEAD_SIZE] = rows[
                        :, half * HEAD_SIZE : (half + 1) * HEAD_SIZE
                    ]


def veil_kernel(sets, stride, bounds_ref, routes_ref, more_ref, *veil_refs):
    rest = jnp.zeros((HEAD_SIZE - stride, more_ref.shape[1]), jnp.float32)
    share = routes_ref.shape[2] // routes_ref.shape[0]

    def one_group(group, carry):
        seats = pl.ds(pl.multiple_of(group * stride, 16), stride)
        last, start = bounds_ref[seats, 0:1], bounds_ref[seats, 1:2]
        both = []
        for routes in (routes_ref[group], more_ref[...]):
            veil = jnp.where((routes <= last) & (routes >= start), 0.0, MASKED)
            veil = jnp.transpose(jnp.concatenate([veil, rest], axis=0))
            both.append(veil.astype(jnp.bfloat16))
        first = 0
        for sources, veil_ref in zip(sets, veil_refs):
            end = first + len(sources) * share
            veil_ref[group] = jnp.concatenate([veil[first:end] for veil in both], axis=0)
            first = end
        return carry

    lax.fori_loop(0, routes_ref.shape[0], one_group, 0)


def attend_kernel(starts, before, spare, stride, more, last, *refs):
    more_ref, queries_ref, veil_ref = refs[:3]
    refs = refs[3:]
    blocks = []
    for first_rows in starts:
        blocks.append(dict(zip(first_rows, refs)))
        refs = refs[len(first_rows) :]
    if more:
        top_ref, sum_ref, total_ref = refs[:3]
        refs = refs[3:]
    if last:
        seat_ref, out_ref, mixed_ref, result_ref, leave = refs[0], refs[1], *refs[-3:]
        refs = refs[:-3]
        mixed_ref[...] = jnp.zeros(mixed_ref.shape, jnp.bfloat16)
    else:
        new_top_ref, new_sum_ref, new_total_ref = refs[:3]
    listed_rows, seen_by, veil, veil_in = refs[-4:]
    fetch_veil = pltpu.make_async_copy(veil_ref, veil, veil_in)
    fetch_veil.start()
    heads, ranks = queries_ref.shape[0], veil_ref.shape[0]
    packed = queries_ref.shape[1] // ranks
    wide = heads * HEAD_SIZE
    share = listed_rows.shape[0] // len(starts)
    count = share * ranks

    token = lax.broadcasted_iota(jnp.int32, (packed, HEAD_SIZE), 0)
    lane = lax.broadcasted_iota(jnp.int32, (packed, HEAD_SIZE), 1)
    own = lane < 0
    for at in range(HEAD_GROUPS):
        own = own | ((token == lane + at * spare) & (lane < spare))
    seen_by[...] = own.astype(jnp.float32).astype(jnp.bfloat16)
    lines = lax.broadcasted_iota(jnp.int32, (share, count), 1)
    for at, block in enumerate(blocks):
        places = more_ref[(before + at) * share : (before + at + 1) * share]
        pick = (lines == places).astype(jnp.float32).astype(jnp.bfloat16)
        for first in range(0, 2 * wide, 2 * HEAD_SIZE):
            lanes = slice(first, first + 2 * HEAD_SIZE)
            found = [
                contract(pick[:, row : row + ref.shape[0]], ref[:, lanes], 1, 0)
                for row, ref in block.items()
            ]
            listed_rows[at * share : (at + 1) * share, lanes] = sum(found).astype(jnp.bfloat16)
    fetch_veil.wait()
    scale = math.log2(math.e) / math.sqrt(HEAD_SIZE)

    def rows_of(group, row, first):
        lanes = slice(first, first + HEAD_SIZE)
        window = pl.ds(pl.multiple_of(group * share - row, 16), share)
        rows = [block[row][window, lanes] for block in blocks]
        return jnp.concatenate(rows + [listed_rows[:, lanes]], axis=0)

    def scores_of(group, row, head, tokens):
        left = jnp.concatenate([queries_ref[head, tokens], seen_by[...]], axis=1)
        keys = rows_of(group, row, head * HEAD_SIZE)
        return contract(left, jnp.concatenate([keys, veil[group]], axis=1), 1, 1)

    def products_of(group, row, head, weight):
        values = rows_of(group, row, wide + head * HEAD_SIZE)
        values = jnp.concatenate([values, jnp.ones_like(values)], axis=1)
        mixed = contract(weight, values, 1, 0)
        return mixed[:, :HEAD_SIZE], mixed[:, HEAD_SIZE:]

    def tile(top, keys):
        return jnp.concatenate([top] * (keys // HEAD_SIZE), axis=1)

    def finish_head(group, head, total, weight_sum):
        mixed = total / weight_sum
        seats = pl.ds(pl.multiple_of(group * stride, 16), spare)
        for at in range(HEAD_GROUPS):
            place = (head * HEAD_GROUPS + at) * HEAD_SIZE
            rows = mixed[at * spare : (at + 1) * spare]
            mixed_ref[seats, place : place + HEAD_SIZE] = rows.astype(jnp.bfloat16)

    def add_heads(group, row, some):
        tokens = pl.ds(pl.multiple_of(group * packed, 16), packed)
        scores = [scores_of(group, row, head, tokens) for head in some]
        tops, weights = [], []
        for head, score in zip(some, scores):
            top = jnp.max(score, axis=1, keepdims=True)
            if more:
                top = jnp.maximum(top_ref[head, tokens], top)
            else:
                top = jnp.broadcast_to(top, (packed, HEAD_SIZE))
            tops.append(top)
            weight = jnp.exp2((score - tile(top, score.shape[1])) * scale)
            weights.append(weight.astype(jnp.bfloat16))
        for head, top, weight in zip(some, tops, weights):
            total, weight_sum = products_of(group, row, head, weight)
            if more:
                fade = jnp.exp2((top_ref[head, tokens] - top) * scale)
                total = total + fade * total_ref[head, tokens]
                weight_sum = weight_sum + fade * sum_ref[head, tokens]
            if last:
                finish_head(group, head, total, weight_sum)
            else:
                new_top_ref[head, tokens] = top
                new_sum_ref[head, tokens] = weight_sum
                new_total_ref[head, tokens] = total

    def add_heads_as_before(group, row, worst):
        tokens = pl.ds(pl.multiple_of(group * packed, 16), packed)
        scores = [scores_of(group, row, head, tokens) for head in range(heads)]
        weights = []
        for head, score in enumerate(scores):
            above = score - tile(top_ref[head, tokens], score.shape[1])
            for first in range(0, score.shape[1], HEAD_SIZE):
                part = above[:, first : first + HEAD_SIZE].reshape(packed // 8, 8, HEAD_SIZE)
                worst = jnp.maximum(worst, jnp.max(part, axis=0))
            weights.append(jnp.exp2(above * scale).astype(jnp.bfloat16))
        for head, weight in enumerate(weights):
            total, weight_sum = products_of(group, row, head, weight)
            total = total + total_ref[head, tokens]
            weight_sum = weight_sum + sum_ref[head, tokens]
            finish_head(group, head, total, weight_sum)
        return worst

    firsts = sorted({row for first_rows in starts for row in first_rows})
    spans = [
        (row, row // share, end // share) for row, end in zip(firsts, firsts[1:] + [count])
    ]

    def add_all(together):
        for row, first, end in spans:

            def one_group(group, carry, row=row):
                for head in range(0, heads, together):
                    add_heads(group, row, range(head, head + together))
                return carry

            lax.fori_loop(first, end, one_group, 0)

    if not last:
        add_all(heads)
        return
    worst = jnp.full((8, HEAD_SIZE), MASKED, jnp.float32)
    for row, first, end in spans:
        worst = lax.fori_loop(
            first,
            end,
            lambda group, worst, row=row: add_heads_as_before(group, row, worst),
            worst,
        )

    @pl.when(jnp.max(worst) * scale > SAFE_POWER)
    def _():
        add_all(1)

    seat_lanes = lax.broadcasted_iota(jnp.int32, (count, mixed_ref.shape[0]), 1)
    seats = (seat_lanes == seat_ref[...]).astype(jnp.float32).astype(jnp.bfloat16)
    span = HEAD_GROUPS * HEAD_SIZE
    leaving = []
    for head in range(heads):
        lanes = slice(head * span, (head + 1) * span)
        rows = contract(seats, mixed_ref[:, lanes], 1, 0)
        result_ref[:, lanes] = rows.astype(jnp.bfloat16)
        lanes = pl.ds(head * span, span)
        leaving.append(
            pltpu.make_async_copy(result_ref.at[:, lanes], out_ref.at[:, lanes], leave.at[head])
        )
        leaving[-1].start()
    for one in leaving:
        one.wait()


def spread(block, ranks, held):
    ring = ring_pairs(ranks)
    across = [(rank, rank ^ 2) for rank in range(ranks)]
    beside = [(rank, rank ^ 1) for rank in range(ranks)]
    steps = ranks // PLANE
    half = block.shape[0] // 32 * 16

    def keep(source, first, array):
        held.setdefault(source, []).append((first, array))
        held.setdefault(source + 2 * steps, []).append((first, lax.ppermute(array, "dp", beside)))

    lane, other = block, None
    for step in range(steps - 1):
        keep(step, 0, lane)
        if step:
            keep(steps + step - 1, 0, other)
        following = lax.ppermute(lane, "dp", across), lax.ppermute(lane, "dp", ring)
        extra = yield
        other, lane, extra = lax.optimization_barrier((*following, extra))
        yield extra
    keep(steps - 1, 0, lane)
    keep(2 * steps - 2, 0, other)
    over = lax.ppermute(lane[:half], "dp", across)
    around = lax.ppermute(other[half:], "dp", ring)
    extra = yield other
    over, around, extra = lax.optimization_barrier((over, around, extra))
    keep(2 * steps - 1, 0, over)
    keep(2 * steps - 1, half, around)
    yield extra


def ring_pairs(ranks, back=False):
    pairs = []
    for rank in range(ranks):
        at = CYCLE.index(rank // PLANE) + (-1 if back else 1)
        pairs.append((rank, CYCLE[at % PLANES] * PLANE + rank % PLANE))
    return pairs


def pick(table, index):
    return sum(jnp.where(index == at, number, 0) for at, number in enumerate(table))


def block_owners(steps, flips):
    me = lax.axis_index("dp")
    lane, plane = lax.rem(me, PLANE), lax.div(me, PLANE)
    place = pick([CYCLE.index(at) for at in range(PLANES)], plane)
    return pick(CYCLE, (place + PLANES - steps) % PLANES) * PLANE + (lane ^ flips)


def source_order(ranks, sources):
    steps = np.array([source % PLANES for source in sources], np.int32)
    flips = np.array([(0, 2, 1, 3)[source // PLANES] for source in sources], np.int32)
    return block_owners(steps, flips)


def weight_order(ranks):
    up = np.array([0, 1, 0, PLANES - 1, 2, 1, 2, PLANES - 1] * 2, np.int32)
    steps = jnp.where(lax.axis_index("groups") == 1, (PLANES - up) % PLANES, up)
    flips = np.array([0, 0, 2, 0, 0, 2, 2, 2], np.int32)
    return block_owners(steps, np.concatenate([flips, flips ^ 1]))


def gather_plan(
    hidden,
    queries,
    route,
    positions,
    key_matrix,
    value_matrix,
    key_projection_bias,
    value_projection_bias,
):
    ranks = lax.axis_size("dp")
    rows = hidden.shape[0]
    slots = positions.shape[0]
    share, extra = rows // ranks, 2
    spare = share + extra
    listed = ranks * extra
    stride = -(-spare // 16) * 16
    packed = -(-HEAD_GROUPS * spare // 16) * 16
    query_width = queries.shape[1]
    shape = jax.ShapeDtypeStruct

    def columns(array, chunk):
        first, heads = chunk
        return array[..., first * HEAD_SIZE : (first + heads) * HEAD_SIZE]

    joined = pl.pallas_call(
        join_kernel,
        out_shape=shape((key_matrix.shape[0], 2 * key_matrix.shape[1]), jnp.bfloat16),
        in_specs=[HBM] * 2,
        out_specs=VMEM,
        scratch_shapes=[pltpu.SemaphoreType.DMA((2,))],
        compiler_params=grant(56),
        name="join",
    )(key_matrix, value_matrix)
    every = [(group, rank) for group in range(2) for rank in range(ranks)]
    ring = [
        (group * ranks + rank, group * ranks + after)
        for group in range(2)
        for rank, after in ring_pairs(ranks, group == 1)
    ]
    across = [(group * ranks + rank, group * ranks + (rank ^ 2)) for group, rank in every]
    beside = [(group * ranks + rank, group * ranks + (rank ^ 1)) for group, rank in every]
    swap = [(group * ranks + rank, (1 - group) * ranks + rank) for group, rank in every]

    def send(array, pairs):
        return lax.ppermute(array, ("groups", "dp"), pairs)

    joined_swap = send(joined, beside)
    other_row, near_lane = send(joined, across), send(joined, ring)
    bucket, seat, sorted_route, more = pl.pallas_call(
        functools.partial(order_kernel, ranks, slots, extra, stride),
        out_shape=(
            shape((1, rows), jnp.int32),
            shape((1, rows), jnp.int32),
            shape((1, rows), jnp.int32),
            shape((2, listed), jnp.int32),
        ),
        in_specs=[VMEM],
        out_specs=(VMEM,) * 4,
        compiler_params=grant(14),
        name="order",
    )(route.reshape(1, rows))
    width = rows + 2 * listed
    plan = jnp.concatenate([sorted_route.reshape(rows), more.reshape(2 * listed), positions])
    plan = lax.all_to_all(
        jnp.broadcast_to(plan, (ranks, width + slots)), "dp", split_axis=0, concat_axis=0, tiled=True
    )
    other_row, near_lane, joined_swap, plan, bucket, seat = lax.optimization_barrier(
        (other_row, near_lane, joined_swap, plan, bucket, seat)
    )
    matrices = {0: (joined, joined_swap)}
    swaps = send(near_lane, beside), send(other_row, beside)
    far_lane, near_other = send(near_lane, swap), send(near_lane, across)
    next_lane = send(near_lane, ring)
    all_positions = plan[:, width:].reshape(-1, HEAD_SIZE)
    planes = ranks // PLANE
    sets = [(0, 2 * planes)] + [
        (step, step + 2 * planes, step + planes - 1, step + 3 * planes - 1)
        for step in range(1, planes)
    ]
    sets.append((2 * planes - 1, 4 * planes - 1))
    owners = weight_order(ranks)

    half = HEAD_SIZE // 2
    frequency = 1000000.0 ** (-(jnp.arange(half, dtype=jnp.float32) * 2.0 / HEAD_SIZE))
    turned, bounds, cosine, sine, seat_column = pl.pallas_call(
        functools.partial(query_kernel, ranks, spare, stride, packed),
        out_shape=(
            shape((KEY_VALUE_HEADS, ranks * packed, HEAD_SIZE), jnp.bfloat16),
            shape((ranks * stride, HEAD_SIZE), jnp.int32),
            shape((rows, HEAD_SIZE), jnp.float32),
            shape((rows, HEAD_SIZE), jnp.float32),
            shape((rows, 1), jnp.int32),
        ),
        in_specs=[VMEM] * 5,
        out_specs=(VMEM,) * 5,
        scratch_shapes=[pltpu.VMEM((ranks * packed, HEAD_SIZE), jnp.float32)],
        compiler_params=grant(14),
        cost_estimate=cost(4 * stride * ranks * rows * query_width, 4 * rows * query_width),
        name="turn_queries",
    )(
        route.reshape(rows, 1),
        seat,
        all_positions,
        jnp.concatenate([frequency, frequency]).reshape(1, HEAD_SIZE),
        queries,
    )

    shard, wide = key_matrix.shape[0], 2 * key_matrix.shape[1]

    def chip_parts(sources):
        chips = [(source, source + ranks // 2) for source in sources]
        return chips, [array for source in sources for array in matrices[source]]

    def scratch(chips):
        return [
            pltpu.VMEM((rows, 2 * shard * len(chips)), jnp.bfloat16),
            pltpu.VMEM((2 * shard * len(chips), wide), jnp.bfloat16),
            pltpu.SemaphoreType.DMA((3 * len(chips),)),
        ]

    def product_cost(chips):
        depth = 2 * shard * len(chips)
        return cost(2 * rows * depth * wide, 2 * depth * (rows + wide) + 8 * rows * wide)

    def add_part(total, sources):
        chips, arrays = chip_parts(sources)
        more = [] if total is None else [total]
        return pl.pallas_call(
            functools.partial(part_kernel, chips, bool(more)),
            out_shape=shape((rows, wide), jnp.float32),
            in_specs=[SMEM] + [HBM] * (1 + len(arrays)) + [VMEM] * len(more),
            out_specs=VMEM,
            scratch_shapes=scratch(chips),
            compiler_params=grant(14),
            cost_estimate=product_cost(chips),
            name="add_part",
        )(owners, hidden, *arrays, *more)

    bias = jnp.concatenate([key_projection_bias, value_projection_bias])
    bias = bias.astype(jnp.float32).reshape(1, -1)
    step = (far_lane, near_other, next_lane, swaps)
    step, turned, bounds, cosine, sine, seat_column, bias, owners = lax.optimization_barrier(
        (step, turned, bounds, cosine, sine, seat_column, bias, owners)
    )
    far_lane, near_other, next_lane, swaps = step
    matrices[1], matrices[2] = (near_lane, swaps[0]), (other_row, swaps[1])
    matrices[3] = (far_lane, send(far_lane, beside))
    matrices[4] = (next_lane, send(next_lane, beside))
    split_at = shard * 21 // 32 // 16 * 16
    below = shard - split_at
    top, rest = pl.pallas_call(
        functools.partial(cut_kernel, split_at),
        out_shape=(
            shape((split_at, wide), jnp.bfloat16),
            shape((2 * below, wide), jnp.bfloat16),
        ),
        in_specs=[HBM] * 3,
        out_specs=(VMEM,) * 2,
        scratch_shapes=[pltpu.SemaphoreType.DMA((3,))],
        compiler_params=grant(14),
        name="cut",
    )(far_lane, next_lane, near_other)
    top, rest, owners = lax.optimization_barrier((top, rest, owners))
    matrices[5] = (near_other, send(near_other, beside))
    far_top, both_rest, next_top = send(top, swap), send(rest, across), send(top, ring)
    total = add_part(add_part(None, (0, 1, 2)), (3, 4, 5))
    both_rest, far_top, next_top, total = lax.optimization_barrier(
        (both_rest, far_top, next_top, total)
    )
    arrays = [next_top, far_top, both_rest]
    arrays += [send(array, beside) for array in arrays]
    chips = [(source, source + ranks // 2) for source in (6, 7)]
    (pairs,) = pl.pallas_call(
        functools.partial(finish_kernel, chips),
        out_shape=tuple(
            shape((rows, 2 * heads * HEAD_SIZE), jnp.bfloat16) for _, heads in CHUNKS
        ),
        in_specs=[SMEM, HBM] + [VMEM] * (5 + len(arrays)),
        out_specs=(VMEM,) * len(CHUNKS),
        scratch_shapes=scratch(chips),
        compiler_params=grant(14),
        cost_estimate=product_cost(chips),
        name="finish",
    )(
        owners,
        hidden,
        bias,
        cosine,
        sine,
        bucket,
        *arrays,
        total,
    )

    blocks = {}
    sending = spread(pairs, ranks, blocks)
    next(sending)
    order = [source for sources in sets for source in sources]
    ordered = plan[:, :width][source_order(ranks, order)]
    key_routes = ordered[:, :rows].reshape(ranks, ranks, share).transpose(1, 0, 2)
    more_places = ordered[:, rows + listed :].reshape(ranks * listed, 1)
    veils = pl.pallas_call(
        functools.partial(veil_kernel, sets, stride),
        out_shape=tuple(
            shape((ranks, 2 * share * len(sources), HEAD_SIZE), jnp.bfloat16) for sources in sets
        ),
        in_specs=[VMEM] * 3,
        out_specs=(VMEM,) * len(sets),
        compiler_params=grant(14),
        cost_estimate=cost(3 * 10**9, 4 * ranks * rows * HEAD_SIZE),
        name="veil",
    )(
        bounds,
        key_routes.reshape(ranks, 1, rows),
        ordered[:, rows : rows + listed].reshape(1, ranks * listed),
    )

    def attend(state, index):
        sources, last = sets[index], index == len(sets) - 1
        starts = [tuple(first for first, _ in blocks[source]) for source in sources]
        arrays = [array for source in sources for _, array in blocks[source]]
        keys = 2 * share * len(sources)
        fixed = [more_places, turned, veils[index], *arrays, *state]
        kept = shape((KEY_VALUE_HEADS, ranks * packed, HEAD_SIZE), jnp.float32)
        outs = [kept] * 3
        out_specs = [VMEM] * 3
        in_specs = [VMEM, VMEM, HBM] + [VMEM] * (len(fixed) - 3)
        handed = {len(fixed) - 3 + at: at + last for at in range(3)} if state else {}
        scratch_shapes = [
            pltpu.VMEM((len(sources) * share, wide), jnp.bfloat16),
            pltpu.VMEM((packed, HEAD_SIZE), jnp.bfloat16),
            pltpu.VMEM((ranks, keys, HEAD_SIZE), jnp.bfloat16),
            pltpu.SemaphoreType.DMA,
        ]
        if last:
            fixed.append(seat_column)
            in_specs.append(VMEM)
            outs.insert(0, shape((rows, query_width), jnp.bfloat16))
            out_specs.insert(0, HBM)
            scratch_shapes += [
                pltpu.VMEM((ranks * stride, query_width), jnp.bfloat16),
                pltpu.VMEM((rows, query_width), jnp.bfloat16),
                pltpu.SemaphoreType.DMA((KEY_VALUE_HEADS,)),
            ]
        return pl.pallas_call(
            functools.partial(
                attend_kernel,
                starts,
                sum(len(one) for one in sets[:index]),
                spare,
                stride,
                bool(state),
                last,
            ),
            out_shape=tuple(outs),
            in_specs=in_specs,
            out_specs=tuple(out_specs),
            scratch_shapes=scratch_shapes,
            input_output_aliases=handed,
            compiler_params=grant(18 if last else 14),
            cost_estimate=cost(
                8 * ranks * KEY_VALUE_HEADS * packed * (keys + 256) * HEAD_SIZE,
                2 * keys * rows * HEAD_SIZE,
            ),
            name="attend",
        )(*fixed)

    state = ()
    for step in range(planes - 1):
        if step:
            next(sending)
        state = sending.send(tuple(attend(state, step)))
    next(sending)
    state = sending.send(tuple(attend(state, planes - 1)))
    return attend(state, planes)[0]


def apply_rotary(rows, slot_offset, heads):
    block_count = rows.shape[0]
    half = HEAD_SIZE // 2
    frequency = 1000000.0 ** (-(jnp.arange(half, dtype=jnp.float32) * 2.0 / HEAD_SIZE))
    angle = slot_offset.astype(jnp.float32)[:, None] * frequency[None, :]
    cosine = jnp.cos(angle)[:, None, :]
    sine = jnp.sin(angle)[:, None, :]
    grid = rows.astype(jnp.float32).reshape(block_count, heads, HEAD_SIZE)
    first = grid[:, :, :half]
    second = grid[:, :, half:]
    turned = jnp.concatenate(
        [first * cosine - second * sine, second * cosine + first * sine], axis=2
    )
    return turned.reshape(block_count, heads * HEAD_SIZE).astype(jnp.bfloat16)


def causal_block_attention(pieces):
    query_tile_rows, key_tile_rows, value_tile_rows, spot_block = pieces
    block_count = query_tile_rows.shape[0]
    head_groups = QUERY_HEADS // KEY_VALUE_HEADS
    query_block_grid = query_tile_rows.reshape(block_count, KEY_VALUE_HEADS, head_groups, HEAD_SIZE)
    key_block_grid = key_tile_rows.reshape(block_count, KEY_VALUE_HEADS, HEAD_SIZE)
    value_block_grid = value_tile_rows.reshape(block_count, KEY_VALUE_HEADS, HEAD_SIZE)
    scores = jnp.einsum(
        "qhgd,khd->hgqk", query_block_grid, key_block_grid, preferred_element_type=jnp.float32
    ) / math.sqrt(HEAD_SIZE)
    inner = jnp.arange(block_count, dtype=jnp.int32)
    visible = (inner[None, :] <= inner[:, None]) & (
        inner[None, :] >= inner[:, None] - spot_block[:, None]
    )
    scores = jnp.where(visible, scores, -jnp.inf)
    top = jnp.max(scores, axis=3, keepdims=True)
    weights = jnp.exp(scores - top)
    totals = jnp.sum(weights, axis=3)
    probs = weights.astype(jnp.bfloat16)
    mixed = jnp.einsum(
        "hgqk,khd->qhgd", probs, value_block_grid, preferred_element_type=jnp.float32
    )
    mixed = mixed / jnp.transpose(totals, (2, 0, 1))[:, :, :, None]
    return mixed.reshape(block_count, QUERY_HEADS * HEAD_SIZE).astype(jnp.bfloat16)


def add_projection(left, pieces):
    return (
        jnp.dot(left, pieces[0], preferred_element_type=jnp.float32),
        jnp.dot(left, pieces[1], preferred_element_type=jnp.float32),
    )


def project_own(hidden, key_matrix, value_matrix, key_projection_bias, value_projection_bias):
    totals = add_projection(
        hidden,
        (
            lax.all_gather(key_matrix, "dp", axis=0, tiled=True),
            lax.all_gather(value_matrix, "dp", axis=0, tiled=True),
        ),
    )
    key_rows = (totals[0] + key_projection_bias.astype(jnp.float32)).astype(jnp.bfloat16)
    value_rows = (totals[1] + value_projection_bias.astype(jnp.float32)).astype(jnp.bfloat16)
    return jnp.concatenate([key_rows, value_rows], axis=1)


def send_plan(
    hidden,
    queries,
    route,
    positions,
    key_matrix,
    value_matrix,
    key_projection_bias,
    value_projection_bias,
):
    ranks = lax.axis_size("dp")
    rows = hidden.shape[0]
    slots = positions.shape[0]
    spare = rows // ranks + 2
    width = ranks * spare
    paired_width = key_matrix.shape[1]
    target = route // slots
    place = route - target * slots
    member = (target[:, None] == jnp.arange(ranks, dtype=jnp.int32)[None, :]).astype(jnp.int32)
    order = jnp.sum(jnp.cumsum(member, axis=0) * member, axis=1) - 1
    bucket = target * spare + order
    outgoing = jnp.full((width,), slots, jnp.int32).at[bucket].set(place)
    arrived = lax.all_to_all(
        outgoing.reshape(ranks, spare), "dp", split_axis=0, concat_axis=0, tiled=True
    ).reshape(width)
    query_buf = jnp.zeros((width, queries.shape[1]), jnp.bfloat16).at[bucket].set(queries)
    own_pairs = project_own(
        hidden, key_matrix, value_matrix, key_projection_bias, value_projection_bias
    )
    pair_buf = jnp.zeros((width, 2 * paired_width), jnp.bfloat16).at[bucket].set(own_pairs)
    got_query, got_pairs = (
        lax.all_to_all(
            query_buf.reshape(ranks, spare, -1), "dp", split_axis=0, concat_axis=0, tiled=True
        ),
        lax.all_to_all(
            pair_buf.reshape(ranks, spare, -1), "dp", split_axis=0, concat_axis=0, tiled=True
        ),
    )
    got_query = got_query.reshape(width, -1)
    got_pairs = got_pairs.reshape(width, -1)
    query_slot_rows = (
        jnp.zeros((slots, got_query.shape[1]), jnp.bfloat16).at[arrived].set(got_query, mode="drop")
    )
    paired_slot_rows = (
        jnp.zeros((slots, 2 * paired_width), jnp.bfloat16).at[arrived].set(got_pairs, mode="drop")
    )
    query_turned = apply_rotary(query_slot_rows, positions, QUERY_HEADS)
    key_rotated = apply_rotary(paired_slot_rows[:, :paired_width], positions, KEY_VALUE_HEADS)
    block_list = slots // BLOCK_SLOTS
    attended = lax.map(
        causal_block_attention,
        (
            query_turned.reshape(block_list, BLOCK_SLOTS, -1),
            key_rotated.reshape(block_list, BLOCK_SLOTS, -1),
            paired_slot_rows[:, paired_width:].reshape(block_list, BLOCK_SLOTS, -1),
            positions.reshape(block_list, BLOCK_SLOTS),
        ),
    )
    attended = attended.reshape(slots, -1)
    leaving = attended[jnp.minimum(arrived, slots - 1)]
    returned = lax.all_to_all(
        leaving.reshape(ranks, spare, -1), "dp", split_axis=0, concat_axis=0, tiled=True
    ).reshape(width, -1)
    return returned[bucket]


def local(*args):
    hidden, queries, _, positions, key_matrix = args[:5]
    ranks = lax.axis_size("dp")
    rows = hidden.shape[0]
    gathered = ranks * ranks * (rows // ranks + 2) * 4 * key_matrix.shape[1]
    chip_rows = 2 * key_matrix.shape[0]
    fits = rows % (16 * ranks) == 0 and chip_rows % HEAD_SIZE == 0 and gathered <= GATHER_LIMIT
    if ranks == PLANES * PLANE and lax.axis_size("groups") == 2 and fits:
        return gather_plan(*args)
    return send_plan(*args)


def solution(mesh):
    placed = (
        P(("groups", "dp"), None),
        P(("groups", "dp"), None),
        P(("groups", "dp")),
        P(("groups", "dp")),
        P("dp", None),
        P("dp", None),
        P(),
        P(),
    )
    return jax.shard_map(
        local, mesh=mesh, in_specs=placed, out_specs=P(("groups", "dp"), None), check_vma=False
    )
```

```python
import functools
import math

import jax
import jax.numpy as jnp
import numpy as np
from jax import lax
from jax.experimental import pallas as pl
from jax.experimental.pallas import tpu as pltpu
from jax.sharding import PartitionSpec as P

QUERY_HEADS = 20
KEY_VALUE_HEADS = 4
HEAD_SIZE = 128
BLOCK_SLOTS = 512
HEAD_GROUPS = QUERY_HEADS // KEY_VALUE_HEADS
CHUNKS = ((0, KEY_VALUE_HEADS),)
PLANE = 4
PLANES = 4
CYCLE = (0, 2, 3, 1)
SAFE_POWER = 64.0
GATHER_LIMIT = 40 * 2**20
MASKED = -1e30
VMEM = pl.BlockSpec(memory_space=pltpu.VMEM)
SMEM = pl.BlockSpec(memory_space=pltpu.SMEM)
HBM = pl.BlockSpec(memory_space=pltpu.HBM)


def grant(mebibytes):
    return pltpu.CompilerParams(vmem_limit_bytes=mebibytes * 2**20)


def cost(flops, moved):
    return pl.CostEstimate(flops=flops, bytes_accessed=moved, transcendentals=0)


def one_hot_rows(count, index_row):
    rows = lax.broadcasted_iota(jnp.int32, (count, index_row.shape[1]), 0)
    return (rows == index_row).astype(jnp.float32).astype(jnp.bfloat16)


def split(number):
    high = lax.shift_right_logical(number, HEAD_SIZE.bit_length() - 1)
    return high, number - high * HEAD_SIZE


def contract(left, right, left_dim, right_dim):
    return lax.dot_general(
        left, right, (((left_dim,), (right_dim,)), ((), ())), preferred_element_type=jnp.float32
    )


def turn(rows, cosine, sine):
    return (rows * cosine + pltpu.roll(rows, HEAD_SIZE // 2, 1) * sine).astype(jnp.bfloat16)


def join_kernel(left_ref, right_ref, out_ref, done):
    wide = left_ref.shape[1]
    copies = [
        pltpu.make_async_copy(ref, out_ref.at[:, pl.ds(at * wide, wide)], done.at[at])
        for at, ref in enumerate((left_ref, right_ref))
    ]
    for copy in copies:
        copy.start()
    for copy in copies:
        copy.wait()


def cut_kernel(split_at, far_ref, next_ref, near_ref, top_ref, rest_ref, done):
    below = far_ref.shape[0] - split_at
    copies = [
        pltpu.make_async_copy(near_ref.at[pl.ds(0, split_at)], top_ref, done.at[0]),
        pltpu.make_async_copy(
            next_ref.at[pl.ds(split_at, below)], rest_ref.at[pl.ds(0, below)], done.at[1]
        ),
        pltpu.make_async_copy(
            far_ref.at[pl.ds(split_at, below)], rest_ref.at[pl.ds(below, below)], done.at[2]
        ),
    ]
    for copy in copies:
        copy.start()
    for copy in copies:
        copy.wait()


def order_kernel(
    ranks, slots, extra, stride, route_ref, bucket_ref, seat_ref, sorted_ref, more_ref
):
    route = route_ref[...]
    count = route.shape[1]
    share = count // ranks
    target = lax.div(route, slots)
    member = (lax.broadcasted_iota(jnp.int32, (ranks, count), 0) == target).astype(jnp.float32)
    before = lax.broadcasted_iota(jnp.int32, (count, count), 0) < lax.broadcasted_iota(
        jnp.int32, (count, count), 1
    )
    before = before.astype(jnp.float32).astype(jnp.bfloat16)
    ahead = contract(member.astype(jnp.bfloat16), before, 1, 0)
    order = jnp.sum(member * ahead, axis=0, keepdims=True).astype(jnp.int32)
    beyond = order >= share
    beyond_rows = jnp.broadcast_to(beyond.astype(jnp.float32), (8, count)).astype(jnp.bfloat16)
    number = contract(beyond_rows, before, 1, 0)[0:1]
    counts = jnp.sum(member, axis=1, keepdims=True)
    free = jnp.maximum(share - counts, 0.0)
    group = lax.broadcasted_iota(jnp.int32, (ranks, ranks), 0)
    lower = (group > lax.broadcasted_iota(jnp.int32, (ranks, ranks), 1)).astype(jnp.float32)
    free_rows = jnp.broadcast_to(free, (ranks, HEAD_SIZE)).astype(jnp.bfloat16)
    free_before = contract(lower.astype(jnp.bfloat16), free_rows, 1, 0)[:, 0:1]
    inside = (number >= free_before) & (number < free_before + free)
    base = lax.broadcasted_iota(jnp.int32, (ranks, 1), 0).astype(jnp.float32) * share + counts
    hole = jnp.sum(jnp.where(inside, base + number - free_before, 0.0), axis=0, keepdims=True)
    bucket = jnp.where(beyond, hole.astype(jnp.int32), target * share + order)
    bucket_ref[...] = bucket
    seat_ref[...] = target * stride + order
    high, low = split(route)
    place_high, place_low = split(bucket)
    line = lax.broadcasted_iota(jnp.int32, (8, count), 0)
    digits = jnp.where(line == 0, high, 0)
    digits = jnp.where(line == 1, low, digits)
    digits = jnp.where(line == 2, place_high, digits)
    digits = jnp.where(line == 3, place_low, digits)
    digits = jnp.where(line == 4, 1, digits).astype(jnp.float32).astype(jnp.bfloat16)
    placed = contract(digits, one_hot_rows(count, bucket), 1, 1)
    sorted_ref[...] = (placed[0:1] * HEAD_SIZE + placed[1:2]).astype(jnp.int32)
    listed = jnp.where(beyond, target * extra + order - share, -1)
    found = contract(digits, one_hot_rows(ranks * extra, listed), 1, 1)
    none = found[4:5] - 1.0
    more_ref[0:1] = (found[0:1] * HEAD_SIZE + found[1:2] + none).astype(jnp.int32)
    more_ref[1:2] = (found[2:3] * HEAD_SIZE + found[3:4] + none).astype(jnp.int32)


def query_kernel(
    ranks, spare, stride, packed, route_ref, seat_ref, positions_ref, frequency_ref, queries_ref, *refs
):
    turned_ref, bounds_ref, cosine_ref, sine_ref, column_ref, rows_ref = refs
    route = route_ref[...]
    count = route.shape[0]
    lines = positions_ref.shape[0]
    line, lane = split(route)
    pick = (lax.broadcasted_iota(jnp.int32, (count, lines), 1) == line).astype(jnp.float32)
    pick = pick.astype(jnp.bfloat16)
    positions = positions_ref[...]
    half = lax.shift_right_logical(positions, 1)
    rest = positions - half * 2
    rows = 2.0 * contract(pick, half.astype(jnp.float32).astype(jnp.bfloat16), 1, 0) + contract(
        pick, rest.astype(jnp.float32).astype(jnp.bfloat16), 1, 0
    )
    lanes = lax.broadcasted_iota(jnp.int32, (count, HEAD_SIZE), 1)
    spot = jnp.sum(jnp.where(lanes == lane, rows, 0.0), axis=1, keepdims=True)
    angle = spot * frequency_ref[...]
    cosine = jnp.cos(angle)
    sine = jnp.sin(angle)
    sine = jnp.where(lanes < HEAD_SIZE // 2, -sine, sine)
    cosine_ref[...] = cosine
    sine_ref[...] = sine
    seats = one_hot_rows(ranks * stride, seat_ref[...])
    seat_line, seat_lane = split(seat_ref[...])
    digit = lax.broadcasted_iota(jnp.int32, (8, count), 0)
    digits = jnp.where(digit == 0, seat_line, jnp.where(digit == 1, seat_lane, 0))
    same = one_hot_rows(count, lax.broadcasted_iota(jnp.int32, (1, count), 1))
    column = contract(same, digits.astype(jnp.float32).astype(jnp.bfloat16), 1, 1)
    column_ref[...] = (column[:, 0:1] * HEAD_SIZE + column[:, 1:2]).astype(jnp.int32)
    first = route - spot.astype(jnp.int32)
    first_line, first_lane = split(first)
    digits = jnp.where(lanes == 0, line, 0)
    digits = jnp.where(lanes == 1, lane, digits)
    digits = jnp.where(lanes == 2, first_line, digits)
    digits = jnp.where(lanes == 3, first_lane, digits)
    digits = jnp.where(lanes == 4, 1, digits)
    placed = contract(seats, digits.astype(jnp.float32).astype(jnp.bfloat16), 1, 0)
    live = placed[:, 4:5] - 1.0
    last = placed[:, 0:1] * HEAD_SIZE + placed[:, 1:2] + live
    start = placed[:, 2:3] * HEAD_SIZE + placed[:, 3:4] - live * 2.0**20
    seat_lanes = lax.broadcasted_iota(jnp.int32, placed.shape, 1)
    bounds_ref[...] = jnp.where(seat_lanes == 0, last, start).astype(jnp.int32)
    rows_ref[...] = jnp.zeros(rows_ref.shape, jnp.float32)
    for head in range(KEY_VALUE_HEADS):
        for place in range(HEAD_GROUPS):
            at = (head * HEAD_GROUPS + place) * HEAD_SIZE
            one = queries_ref[:, at : at + HEAD_SIZE].astype(jnp.float32)
            rows = contract(seats, turn(one, cosine, sine), 1, 0)
            for group in range(ranks):
                at = group * packed + place * spare
                rows_ref[at : at + spare] = rows[group * stride : group * stride + spare]
        turned_ref[head] = rows_ref[...].astype(jnp.bfloat16)


def fetch_columns(chips, owners_ref, hidden_ref, columns, done):
    deep = columns.shape[1] // len(chips)
    copies = []
    for place, chip in enumerate(chips):
        first = pl.multiple_of(lax.div(owners_ref[chip[0]], 2) * deep, HEAD_SIZE)
        copies.append(
            pltpu.make_async_copy(
                hidden_ref.at[:, pl.ds(first, deep)],
                columns.at[:, pl.ds(place * deep, deep)],
                done.at[place],
            )
        )
        copies[-1].start()
    return copies


def place_rows(owners_ref, chips, matrix):
    shard = matrix.shape[0] // len(chips) // 2
    return [
        pl.ds(pl.multiple_of((2 * place + lax.rem(owners_ref[source], 2)) * shard, 16), shard)
        for place, chip in enumerate(chips)
        for source in chip
    ]


def part_kernel(chips, more, owners_ref, hidden_ref, *refs):
    count = 2 * len(chips)
    parts, refs = refs[:count], refs[count:]
    if more:
        total_ref, refs = refs[0], refs[1:]
    out_ref, columns, matrix, done = refs
    copies = fetch_columns(chips, owners_ref, hidden_ref, columns, done)
    for at, (ref, rows) in enumerate(zip(parts, place_rows(owners_ref, chips, matrix))):
        copies.append(pltpu.make_async_copy(ref, matrix.at[rows], done.at[len(chips) + at]))
        copies[-1].start()
    for copy in copies:
        copy.wait()
    for first in range(0, out_ref.shape[1], 2 * HEAD_SIZE):
        span = slice(first, first + 2 * HEAD_SIZE)
        product = contract(columns[...], matrix[:, span], 1, 0)
        out_ref[:, span] = total_ref[:, span] + product if more else product


def finish_kernel(
    chips, owners_ref, hidden_ref, bias_ref, cosine_ref, sine_ref, bucket_ref, *refs
):
    count = 3 * len(chips)
    parts, total_ref = refs[:count], refs[count]
    outs, (columns, matrix, done) = refs[count + 1 : -3], refs[-3:]
    copies = fetch_columns(chips, owners_ref, hidden_ref, columns, done)
    split_at, below = parts[0].shape[0], parts[2].shape[0] // 2
    shard = split_at + below
    for side in range(2):
        rest = parts[3 * side + 2]
        for place, chip in enumerate(chips):
            first = (2 * place + lax.rem(owners_ref[chip[side]], 2)) * shard
            matrix[pl.ds(pl.multiple_of(first, 16), split_at)] = parts[3 * side + place][...]
            matrix[pl.ds(pl.multiple_of(first + split_at, 16), below)] = rest[
                place * below : (place + 1) * below
            ]
    places = one_hot_rows(outs[0].shape[0], bucket_ref[...])
    for copy in copies:
        copy.wait()
    wide = KEY_VALUE_HEADS * HEAD_SIZE
    for first in range(0, 2 * wide, 2 * HEAD_SIZE):
        span = slice(first, first + 2 * HEAD_SIZE)
        rows = contract(columns[...], matrix[:, span], 1, 0) + total_ref[:, span]
        rows = (rows + bias_ref[:, span]).astype(jnp.bfloat16)
        if first < wide:
            cosine, sine = cosine_ref[...], sine_ref[...]
            halves = [
                turn(rows[:, at : at + HEAD_SIZE].astype(jnp.float32), cosine, sine)
                for at in (0, HEAD_SIZE)
            ]
            rows = jnp.concatenate(halves, axis=1)
        rows = contract(places, rows, 1, 0).astype(jnp.bfloat16)
        for half in range(2):
            head = first % wide // HEAD_SIZE + half
            for (first_head, heads), out_ref in zip(CHUNKS, outs):
                if first_head <= head < first_head + heads:
                    at = (head - first_head + first // wide * heads) * HEAD_SIZE
                    out_ref[:, at : at + HEAD_SIZE] = rows[
                        :, half * HEAD_SIZE : (half + 1) * HEAD_SIZE
                    ]


def veil_kernel(sets, stride, bounds_ref, routes_ref, more_ref, *veil_refs):
    rest = jnp.zeros((HEAD_SIZE - stride, more_ref.shape[1]), jnp.float32)
    share = routes_ref.shape[2] // routes_ref.shape[0]

    def one_group(group, carry):
        seats = pl.ds(pl.multiple_of(group * stride, 16), stride)
        last, start = bounds_ref[seats, 0:1], bounds_ref[seats, 1:2]
        both = []
        for routes in (routes_ref[group], more_ref[...]):
            veil = jnp.where((routes <= last) & (routes >= start), 0.0, MASKED)
            veil = jnp.transpose(jnp.concatenate([veil, rest], axis=0))
            both.append(veil.astype(jnp.bfloat16))
        first = 0
        for sources, veil_ref in zip(sets, veil_refs):
            end = first + len(sources) * share
            veil_ref[group] = jnp.concatenate([veil[first:end] for veil in both], axis=0)
            first = end
        return carry

    lax.fori_loop(0, routes_ref.shape[0], one_group, 0)


def attend_kernel(starts, before, spare, stride, more, last, *refs):
    more_ref, queries_ref, veil_ref = refs[:3]
    refs = refs[3:]
    blocks = []
    for first_rows in starts:
        blocks.append(dict(zip(first_rows, refs)))
        refs = refs[len(first_rows) :]
    if more:
        top_ref, sum_ref, total_ref = refs[:3]
        refs = refs[3:]
    if last:
        seat_ref, out_ref, mixed_ref, result_ref, leave = refs[0], refs[1], *refs[-3:]
        refs = refs[:-3]
        mixed_ref[...] = jnp.zeros(mixed_ref.shape, jnp.bfloat16)
    else:
        new_top_ref, new_sum_ref, new_total_ref = refs[:3]
    listed_rows, seen_by, veil, veil_in = refs[-4:]
    fetch_veil = pltpu.make_async_copy(veil_ref, veil, veil_in)
    fetch_veil.start()
    heads, ranks = queries_ref.shape[0], veil_ref.shape[0]
    packed = queries_ref.shape[1] // ranks
    wide = heads * HEAD_SIZE
    share = listed_rows.shape[0] // len(starts)
    count = share * ranks

    token = lax.broadcasted_iota(jnp.int32, (packed, HEAD_SIZE), 0)
    lane = lax.broadcasted_iota(jnp.int32, (packed, HEAD_SIZE), 1)
    own = lane < 0
    for at in range(HEAD_GROUPS):
        own = own | ((token == lane + at * spare) & (lane < spare))
    seen_by[...] = own.astype(jnp.float32).astype(jnp.bfloat16)
    lines = lax.broadcasted_iota(jnp.int32, (share, count), 1)
    for at, block in enumerate(blocks):
        places = more_ref[(before + at) * share : (before + at + 1) * share]
        pick = (lines == places).astype(jnp.float32).astype(jnp.bfloat16)
        for first in range(0, 2 * wide, 2 * HEAD_SIZE):
            lanes = slice(first, first + 2 * HEAD_SIZE)
            found = [
                contract(pick[:, row : row + ref.shape[0]], ref[:, lanes], 1, 0)
                for row, ref in block.items()
            ]
            listed_rows[at * share : (at + 1) * share, lanes] = sum(found).astype(jnp.bfloat16)
    fetch_veil.wait()
    scale = math.log2(math.e) / math.sqrt(HEAD_SIZE)

    def rows_of(group, row, first):
        lanes = slice(first, first + HEAD_SIZE)
        window = pl.ds(pl.multiple_of(group * share - row, 16), share)
        rows = [block[row][window, lanes] for block in blocks]
        return jnp.concatenate(rows + [listed_rows[:, lanes]], axis=0)

    def scores_of(group, row, head, tokens):
        left = jnp.concatenate([queries_ref[head, tokens], seen_by[...]], axis=1)
        keys = rows_of(group, row, head * HEAD_SIZE)
        return contract(left, jnp.concatenate([keys, veil[group]], axis=1), 1, 1)

    def products_of(group, row, head, weight):
        values = rows_of(group, row, wide + head * HEAD_SIZE)
        values = jnp.concatenate([values, jnp.ones_like(values)], axis=1)
        mixed = contract(weight, values, 1, 0)
        return mixed[:, :HEAD_SIZE], mixed[:, HEAD_SIZE:]

    def tile(top, keys):
        return jnp.concatenate([top] * (keys // HEAD_SIZE), axis=1)

    def finish_head(group, head, total, weight_sum):
        mixed = total / weight_sum
        seats = pl.ds(pl.multiple_of(group * stride, 16), spare)
        for at in range(HEAD_GROUPS):
            place = (head * HEAD_GROUPS + at) * HEAD_SIZE
            rows = mixed[at * spare : (at + 1) * spare]
            mixed_ref[seats, place : place + HEAD_SIZE] = rows.astype(jnp.bfloat16)

    def add_heads(group, row, some):
        tokens = pl.ds(pl.multiple_of(group * packed, 16), packed)
        scores = [scores_of(group, row, head, tokens) for head in some]
        tops, weights = [], []
        for head, score in zip(some, scores):
            top = jnp.max(score, axis=1, keepdims=True)
            if more:
                top = jnp.maximum(top_ref[head, tokens], top)
            else:
                top = jnp.broadcast_to(top, (packed, HEAD_SIZE))
            tops.append(top)
            weight = jnp.exp2((score - tile(top, score.shape[1])) * scale)
            weights.append(weight.astype(jnp.bfloat16))
        for head, top, weight in zip(some, tops, weights):
            total, weight_sum = products_of(group, row, head, weight)
            if more:
                fade = jnp.exp2((top_ref[head, tokens] - top) * scale)
                total = total + fade * total_ref[head, tokens]
                weight_sum = weight_sum + fade * sum_ref[head, tokens]
            if last:
                finish_head(group, head, total, weight_sum)
            else:
                new_top_ref[head, tokens] = top
                new_sum_ref[head, tokens] = weight_sum
                new_total_ref[head, tokens] = total

    def add_heads_as_before(groups, row, worst):
        units = [
            (group, head, pl.ds(pl.multiple_of(group * packed, 16), packed))
            for group in groups
            for head in range(heads)
        ]
        scores = [scores_of(group, row, head, tokens) for group, head, tokens in units]
        weights = []
        for (group, head, tokens), score in zip(units, scores):
            above = score - tile(top_ref[head, tokens], score.shape[1])
            for first in range(0, score.shape[1], HEAD_SIZE):
                part = above[:, first : first + HEAD_SIZE].reshape(packed // 8, 8, HEAD_SIZE)
                worst = jnp.maximum(worst, jnp.max(part, axis=0))
            weights.append(jnp.exp2(above * scale).astype(jnp.bfloat16))
        for (group, head, tokens), weight in zip(units, weights):
            total, weight_sum = products_of(group, row, head, weight)
            total = total + total_ref[head, tokens]
            weight_sum = weight_sum + sum_ref[head, tokens]
            finish_head(group, head, total, weight_sum)
        return worst

    firsts = sorted({row for first_rows in starts for row in first_rows})
    spans = [
        (row, row // share, end // share) for row, end in zip(firsts, firsts[1:] + [count])
    ]

    def add_all(together):
        for row, first, end in spans:

            def one_group(group, carry, row=row):
                for head in range(0, heads, together):
                    add_heads(group, row, range(head, head + together))
                return carry

            lax.fori_loop(first, end, one_group, 0)

    if not last:
        add_all(heads)
        return
    worst = jnp.full((8, HEAD_SIZE), MASKED, jnp.float32)
    for row, first, end in spans:
        many = 2 if (end - first) % 2 == 0 else 1

        def some_groups(step, worst, row=row, first=first, many=many):
            groups = [first + step * many + at for at in range(many)]
            return add_heads_as_before(groups, row, worst)

        worst = lax.fori_loop(0, (end - first) // many, some_groups, worst)

    @pl.when(jnp.max(worst) * scale > SAFE_POWER)
    def _():
        add_all(1)

    seat_lanes = lax.broadcasted_iota(jnp.int32, (count, mixed_ref.shape[0]), 1)
    seats = (seat_lanes == seat_ref[...]).astype(jnp.float32).astype(jnp.bfloat16)
    span = HEAD_GROUPS * HEAD_SIZE
    leaving = []
    for head in range(heads):
        lanes = slice(head * span, (head + 1) * span)
        rows = contract(seats, mixed_ref[:, lanes], 1, 0)
        result_ref[:, lanes] = rows.astype(jnp.bfloat16)
        lanes = pl.ds(head * span, span)
        leaving.append(
            pltpu.make_async_copy(result_ref.at[:, lanes], out_ref.at[:, lanes], leave.at[head])
        )
        leaving[-1].start()
    for one in leaving:
        one.wait()


def spread(block, ranks, held):
    ring = ring_pairs(ranks)
    across = [(rank, rank ^ 2) for rank in range(ranks)]
    beside = [(rank, rank ^ 1) for rank in range(ranks)]
    steps = ranks // PLANE
    half = block.shape[0] // 32 * 16

    def keep(source, first, array):
        held.setdefault(source, []).append((first, array))
        held.setdefault(source + 2 * steps, []).append((first, lax.ppermute(array, "dp", beside)))

    lane, other = block, None
    for step in range(steps - 1):
        keep(step, 0, lane)
        if step:
            keep(steps + step - 1, 0, other)
        following = lax.ppermute(lane, "dp", across), lax.ppermute(lane, "dp", ring)
        extra = yield
        other, lane, extra = lax.optimization_barrier((*following, extra))
        yield extra
    keep(steps - 1, 0, lane)
    keep(2 * steps - 2, 0, other)
    over = lax.ppermute(lane[:half], "dp", across)
    around = lax.ppermute(other[half:], "dp", ring)
    extra = yield other
    over, around, extra = lax.optimization_barrier((over, around, extra))
    keep(2 * steps - 1, 0, over)
    keep(2 * steps - 1, half, around)
    yield extra


def ring_pairs(ranks, back=False):
    pairs = []
    for rank in range(ranks):
        at = CYCLE.index(rank // PLANE) + (-1 if back else 1)
        pairs.append((rank, CYCLE[at % PLANES] * PLANE + rank % PLANE))
    return pairs


def pick(table, index):
    return sum(jnp.where(index == at, number, 0) for at, number in enumerate(table))


def block_owners(steps, flips):
    me = lax.axis_index("dp")
    lane, plane = lax.rem(me, PLANE), lax.div(me, PLANE)
    place = pick([CYCLE.index(at) for at in range(PLANES)], plane)
    return pick(CYCLE, (place + PLANES - steps) % PLANES) * PLANE + (lane ^ flips)


def source_order(ranks, sources):
    steps = np.array([source % PLANES for source in sources], np.int32)
    flips = np.array([(0, 2, 1, 3)[source // PLANES] for source in sources], np.int32)
    return block_owners(steps, flips)


def weight_order(ranks):
    up = np.array([0, 1, 0, PLANES - 1, 2, 1, 2, PLANES - 1] * 2, np.int32)
    steps = jnp.where(lax.axis_index("groups") == 1, (PLANES - up) % PLANES, up)
    flips = np.array([0, 0, 2, 0, 0, 2, 2, 2], np.int32)
    return block_owners(steps, np.concatenate([flips, flips ^ 1]))


def gather_plan(
    hidden,
    queries,
    route,
    positions,
    key_matrix,
    value_matrix,
    key_projection_bias,
    value_projection_bias,
):
    ranks = lax.axis_size("dp")
    rows = hidden.shape[0]
    slots = positions.shape[0]
    share, extra = rows // ranks, 2
    spare = share + extra
    listed = ranks * extra
    stride = -(-spare // 16) * 16
    packed = -(-HEAD_GROUPS * spare // 16) * 16
    query_width = queries.shape[1]
    shape = jax.ShapeDtypeStruct

    def columns(array, chunk):
        first, heads = chunk
        return array[..., first * HEAD_SIZE : (first + heads) * HEAD_SIZE]

    joined = pl.pallas_call(
        join_kernel,
        out_shape=shape((key_matrix.shape[0], 2 * key_matrix.shape[1]), jnp.bfloat16),
        in_specs=[HBM] * 2,
        out_specs=VMEM,
        scratch_shapes=[pltpu.SemaphoreType.DMA((2,))],
        compiler_params=grant(56),
        name="join",
    )(key_matrix, value_matrix)
    every = [(group, rank) for group in range(2) for rank in range(ranks)]
    ring = [
        (group * ranks + rank, group * ranks + after)
        for group in range(2)
        for rank, after in ring_pairs(ranks, group == 1)
    ]
    across = [(group * ranks + rank, group * ranks + (rank ^ 2)) for group, rank in every]
    beside = [(group * ranks + rank, group * ranks + (rank ^ 1)) for group, rank in every]
    swap = [(group * ranks + rank, (1 - group) * ranks + rank) for group, rank in every]

    def send(array, pairs):
        return lax.ppermute(array, ("groups", "dp"), pairs)

    joined_swap = send(joined, beside)
    other_row, near_lane = send(joined, across), send(joined, ring)
    bucket, seat, sorted_route, more = pl.pallas_call(
        functools.partial(order_kernel, ranks, slots, extra, stride),
        out_shape=(
            shape((1, rows), jnp.int32),
            shape((1, rows), jnp.int32),
            shape((1, rows), jnp.int32),
            shape((2, listed), jnp.int32),
        ),
        in_specs=[VMEM],
        out_specs=(VMEM,) * 4,
        compiler_params=grant(14),
        name="order",
    )(route.reshape(1, rows))
    width = rows + 2 * listed
    plan = jnp.concatenate([sorted_route.reshape(rows), more.reshape(2 * listed), positions])
    plan = lax.all_to_all(
        jnp.broadcast_to(plan, (ranks, width + slots)), "dp", split_axis=0, concat_axis=0, tiled=True
    )
    other_row, near_lane, joined_swap, plan, bucket, seat = lax.optimization_barrier(
        (other_row, near_lane, joined_swap, plan, bucket, seat)
    )
    matrices = {0: (joined, joined_swap)}
    swaps = send(near_lane, beside), send(other_row, beside)
    far_lane, near_other = send(near_lane, swap), send(near_lane, across)
    next_lane = send(near_lane, ring)
    all_positions = plan[:, width:].reshape(-1, HEAD_SIZE)
    planes = ranks // PLANE
    sets = [(0, 2 * planes)] + [
        (step, step + 2 * planes, step + planes - 1, step + 3 * planes - 1)
        for step in range(1, planes)
    ]
    sets.append((2 * planes - 1, 4 * planes - 1))
    owners = weight_order(ranks)

    half = HEAD_SIZE // 2
    frequency = 1000000.0 ** (-(jnp.arange(half, dtype=jnp.float32) * 2.0 / HEAD_SIZE))
    turned, bounds, cosine, sine, seat_column = pl.pallas_call(
        functools.partial(query_kernel, ranks, spare, stride, packed),
        out_shape=(
            shape((KEY_VALUE_HEADS, ranks * packed, HEAD_SIZE), jnp.bfloat16),
            shape((ranks * stride, HEAD_SIZE), jnp.int32),
            shape((rows, HEAD_SIZE), jnp.float32),
            shape((rows, HEAD_SIZE), jnp.float32),
            shape((rows, 1), jnp.int32),
        ),
        in_specs=[VMEM] * 5,
        out_specs=(VMEM,) * 5,
        scratch_shapes=[pltpu.VMEM((ranks * packed, HEAD_SIZE), jnp.float32)],
        compiler_params=grant(14),
        cost_estimate=cost(4 * stride * ranks * rows * query_width, 4 * rows * query_width),
        name="turn_queries",
    )(
        route.reshape(rows, 1),
        seat,
        all_positions,
        jnp.concatenate([frequency, frequency]).reshape(1, HEAD_SIZE),
        queries,
    )

    shard, wide = key_matrix.shape[0], 2 * key_matrix.shape[1]

    def chip_parts(sources):
        chips = [(source, source + ranks // 2) for source in sources]
        return chips, [array for source in sources for array in matrices[source]]

    def scratch(chips):
        return [
            pltpu.VMEM((rows, 2 * shard * len(chips)), jnp.bfloat16),
            pltpu.VMEM((2 * shard * len(chips), wide), jnp.bfloat16),
            pltpu.SemaphoreType.DMA((3 * len(chips),)),
        ]

    def product_cost(chips):
        depth = 2 * shard * len(chips)
        return cost(2 * rows * depth * wide, 2 * depth * (rows + wide) + 8 * rows * wide)

    def add_part(total, sources):
        chips, arrays = chip_parts(sources)
        more = [] if total is None else [total]
        return pl.pallas_call(
            functools.partial(part_kernel, chips, bool(more)),
            out_shape=shape((rows, wide), jnp.float32),
            in_specs=[SMEM] + [HBM] * (1 + len(arrays)) + [VMEM] * len(more),
            out_specs=VMEM,
            scratch_shapes=scratch(chips),
            compiler_params=grant(14),
            cost_estimate=product_cost(chips),
            name="add_part",
        )(owners, hidden, *arrays, *more)

    bias = jnp.concatenate([key_projection_bias, value_projection_bias])
    bias = bias.astype(jnp.float32).reshape(1, -1)
    step = (far_lane, near_other, next_lane, swaps)
    step, turned, bounds, cosine, sine, seat_column, bias, owners = lax.optimization_barrier(
        (step, turned, bounds, cosine, sine, seat_column, bias, owners)
    )
    far_lane, near_other, next_lane, swaps = step
    matrices[1], matrices[2] = (near_lane, swaps[0]), (other_row, swaps[1])
    matrices[3] = (far_lane, send(far_lane, beside))
    matrices[4] = (next_lane, send(next_lane, beside))
    split_at = shard * 21 // 32 // 16 * 16
    below = shard - split_at
    top, rest = pl.pallas_call(
        functools.partial(cut_kernel, split_at),
        out_shape=(
            shape((split_at, wide), jnp.bfloat16),
            shape((2 * below, wide), jnp.bfloat16),
        ),
        in_specs=[HBM] * 3,
        out_specs=(VMEM,) * 2,
        scratch_shapes=[pltpu.SemaphoreType.DMA((3,))],
        compiler_params=grant(14),
        name="cut",
    )(far_lane, next_lane, near_other)
    top, rest, owners = lax.optimization_barrier((top, rest, owners))
    matrices[5] = (near_other, send(near_other, beside))
    far_top, both_rest, next_top = send(top, swap), send(rest, across), send(top, ring)
    total = add_part(add_part(None, (0, 1, 2)), (3, 4, 5))
    both_rest, far_top, next_top, total = lax.optimization_barrier(
        (both_rest, far_top, next_top, total)
    )
    arrays = [next_top, far_top, both_rest]
    arrays += [send(array, beside) for array in arrays]
    chips = [(source, source + ranks // 2) for source in (6, 7)]
    (pairs,) = pl.pallas_call(
        functools.partial(finish_kernel, chips),
        out_shape=tuple(
            shape((rows, 2 * heads * HEAD_SIZE), jnp.bfloat16) for _, heads in CHUNKS
        ),
        in_specs=[SMEM, HBM] + [VMEM] * (5 + len(arrays)),
        out_specs=(VMEM,) * len(CHUNKS),
        scratch_shapes=scratch(chips),
        compiler_params=grant(14),
        cost_estimate=product_cost(chips),
        name="finish",
    )(
        owners,
        hidden,
        bias,
        cosine,
        sine,
        bucket,
        *arrays,
        total,
    )

    blocks = {}
    sending = spread(pairs, ranks, blocks)
    next(sending)
    order = [source for sources in sets for source in sources]
    ordered = plan[:, :width][source_order(ranks, order)]
    key_routes = ordered[:, :rows].reshape(ranks, ranks, share).transpose(1, 0, 2)
    more_places = ordered[:, rows + listed :].reshape(ranks * listed, 1)
    veils = pl.pallas_call(
        functools.partial(veil_kernel, sets, stride),
        out_shape=tuple(
            shape((ranks, 2 * share * len(sources), HEAD_SIZE), jnp.bfloat16) for sources in sets
        ),
        in_specs=[VMEM] * 3,
        out_specs=(VMEM,) * len(sets),
        compiler_params=grant(14),
        cost_estimate=cost(3 * 10**9, 4 * ranks * rows * HEAD_SIZE),
        name="veil",
    )(
        bounds,
        key_routes.reshape(ranks, 1, rows),
        ordered[:, rows : rows + listed].reshape(1, ranks * listed),
    )

    def attend(state, index):
        sources, last = sets[index], index == len(sets) - 1
        starts = [tuple(first for first, _ in blocks[source]) for source in sources]
        arrays = [array for source in sources for _, array in blocks[source]]
        keys = 2 * share * len(sources)
        fixed = [more_places, turned, veils[index], *arrays, *state]
        kept = shape((KEY_VALUE_HEADS, ranks * packed, HEAD_SIZE), jnp.float32)
        outs = [kept] * 3
        out_specs = [VMEM] * 3
        in_specs = [VMEM, VMEM, HBM] + [VMEM] * (len(fixed) - 3)
        handed = {len(fixed) - 3 + at: at + last for at in range(3)} if state else {}
        scratch_shapes = [
            pltpu.VMEM((len(sources) * share, wide), jnp.bfloat16),
            pltpu.VMEM((packed, HEAD_SIZE), jnp.bfloat16),
            pltpu.VMEM((ranks, keys, HEAD_SIZE), jnp.bfloat16),
            pltpu.SemaphoreType.DMA,
        ]
        if last:
            fixed.append(seat_column)
            in_specs.append(VMEM)
            outs.insert(0, shape((rows, query_width), jnp.bfloat16))
            out_specs.insert(0, HBM)
            scratch_shapes += [
                pltpu.VMEM((ranks * stride, query_width), jnp.bfloat16),
                pltpu.VMEM((rows, query_width), jnp.bfloat16),
                pltpu.SemaphoreType.DMA((KEY_VALUE_HEADS,)),
            ]
        return pl.pallas_call(
            functools.partial(
                attend_kernel,
                starts,
                sum(len(one) for one in sets[:index]),
                spare,
                stride,
                bool(state),
                last,
            ),
            out_shape=tuple(outs),
            in_specs=in_specs,
            out_specs=tuple(out_specs),
            scratch_shapes=scratch_shapes,
            input_output_aliases=handed,
            compiler_params=grant(18 if last else 14),
            cost_estimate=cost(
                8 * ranks * KEY_VALUE_HEADS * packed * (keys + 256) * HEAD_SIZE,
                2 * keys * rows * HEAD_SIZE,
            ),
            name="attend",
        )(*fixed)

    state = ()
    for step in range(planes - 1):
        if step:
            next(sending)
        state = sending.send(tuple(attend(state, step)))
    next(sending)
    state = sending.send(tuple(attend(state, planes - 1)))
    return attend(state, planes)[0]


def apply_rotary(rows, slot_offset, heads):
    block_count = rows.shape[0]
    half = HEAD_SIZE // 2
    frequency = 1000000.0 ** (-(jnp.arange(half, dtype=jnp.float32) * 2.0 / HEAD_SIZE))
    angle = slot_offset.astype(jnp.float32)[:, None] * frequency[None, :]
    cosine = jnp.cos(angle)[:, None, :]
    sine = jnp.sin(angle)[:, None, :]
    grid = rows.astype(jnp.float32).reshape(block_count, heads, HEAD_SIZE)
    first = grid[:, :, :half]
    second = grid[:, :, half:]
    turned = jnp.concatenate(
        [first * cosine - second * sine, second * cosine + first * sine], axis=2
    )
    return turned.reshape(block_count, heads * HEAD_SIZE).astype(jnp.bfloat16)


def causal_block_attention(pieces):
    query_tile_rows, key_tile_rows, value_tile_rows, spot_block = pieces
    block_count = query_tile_rows.shape[0]
    head_groups = QUERY_HEADS // KEY_VALUE_HEADS
    query_block_grid = query_tile_rows.reshape(block_count, KEY_VALUE_HEADS, head_groups, HEAD_SIZE)
    key_block_grid = key_tile_rows.reshape(block_count, KEY_VALUE_HEADS, HEAD_SIZE)
    value_block_grid = value_tile_rows.reshape(block_count, KEY_VALUE_HEADS, HEAD_SIZE)
    scores = jnp.einsum(
        "qhgd,khd->hgqk", query_block_grid, key_block_grid, preferred_element_type=jnp.float32
    ) / math.sqrt(HEAD_SIZE)
    inner = jnp.arange(block_count, dtype=jnp.int32)
    visible = (inner[None, :] <= inner[:, None]) & (
        inner[None, :] >= inner[:, None] - spot_block[:, None]
    )
    scores = jnp.where(visible, scores, -jnp.inf)
    top = jnp.max(scores, axis=3, keepdims=True)
    weights = jnp.exp(scores - top)
    totals = jnp.sum(weights, axis=3)
    probs = weights.astype(jnp.bfloat16)
    mixed = jnp.einsum(
        "hgqk,khd->qhgd", probs, value_block_grid, preferred_element_type=jnp.float32
    )
    mixed = mixed / jnp.transpose(totals, (2, 0, 1))[:, :, :, None]
    return mixed.reshape(block_count, QUERY_HEADS * HEAD_SIZE).astype(jnp.bfloat16)


def add_projection(left, pieces):
    return (
        jnp.dot(left, pieces[0], preferred_element_type=jnp.float32),
        jnp.dot(left, pieces[1], preferred_element_type=jnp.float32),
    )


def project_own(hidden, key_matrix, value_matrix, key_projection_bias, value_projection_bias):
    totals = add_projection(
        hidden,
        (
            lax.all_gather(key_matrix, "dp", axis=0, tiled=True),
            lax.all_gather(value_matrix, "dp", axis=0, tiled=True),
        ),
    )
    key_rows = (totals[0] + key_projection_bias.astype(jnp.float32)).astype(jnp.bfloat16)
    value_rows = (totals[1] + value_projection_bias.astype(jnp.float32)).astype(jnp.bfloat16)
    return jnp.concatenate([key_rows, value_rows], axis=1)


def send_plan(
    hidden,
    queries,
    route,
    positions,
    key_matrix,
    value_matrix,
    key_projection_bias,
    value_projection_bias,
):
    ranks = lax.axis_size("dp")
    rows = hidden.shape[0]
    slots = positions.shape[0]
    spare = rows // ranks + 2
    width = ranks * spare
    paired_width = key_matrix.shape[1]
    target = route // slots
    place = route - target * slots
    member = (target[:, None] == jnp.arange(ranks, dtype=jnp.int32)[None, :]).astype(jnp.int32)
    order = jnp.sum(jnp.cumsum(member, axis=0) * member, axis=1) - 1
    bucket = target * spare + order
    outgoing = jnp.full((width,), slots, jnp.int32).at[bucket].set(place)
    arrived = lax.all_to_all(
        outgoing.reshape(ranks, spare), "dp", split_axis=0, concat_axis=0, tiled=True
    ).reshape(width)
    query_buf = jnp.zeros((width, queries.shape[1]), jnp.bfloat16).at[bucket].set(queries)
    own_pairs = project_own(
        hidden, key_matrix, value_matrix, key_projection_bias, value_projection_bias
    )
    pair_buf = jnp.zeros((width, 2 * paired_width), jnp.bfloat16).at[bucket].set(own_pairs)
    got_query, got_pairs = (
        lax.all_to_all(
            query_buf.reshape(ranks, spare, -1), "dp", split_axis=0, concat_axis=0, tiled=True
        ),
        lax.all_to_all(
            pair_buf.reshape(ranks, spare, -1), "dp", split_axis=0, concat_axis=0, tiled=True
        ),
    )
    got_query = got_query.reshape(width, -1)
    got_pairs = got_pairs.reshape(width, -1)
    query_slot_rows = (
        jnp.zeros((slots, got_query.shape[1]), jnp.bfloat16).at[arrived].set(got_query, mode="drop")
    )
    paired_slot_rows = (
        jnp.zeros((slots, 2 * paired_width), jnp.bfloat16).at[arrived].set(got_pairs, mode="drop")
    )
    query_turned = apply_rotary(query_slot_rows, positions, QUERY_HEADS)
    key_rotated = apply_rotary(paired_slot_rows[:, :paired_width], positions, KEY_VALUE_HEADS)
    block_list = slots // BLOCK_SLOTS
    attended = lax.map(
        causal_block_attention,
        (
            query_turned.reshape(block_list, BLOCK_SLOTS, -1),
            key_rotated.reshape(block_list, BLOCK_SLOTS, -1),
            paired_slot_rows[:, paired_width:].reshape(block_list, BLOCK_SLOTS, -1),
            positions.reshape(block_list, BLOCK_SLOTS),
        ),
    )
    attended = attended.reshape(slots, -1)
    leaving = attended[jnp.minimum(arrived, slots - 1)]
    returned = lax.all_to_all(
        leaving.reshape(ranks, spare, -1), "dp", split_axis=0, concat_axis=0, tiled=True
    ).reshape(width, -1)
    return returned[bucket]


def local(*args):
    hidden, queries, _, positions, key_matrix = args[:5]
    ranks = lax.axis_size("dp")
    rows = hidden.shape[0]
    gathered = ranks * ranks * (rows // ranks + 2) * 4 * key_matrix.shape[1]
    chip_rows = 2 * key_matrix.shape[0]
    fits = rows % (16 * ranks) == 0 and chip_rows % HEAD_SIZE == 0 and gathered <= GATHER_LIMIT
    if ranks == PLANES * PLANE and lax.axis_size("groups") == 2 and fits:
        return gather_plan(*args)
    return send_plan(*args)


def solution(mesh):
    placed = (
        P(("groups", "dp"), None),
        P(("groups", "dp"), None),
        P(("groups", "dp")),
        P(("groups", "dp")),
        P("dp", None),
        P("dp", None),
        P(),
        P(),
    )
    return jax.shard_map(
        local, mesh=mesh, in_specs=placed, out_specs=P(("groups", "dp"), None), check_vma=False
    )
```
